32 devices in a mesh: region: 4 (over z), col: 8 (over y, x, core).
Axes of the slice: x: 2, y: 2, z: 4, core: 2. Of those that a mesh axis runs over, the one named last changes fastest.
Arguments:
- forcing: float32 [3, 256, 1024], P(None, 'region', 'col'), may hold values from 0.05 to 3
- river_storage: float32 [256, 1024], P('region', 'col'), may hold values from 0.1 to 4
- river_rate: float32 [256, 1024], P('region', 'col'), may hold values from 0.2 to 0.9
- flow_code: int32 [256, 1024], P('region', 'col'), may hold values from 1 to 128, as said below
- home_slot: int32 [32, 1024], P(('region', 'col')), may hold values from -1 to 1023, as said below
- home_offset: int32 [32, 1024], P(('region', 'col')), may hold values from 0 to 8184, as said below
- worker_list: int32 [15360], P(('region', 'col')), may hold values from 0 to 1023, as said below
- patch_cell: int32 [15360, 128], P(('region', 'col')), may hold values from 0 to 63, as said below
- patch_area: float32 [15360, 128], P(('region', 'col')), may hold values from 0.02 to 0.3
- canopy_water: float32 [15360, 128], P(('region', 'col')), may hold values from 0 to 1
- canopy_cap: float32 [15360, 128], P(('region', 'col')), may hold values from 0.1 to 2
- soil_water: float32 [15, 15360, 128], P(None, ('region', 'col')), may hold values from 0.05 to 0.5
- porosity: float32 [15, 15360, 128], P(None, ('region', 'col')), may hold values from 0.3 to 0.55
- drainage: float32 [15, 15360, 128], P(None, ('region', 'col')), may hold values from 0.02 to 0.8
Outputs:
- soil_new: float32 [15, 15360, 128], P(None, ('region', 'col'))
- canopy_new: float32 [15360, 128], P(('region', 'col'))
- cell_runoff: float32 [256, 1024], P('region', 'col')
- cell_evap: float32 [256, 1024], P('region', 'col')
- river_new: float32 [256, 1024], P('region', 'col')
The draws below stay inside these ranges and needn't reach their ends.
Inputs may be any that keep to these rules, and one draw needn't show every extreme that they name: `home_slot`: A home's live block slots come first and hold w * 32 + k (worker w, position k), distinct within the home; -1 marks unused slots. A home has 1024, 512, 256 or 128 live blocks, each for a quarter of the homes; at most 32 of one home's blocks go to one worker, and the busiest homes send exactly 32 to every worker. `worker_list`: every slot of every worker holds a live block; h * 32 + k at block b of worker w means home_slot[h, j] = w * 32 + k for exactly one j. `home_offset`: the first home cell of a live block, row-major over the home's cells; 0 for unused slots. Offset plus patch_cell stays below 8192. `patch_cell`: never falling along a block. `flow_code`: One-hot D8 codes as in the reference program.
All inputs are finite; a program needn't handle non-finite values.
Results may differ from the reference program's by a relative error of at most 0.000073.
Values sent between devices are 32-bit elements; how exact they have to be, the bound alone decides.
No kernel may reach another device: no remote copies, remote signals or barrier semaphores. Data moves between devices by JAX's collectives and lax.ppermute only.
A program may use at most 64 MiB of HBM per device.

```python
import math
import jax
import jax.numpy as jnp
from jax import lax

LAYERS = 15
CR = 64
CC = 128
HB = 1024
ITERS = 4
CAP = 32
WB = 480
BLOCKS = 15360
NR = 256
NC = 1024
N_REGION = 4
N_COL = 8


def plan_tables(key):
    home_count = N_REGION * N_COL
    order = jax.random.permutation(jax.random.fold_in(key, 11), home_count).astype(jnp.int32)
    rank = jnp.zeros((home_count,), jnp.int32).at[order].set(jnp.arange(home_count, dtype=jnp.int32))
    rank = (rank - rank[home_count - 1] + home_count) % home_count
    divisor = jnp.array([1, 2, 4, 8], jnp.int32)[rank % 4]
    live_count = (HB // divisor).astype(jnp.int32)
    first = (jnp.cumsum(live_count) - live_count).astype(jnp.int32)
    slot_index = jnp.arange(HB, dtype=jnp.int32)[None, :]
    live_slot = slot_index < live_count[:, None]
    global_index = first[:, None] + slot_index
    worker = global_index % home_count
    worker_slot = global_index // home_count
    position = slot_index // home_count
    home_slot = jnp.where(live_slot, worker * CAP + position, -1).astype(jnp.int32)
    offset = jnp.where(live_slot, slot_index * (CR * CC) // live_count[:, None], 0).astype(jnp.int32)
    span_end = (slot_index + 1) * (CR * CC) // live_count[:, None]
    span = jnp.where(live_slot, span_end - offset, 1).astype(jnp.int32)
    target = jnp.where(live_slot, worker * WB + worker_slot, home_count * WB).reshape(-1)
    home_ids = jnp.broadcast_to(jnp.arange(home_count, dtype=jnp.int32)[:, None], (home_count, HB))
    worker_list = jnp.zeros((BLOCKS,), jnp.int32).at[target].set((home_ids * CAP + position).reshape(-1), mode='drop')
    block_span = jnp.ones((BLOCKS,), jnp.int32).at[target].set(span.reshape(-1), mode='drop')
    return (home_slot, offset, worker_list, block_span)


def draw_home_slot(key, part):
    return plan_tables(key)[0]


def draw_home_offset(key, part):
    return plan_tables(key)[1]


def draw_worker_list(key, part):
    return plan_tables(key)[2]


def draw_patch_cell(key, part):
    block_span = plan_tables(key)[3]
    coins = jax.random.randint(jax.random.fold_in(key, 23), (BLOCKS, 128), 0, 128)
    advance = (coins < block_span[:, None]).astype(jnp.int32)
    advance = advance.at[:, 0].set(0)
    cells = jnp.minimum(jnp.cumsum(advance, axis=1), block_span[:, None] - 1)
    cells = cells.at[:, 127].set(block_span - 1)
    return cells.astype(jnp.int32)


def draw_flow_code(key, part):
    powers = jax.random.randint(jax.random.fold_in(key, 31), (NR, NC), 0, 8)
    return jnp.left_shift(jnp.ones((NR, NC), jnp.int32), powers.astype(jnp.int32))


def block_scale(stream_key, extent, split, low, largest):
    def one(dim, blocks):
        steps = jax.random.uniform(jax.random.fold_in(jax.random.fold_in(stream_key, 6), dim), (blocks,), jnp.float32, low / len(split), largest / len(split))
        return jnp.repeat(jnp.exp(steps), extent[dim] // blocks).reshape((-1,) + (1,) * (len(extent) - dim - 1))

    gain = one(*split[0])
    for cut in split[1:]:
        gain = gain * one(*cut)
    return gain


def setup_inputs(seed: int = 0) -> dict:
    keys = jax.random.split(jax.random.key(seed), 15)
    forcing = jnp.clip(jnp.exp(math.log(3.0) - 4.0943445 * jax.random.uniform(keys[0], (3, NR, NC), jnp.float32) ** block_scale(keys[0], (3, NR, NC), ((1, 4), (2, 8)), -0.2, 0.2)), 0.05, 3.0)
    river_storage = jnp.clip(jnp.exp(math.log(4.0) - 3.6888794 * jax.random.uniform(keys[1], (NR, NC), jnp.float32) ** block_scale(keys[1], (NR, NC), ((0, 4), (1, 8)), -0.2, 0.2)), 0.1, 4.0)
    river_rate = jnp.clip(0.2 + 0.7 * jax.random.uniform(keys[2], (NR, NC), jnp.float32) ** block_scale(keys[2], (NR, NC), ((0, 4), (1, 8)), -0.2, 0.2), 0.2, 0.9)
    flow_code = draw_flow_code(jax.random.fold_in(keys[14], 71), 0)
    home_slot = draw_home_slot(jax.random.fold_in(keys[14], 71), 0)
    home_offset = draw_home_offset(jax.random.fold_in(keys[14], 71), 0)
    worker_list = draw_worker_list(jax.random.fold_in(keys[14], 71), 0)
    patch_cell = draw_patch_cell(jax.random.fold_in(keys[14], 71), 0)
    patch_area = jnp.clip(0.02 + 0.28 * jax.random.uniform(keys[8], (BLOCKS, 128), jnp.float32) ** block_scale(keys[8], (BLOCKS, 128), ((0, 32),), -0.2, 0.2), 0.02, 0.3)
    canopy_water = jnp.clip(1.0 * jax.random.uniform(keys[9], (BLOCKS, 128), jnp.float32) ** block_scale(keys[9], (BLOCKS, 128), ((0, 32),), -0.2, 0.2), 0.0, 1.0)
    canopy_cap = jnp.clip(jnp.exp(math.log(2.0) - 2.9957323 * jax.random.uniform(keys[10], (BLOCKS, 128), jnp.float32) ** block_scale(keys[10], (BLOCKS, 128), ((0, 32),), -0.2, 0.2)), 0.1, 2.0)
    soil_water = jnp.clip(0.05 + 0.45 * jax.random.uniform(keys[11], (LAYERS, BLOCKS, 128), jnp.float32) ** block_scale(keys[11], (LAYERS, BLOCKS, 128), ((1, 32),), -0.2, 0.2), 0.05, 0.5)
    porosity = jnp.clip(0.3 + 0.25 * jax.random.uniform(keys[12], (LAYERS, BLOCKS, 128), jnp.float32) ** block_scale(keys[12], (LAYERS, BLOCKS, 128), ((1, 32),), -0.2, 0.2), 0.3, 0.55)
    drainage = jnp.clip(jnp.exp(math.log(0.8) - 3.6888795 * jax.random.uniform(keys[13], (LAYERS, BLOCKS, 128), jnp.float32) ** block_scale(keys[13], (LAYERS, BLOCKS, 128), ((1, 32),), -0.2, 0.2)), 0.02, 0.8)
    return dict(forcing=forcing, river_storage=river_storage, river_rate=river_rate, flow_code=flow_code, home_slot=home_slot, home_offset=home_offset, worker_list=worker_list, patch_cell=patch_cell, patch_area=patch_area, canopy_water=canopy_water, canopy_cap=canopy_cap, soil_water=soil_water, porosity=porosity, drainage=drainage)


directions = ((0, 1), (1, 1), (1, 0), (1, -1), (0, -1), (-1, -1), (-1, 0), (-1, 1))


def inflow_from(out_pad, code_pad):
    inner_rows = out_pad.shape[0] - 2
    inner_cols = out_pad.shape[1] - 2
    arriving = jnp.zeros((inner_rows, inner_cols), jnp.float32)
    for code_bit, (row_step, col_step) in enumerate(directions):
        leaving_cell = jnp.where(code_pad == (1 << code_bit), out_pad, jnp.float32(0.0))
        arriving = arriving + leaving_cell[1 - row_step:1 - row_step + inner_rows, 1 - col_step:1 - col_step + inner_cols]
    return arriving


def layer_pass(state_in, layer_in):
    flowing, surface = state_in
    content, pore_room, drain_rate = layer_in
    filled = content + flowing
    excess = jnp.maximum(filled - pore_room, 0.0)
    filled = filled - excess
    drained = drain_rate * filled
    return (drained, surface + excess), filled - drained


def land_step(rainfall, demand, soil_demand, canopy_water, canopy_cap, soil_water, porosity, drainage):
    wetted = canopy_water + rainfall
    through = jnp.maximum(wetted - canopy_cap, 0.0)
    retained = jnp.minimum(wetted, canopy_cap)
    canopy_loss = jnp.minimum(demand, retained)
    canopy_new = retained - canopy_loss
    (bottom, surface), soil_mid = lax.scan(layer_pass, (through, jnp.zeros_like(through)), (soil_water, porosity, drainage))
    soil_loss = jnp.minimum(jnp.minimum(soil_demand, demand - canopy_loss), 0.5 * soil_mid[0])
    soil_new = soil_mid.at[0].add(-soil_loss)
    return canopy_new, soil_new, surface + bottom, canopy_loss + soil_loss


def reference(forcing, river_storage, river_rate, flow_code, home_slot, home_offset, worker_list, patch_cell, patch_area, canopy_water, canopy_cap, soil_water, porosity, drainage):
    home_count = N_REGION * N_COL
    cell_count = CR * CC
    source_home = worker_list // CAP
    position = worker_list % CAP
    worker_ids = jnp.arange(BLOCKS, dtype=jnp.int32) // WB
    pair_slot = worker_ids * CAP + position
    live_slot = home_slot >= 0
    home_rows = jnp.broadcast_to(jnp.arange(home_count, dtype=jnp.int32)[:, None], home_slot.shape)
    offset_table = jnp.zeros((home_count, HB), jnp.int32).at[home_rows, jnp.where(live_slot, home_slot, HB)].set(home_offset, mode="drop")
    block_offset = offset_table[source_home, pair_slot]
    patch_index = block_offset[:, None] + patch_cell
    home_of_patch = jnp.broadcast_to(source_home[:, None], patch_cell.shape)
    forcing_home = forcing.reshape(3, N_REGION, CR, N_COL, CC).transpose(0, 1, 3, 2, 4).reshape(3, home_count, cell_count)
    rainfall = forcing_home[0][home_of_patch, patch_index]
    demand = forcing_home[1][home_of_patch, patch_index]
    soil_demand = forcing_home[2][home_of_patch, patch_index]
    canopy_new, soil_new, runoff, transpired = land_step(rainfall, demand, soil_demand, canopy_water, canopy_cap, soil_water, porosity, drainage)
    runoff_home = jnp.zeros((home_count, cell_count), jnp.float32).at[home_of_patch, patch_index].add(patch_area * runoff)
    evap_home = jnp.zeros((home_count, cell_count), jnp.float32).at[home_of_patch, patch_index].add(patch_area * transpired)
    cell_runoff = runoff_home.reshape(N_REGION, N_COL, CR, CC).transpose(0, 2, 1, 3).reshape(NR, NC)
    cell_evap = evap_home.reshape(N_REGION, N_COL, CR, CC).transpose(0, 2, 1, 3).reshape(NR, NC)
    storage = river_storage + cell_runoff
    code_pad = jnp.pad(flow_code, 1)
    for sweep_index in range(ITERS):
        outflow = river_rate * storage
        storage = storage - outflow + inflow_from(jnp.pad(outflow, 1), code_pad)
    return soil_new, canopy_new, cell_runoff, cell_evap, storage
```

```python
import functools

import jax
import jax.numpy as jnp
from jax import lax
from jax.experimental import pallas as pl
from jax.experimental.pallas import tpu as pltpu
from jax.sharding import PartitionSpec as P

ITERS = 4
WINDOW = 64
LANES = 128
MIB = 1024 * 1024

directions = ((0, 1), (1, 1), (1, 0), (1, -1), (0, -1), (-1, -1), (-1, 0), (-1, 1))
axes = ("region", "col")


def iota(shape, dim):
    return lax.broadcasted_iota(jnp.int32, shape, dim)


def onehot(mask):
    return jnp.where(mask, jnp.float32(1.0), jnp.float32(0.0)).astype(jnp.bfloat16)


def lane_pick(values, index):
    return jnp.take_along_axis(values, index, axis=1, mode="promise_in_bounds")


def thirds(value):
    high = value.astype(jnp.bfloat16)
    rest = value - high.astype(jnp.float32)
    middle = rest.astype(jnp.bfloat16)
    low = (rest - middle.astype(jnp.float32)).astype(jnp.bfloat16)
    return high, middle, low


def matmul(a, b, a_dim=1, b_dim=0):
    return lax.dot_general(
        a, b, (((a_dim,), (b_dim,)), ((), ())), preferred_element_type=jnp.float32
    )


def slot_factors(slot, offset, homes, capacity):
    slots = slot.shape[1]
    worker = slot // capacity if capacity & (capacity - 1) else slot >> (capacity.bit_length() - 1)
    position = slot - worker * capacity
    by_worker = onehot(iota((homes, slots), 0) == worker)
    at_position = iota((capacity, slots), 0) == position
    row = jnp.where(at_position, ((offset >> 7) + 1).astype(jnp.float32), 0.0)
    lane = jnp.where(at_position, (offset & 127).astype(jnp.float32), 0.0)
    return by_worker, row.astype(jnp.bfloat16), lane.astype(jnp.bfloat16)


def slot_columns(slot, offset, homes, capacity):
    slots = slot.shape[1]
    by_worker, row, lane = slot_factors(slot, offset, homes, capacity)
    table = matmul(by_worker, jnp.concatenate([row, lane], axis=0), 1, 1)
    spread = jnp.broadcast_to(table[:, None, :], (homes, capacity, 2 * capacity))
    spread = spread.reshape(slots, 2 * capacity)
    place = iota(spread.shape, 0) % capacity == iota(spread.shape, 1) % capacity
    kept = jnp.where(place, spread, 0.0).astype(jnp.bfloat16)
    shape = (2 * capacity, 2 * LANES)
    gather = onehot((iota(shape, 0) >= capacity) == (iota(shape, 1) >= LANES))
    columns = matmul(kept, gather).astype(jnp.int32)
    return columns[:, :LANES] - 1, columns[:, LANES:]


def pack_kernel(homes, capacity, slot, offset, forcing, rain_out, loss_out, row_of, lane_of, rain):
    slots = slot.shape[1]
    lane_rows = forcing.shape[1]
    row_of[...], lane_of[...] = slot_columns(slot[...], offset[...], homes, capacity)
    parts = []
    for var in range(3):
        here = forcing[var]
        following = jnp.concatenate([here[1:], here[:1]], axis=0)
        parts += [here, following]
    table = jnp.concatenate(thirds(jnp.concatenate(parts, axis=1)), axis=0)
    chunk = 128
    for start in range(0, slots, chunk):
        row = row_of[pl.ds(start, chunk), :]
        lane = lane_of[pl.ds(start, chunk), :]
        shape = (chunk, 3 * lane_rows)
        wide = jnp.concatenate([row, row], axis=1)[:, : 3 * lane_rows]
        pick = onehot(wide == iota(shape, 1) % lane_rows)
        rows = matmul(pick, table)
        here = iota((chunk, LANES), 1)
        after = here >= lane
        joined = [
            jnp.where(
                after,
                rows[:, 2 * var * LANES : (2 * var + 1) * LANES],
                rows[:, (2 * var + 1) * LANES : (2 * var + 2) * LANES],
            )
            for var in range(3)
        ]
        first = (here + lane) & 127
        second = (first + WINDOW) & 127
        odd = iota((chunk, LANES), 0) & 1 == 1
        rain[pl.ds(start, chunk), :] = lane_pick(joined[0], jnp.where(odd, second, first))
        loss_out[pl.ds(start, chunk), :] = jnp.where(
            here < WINDOW, lane_pick(joined[1], first), lane_pick(joined[2], second)
        )
    even_rows = rain[pl.ds(0, slots // 2, stride=2), :]
    odd_rows = rain[pl.ds(1, slots // 2, stride=2), :]
    rain_out[...] = jnp.where(iota(even_rows.shape, 1) < WINDOW, even_rows, odd_rows)


def pack(homes, capacity, slot, offset, forcing):
    slots = slot.shape[1]
    return pl.pallas_call(
        functools.partial(pack_kernel, homes, capacity),
        out_shape=(
            jax.ShapeDtypeStruct((slots // 2, LANES), jnp.float32),
            jax.ShapeDtypeStruct((slots, LANES), jnp.float32),
        ),
        scratch_shapes=[
            pltpu.VMEM((slots, LANES), jnp.int32),
            pltpu.VMEM((slots, LANES), jnp.int32),
            pltpu.VMEM((slots, LANES), jnp.float32),
        ],
        compiler_params=pltpu.CompilerParams(vmem_limit_bytes=24 * MIB),
        cost_estimate=pl.CostEstimate(flops=10**9, bytes_accessed=2 * MIB, transcendentals=0),
        name="pack_forcing",
    )(slot, offset, forcing)


def unpack_plan_kernel(homes, capacity, lane_rows, slot, offset, code_out, place_out, code):
    slots = slot.shape[1]
    row, lane = slot_columns(slot[...], offset[...], homes, capacity)
    here = iota((slots, LANES), 1)
    index = (here - lane) & 127
    inside = (index < WINDOW) & (row >= 0)
    half = (iota((slots, LANES), 0) & 1) * WINDOW
    code[...] = jnp.where(inside, index + half + jnp.where(here >= lane, 0, LANES), -1)
    code_out[pl.ds(0, slots // 2), :] = code[pl.ds(0, slots // 2, stride=2), :]
    code_out[pl.ds(slots // 2, slots // 2), :] = code[pl.ds(1, slots // 2, stride=2), :]
    by_worker, start_row, _ = slot_factors(slot[...], offset[...], homes, capacity)
    table = matmul(start_row, by_worker, 1, 1).astype(jnp.bfloat16)
    number = iota((1, slots), 1)
    number = jnp.where(number < slots // 2, 2 * number, 2 * number - slots + 1)
    worker = number // capacity
    spread = matmul(table, onehot(iota((homes, slots), 0) == worker))
    position = number - worker * capacity
    kept = jnp.where(iota((capacity, slots), 0) == position, spread, 0.0)
    row_lane = jnp.sum(kept, axis=0, keepdims=True).astype(jnp.int32) - 1
    place_out[...] = onehot(iota((lane_rows, slots), 0) == row_lane)


def unpack_plan(homes, capacity, lane_rows, slot, offset):
    slots = slot.shape[1]
    return pl.pallas_call(
        functools.partial(unpack_plan_kernel, homes, capacity, lane_rows),
        out_shape=(
            jax.ShapeDtypeStruct((slots, LANES), jnp.int32),
            jax.ShapeDtypeStruct((lane_rows, slots), jnp.bfloat16),
        ),
        scratch_shapes=[pltpu.VMEM((slots, LANES), jnp.int32)],
        compiler_params=pltpu.CompilerParams(vmem_limit_bytes=24 * MIB),
        cost_estimate=pl.CostEstimate(flops=10**9, bytes_accessed=2 * MIB, transcendentals=0),
        name="unpack_plan",
    )(slot, offset)


def unpack_kernel(arrived, code, place, *rest):
    half_slots = arrived.shape[0]
    lane_rows = place.shape[0]
    pieces = []
    for half in range(2):
        marks = code[pl.ds(half * half_slots, half_slots), :]
        window = jnp.where(marks >= 0, lane_pick(arrived[...], marks & 127), 0.0)
        pieces.append(
            jnp.concatenate(
                [jnp.where(marks < LANES, window, 0.0), jnp.where(marks >= LANES, window, 0.0)],
                axis=1,
            )
        )
    placed = jnp.concatenate(pieces, axis=0)
    totals = matmul(place[...], jnp.concatenate(thirds(placed), axis=1))
    totals = totals[:, :256] + totals[:, 256:512] + totals[:, 512:]
    over = totals[:, LANES:]
    over = jnp.concatenate([over[lane_rows - 1 :], over[: lane_rows - 1]], axis=0)
    over = jnp.where(iota(over.shape, 0) == 0, 0.0, over)
    result = totals[:, :LANES] + over
    if len(rest) == 1:
        rest[0][...] = result
    else:
        river, out, storage = rest
        out[...] = result
        storage[...] = river[...] + result


def unpack(arrived, code, place, river=None):
    shape = jax.ShapeDtypeStruct((place.shape[0], LANES), jnp.float32)
    return pl.pallas_call(
        unpack_kernel,
        out_shape=shape if river is None else (shape, shape),
        compiler_params=pltpu.CompilerParams(vmem_limit_bytes=24 * MIB),
        cost_estimate=pl.CostEstimate(flops=10**9, bytes_accessed=1 * MIB, transcendentals=0),
        name="unpack_cells",
    )(*((arrived, code, place) + (() if river is None else (river,))))


def segment_plan_kernel(cell, worker, meta):
    values = cell[...]
    here = iota(values.shape, 1)
    target = here & (WINDOW - 1)
    count = jnp.zeros_like(values)
    for step in (64, 32, 16, 8, 4, 2, 1):
        probe = lane_pick(values, count + (step - 1))
        count = jnp.where(probe <= target, count + step, count)
    count = jnp.where(lane_pick(values, count) <= target, count + 1, count)
    last = jnp.maximum(count - 1, 0)
    half = (worker[...] & 1) == 1
    mine = (here >= WINDOW) == half
    found = (count > 0) & (lane_pick(values, last) == target) & mine
    marks = jnp.where(found, last + 128, 0)
    for bit in range(7):
        step = 1 << bit
        same = (pltpu.roll(values, step, 1) == values) & (here >= step)
        marks = marks + jnp.where(same, 256 << bit, 0)
    meta[...] = marks


def segment_plan(cell, worker):
    rows = cell.shape[0]
    block = 32
    return pl.pallas_call(
        segment_plan_kernel,
        grid=(rows // block,),
        in_specs=[
            pl.BlockSpec((block, LANES), lambda i: (i, 0)),
            pl.BlockSpec((block, 1), lambda i: (i, 0)),
        ],
        out_specs=pl.BlockSpec((block, LANES), lambda i: (i, 0)),
        out_shape=jax.ShapeDtypeStruct(cell.shape, jnp.int32),
        compiler_params=pltpu.CompilerParams(vmem_limit_bytes=24 * MIB),
        cost_estimate=pl.CostEstimate(flops=10**8, bytes_accessed=1 * MIB, transcendentals=0),
        name="segment_plan",
    )(cell, worker)


def segment_totals(values, marks):
    total = values
    for bit in range(7):
        moved = pltpu.roll(total, 1 << bit, 1)
        total = total + jnp.where((marks & (256 << bit)) != 0, moved, 0.0)
    return jnp.where((marks & 128) != 0, lane_pick(total, marks & 127), 0.0)


def hand_back(worker_list, base, count, rows, out):
    here = iota((1, LANES), 1)

    def one(i, carry):
        slot = worker_list[base + i]
        mine = (here >= WINDOW) == ((slot & 1) == 1)
        pltpu.store(out.at[pl.ds(slot >> 1, 1), :], rows[pl.ds(i, 1), :], mask=mine)
        return carry

    lax.fori_loop(0, count, one, 0, unroll=8)


def soil_kernel(
    worker_list, rain, worker, cell, meta, area, water, cap, soil, porosity, drainage,
    soil_mid, kept, runoff_out, fetched, totals,
):
    layers, block = soil.shape[:2]
    base = pl.program_id(0) * block

    @pl.when(pl.program_id(0) == 0)
    def _():
        runoff_out[...] = jnp.zeros_like(runoff_out)

    def fetch(i, carry):
        fetched[pl.ds(i, 1), :] = rain[pl.ds(worker_list[base + i] >> 1, 1), :]
        return carry

    lax.fori_loop(0, block, fetch, 0, unroll=8)
    chunk = 32
    for start in range(0, block, chunk):
        part = pl.ds(start, chunk)
        index = cell[part, :] + (worker[part, :] & 1) * WINDOW
        wetted = water[part, :] + lane_pick(fetched[part, :], index)
        flowing = jnp.maximum(wetted - cap[part, :], 0.0)
        kept[part, :] = jnp.minimum(wetted, cap[part, :])
        surface = jnp.zeros_like(flowing)
        for layer in range(layers):
            filled = soil[layer, part, :] + flowing
            excess = jnp.maximum(filled - porosity[layer, part, :], 0.0)
            surface = surface + excess
            filled = filled - excess
            flowing = drainage[layer, part, :] * filled
            soil_mid[layer, part, :] = filled - flowing
        runoff = surface + flowing
        totals[part, :] = segment_totals(area[part, :] * runoff, meta[part, :])
    hand_back(worker_list, base, block, totals, runoff_out)


def soil_step(worker_list, rain, worker, cell, meta, area, water, cap, soil, porosity, drainage):
    layers, rows = soil.shape[:2]
    block = 96
    flat = pl.BlockSpec((block, LANES), lambda i, _: (i, 0))
    deep = pl.BlockSpec((layers, block, LANES), lambda i, _: (0, i, 0))
    whole = pl.BlockSpec(rain.shape, lambda i, _: (0, 0))
    column = pl.BlockSpec((block, 1), lambda i, _: (i, 0))
    return pl.pallas_call(
        soil_kernel,
        grid_spec=pltpu.PrefetchScalarGridSpec(
            num_scalar_prefetch=1,
            grid=(rows // block,),
            in_specs=[whole, column, flat, flat, flat, flat, flat, deep, deep, deep],
            out_specs=[deep, flat, whole],
            scratch_shapes=[
                pltpu.VMEM((block, LANES), jnp.float32),
                pltpu.VMEM((block, LANES), jnp.float32),
            ],
        ),
        out_shape=(
            jax.ShapeDtypeStruct(soil.shape, jnp.float32),
            jax.ShapeDtypeStruct((rows, LANES), jnp.float32),
            jax.ShapeDtypeStruct(rain.shape, jnp.float32),
        ),
        compiler_params=pltpu.CompilerParams(vmem_limit_bytes=24 * MIB),
        cost_estimate=pl.CostEstimate(flops=10**8, bytes_accessed=18 * MIB, transcendentals=0),
        name="soil_layers",
    )(worker_list, rain, worker, cell, meta, area, water, cap, soil, porosity, drainage)


def loss_kernel(
    worker_list, loss, cell, meta, area, kept, soil_mid, soil_new, canopy_new, evap_out,
    fetched, totals,
):
    block = cell.shape[0]
    base = pl.program_id(0) * block

    @pl.when(pl.program_id(0) == 0)
    def _():
        evap_out[...] = jnp.zeros_like(evap_out)

    def fetch(i, carry):
        fetched[pl.ds(i, 1), :] = loss[pl.ds(worker_list[base + i], 1), :]
        return carry

    lax.fori_loop(0, block, fetch, 0, unroll=8)
    chunk = 32
    for start in range(0, block, chunk):
        part = pl.ds(start, chunk)
        index = cell[part, :]
        windows = fetched[part, :]
        demand = lane_pick(windows, index)
        limit = lane_pick(windows, index + WINDOW)
        retained = kept[part, :]
        canopy_loss = jnp.minimum(demand, retained)
        canopy_new[part, :] = retained - canopy_loss
        top = soil_mid[0, part, :]
        soil_loss = jnp.minimum(jnp.minimum(limit, demand - canopy_loss), 0.5 * top)
        soil_new[0, part, :] = top - soil_loss
        transpired = canopy_loss + soil_loss
        totals[part, :] = segment_totals(area[part, :] * transpired, meta[part, :])
    hand_back(worker_list, base, block, totals, evap_out)


def loss_step(worker_list, loss, cell, meta, area, kept, soil_mid):
    rows = cell.shape[0]
    block = 96
    flat = pl.BlockSpec((block, LANES), lambda i, _: (i, 0))
    top = pl.BlockSpec((1, block, LANES), lambda i, _: (0, i, 0))
    whole = pl.BlockSpec(loss.shape, lambda i, _: (0, 0))
    packed = (loss.shape[0] // 2, LANES)
    return pl.pallas_call(
        loss_kernel,
        grid_spec=pltpu.PrefetchScalarGridSpec(
            num_scalar_prefetch=1,
            grid=(rows // block,),
            in_specs=[whole, flat, flat, flat, flat, top],
            out_specs=[top, flat, pl.BlockSpec(packed, lambda i, _: (0, 0))],
            scratch_shapes=[
                pltpu.VMEM((block, LANES), jnp.float32),
                pltpu.VMEM((block, LANES), jnp.float32),
            ],
        ),
        out_shape=(
            jax.ShapeDtypeStruct(soil_mid.shape, jnp.float32),
            jax.ShapeDtypeStruct((rows, LANES), jnp.float32),
            jax.ShapeDtypeStruct(packed, jnp.float32),
        ),
        input_output_aliases={6: 0},
        compiler_params=pltpu.CompilerParams(vmem_limit_bytes=24 * MIB),
        cost_estimate=pl.CostEstimate(flops=10**8, bytes_accessed=3 * MIB, transcendentals=0),
        name="canopy_and_top_layer",
    )(worker_list, loss, cell, meta, area, kept, soil_mid)


def halo_parts(value, axis, dim, width):
    count, length = (lax.axis_size(axis), value.shape[dim])
    up = [(i, i + 1) for i in range(count - 1)]
    down = [(j, i) for i, j in up]
    last = lax.slice_in_dim(value, length - width, length, axis=dim)
    initial = lax.slice_in_dim(value, 0, width, axis=dim)
    return lax.ppermute(last, axis, up), lax.ppermute(initial, axis, down)


def with_halo(value, width):
    rows, cols = value.ndim - 2, value.ndim - 1
    before, after = halo_parts(value, "region", rows, width)
    tall = jnp.concatenate([value, after, before], axis=rows)
    before, after = halo_parts(tall, "col", cols, width)
    gap = jnp.zeros(tall.shape[:-1] + (LANES - 2 * width,), value.dtype)
    return jnp.concatenate([tall, after, gap, before], axis=cols)


def river_kernel(state, fixed, out):
    storage = state[...]
    rate = fixed[0]
    code = fixed[1]
    rows, cols = storage.shape
    for _ in range(ITERS):
        outflow = rate * storage
        inflow = jnp.zeros_like(storage)
        for col_step in (-1, 0, 1):
            column = jnp.zeros_like(storage)
            for bit, (row_step, step) in enumerate(directions):
                if step != col_step:
                    continue
                leaving = jnp.where(code == float(1 << bit), outflow, 0.0)
                if row_step:
                    leaving = pltpu.roll(leaving, row_step % rows, 0)
                column = column + leaving
            if col_step:
                column = pltpu.roll(column, col_step % cols, 1)
            inflow = inflow + column
        storage = storage - outflow + inflow
    out[...] = storage[: out.shape[0], : out.shape[1]]


def river(state, fixed, shape):
    return pl.pallas_call(
        river_kernel,
        out_shape=jax.ShapeDtypeStruct(shape, jnp.float32),
        compiler_params=pltpu.CompilerParams(vmem_limit_bytes=24 * MIB),
        cost_estimate=pl.CostEstimate(flops=10**7, bytes_accessed=1 * MIB, transcendentals=0),
        name="river_steps",
    )(state, fixed)


def exchange(value):
    return lax.all_to_all(value, axes, split_axis=0, concat_axis=0, tiled=True)


def shards(
    forcing,
    river_storage,
    river_rate,
    flow_code,
    home_slot,
    home_offset,
    worker_list,
    patch_cell,
    patch_area,
    canopy_water,
    canopy_cap,
    soil_water,
    porosity,
    drainage,
):
    homes = lax.axis_size("region") * lax.axis_size("col")
    capacity = home_slot.shape[1] // homes
    grid_rows, grid_cols = river_storage.shape
    lane_rows = grid_rows * grid_cols // LANES
    rain_out, loss_out = pack(
        homes, capacity, home_slot, home_offset, forcing.reshape(3, lane_rows, LANES)
    )
    rain = exchange(rain_out)
    loss = exchange(loss_out)
    worker = worker_list[:, None]
    meta = segment_plan(patch_cell, worker)
    code, place = unpack_plan(homes, capacity, lane_rows, home_slot, home_offset)
    fixed = with_halo(jnp.stack([river_rate, flow_code.astype(jnp.float32)]), ITERS)
    soil_mid, kept, runoff_rows = soil_step(
        worker_list, rain, worker, patch_cell, meta, patch_area, canopy_water, canopy_cap,
        soil_water, porosity, drainage,
    )
    runoff_back = exchange(runoff_rows)
    soil_new, canopy_new, evap_rows = loss_step(
        worker_list, loss, patch_cell, meta, patch_area, kept, soil_mid
    )
    evap_back = exchange(evap_rows)
    cell_runoff, storage = unpack(
        runoff_back, code, place, river_storage.reshape(lane_rows, LANES)
    )
    river_new = river(with_halo(storage, ITERS), fixed, river_storage.shape)
    cell_evap = unpack(evap_back, code, place)
    return (
        soil_new,
        canopy_new,
        cell_runoff.reshape(river_storage.shape),
        cell_evap.reshape(river_storage.shape),
        river_new,
    )


def solution(mesh):
    placed = (
        P(None, "region", "col"),
        P("region", "col"),
        P("region", "col"),
        P("region", "col"),
        P(("region", "col"), None),
        P(("region", "col"), None),
        P(("region", "col")),
        P(("region", "col"), None),
        P(("region", "col"), None),
        P(("region", "col"), None),
        P(("region", "col"), None),
        P(None, ("region", "col"), None),
        P(None, ("region", "col"), None),
        P(None, ("region", "col"), None),
    )
    return jax.shard_map(
        shards,
        mesh=mesh,
        in_specs=placed,
        out_specs=(
            P(None, ("region", "col"), None),
            P(("region", "col"), None),
            P("region", "col"),
            P("region", "col"),
            P("region", "col"),
        ),
        check_vma=False,
    )
```

```python
import functools

import jax
import jax.numpy as jnp
from jax import lax
from jax.experimental import pallas as pl
from jax.experimental.pallas import tpu as pltpu
from jax.sharding import PartitionSpec as P

ITERS = 4
WINDOW = 64
LANES = 128
MIB = 1024 * 1024

directions = ((0, 1), (1, 1), (1, 0), (1, -1), (0, -1), (-1, -1), (-1, 0), (-1, 1))
axes = ("region", "col")


def iota(shape, dim):
    return lax.broadcasted_iota(jnp.int32, shape, dim)


def onehot(mask):
    return jnp.where(mask, jnp.float32(1.0), jnp.float32(0.0)).astype(jnp.bfloat16)


def lane_pick(values, index):
    return jnp.take_along_axis(values, index, axis=1, mode="promise_in_bounds")


def thirds(value):
    high = value.astype(jnp.bfloat16)
    rest = value - high.astype(jnp.float32)
    middle = rest.astype(jnp.bfloat16)
    low = (rest - middle.astype(jnp.float32)).astype(jnp.bfloat16)
    return high, middle, low


def matmul(a, b, a_dim=1, b_dim=0):
    return lax.dot_general(
        a, b, (((a_dim,), (b_dim,)), ((), ())), preferred_element_type=jnp.float32
    )


def slot_factors(slot, offset, homes, capacity):
    slots = slot.shape[1]
    worker = slot // capacity if capacity & (capacity - 1) else slot >> (capacity.bit_length() - 1)
    position = slot - worker * capacity
    by_worker = onehot(iota((homes, slots), 0) == worker)
    at_position = iota((capacity, slots), 0) == position
    row = jnp.where(at_position, ((offset >> 7) + 1).astype(jnp.float32), 0.0)
    lane = jnp.where(at_position, (offset & 127).astype(jnp.float32), 0.0)
    return by_worker, row.astype(jnp.bfloat16), lane.astype(jnp.bfloat16)


def slot_columns(slot, offset, homes, capacity):
    slots = slot.shape[1]
    by_worker, row, lane = slot_factors(slot, offset, homes, capacity)
    table = matmul(by_worker, jnp.concatenate([row, lane], axis=0), 1, 1)
    spread = jnp.broadcast_to(table[:, None, :], (homes, capacity, 2 * capacity))
    spread = spread.reshape(slots, 2 * capacity)
    place = iota(spread.shape, 0) % capacity == iota(spread.shape, 1) % capacity
    kept = jnp.where(place, spread, 0.0).astype(jnp.bfloat16)
    shape = (2 * capacity, 2 * LANES)
    gather = onehot((iota(shape, 0) >= capacity) == (iota(shape, 1) >= LANES))
    columns = matmul(kept, gather).astype(jnp.int32)
    return columns[:, :LANES] - 1, columns[:, LANES:]


def slot_rows(slot, offset, homes, capacity):
    slots = slot.shape[1]
    by_worker, row, lane = slot_factors(slot, offset, homes, capacity)
    table = matmul(jnp.concatenate([row, lane], axis=0), by_worker, 1, 1).astype(jnp.bfloat16)
    number = iota((1, slots), 1)
    worker = number // capacity
    position = number - worker * capacity
    spread = matmul(table, onehot(iota((homes, slots), 0) == worker))
    at_position = iota((capacity, slots), 0) == position
    rows = jnp.sum(jnp.where(at_position, spread[:capacity], 0.0), axis=0, keepdims=True)
    lanes = jnp.sum(jnp.where(at_position, spread[capacity:], 0.0), axis=0, keepdims=True)
    return rows.astype(jnp.int32) - 1, lanes.astype(jnp.int32)


def home_kernel(homes, capacity, slot, offset, forcing, out):
    lane_rows = forcing.shape[1]
    slots = slot.shape[1]
    for var in range(3):
        out[pl.ds(var, lane_rows, stride=3), :] = forcing[var]
    row, lane = slot_rows(slot[...], offset[...], homes, capacity)
    first = (jnp.maximum(row, 0) * LANES + lane).astype(jnp.float32)
    for part in range(slots // LANES):
        out[pl.ds(3 * lane_rows + part, 1), :] = first[:, part * LANES : (part + 1) * LANES]


def home_rows(homes, capacity, slot, offset, forcing):
    rows = 3 * forcing.shape[1] + slot.shape[1] // LANES
    return pl.pallas_call(
        functools.partial(home_kernel, homes, capacity),
        out_shape=jax.ShapeDtypeStruct((rows, LANES), jnp.float32),
        compiler_params=pltpu.CompilerParams(vmem_limit_bytes=24 * MIB),
        cost_estimate=pl.CostEstimate(flops=10**8, bytes_accessed=1 * MIB, transcendentals=0),
        name="home_rows",
    )(slot, offset, forcing)


def unpack_plan_kernel(homes, capacity, lane_rows, slot, offset, code, place):
    slots = slot.shape[1]
    row, lane = slot_columns(slot[...], offset[...], homes, capacity)
    here = iota((slots, LANES), 1)
    index = (here - lane) & 127
    inside = (index < WINDOW) & (row >= 0)
    code[...] = jnp.where(inside, index + jnp.where(here >= lane, 0, LANES), -1)
    row_lane, _ = slot_rows(slot[...], offset[...], homes, capacity)
    place[...] = onehot(iota((lane_rows, slots), 0) == row_lane)


def unpack_plan(homes, capacity, lane_rows, slot, offset):
    slots = slot.shape[1]
    return pl.pallas_call(
        functools.partial(unpack_plan_kernel, homes, capacity, lane_rows),
        out_shape=(
            jax.ShapeDtypeStruct((slots, LANES), jnp.int32),
            jax.ShapeDtypeStruct((lane_rows, slots), jnp.bfloat16),
        ),
        compiler_params=pltpu.CompilerParams(vmem_limit_bytes=24 * MIB),
        cost_estimate=pl.CostEstimate(flops=10**9, bytes_accessed=2 * MIB, transcendentals=0),
        name="unpack_plan",
    )(slot, offset)


def unpack_kernel(arrived, code, place, river, runoff, evap, storage):
    lane_rows = place.shape[0]
    marks = code[...]
    values = arrived[...]
    index = marks & 127
    results = []
    for first in (0, WINDOW):
        window = jnp.where(marks >= 0, lane_pick(values, (index + first) & 127), 0.0)
        placed = jnp.concatenate(
            [jnp.where(marks < LANES, window, 0.0), jnp.where(marks >= LANES, window, 0.0)],
            axis=1,
        )
        totals = matmul(place[...], jnp.concatenate(thirds(placed), axis=1))
        totals = totals[:, :256] + totals[:, 256:512] + totals[:, 512:]
        over = totals[:, LANES:]
        over = jnp.concatenate([over[lane_rows - 1 :], over[: lane_rows - 1]], axis=0)
        over = jnp.where(iota(over.shape, 0) == 0, 0.0, over)
        results.append(totals[:, :LANES] + over)
    runoff[...], evap[...] = results
    storage[...] = river[...] + results[0]


def unpack(arrived, code, place, river):
    shape = jax.ShapeDtypeStruct((place.shape[0], LANES), jnp.float32)
    return pl.pallas_call(
        unpack_kernel,
        out_shape=(shape, shape, shape),
        compiler_params=pltpu.CompilerParams(vmem_limit_bytes=24 * MIB),
        cost_estimate=pl.CostEstimate(flops=10**9, bytes_accessed=1 * MIB, transcendentals=0),
        name="unpack_cells",
    )(arrived, code, place, river)


def segment_plan_kernel(cell, meta):
    chunk = 96
    for start in range(0, cell.shape[0], chunk):
        values = cell[pl.ds(start, chunk), :]
        here = iota(values.shape, 1)
        target = here & (WINDOW - 1)
        count = jnp.zeros_like(values)
        for step in (64, 32, 16, 8, 4, 2, 1):
            probe = lane_pick(values, count + (step - 1))
            count = jnp.where(probe <= target, count + step, count)
        count = jnp.where(lane_pick(values, count) <= target, count + 1, count)
        last = jnp.maximum(count - 1, 0)
        found = (count > 0) & (lane_pick(values, last) == target)
        marks = jnp.where(found, last + 128, 0)
        for bit in range(7):
            step = 1 << bit
            same = (pltpu.roll(values, step, 1) == values) & (here >= step)
            marks = marks + jnp.where(same, 256 << bit, 0)
        meta[pl.ds(start, chunk), :] = marks


def segment_plan(cell):
    return pl.pallas_call(
        segment_plan_kernel,
        out_shape=jax.ShapeDtypeStruct(cell.shape, jnp.int32),
        compiler_params=pltpu.CompilerParams(vmem_limit_bytes=24 * MIB),
        cost_estimate=pl.CostEstimate(flops=10**8, bytes_accessed=1 * MIB, transcendentals=0),
        name="segment_plan",
    )(cell)


def segment_totals(values, marks):
    total = values
    for bit in range(7):
        moved = pltpu.roll(total, 1 << bit, 1)
        total = total + jnp.where((marks & (256 << bit)) != 0, moved, 0.0)
    return lane_pick(total, marks & 127)


def land_kernel(
    home_size, capacity, worker_list, offsets, homes, cell, meta, area, water, cap, soil, porosity,
    drainage, soil_new, canopy_new, sums_out, fetched, lanes, sums,
):
    layers, block = soil.shape[:2]
    base = pl.program_id(0) * block

    @pl.when(pl.program_id(0) == 0)
    def _():
        sums_out[...] = jnp.zeros_like(sums_out)

    def fetch(i, carry):
        slot = worker_list[base + i]
        home = lax.div(slot, capacity)
        first = offsets[home, slot - home * capacity]
        row = home * home_size + (first >> 7) * 3
        fetched[pl.ds(pl.multiple_of(i * 8, 8), 8), :] = homes[pl.ds(row, 8), :]
        lanes[pl.ds(i, 1), :] = jnp.full((1, LANES), first & 127, jnp.int32)
        return carry

    lax.fori_loop(0, block, fetch, 0, unroll=8)
    chunk = 32
    for start in range(0, block, chunk):
        part = pl.ds(start, chunk)
        first = lanes[part, :]
        here = iota(first.shape, 1)
        index = (cell[part, :] + first) & 127
        after = here >= first
        given = []
        for var in range(3):
            low = fetched[pl.ds(start * 8 + var, chunk, stride=8), :]
            high = fetched[pl.ds(start * 8 + var + 3, chunk, stride=8), :]
            given.append(lane_pick(jnp.where(after, low, high), index))
        rain, demand, limit = given
        wetted = water[part, :] + rain
        flowing = jnp.maximum(wetted - cap[part, :], 0.0)
        retained = jnp.minimum(wetted, cap[part, :])
        canopy_loss = jnp.minimum(demand, retained)
        canopy_new[part, :] = retained - canopy_loss
        surface = jnp.zeros_like(flowing)
        for layer in range(layers):
            filled = soil[layer, part, :] + flowing
            excess = jnp.maximum(filled - porosity[layer, part, :], 0.0)
            surface = surface + excess
            filled = filled - excess
            flowing = drainage[layer, part, :] * filled
            middle = filled - flowing
            if layer == 0:
                soil_loss = jnp.minimum(jnp.minimum(limit, demand - canopy_loss), 0.5 * middle)
                middle = middle - soil_loss
            soil_new[layer, part, :] = middle
        weight = area[part, :]
        marks = meta[part, :]
        runoff = segment_totals(weight * (surface + flowing), marks)
        evap = segment_totals(weight * (canopy_loss + soil_loss), marks)
        both = jnp.where(here < WINDOW, runoff, evap)
        sums[part, :] = jnp.where((marks & 128) != 0, both, 0.0)

    def hand_back(i, carry):
        sums_out[pl.ds(worker_list[base + i], 1), :] = sums[pl.ds(i, 1), :]
        return carry

    lax.fori_loop(0, block, hand_back, 0, unroll=8)


def land_step(
    capacity, worker_list, offsets, homes, cell, meta, area, water, cap, soil, porosity, drainage
):
    layers, rows = soil.shape[:2]
    block = 96
    home_count = offsets.shape[0]
    flat = pl.BlockSpec((block, LANES), lambda i, *_: (i, 0))
    deep = pl.BlockSpec((layers, block, LANES), lambda i, *_: (0, i, 0))
    sums = (home_count * capacity, LANES)
    return pl.pallas_call(
        functools.partial(land_kernel, homes.shape[0] // home_count, capacity),
        grid_spec=pltpu.PrefetchScalarGridSpec(
            num_scalar_prefetch=2,
            grid=(rows // block,),
            in_specs=[
                pl.BlockSpec(homes.shape, lambda i, *_: (0, 0), pipeline_mode=pl.Buffered(1)),
                flat, flat, flat, flat, flat, deep, deep, deep,
            ],
            out_specs=[deep, flat, pl.BlockSpec(sums, lambda i, *_: (0, 0))],
            scratch_shapes=[
                pltpu.VMEM((block * 8, LANES), jnp.float32),
                pltpu.VMEM((block, LANES), jnp.int32),
                pltpu.VMEM((block, LANES), jnp.float32),
            ],
        ),
        out_shape=(
            jax.ShapeDtypeStruct(soil.shape, jnp.float32),
            jax.ShapeDtypeStruct((rows, LANES), jnp.float32),
            jax.ShapeDtypeStruct(sums, jnp.float32),
        ),
        compiler_params=pltpu.CompilerParams(vmem_limit_bytes=60 * MIB),
        cost_estimate=pl.CostEstimate(flops=10**8, bytes_accessed=20 * MIB, transcendentals=0),
        name="land_layers",
    )(worker_list, offsets, homes, cell, meta, area, water, cap, soil, porosity, drainage)


def halo_parts(value, axis, dim, width):
    count, length = (lax.axis_size(axis), value.shape[dim])
    up = [(i, i + 1) for i in range(count - 1)]
    down = [(j, i) for i, j in up]
    last = lax.slice_in_dim(value, length - width, length, axis=dim)
    initial = lax.slice_in_dim(value, 0, width, axis=dim)
    return lax.ppermute(last, axis, up), lax.ppermute(initial, axis, down)


def with_halo(value, width):
    rows, cols = value.ndim - 2, value.ndim - 1
    before, after = halo_parts(value, "region", rows, width)
    tall = jnp.concatenate([value, after, before], axis=rows)
    before, after = halo_parts(tall, "col", cols, width)
    gap = jnp.zeros(tall.shape[:-1] + (LANES - 2 * width,), value.dtype)
    return jnp.concatenate([tall, after, gap, before], axis=cols)


def river_kernel(state, fixed, out):
    storage = state[...]
    rate = fixed[0]
    code = fixed[1]
    rows, cols = storage.shape
    for _ in range(ITERS):
        outflow = rate * storage
        inflow = jnp.zeros_like(storage)
        for col_step in (-1, 0, 1):
            column = jnp.zeros_like(storage)
            for bit, (row_step, step) in enumerate(directions):
                if step != col_step:
                    continue
                leaving = jnp.where(code == float(1 << bit), outflow, 0.0)
                if row_step:
                    leaving = pltpu.roll(leaving, row_step % rows, 0)
                column = column + leaving
            if col_step:
                column = pltpu.roll(column, col_step % cols, 1)
            inflow = inflow + column
        storage = storage - outflow + inflow
    out[...] = storage[: out.shape[0], : out.shape[1]]


def river(state, fixed, shape):
    return pl.pallas_call(
        river_kernel,
        out_shape=jax.ShapeDtypeStruct(shape, jnp.float32),
        compiler_params=pltpu.CompilerParams(vmem_limit_bytes=24 * MIB),
        cost_estimate=pl.CostEstimate(flops=10**7, bytes_accessed=1 * MIB, transcendentals=0),
        name="river_steps",
    )(state, fixed)


def exchange(value):
    return lax.all_to_all(value, axes, split_axis=0, concat_axis=0, tiled=True)


def shards(
    forcing,
    river_storage,
    river_rate,
    flow_code,
    home_slot,
    home_offset,
    worker_list,
    patch_cell,
    patch_area,
    canopy_water,
    canopy_cap,
    soil_water,
    porosity,
    drainage,
):
    homes = lax.axis_size("region") * lax.axis_size("col")
    capacity = home_slot.shape[1] // homes
    grid_rows, grid_cols = river_storage.shape
    lane_rows = grid_rows * grid_cols // LANES
    own = home_rows(
        homes, capacity, home_slot, home_offset, forcing.reshape(3, lane_rows, LANES)
    )
    gathered = lax.all_gather(own, axes, axis=0, tiled=True)
    first_slot = (lax.axis_index("region") * lax.axis_size("col") + lax.axis_index("col")) * capacity
    offsets = lax.dynamic_slice(
        gathered.reshape(homes, own.shape[0], LANES),
        (0, 3 * lane_rows + first_slot // LANES, first_slot % LANES),
        (homes, 1, capacity),
    ).reshape(homes, capacity).astype(jnp.int32)
    meta = segment_plan(patch_cell)
    code, place = unpack_plan(homes, capacity, lane_rows, home_slot, home_offset)
    fixed = with_halo(jnp.stack([river_rate, flow_code.astype(jnp.float32)]), ITERS)
    soil_new, canopy_new, sums = land_step(
        capacity, worker_list, offsets, gathered, patch_cell, meta, patch_area, canopy_water,
        canopy_cap, soil_water, porosity, drainage,
    )
    cell_runoff, cell_evap, storage = unpack(
        exchange(sums), code, place, river_storage.reshape(lane_rows, LANES)
    )
    river_new = river(
        with_halo(storage.reshape(river_storage.shape), ITERS), fixed, river_storage.shape
    )
    return (
        soil_new,
        canopy_new,
        cell_runoff.reshape(river_storage.shape),
        cell_evap.reshape(river_storage.shape),
        river_new,
    )


def solution(mesh):
    placed = (
        P(None, "region", "col"),
        P("region", "col"),
        P("region", "col"),
        P("region", "col"),
        P(("region", "col"), None),
        P(("region", "col"), None),
        P(("region", "col")),
        P(("region", "col"), None),
        P(("region", "col"), None),
        P(("region", "col"), None),
        P(("region", "col"), None),
        P(None, ("region", "col"), None),
        P(None, ("region", "col"), None),
        P(None, ("region", "col"), None),
    )
    return jax.shard_map(
        shards,
        mesh=mesh,
        in_specs=placed,
        out_specs=(
            P(None, ("region", "col"), None),
            P(("region", "col"), None),
            P("region", "col"),
            P("region", "col"),
            P("region", "col"),
        ),
        check_vma=False,
    )
```

```python
import functools

import jax
import jax.numpy as jnp
from jax import lax
from jax.experimental import pallas as pl
from jax.experimental.pallas import tpu as pltpu
from jax.sharding import PartitionSpec as P

ITERS = 4
WINDOW = 64
LANES = 128
MIB = 1024 * 1024
VMEM_LIMIT = 60 * MIB

directions = ((0, 1), (1, 1), (1, 0), (1, -1), (0, -1), (-1, -1), (-1, 0), (-1, 1))
axes = ("region", "col")


def iota(shape, dim):
    return lax.broadcasted_iota(jnp.int32, shape, dim)


def onehot(mask):
    return jnp.where(mask, jnp.float32(1.0), jnp.float32(0.0)).astype(jnp.bfloat16)


def lane_pick(values, index):
    return jnp.take_along_axis(values, index, axis=1, mode="promise_in_bounds")


def thirds(value):
    high = value.astype(jnp.bfloat16)
    rest = value - high.astype(jnp.float32)
    middle = rest.astype(jnp.bfloat16)
    low = (rest - middle.astype(jnp.float32)).astype(jnp.bfloat16)
    return high, middle, low


def matmul(a, b, a_dim=1, b_dim=0):
    return lax.dot_general(
        a, b, (((a_dim,), (b_dim,)), ((), ())), preferred_element_type=jnp.float32
    )


def slot_factors(slot, offset, homes, capacity):
    slots = slot.shape[1]
    worker = slot // capacity if capacity & (capacity - 1) else slot >> (capacity.bit_length() - 1)
    position = slot - worker * capacity
    by_worker = onehot(iota((homes, slots), 0) == worker)
    at_position = iota((capacity, slots), 0) == position
    row = jnp.where(at_position, ((offset >> 7) + 1).astype(jnp.float32), 0.0)
    lane = jnp.where(at_position, (offset & 127).astype(jnp.float32), 0.0)
    return by_worker, row.astype(jnp.bfloat16), lane.astype(jnp.bfloat16)


def slot_columns(slot, offset, homes, capacity):
    slots = slot.shape[1]
    by_worker, row, lane = slot_factors(slot, offset, homes, capacity)
    table = matmul(by_worker, jnp.concatenate([row, lane], axis=0), 1, 1)
    spread = jnp.broadcast_to(table[:, None, :], (homes, capacity, 2 * capacity))
    spread = spread.reshape(slots, 2 * capacity)
    place = iota(spread.shape, 0) % capacity == iota(spread.shape, 1) % capacity
    kept = jnp.where(place, spread, 0.0).astype(jnp.bfloat16)
    shape = (2 * capacity, 2 * LANES)
    gather = onehot((iota(shape, 0) >= capacity) == (iota(shape, 1) >= LANES))
    columns = matmul(kept, gather).astype(jnp.int32)
    return columns[:, :LANES] - 1, columns[:, LANES:]


def slot_rows(slot, offset, homes, capacity):
    slots = slot.shape[1]
    by_worker, row, lane = slot_factors(slot, offset, homes, capacity)
    table = matmul(jnp.concatenate([row, lane], axis=0), by_worker, 1, 1).astype(jnp.bfloat16)
    number = iota((1, slots), 1)
    worker = number // capacity
    position = number - worker * capacity
    spread = matmul(table, onehot(iota((homes, slots), 0) == worker))
    at_position = iota((capacity, slots), 0) == position
    rows = jnp.sum(jnp.where(at_position, spread[:capacity], 0.0), axis=0, keepdims=True)
    lanes = jnp.sum(jnp.where(at_position, spread[capacity:], 0.0), axis=0, keepdims=True)
    return rows.astype(jnp.int32) - 1, lanes.astype(jnp.int32)


def pack_kernel(homes, capacity, slot, offset, forcing, out, row_of, lane_of, rain, losses):
    slots = slot.shape[1]
    lane_rows = forcing.shape[1]
    row_of[...], lane_of[...] = slot_columns(slot[...], offset[...], homes, capacity)
    parts = []
    for var in range(3):
        here = forcing[var]
        following = jnp.concatenate([here[1:], here[:1]], axis=0)
        parts += [here, following]
    table = jnp.concatenate(thirds(jnp.concatenate(parts, axis=1)), axis=0)
    chunk = 128
    for start in range(0, slots, chunk):
        row = row_of[pl.ds(start, chunk), :]
        lane = lane_of[pl.ds(start, chunk), :]
        shape = (chunk, 3 * lane_rows)
        wide = jnp.concatenate([row, row], axis=1)[:, : 3 * lane_rows]
        pick = onehot(wide == iota(shape, 1) % lane_rows)
        rows = matmul(pick, table)
        here = iota((chunk, LANES), 1)
        after = here >= lane
        joined = [
            jnp.where(
                after,
                rows[:, 2 * var * LANES : (2 * var + 1) * LANES],
                rows[:, (2 * var + 1) * LANES : (2 * var + 2) * LANES],
            )
            for var in range(3)
        ]
        first = (here + lane) & 127
        second = (first + WINDOW) & 127
        odd = iota((chunk, LANES), 0) & 1 == 1
        rain[pl.ds(start, chunk), :] = lane_pick(joined[0], jnp.where(odd, second, first))
        losses[pl.ds(start, chunk), :] = jnp.where(
            here < WINDOW, lane_pick(joined[1], first), lane_pick(joined[2], second)
        )
    pairs = capacity // 2
    for home in range(homes):
        start = home * capacity
        out[home, :capacity, :] = losses[pl.ds(start, capacity), :]
        even_rows = rain[pl.ds(start, pairs, stride=2), :]
        odd_rows = rain[pl.ds(start + 1, pairs, stride=2), :]
        out[home, capacity:, :] = jnp.where(
            iota(even_rows.shape, 1) < WINDOW, even_rows, odd_rows
        )


def pack(homes, capacity, slot, offset, forcing):
    slots = slot.shape[1]
    return pl.pallas_call(
        functools.partial(pack_kernel, homes, capacity),
        out_shape=jax.ShapeDtypeStruct((homes, capacity + capacity // 2, LANES), jnp.float32),
        scratch_shapes=[
            pltpu.VMEM((slots, LANES), jnp.int32),
            pltpu.VMEM((slots, LANES), jnp.int32),
            pltpu.VMEM((slots, LANES), jnp.float32),
            pltpu.VMEM((slots, LANES), jnp.float32),
        ],
        compiler_params=pltpu.CompilerParams(vmem_limit_bytes=VMEM_LIMIT),
        cost_estimate=pl.CostEstimate(flops=10**9, bytes_accessed=2 * MIB, transcendentals=0),
        name="pack_forcing",
    )(slot, offset, forcing)


def unpack_plan_kernel(homes, capacity, lane_rows, slot, offset, code, place):
    slots = slot.shape[1]
    row, lane = slot_columns(slot[...], offset[...], homes, capacity)
    here = iota((slots, LANES), 1)
    index = (here - lane) & 127
    inside = (index < WINDOW) & (row >= 0)
    code[...] = jnp.where(inside, index + jnp.where(here >= lane, 0, LANES), -1)
    row_lane, _ = slot_rows(slot[...], offset[...], homes, capacity)
    place[...] = onehot(iota((lane_rows, slots), 0) == row_lane)


def unpack_plan(homes, capacity, lane_rows, slot, offset):
    slots = slot.shape[1]
    return pl.pallas_call(
        functools.partial(unpack_plan_kernel, homes, capacity, lane_rows),
        out_shape=(
            jax.ShapeDtypeStruct((slots, LANES), jnp.int32),
            jax.ShapeDtypeStruct((lane_rows, slots), jnp.bfloat16),
        ),
        compiler_params=pltpu.CompilerParams(vmem_limit_bytes=VMEM_LIMIT),
        cost_estimate=pl.CostEstimate(flops=10**9, bytes_accessed=2 * MIB, transcendentals=0),
        name="unpack_plan",
    )(slot, offset)


def strips_for_neighbours(state, rows):
    device = iota((rows, LANES), 0) // ITERS
    down = device // lax.axis_size("col") - lax.axis_index("region")
    right = device % lax.axis_size("col") - lax.axis_index("col")
    height, width = state.shape
    columns = jnp.transpose(state)
    empty = jnp.zeros((ITERS, LANES - height), jnp.float32)

    def repeated(strip):
        if strip.shape[1] < LANES:
            strip = jnp.concatenate([strip, empty], axis=1)
        return jnp.concatenate([strip] * (rows // ITERS), axis=0)

    near = (jnp.abs(down) <= 1).astype(jnp.int32)
    strips = jnp.zeros((rows, LANES), jnp.float32)
    strips = jnp.where((right == 0) & (down == 1), repeated(state[height - ITERS :]), strips)
    strips = jnp.where((right == 0) & (down == -1), repeated(state[:ITERS]), strips)
    strips = jnp.where((right == 1) & (near == 1), repeated(columns[width - ITERS :]), strips)
    return jnp.where((right == -1) & (near == 1), repeated(columns[:ITERS]), strips)


def unpack_kernel(arrived, code, place, river, runoff, evap, storage, strips):
    lane_rows = place.shape[0]
    marks = code[...]
    values = arrived[...]
    index = marks & 127
    results = []
    for first in (0, WINDOW):
        window = jnp.where(marks >= 0, lane_pick(values, (index + first) & 127), 0.0)
        placed = jnp.concatenate(
            [jnp.where(marks < LANES, window, 0.0), jnp.where(marks >= LANES, window, 0.0)],
            axis=1,
        )
        totals = matmul(place[...], jnp.concatenate(thirds(placed), axis=1))
        totals = totals[:, :256] + totals[:, 256:512] + totals[:, 512:]
        over = totals[:, LANES:]
        over = jnp.concatenate([over[lane_rows - 1 :], over[: lane_rows - 1]], axis=0)
        over = jnp.where(iota(over.shape, 0) == 0, 0.0, over)
        results.append(totals[:, :LANES] + over)
    runoff[...], evap[...] = results
    state = river[...] + results[0]
    storage[...] = state
    strips[...] = strips_for_neighbours(state, strips.shape[0])


def unpack(homes, arrived, code, place, river):
    shape = jax.ShapeDtypeStruct((place.shape[0], LANES), jnp.float32)
    strips = jax.ShapeDtypeStruct((homes * ITERS, LANES), jnp.float32)
    return pl.pallas_call(
        unpack_kernel,
        out_shape=(shape, shape, shape, strips),
        compiler_params=pltpu.CompilerParams(vmem_limit_bytes=VMEM_LIMIT),
        cost_estimate=pl.CostEstimate(flops=10**9, bytes_accessed=1 * MIB, transcendentals=0),
        name="unpack_cells",
    )(arrived, code, place, river)


def segment_plan_kernel(cell, worker, meta):
    chunk = 96
    for start in range(0, cell.shape[0], chunk):
        values = cell[pl.ds(start, chunk), :]
        here = iota(values.shape, 1)
        target = here & (WINDOW - 1)
        count = jnp.zeros_like(values)
        for step in (64, 32, 16, 8, 4, 2, 1):
            probe = lane_pick(values, count + (step - 1))
            count = jnp.where(probe <= target, count + step, count)
        count = jnp.where(lane_pick(values, count) <= target, count + 1, count)
        last = jnp.maximum(count - 1, 0)
        found = (count > 0) & (lane_pick(values, last) == target)
        marks = jnp.where(found, last + 128, 0)
        for bit in range(7):
            step = 1 << bit
            same = (pltpu.roll(values, step, 1) == values) & (here >= step)
            marks = marks + jnp.where(same, 256 << bit, 0)
        odd = worker[pl.ds(start, chunk), :] & 1
        meta[pl.ds(start, chunk), :] = marks + (odd << 15)


def segment_plan(cell, worker):
    return pl.pallas_call(
        segment_plan_kernel,
        out_shape=jax.ShapeDtypeStruct(cell.shape, jnp.int32),
        compiler_params=pltpu.CompilerParams(vmem_limit_bytes=VMEM_LIMIT),
        cost_estimate=pl.CostEstimate(flops=10**8, bytes_accessed=1 * MIB, transcendentals=0),
        name="segment_plan",
    )(cell, worker)


def segment_totals(values, marks):
    total = values
    for bit in range(7):
        moved = pltpu.roll(total, 1 << bit, 1)
        total = total + jnp.where((marks & (256 << bit)) != 0, moved, 0.0)
    return lane_pick(total, marks & 127)


def land_kernel(
    slots, loss_rows, rain_rows, arrived, cell, meta, area, water, cap, soil, porosity, drainage,
    soil_new, canopy_new, sums_out, losses, rains, runoffs, evaps,
):
    layers, block = soil.shape[:2]
    base = pl.program_id(0) * block

    @pl.when(pl.program_id(0) == 0)
    def _():
        sums_out[...] = jnp.zeros_like(sums_out)

    def fetch(i, carry):
        losses[pl.ds(i, 1), :] = arrived[pl.ds(loss_rows[base + i], 1), :]
        rains[pl.ds(i, 1), :] = arrived[pl.ds(rain_rows[base + i], 1), :]
        return carry

    lax.fori_loop(0, block, fetch, 0, unroll=16)
    chunk = 32
    for start in range(0, block, chunk):
        part = pl.ds(start, chunk)
        index = cell[part, :]
        rain = lane_pick(rains[part, :], index + (meta[part, :] >> 9 & WINDOW))
        demand = lane_pick(losses[part, :], index)
        limit = lane_pick(losses[part, :], index + WINDOW)
        wetted = water[part, :] + rain
        flowing = jnp.maximum(wetted - cap[part, :], 0.0)
        retained = jnp.minimum(wetted, cap[part, :])
        canopy_loss = jnp.minimum(demand, retained)
        canopy_new[part, :] = retained - canopy_loss
        surface = jnp.zeros_like(flowing)
        for layer in range(layers):
            filled = soil[layer, part, :] + flowing
            excess = jnp.maximum(filled - porosity[layer, part, :], 0.0)
            surface = surface + excess
            filled = filled - excess
            flowing = drainage[layer, part, :] * filled
            middle = filled - flowing
            if layer == 0:
                soil_loss = jnp.minimum(jnp.minimum(limit, demand - canopy_loss), 0.5 * middle)
                middle = middle - soil_loss
                evaps[part, :] = area[part, :] * (canopy_loss + soil_loss)
            soil_new[layer, part, :] = middle
        runoffs[part, :] = area[part, :] * (surface + flowing)
    marks = meta[...]
    runoff = segment_totals(runoffs[...], marks)
    evap = segment_totals(evaps[...], marks)
    both = jnp.where(iota(runoff.shape, 1) < WINDOW, runoff, evap)
    runoffs[...] = jnp.where((marks & 128) != 0, both, 0.0)

    def hand_back(i, carry):
        sums_out[pl.ds(slots[base + i], 1), :] = runoffs[pl.ds(i, 1), :]
        return carry

    lax.fori_loop(0, block, hand_back, 0, unroll=16)


def land_step(
    sums_shape, slots, loss_rows, rain_rows, arrived, cell, meta, area, water, cap, soil,
    porosity, drainage,
):
    layers, rows = soil.shape[:2]
    block = 96
    flat = pl.BlockSpec((block, LANES), lambda i, *_: (i, 0))
    deep = pl.BlockSpec((layers, block, LANES), lambda i, *_: (0, i, 0))
    whole = pl.BlockSpec(arrived.shape, lambda i, *_: (0, 0), pipeline_mode=pl.Buffered(1))
    return pl.pallas_call(
        land_kernel,
        grid_spec=pltpu.PrefetchScalarGridSpec(
            num_scalar_prefetch=3,
            grid=(rows // block,),
            in_specs=[whole, flat, flat, flat, flat, flat, deep, deep, deep],
            out_specs=[deep, flat, pl.BlockSpec(sums_shape, lambda i, *_: (0, 0))],
            scratch_shapes=[pltpu.VMEM((block, LANES), jnp.float32)] * 4,
        ),
        out_shape=(
            jax.ShapeDtypeStruct(soil.shape, jnp.float32),
            jax.ShapeDtypeStruct((rows, LANES), jnp.float32),
            jax.ShapeDtypeStruct(sums_shape, jnp.float32),
        ),
        compiler_params=pltpu.CompilerParams(vmem_limit_bytes=VMEM_LIMIT),
        cost_estimate=pl.CostEstimate(flops=10**8, bytes_accessed=20 * MIB, transcendentals=0),
        name="land_layers",
    )(
        slots, loss_rows, rain_rows, arrived, cell, meta, area, water, cap, soil, porosity,
        drainage,
    )


def halo_parts(value, axis, dim, width):
    count, length = (lax.axis_size(axis), value.shape[dim])
    up = [(i, i + 1) for i in range(count - 1)]
    down = [(j, i) for i, j in up]
    last = lax.slice_in_dim(value, length - width, length, axis=dim)
    initial = lax.slice_in_dim(value, 0, width, axis=dim)
    return lax.ppermute(last, axis, up), lax.ppermute(initial, axis, down)


def with_halo(value, width):
    rows, cols = value.ndim - 2, value.ndim - 1
    before, after = halo_parts(value, "region", rows, width)
    tall = jnp.concatenate([value, after, before], axis=rows)
    before, after = halo_parts(tall, "col", cols, width)
    gap = jnp.zeros(tall.shape[:-1] + (LANES - 2 * width,), value.dtype)
    return jnp.concatenate([tall, after, gap, before], axis=cols)


def river_kernel(state, strips, fixed, out):
    height, width = state.shape
    region, col = lax.axis_index("region"), lax.axis_index("col")

    def strip(down, right):
        row, column = region + down, col + right
        there = (row >= 0) & (row < lax.axis_size("region"))
        there &= (column >= 0) & (column < lax.axis_size("col"))
        device = jnp.where(there, row * lax.axis_size("col") + column, 0)
        return strips[pl.ds(device * ITERS, ITERS), :] * jnp.where(there, 1.0, 0.0)

    def column_strip(right):
        middle, above, below = strip(0, right), strip(-1, right), strip(1, right)
        return jnp.concatenate(
            [
                middle[:, :height],
                below[:, :ITERS],
                above[:, height - ITERS : height],
                jnp.zeros((ITERS, LANES - height - 2 * ITERS), jnp.float32),
            ],
            axis=1,
        )

    gap = jnp.zeros((LANES - 2 * ITERS, LANES), jnp.float32)
    sides = jnp.concatenate([column_strip(1), gap, column_strip(-1)], axis=0)
    sides = jnp.transpose(sides)[: height + 2 * ITERS]
    tall = jnp.concatenate([state[...], strip(1, 0), strip(-1, 0)], axis=0)
    storage = jnp.concatenate([tall, sides], axis=1)
    rate = fixed[0]
    code = fixed[1]
    rows, cols = storage.shape
    for _ in range(ITERS):
        outflow = rate * storage
        inflow = jnp.zeros_like(storage)
        for col_step in (-1, 0, 1):
            column = jnp.zeros_like(storage)
            for bit, (row_step, step) in enumerate(directions):
                if step != col_step:
                    continue
                leaving = jnp.where(code == float(1 << bit), outflow, 0.0)
                if row_step:
                    leaving = pltpu.roll(leaving, row_step % rows, 0)
                column = column + leaving
            if col_step:
                column = pltpu.roll(column, col_step % cols, 1)
            inflow = inflow + column
        storage = storage - outflow + inflow
    out[...] = storage[:height, :width]


def river(state, strips, fixed):
    return pl.pallas_call(
        river_kernel,
        out_shape=jax.ShapeDtypeStruct(state.shape, jnp.float32),
        compiler_params=pltpu.CompilerParams(vmem_limit_bytes=VMEM_LIMIT),
        cost_estimate=pl.CostEstimate(flops=10**7, bytes_accessed=1 * MIB, transcendentals=0),
        name="river_steps",
    )(state, strips, fixed)


def exchange(value):
    return lax.all_to_all(value, axes, split_axis=0, concat_axis=0, tiled=True)


def shards(
    forcing,
    river_storage,
    river_rate,
    flow_code,
    home_slot,
    home_offset,
    worker_list,
    patch_cell,
    patch_area,
    canopy_water,
    canopy_cap,
    soil_water,
    porosity,
    drainage,
):
    homes = lax.axis_size("region") * lax.axis_size("col")
    capacity = home_slot.shape[1] // homes
    grid_rows, grid_cols = river_storage.shape
    lane_rows = grid_rows * grid_cols // LANES
    outgoing = pack(
        homes, capacity, home_slot, home_offset, forcing.reshape(3, lane_rows, LANES)
    )
    arrived = exchange(outgoing).reshape(-1, LANES)
    home = worker_list // capacity
    position = worker_list - home * capacity
    loss_rows = home * outgoing.shape[1] + position
    rain_rows = home * outgoing.shape[1] + capacity + position // 2
    meta = segment_plan(patch_cell, worker_list[:, None])
    code, place = unpack_plan(homes, capacity, lane_rows, home_slot, home_offset)
    fixed = with_halo(jnp.stack([river_rate, flow_code.astype(jnp.float32)]), ITERS)
    soil_new, canopy_new, sums = land_step(
        (homes * capacity, LANES), worker_list, loss_rows, rain_rows, arrived, patch_cell, meta,
        patch_area, canopy_water, canopy_cap, soil_water, porosity, drainage,
    )
    cell_runoff, cell_evap, storage, strips = unpack(
        homes, exchange(sums), code, place, river_storage.reshape(lane_rows, LANES)
    )
    river_new = river(storage.reshape(river_storage.shape), exchange(strips), fixed)
    return (
        soil_new,
        canopy_new,
        cell_runoff.reshape(river_storage.shape),
        cell_evap.reshape(river_storage.shape),
        river_new,
    )


def solution(mesh):
    placed = (
        P(None, "region", "col"),
        P("region", "col"),
        P("region", "col"),
        P("region", "col"),
        P(("region", "col"), None),
        P(("region", "col"), None),
        P(("region", "col")),
        P(("region", "col"), None),
        P(("region", "col"), None),
        P(("region", "col"), None),
        P(("region", "col"), None),
        P(None, ("region", "col"), None),
        P(None, ("region", "col"), None),
        P(None, ("region", "col"), None),
    )
    return jax.shard_map(
        shards,
        mesh=mesh,
        in_specs=placed,
        out_specs=(
            P(None, ("region", "col"), None),
            P(("region", "col"), None),
            P("region", "col"),
            P("region", "col"),
            P("region", "col"),
        ),
        check_vma=False,
    )
```

```python
import functools

import jax
import jax.numpy as jnp
from jax import lax
from jax.experimental import pallas as pl
from jax.experimental.pallas import tpu as pltpu
from jax.sharding import PartitionSpec as P

ITERS = 4
WINDOW = 64
LANES = 128
MIB = 1024 * 1024
VMEM_LIMIT = 24 * MIB

directions = ((0, 1), (1, 1), (1, 0), (1, -1), (0, -1), (-1, -1), (-1, 0), (-1, 1))
axes = ("region", "col")


def iota(shape, dim):
    return lax.broadcasted_iota(jnp.int32, shape, dim)


def onehot(mask):
    return jnp.where(mask, jnp.float32(1.0), jnp.float32(0.0)).astype(jnp.bfloat16)


def lane_pick(values, index):
    return jnp.take_along_axis(values, index, axis=1, mode="promise_in_bounds")


def in_hbm(value):
    return pltpu.with_memory_space_constraint(value, pltpu.HBM)


def thirds(value):
    high = value.astype(jnp.bfloat16)
    rest = value - high.astype(jnp.float32)
    middle = rest.astype(jnp.bfloat16)
    low = (rest - middle.astype(jnp.float32)).astype(jnp.bfloat16)
    return high, middle, low


def halves(value):
    high = value.astype(jnp.bfloat16)
    return high, (value - high.astype(jnp.float32)).astype(jnp.bfloat16)


def matmul(a, b, a_dim=1, b_dim=0):
    return lax.dot_general(
        a, b, (((a_dim,), (b_dim,)), ((), ())), preferred_element_type=jnp.float32
    )


def slot_factors(slot, offset, homes, capacity):
    slots = slot.shape[1]
    worker = slot // capacity if capacity & (capacity - 1) else slot >> (capacity.bit_length() - 1)
    position = slot - worker * capacity
    by_worker = onehot(iota((homes, slots), 0) == worker)
    at_position = iota((capacity, slots), 0) == position
    row = jnp.where(at_position, ((offset >> 7) + 1).astype(jnp.float32), 0.0)
    lane = jnp.where(at_position, (offset & 127).astype(jnp.float32), 0.0)
    return by_worker, row.astype(jnp.bfloat16), lane.astype(jnp.bfloat16)


def slot_columns(slot, offset, homes, capacity):
    slots = slot.shape[1]
    by_worker, row, lane = slot_factors(slot, offset, homes, capacity)
    table = matmul(by_worker, jnp.concatenate([row, lane], axis=0), 1, 1)
    spread = jnp.broadcast_to(table[:, None, :], (homes, capacity, 2 * capacity))
    spread = spread.reshape(slots, 2 * capacity)
    place = iota(spread.shape, 0) % capacity == iota(spread.shape, 1) % capacity
    kept = jnp.where(place, spread, 0.0).astype(jnp.bfloat16)
    shape = (2 * capacity, 2 * LANES)
    gather = onehot((iota(shape, 0) >= capacity) == (iota(shape, 1) >= LANES))
    columns = matmul(kept, gather).astype(jnp.int32)
    return columns[:, :LANES] - 1, columns[:, LANES:]


def slot_rows(slot, offset, homes, capacity):
    slots = slot.shape[1]
    by_worker, row, lane = slot_factors(slot, offset, homes, capacity)
    table = matmul(jnp.concatenate([row, lane], axis=0), by_worker, 1, 1).astype(jnp.bfloat16)
    number = iota((1, slots), 1)
    worker = number // capacity
    position = number - worker * capacity
    spread = matmul(table, onehot(iota((homes, slots), 0) == worker))
    at_position = iota((capacity, slots), 0) == position
    rows = jnp.sum(jnp.where(at_position, spread[:capacity], 0.0), axis=0, keepdims=True)
    lanes = jnp.sum(jnp.where(at_position, spread[capacity:], 0.0), axis=0, keepdims=True)
    return rows.astype(jnp.int32) - 1, lanes.astype(jnp.int32)


def pack_kernel(
    homes, capacity, slot_in, offset_in, forcing_in, out, slot, offset, forcing, row_of, lane_of,
    rain, losses, ready,
):
    copies = [
        pltpu.make_async_copy(source, target, ready.at[i])
        for i, (source, target) in enumerate(
            ((slot_in, slot), (offset_in, offset), (forcing_in, forcing))
        )
    ]
    for copy in copies:
        copy.start()
    for copy in copies:
        copy.wait()
    slots = slot.shape[1]
    lane_rows = forcing.shape[1]
    row_of[...], lane_of[...] = slot_columns(slot[...], offset[...], homes, capacity)
    parts = []
    for var in range(3):
        here = forcing[var]
        following = jnp.concatenate([here[1:], here[:1]], axis=0)
        parts += [here, following]
    table = jnp.concatenate(thirds(jnp.concatenate(parts, axis=1)), axis=0)
    chunk = 128
    for start in range(0, slots, chunk):
        row = row_of[pl.ds(start, chunk), :]
        lane = lane_of[pl.ds(start, chunk), :]
        shape = (chunk, 3 * lane_rows)
        wide = jnp.concatenate([row, row], axis=1)[:, : 3 * lane_rows]
        pick = onehot(wide == iota(shape, 1) % lane_rows)
        rows = matmul(pick, table)
        here = iota((chunk, LANES), 1)
        after = here >= lane
        joined = [
            jnp.where(
                after,
                rows[:, 2 * var * LANES : (2 * var + 1) * LANES],
                rows[:, (2 * var + 1) * LANES : (2 * var + 2) * LANES],
            )
            for var in range(3)
        ]
        first = (here + lane) & 127
        second = (first + WINDOW) & 127
        odd = iota((chunk, LANES), 0) & 1 == 1
        rain[pl.ds(start, chunk), :] = lane_pick(joined[0], jnp.where(odd, second, first))
        losses[pl.ds(start, chunk), :] = jnp.where(
            here < WINDOW, lane_pick(joined[1], first), lane_pick(joined[2], second)
        )
    pairs = capacity // 2
    for home in range(homes):
        start = home * capacity
        out[home, :capacity, :] = losses[pl.ds(start, capacity), :]
        even_rows = rain[pl.ds(start, pairs, stride=2), :]
        odd_rows = rain[pl.ds(start + 1, pairs, stride=2), :]
        out[home, capacity:, :] = jnp.where(
            iota(even_rows.shape, 1) < WINDOW, even_rows, odd_rows
        )


def pack(homes, capacity, slot, offset, forcing):
    slots = slot.shape[1]
    return pl.pallas_call(
        functools.partial(pack_kernel, homes, capacity),
        in_specs=[pl.BlockSpec(memory_space=pltpu.HBM)] * 3,
        out_shape=jax.ShapeDtypeStruct((homes, capacity + capacity // 2, LANES), jnp.float32),
        scratch_shapes=[
            pltpu.VMEM(slot.shape, jnp.int32),
            pltpu.VMEM(offset.shape, jnp.int32),
            pltpu.VMEM(forcing.shape, jnp.float32),
            pltpu.VMEM((slots, LANES), jnp.int32),
            pltpu.VMEM((slots, LANES), jnp.int32),
            pltpu.VMEM((slots, LANES), jnp.float32),
            pltpu.VMEM((slots, LANES), jnp.float32),
            pltpu.SemaphoreType.DMA((3,)),
        ],
        compiler_params=pltpu.CompilerParams(vmem_limit_bytes=VMEM_LIMIT),
        cost_estimate=pl.CostEstimate(flops=10**9, bytes_accessed=2 * MIB, transcendentals=0),
        name="pack_forcing",
    )(in_hbm(slot), in_hbm(offset), in_hbm(forcing))


def unpack_plan_kernel(homes, capacity, lane_rows, slot, offset, code, place):
    slots = slot.shape[1]
    row, lane = slot_columns(slot[...], offset[...], homes, capacity)
    here = iota((slots, LANES), 1)
    index = (here - lane) & 127
    inside = (index < WINDOW) & (row >= 0)
    code[...] = jnp.where(inside, index + jnp.where(here >= lane, 0, LANES), -1)
    row_lane, _ = slot_rows(slot[...], offset[...], homes, capacity)
    place[...] = onehot(iota((lane_rows, slots), 0) == row_lane)


def unpack_plan(homes, capacity, lane_rows, slot, offset):
    slots = slot.shape[1]
    return pl.pallas_call(
        functools.partial(unpack_plan_kernel, homes, capacity, lane_rows),
        out_shape=(
            jax.ShapeDtypeStruct((slots, LANES), jnp.int32),
            jax.ShapeDtypeStruct((lane_rows, slots), jnp.bfloat16),
        ),
        compiler_params=pltpu.CompilerParams(vmem_limit_bytes=VMEM_LIMIT),
        cost_estimate=pl.CostEstimate(flops=10**9, bytes_accessed=2 * MIB, transcendentals=0),
        name="unpack_plan",
    )(slot, offset)


def strips_for_neighbours(state, rows):
    device = iota((rows, LANES), 0) // ITERS
    down = device // lax.axis_size("col") - lax.axis_index("region")
    right = device % lax.axis_size("col") - lax.axis_index("col")
    height, width = state.shape
    columns = jnp.transpose(state)
    empty = jnp.zeros((ITERS, LANES - height), jnp.float32)

    def repeated(strip):
        if strip.shape[1] < LANES:
            strip = jnp.concatenate([strip, empty], axis=1)
        return jnp.concatenate([strip] * (rows // ITERS), axis=0)

    near = (jnp.abs(down) <= 1).astype(jnp.int32)
    strips = jnp.zeros((rows, LANES), jnp.float32)
    strips = jnp.where((right == 0) & (down == 1), repeated(state[height - ITERS :]), strips)
    strips = jnp.where((right == 0) & (down == -1), repeated(state[:ITERS]), strips)
    strips = jnp.where((right == 1) & (near == 1), repeated(columns[width - ITERS :]), strips)
    return jnp.where((right == -1) & (near == 1), repeated(columns[:ITERS]), strips)


def cell_totals(arrived, code, place, first):
    lane_rows = place.shape[0]
    marks = code[...]
    window = lane_pick(arrived[...], (marks + first) & 127)
    placed = jnp.concatenate(
        [
            jnp.where((marks >= 0) & (marks < LANES), window, 0.0),
            jnp.where(marks >= LANES, window, 0.0),
        ],
        axis=1,
    )
    totals = matmul(place[...], jnp.concatenate(halves(placed), axis=1))
    totals = totals[:, :256] + totals[:, 256:]
    over = totals[:, LANES:]
    over = jnp.concatenate([over[lane_rows - 1 :], over[: lane_rows - 1]], axis=0)
    over = jnp.where(iota(over.shape, 0) == 0, 0.0, over)
    return totals[:, :LANES] + over


def unpack_runoff_kernel(arrived, code, place, river, runoff, storage, strips):
    total = cell_totals(arrived, code, place, 0)
    state = river[...] + total
    runoff[...] = total
    storage[...] = state
    strips[...] = strips_for_neighbours(state, strips.shape[0])


def unpack_runoff(homes, arrived, code, place, river):
    shape = jax.ShapeDtypeStruct((place.shape[0], LANES), jnp.float32)
    strips = jax.ShapeDtypeStruct((homes * ITERS, LANES), jnp.float32)
    return pl.pallas_call(
        unpack_runoff_kernel,
        out_shape=(shape, shape, strips),
        compiler_params=pltpu.CompilerParams(vmem_limit_bytes=VMEM_LIMIT),
        cost_estimate=pl.CostEstimate(flops=10**9, bytes_accessed=1 * MIB, transcendentals=0),
        name="unpack_runoff",
    )(arrived, code, place, river)


def unpack_evap_kernel(arrived, code, place, evap):
    evap[...] = cell_totals(arrived, code, place, WINDOW)


def unpack_evap(arrived, code, place):
    return pl.pallas_call(
        unpack_evap_kernel,
        out_shape=jax.ShapeDtypeStruct((place.shape[0], LANES), jnp.float32),
        compiler_params=pltpu.CompilerParams(vmem_limit_bytes=VMEM_LIMIT),
        cost_estimate=pl.CostEstimate(flops=10**9, bytes_accessed=1 * MIB, transcendentals=0),
        name="unpack_evap",
    )(arrived, code, place)


def segment_plan_kernel(cell, worker, meta):
    chunk = 96
    for start in range(0, cell.shape[0], chunk):
        values = cell[pl.ds(start, chunk), :]
        here = iota(values.shape, 1)
        target = here & (WINDOW - 1)
        count = jnp.zeros_like(values)
        for step in (64, 32, 16, 8, 4, 2, 1):
            probe = lane_pick(values, count + (step - 1))
            count = jnp.where(probe <= target, count + step, count)
        count = jnp.where(lane_pick(values, count) <= target, count + 1, count)
        last = jnp.maximum(count - 1, 0)
        found = (count > 0) & (lane_pick(values, last) == target)
        marks = jnp.where(found, last + 128, 0)
        for bit in range(7):
            step = 1 << bit
            same = (pltpu.roll(values, step, 1) == values) & (here >= step)
            marks = marks + jnp.where(same, 256 << bit, 0)
        odd = worker[pl.ds(start, chunk), :] & 1
        meta[pl.ds(start, chunk), :] = marks + (odd << 15)


def segment_plan(cell, worker):
    return pl.pallas_call(
        segment_plan_kernel,
        out_shape=jax.ShapeDtypeStruct(cell.shape, jnp.int32),
        compiler_params=pltpu.CompilerParams(vmem_limit_bytes=VMEM_LIMIT),
        cost_estimate=pl.CostEstimate(flops=10**8, bytes_accessed=1 * MIB, transcendentals=0),
        name="segment_plan",
    )(cell, worker)


def segment_totals(values, marks):
    total = values
    for bit in range(7):
        moved = pltpu.roll(total, 1 << bit, 1)
        total = total + jnp.where((marks & (256 << bit)) != 0, moved, 0.0)
    return lane_pick(total, marks & 127)


def land_kernel(
    slots, loss_rows, rain_rows, arrived, cell, meta, area, water, cap, soil_in, porosity_in,
    drainage_in, _, soil_out, canopy_new, sums_out, soil, porosity, drainage, losses, rains,
    runoffs, evaps, ready, written,
):
    layers, rows = soil.shape[:2]
    block = rows // ready.shape[0]
    chunk = block // 2
    steps = rows // block
    arrays = ((soil_in, soil), (porosity_in, porosity), (drainage_in, drainage))

    def part_of(step):
        return pl.ds(step * block, block)

    def reads(step):
        return [
            pltpu.make_async_copy(
                source.at[:, part_of(step), :], target.at[:, part_of(step), :], ready.at[step, i]
            )
            for i, (source, target) in enumerate(arrays)
        ]

    def write(step):
        return pltpu.make_async_copy(
            soil.at[:, part_of(step), :], soil_out.at[:, part_of(step), :], written.at[step]
        )

    def fetch(i, carry):
        losses[pl.ds(i, 1), :] = arrived[pl.ds(loss_rows[i], 1), :]
        rains[pl.ds(i, 1), :] = arrived[pl.ds(rain_rows[i], 1), :]
        return carry

    def cascade(part):
        index = cell[part, :]
        rain = lane_pick(rains[part, :], index + (meta[part, :] >> 9 & WINDOW))
        demand = lane_pick(losses[part, :], index)
        limit = lane_pick(losses[part, :], index + WINDOW)
        wetted = water[part, :] + rain
        flowing = jnp.maximum(wetted - cap[part, :], 0.0)
        retained = jnp.minimum(wetted, cap[part, :])
        canopy_loss = jnp.minimum(demand, retained)
        canopy_new[part, :] = retained - canopy_loss
        surface = jnp.zeros_like(flowing)
        for layer in range(layers):
            filled = soil[layer, part, :] + flowing
            excess = jnp.maximum(filled - porosity[layer, part, :], 0.0)
            surface = surface + excess
            filled = filled - excess
            flowing = drainage[layer, part, :] * filled
            middle = filled - flowing
            if layer == 0:
                soil_loss = jnp.minimum(jnp.minimum(limit, demand - canopy_loss), 0.5 * middle)
                middle = middle - soil_loss
                evaps[part, :] = area[part, :] * (canopy_loss + soil_loss)
            soil[layer, part, :] = middle
        runoffs[part, :] = area[part, :] * (surface + flowing)

    def scan(step):
        part = part_of(step)
        marks = meta[part, :]
        runoff = segment_totals(runoffs[part, :], marks)
        evap = segment_totals(evaps[part, :], marks)
        both = jnp.where(iota(runoff.shape, 1) < WINDOW, runoff, evap)
        runoffs[part, :] = jnp.where((marks & 128) != 0, both, 0.0)

    def hand_back(step):
        for i in range(step * block, (step + 1) * block):
            sums_out[pl.ds(slots[i], 1), :] = runoffs[pl.ds(i, 1), :]

    for step in range(steps):
        for copy in reads(step):
            copy.start()
    sums_out[...] = jnp.zeros_like(sums_out)
    lax.fori_loop(0, rows, fetch, 0, unroll=16)
    for step in range(steps + 2):
        if step < steps:
            for copy in reads(step):
                copy.wait()
            for start in range(step * block, (step + 1) * block, chunk):
                cascade(pl.ds(start, chunk))
        if 1 <= step <= steps:
            scan(step - 1)
        if step >= 2:
            hand_back(step - 2)
        if step < steps:
            write(step).start()
    for step in range(steps):
        write(step).wait()


def land_step(
    sums_shape, slots, loss_rows, rain_rows, arrived, cell, meta, area, water, cap, soil,
    porosity, drainage, fixed,
):
    layers, rows = soil.shape[:2]
    steps = 5
    near = pl.BlockSpec(memory_space=pltpu.VMEM)
    far = pl.BlockSpec(memory_space=pltpu.HBM)
    return pl.pallas_call(
        land_kernel,
        in_specs=[pl.BlockSpec(memory_space=pltpu.SMEM)] * 3 + [near] * 6 + [far] * 3
        + [pl.BlockSpec(memory_space=pl.ANY)],
        out_specs=[far, near, near],
        scratch_shapes=[pltpu.VMEM(soil.shape, jnp.float32)] * 3
        + [pltpu.VMEM((rows, LANES), jnp.float32)] * 4
        + [pltpu.SemaphoreType.DMA((steps, 3)), pltpu.SemaphoreType.DMA((steps,))],
        out_shape=(
            jax.ShapeDtypeStruct(soil.shape, jnp.float32),
            jax.ShapeDtypeStruct((rows, LANES), jnp.float32),
            jax.ShapeDtypeStruct(sums_shape, jnp.float32),
        ),
        compiler_params=pltpu.CompilerParams(vmem_limit_bytes=VMEM_LIMIT),
        cost_estimate=pl.CostEstimate(flops=10**8, bytes_accessed=20 * MIB, transcendentals=0),
        name="land_layers",
    )(
        slots, loss_rows, rain_rows, arrived, cell, meta, area, water, cap, in_hbm(soil),
        in_hbm(porosity), in_hbm(drainage), fixed,
    )


def halo_parts(value, axis, dim, width):
    count, length = (lax.axis_size(axis), value.shape[dim])
    up = [(i, i + 1) for i in range(count - 1)]
    down = [(j, i) for i, j in up]
    last = lax.slice_in_dim(value, length - width, length, axis=dim)
    initial = lax.slice_in_dim(value, 0, width, axis=dim)
    return lax.ppermute(last, axis, up), lax.ppermute(initial, axis, down)


def with_halo(value, width):
    rows, cols = value.ndim - 2, value.ndim - 1
    before, after = halo_parts(value, "region", rows, width)
    tall = jnp.concatenate([value, after, before], axis=rows)
    before, after = halo_parts(tall, "col", cols, width)
    gap = jnp.zeros(tall.shape[:-1] + (LANES - 2 * width,), value.dtype)
    return jnp.concatenate([tall, after, gap, before], axis=cols)


def river_kernel(state, strips, fixed, out):
    height, width = state.shape
    region, col = lax.axis_index("region"), lax.axis_index("col")

    def strip(down, right):
        row, column = region + down, col + right
        there = (row >= 0) & (row < lax.axis_size("region"))
        there &= (column >= 0) & (column < lax.axis_size("col"))
        device = jnp.where(there, row * lax.axis_size("col") + column, 0)
        return strips[pl.ds(device * ITERS, ITERS), :] * jnp.where(there, 1.0, 0.0)

    def column_strip(right):
        middle, above, below = strip(0, right), strip(-1, right), strip(1, right)
        return jnp.concatenate(
            [
                middle[:, :height],
                below[:, :ITERS],
                above[:, height - ITERS : height],
                jnp.zeros((ITERS, LANES - height - 2 * ITERS), jnp.float32),
            ],
            axis=1,
        )

    gap = jnp.zeros((LANES - 2 * ITERS, LANES), jnp.float32)
    sides = jnp.concatenate([column_strip(1), gap, column_strip(-1)], axis=0)
    sides = jnp.transpose(sides)[: height + 2 * ITERS]
    tall = jnp.concatenate([state[...], strip(1, 0), strip(-1, 0)], axis=0)
    storage = jnp.concatenate([tall, sides], axis=1)
    rate = fixed[0]
    code = fixed[1]
    rows, cols = storage.shape
    for _ in range(ITERS):
        outflow = rate * storage
        inflow = jnp.zeros_like(storage)
        for col_step in (-1, 0, 1):
            column = jnp.zeros_like(storage)
            for bit, (row_step, step) in enumerate(directions):
                if step != col_step:
                    continue
                leaving = jnp.where(code == float(1 << bit), outflow, 0.0)
                if row_step:
                    leaving = pltpu.roll(leaving, row_step % rows, 0)
                column = column + leaving
            if col_step:
                column = pltpu.roll(column, col_step % cols, 1)
            inflow = inflow + column
        storage = storage - outflow + inflow
    out[...] = storage[:height, :width]


def river(state, strips, fixed):
    return pl.pallas_call(
        river_kernel,
        out_shape=jax.ShapeDtypeStruct(state.shape, jnp.float32),
        compiler_params=pltpu.CompilerParams(vmem_limit_bytes=VMEM_LIMIT),
        cost_estimate=pl.CostEstimate(flops=10**7, bytes_accessed=1 * MIB, transcendentals=0),
        name="river_steps",
    )(state, strips, fixed)


def exchange(value):
    return lax.all_to_all(value, axes, split_axis=0, concat_axis=0, tiled=True)


def shards(
    forcing,
    river_storage,
    river_rate,
    flow_code,
    home_slot,
    home_offset,
    worker_list,
    patch_cell,
    patch_area,
    canopy_water,
    canopy_cap,
    soil_water,
    porosity,
    drainage,
):
    homes = lax.axis_size("region") * lax.axis_size("col")
    capacity = home_slot.shape[1] // homes
    grid_rows, grid_cols = river_storage.shape
    lane_rows = grid_rows * grid_cols // LANES
    outgoing = pack(
        homes, capacity, home_slot, home_offset, forcing.reshape(3, lane_rows, LANES)
    )
    arrived = exchange(outgoing).reshape(-1, LANES)
    home = worker_list // capacity
    position = worker_list - home * capacity
    loss_rows = home * outgoing.shape[1] + position
    rain_rows = home * outgoing.shape[1] + capacity + position // 2
    meta = segment_plan(patch_cell, worker_list[:, None])
    code, place = unpack_plan(homes, capacity, lane_rows, home_slot, home_offset)
    fixed = with_halo(jnp.stack([river_rate, flow_code.astype(jnp.float32)]), ITERS)
    soil_new, canopy_new, sums = land_step(
        (homes * capacity, LANES), worker_list, loss_rows, rain_rows, arrived, patch_cell, meta,
        patch_area, canopy_water, canopy_cap, soil_water, porosity, drainage, fixed,
    )
    returned = exchange(sums)
    cell_runoff, storage, strips = unpack_runoff(
        homes, returned, code, place, river_storage.reshape(lane_rows, LANES)
    )
    cell_evap = unpack_evap(returned, code, place)
    river_new = river(storage.reshape(river_storage.shape), exchange(strips), fixed)
    return (
        soil_new,
        canopy_new,
        cell_runoff.reshape(river_storage.shape),
        cell_evap.reshape(river_storage.shape),
        river_new,
    )


def solution(mesh):
    placed = (
        P(None, "region", "col"),
        P("region", "col"),
        P("region", "col"),
        P("region", "col"),
        P(("region", "col"), None),
        P(("region", "col"), None),
        P(("region", "col")),
        P(("region", "col"), None),
        P(("region", "col"), None),
        P(("region", "col"), None),
        P(("region", "col"), None),
        P(None, ("region", "col"), None),
        P(None, ("region", "col"), None),
        P(None, ("region", "col"), None),
    )
    return jax.shard_map(
        shards,
        mesh=mesh,
        in_specs=placed,
        out_specs=(
            P(None, ("region", "col"), None),
            P(("region", "col"), None),
            P("region", "col"),
            P("region", "col"),
            P("region", "col"),
        ),
        check_vma=False,
    )
```

```python
import functools

import jax
import jax.numpy as jnp
from jax import lax
from jax.experimental import pallas as pl
from jax.experimental.pallas import tpu as pltpu
from jax.sharding import PartitionSpec as P

ITERS = 4
WINDOW = 64
LANES = 128
MIB = 1024 * 1024
VMEM_LIMIT = 24 * MIB

directions = ((0, 1), (1, 1), (1, 0), (1, -1), (0, -1), (-1, -1), (-1, 0), (-1, 1))
axes = ("region", "col")


def iota(shape, dim):
    return lax.broadcasted_iota(jnp.int32, shape, dim)


def onehot(mask):
    return jnp.where(mask, jnp.float32(1.0), jnp.float32(0.0)).astype(jnp.bfloat16)


def lane_pick(values, index):
    return jnp.take_along_axis(values, index, axis=1, mode="promise_in_bounds")


def in_hbm(value):
    return pltpu.with_memory_space_constraint(value, pltpu.HBM)


def thirds(value):
    high = value.astype(jnp.bfloat16)
    rest = value - high.astype(jnp.float32)
    middle = rest.astype(jnp.bfloat16)
    low = (rest - middle.astype(jnp.float32)).astype(jnp.bfloat16)
    return high, middle, low


def halves(value):
    high = value.astype(jnp.bfloat16)
    return high, (value - high.astype(jnp.float32)).astype(jnp.bfloat16)


def matmul(a, b, a_dim=1, b_dim=0):
    return lax.dot_general(
        a, b, (((a_dim,), (b_dim,)), ((), ())), preferred_element_type=jnp.float32
    )


def slot_factors(slot, offset, homes, capacity):
    slots = slot.shape[1]
    worker = slot // capacity if capacity & (capacity - 1) else slot >> (capacity.bit_length() - 1)
    position = slot - worker * capacity
    by_worker = onehot(iota((homes, slots), 0) == worker)
    at_position = iota((capacity, slots), 0) == position
    row = jnp.where(at_position, ((offset >> 7) + 1).astype(jnp.float32), 0.0)
    lane = jnp.where(at_position, (offset & 127).astype(jnp.float32), 0.0)
    return by_worker, row.astype(jnp.bfloat16), lane.astype(jnp.bfloat16)


def slot_columns(slot, offset, homes, capacity):
    slots = slot.shape[1]
    by_worker, row, lane = slot_factors(slot, offset, homes, capacity)
    table = matmul(by_worker, jnp.concatenate([row, lane], axis=0), 1, 1)
    spread = jnp.broadcast_to(table[:, None, :], (homes, capacity, 2 * capacity))
    spread = spread.reshape(slots, 2 * capacity)
    place = iota(spread.shape, 0) % capacity == iota(spread.shape, 1) % capacity
    kept = jnp.where(place, spread, 0.0).astype(jnp.bfloat16)
    shape = (2 * capacity, 2 * LANES)
    gather = onehot((iota(shape, 0) >= capacity) == (iota(shape, 1) >= LANES))
    columns = matmul(kept, gather).astype(jnp.int32)
    return columns[:, :LANES] - 1, columns[:, LANES:]


def slot_rows(slot, offset, homes, capacity):
    slots = slot.shape[1]
    by_worker, row, lane = slot_factors(slot, offset, homes, capacity)
    table = matmul(jnp.concatenate([row, lane], axis=0), by_worker, 1, 1).astype(jnp.bfloat16)
    number = iota((1, slots), 1)
    worker = number // capacity
    position = number - worker * capacity
    spread = matmul(table, onehot(iota((homes, slots), 0) == worker))
    at_position = iota((capacity, slots), 0) == position
    rows = jnp.sum(jnp.where(at_position, spread[:capacity], 0.0), axis=0, keepdims=True)
    lanes = jnp.sum(jnp.where(at_position, spread[capacity:], 0.0), axis=0, keepdims=True)
    return rows.astype(jnp.int32) - 1, lanes.astype(jnp.int32)


def pack_kernel(
    homes, capacity, slot_in, offset_in, forcing_in, out, slot, offset, forcing, row_of, lane_of,
    rain, losses, ready,
):
    copies = [
        pltpu.make_async_copy(source, target, ready.at[i])
        for i, (source, target) in enumerate(
            ((slot_in, slot), (offset_in, offset), (forcing_in, forcing))
        )
    ]
    for copy in copies:
        copy.start()
    for copy in copies:
        copy.wait()
    slots = slot.shape[1]
    lane_rows = forcing.shape[1]
    row_of[...], lane_of[...] = slot_columns(slot[...], offset[...], homes, capacity)
    parts = []
    for var in range(3):
        here = forcing[var]
        following = jnp.concatenate([here[1:], here[:1]], axis=0)
        parts += [here, following]
    table = jnp.concatenate(thirds(jnp.concatenate(parts, axis=1)), axis=0)
    chunk = 128
    for start in range(0, slots, chunk):
        row = row_of[pl.ds(start, chunk), :]
        lane = lane_of[pl.ds(start, chunk), :]
        shape = (chunk, 3 * lane_rows)
        wide = jnp.concatenate([row, row], axis=1)[:, : 3 * lane_rows]
        pick = onehot(wide == iota(shape, 1) % lane_rows)
        rows = matmul(pick, table)
        here = iota((chunk, LANES), 1)
        after = here >= lane
        joined = [
            jnp.where(
                after,
                rows[:, 2 * var * LANES : (2 * var + 1) * LANES],
                rows[:, (2 * var + 1) * LANES : (2 * var + 2) * LANES],
            )
            for var in range(3)
        ]
        first = (here + lane) & 127
        second = (first + WINDOW) & 127
        odd = iota((chunk, LANES), 0) & 1 == 1
        rain[pl.ds(start, chunk), :] = lane_pick(joined[0], jnp.where(odd, second, first))
        losses[pl.ds(start, chunk), :] = jnp.where(
            here < WINDOW, lane_pick(joined[1], first), lane_pick(joined[2], second)
        )
    pairs = capacity // 2
    for home in range(homes):
        start = home * capacity
        out[home, :capacity, :] = losses[pl.ds(start, capacity), :]
        even_rows = rain[pl.ds(start, pairs, stride=2), :]
        odd_rows = rain[pl.ds(start + 1, pairs, stride=2), :]
        out[home, capacity:, :] = jnp.where(
            iota(even_rows.shape, 1) < WINDOW, even_rows, odd_rows
        )


def pack(homes, capacity, slot, offset, forcing):
    slots = slot.shape[1]
    return pl.pallas_call(
        functools.partial(pack_kernel, homes, capacity),
        in_specs=[pl.BlockSpec(memory_space=pltpu.HBM)] * 3,
        out_shape=jax.ShapeDtypeStruct((homes, capacity + capacity // 2, LANES), jnp.float32),
        scratch_shapes=[
            pltpu.VMEM(slot.shape, jnp.int32),
            pltpu.VMEM(offset.shape, jnp.int32),
            pltpu.VMEM(forcing.shape, jnp.float32),
            pltpu.VMEM((slots, LANES), jnp.int32),
            pltpu.VMEM((slots, LANES), jnp.int32),
            pltpu.VMEM((slots, LANES), jnp.float32),
            pltpu.VMEM((slots, LANES), jnp.float32),
            pltpu.SemaphoreType.DMA((3,)),
        ],
        compiler_params=pltpu.CompilerParams(vmem_limit_bytes=VMEM_LIMIT),
        cost_estimate=pl.CostEstimate(flops=10**9, bytes_accessed=2 * MIB, transcendentals=0),
        name="pack_forcing",
    )(in_hbm(slot), in_hbm(offset), in_hbm(forcing))


def unpack_plan_kernel(homes, capacity, lane_rows, slot, offset, code, place):
    slots = slot.shape[1]
    row, lane = slot_columns(slot[...], offset[...], homes, capacity)
    here = iota((slots, LANES), 1)
    index = (here - lane) & 127
    inside = (index < WINDOW) & (row >= 0)
    code[...] = jnp.where(inside, index + jnp.where(here >= lane, 0, LANES), -1)
    row_lane, _ = slot_rows(slot[...], offset[...], homes, capacity)
    place[...] = onehot(iota((lane_rows, slots), 0) == row_lane)


def unpack_plan(homes, capacity, lane_rows, slot, offset):
    slots = slot.shape[1]
    return pl.pallas_call(
        functools.partial(unpack_plan_kernel, homes, capacity, lane_rows),
        out_shape=(
            jax.ShapeDtypeStruct((slots, LANES), jnp.int32),
            jax.ShapeDtypeStruct((lane_rows, slots), jnp.bfloat16),
        ),
        compiler_params=pltpu.CompilerParams(vmem_limit_bytes=VMEM_LIMIT),
        cost_estimate=pl.CostEstimate(flops=10**9, bytes_accessed=2 * MIB, transcendentals=0),
        name="unpack_plan",
    )(slot, offset)


def strips_for_neighbours(state, rows):
    device = iota((rows, LANES), 0) // ITERS
    down = device // lax.axis_size("col") - lax.axis_index("region")
    right = device % lax.axis_size("col") - lax.axis_index("col")
    height, width = state.shape
    columns = jnp.transpose(state)
    empty = jnp.zeros((ITERS, LANES - height), jnp.float32)

    def repeated(strip):
        if strip.shape[1] < LANES:
            strip = jnp.concatenate([strip, empty], axis=1)
        return jnp.concatenate([strip] * (rows // ITERS), axis=0)

    near = (jnp.abs(down) <= 1).astype(jnp.int32)
    strips = jnp.zeros((rows, LANES), jnp.float32)
    strips = jnp.where((right == 0) & (down == 1), repeated(state[height - ITERS :]), strips)
    strips = jnp.where((right == 0) & (down == -1), repeated(state[:ITERS]), strips)
    strips = jnp.where((right == 1) & (near == 1), repeated(columns[width - ITERS :]), strips)
    return jnp.where((right == -1) & (near == 1), repeated(columns[:ITERS]), strips)


def cell_totals(arrived, code, place, first):
    lane_rows = place.shape[0]
    marks = code[...]
    window = lane_pick(arrived[...], (marks + first) & 127)
    placed = jnp.concatenate(
        [
            jnp.where((marks >= 0) & (marks < LANES), window, 0.0),
            jnp.where(marks >= LANES, window, 0.0),
        ],
        axis=1,
    )
    totals = matmul(place[...], jnp.concatenate(halves(placed), axis=1))
    totals = totals[:, :256] + totals[:, 256:]
    over = totals[:, LANES:]
    over = jnp.concatenate([over[lane_rows - 1 :], over[: lane_rows - 1]], axis=0)
    over = jnp.where(iota(over.shape, 0) == 0, 0.0, over)
    return totals[:, :LANES] + over


def unpack_runoff_kernel(arrived, code, place, river, runoff, storage, strips):
    total = cell_totals(arrived, code, place, 0)
    state = river[...] + total
    runoff[...] = total
    storage[...] = state
    strips[...] = strips_for_neighbours(state, strips.shape[0])


def unpack_runoff(homes, arrived, code, place, river):
    shape = jax.ShapeDtypeStruct((place.shape[0], LANES), jnp.float32)
    strips = jax.ShapeDtypeStruct((homes * ITERS, LANES), jnp.float32)
    return pl.pallas_call(
        unpack_runoff_kernel,
        out_shape=(shape, shape, strips),
        compiler_params=pltpu.CompilerParams(vmem_limit_bytes=VMEM_LIMIT),
        cost_estimate=pl.CostEstimate(flops=10**9, bytes_accessed=1 * MIB, transcendentals=0),
        name="unpack_runoff",
    )(arrived, code, place, river)


def unpack_evap_kernel(arrived, code, place, evap):
    evap[...] = cell_totals(arrived, code, place, WINDOW)


def unpack_evap(arrived, code, place):
    return pl.pallas_call(
        unpack_evap_kernel,
        out_shape=jax.ShapeDtypeStruct((place.shape[0], LANES), jnp.float32),
        compiler_params=pltpu.CompilerParams(vmem_limit_bytes=VMEM_LIMIT),
        cost_estimate=pl.CostEstimate(flops=10**9, bytes_accessed=1 * MIB, transcendentals=0),
        name="unpack_evap",
    )(arrived, code, place)


def segment_plan_kernel(cell, worker, meta):
    chunk = 96
    for start in range(0, cell.shape[0], chunk):
        values = cell[pl.ds(start, chunk), :]
        here = iota(values.shape, 1)
        target = here & (WINDOW - 1)
        count = jnp.zeros_like(values)
        for step in (64, 32, 16, 8, 4, 2, 1):
            probe = lane_pick(values, count + (step - 1))
            count = jnp.where(probe <= target, count + step, count)
        count = jnp.where(lane_pick(values, count) <= target, count + 1, count)
        last = jnp.maximum(count - 1, 0)
        found = (count > 0) & (lane_pick(values, last) == target)
        marks = jnp.where(found, last + 128, 0)
        for bit in range(7):
            step = 1 << bit
            same = (pltpu.roll(values, step, 1) == values) & (here >= step)
            marks = marks + jnp.where(same, 256 << bit, 0)
        odd = worker[pl.ds(start, chunk), :] & 1
        meta[pl.ds(start, chunk), :] = marks + (odd << 15)


def segment_plan(cell, worker):
    return pl.pallas_call(
        segment_plan_kernel,
        out_shape=jax.ShapeDtypeStruct(cell.shape, jnp.int32),
        compiler_params=pltpu.CompilerParams(vmem_limit_bytes=VMEM_LIMIT),
        cost_estimate=pl.CostEstimate(flops=10**8, bytes_accessed=1 * MIB, transcendentals=0),
        name="segment_plan",
    )(cell, worker)


def segment_totals(values, marks):
    total = values
    for bit in range(7):
        moved = pltpu.roll(total, 1 << bit, 1)
        total = total + jnp.where((marks & (256 << bit)) != 0, moved, 0.0)
    return lane_pick(total, marks & 127)


def stage_kernel(soil_in, porosity_in, drainage_in, _, soil, porosity, drainage, ready):
    pairs = ((soil_in, soil), (porosity_in, porosity), (drainage_in, drainage))
    copies = [pltpu.make_async_copy(a, b, ready.at[i]) for i, (a, b) in enumerate(pairs)]
    for copy in copies:
        copy.start()
    for copy in copies:
        copy.wait()


def stage(soil, porosity, drainage, after):
    far = pl.BlockSpec(memory_space=pltpu.HBM)
    near = pl.BlockSpec(memory_space=pltpu.VMEM)
    return pl.pallas_call(
        stage_kernel,
        in_specs=[far] * 3 + [pl.BlockSpec(memory_space=pl.ANY)],
        out_specs=[near] * 3,
        out_shape=[pltpu.VMEM(soil.shape, jnp.float32)] * 3,
        scratch_shapes=[pltpu.SemaphoreType.DMA((3,))],
        compiler_params=pltpu.CompilerParams(vmem_limit_bytes=4 * MIB),
        cost_estimate=pl.CostEstimate(flops=0, bytes_accessed=22 * MIB, transcendentals=0),
        name="stage_soil",
    )(in_hbm(soil), in_hbm(porosity), in_hbm(drainage), after)


def land_kernel(
    slots, loss_rows, rain_rows, arrived, cell, meta, area, water, cap, soil, porosity,
    drainage, soil_out, canopy_new, sums_out, soil_new, losses, rains, runoffs, evaps, written,
):
    layers, rows = soil.shape[:2]
    steps = written.shape[0]
    block = rows // steps
    chunk = block // 2

    def part_of(step):
        return pl.ds(step * block, block)

    def write(step):
        return pltpu.make_async_copy(
            soil_new.at[:, part_of(step), :], soil_out.at[:, part_of(step), :], written.at[step]
        )

    def fetch(step):
        for i in range(step * block, (step + 1) * block):
            losses[pl.ds(i, 1), :] = arrived[pl.ds(loss_rows[i], 1), :]
            rains[pl.ds(i, 1), :] = arrived[pl.ds(rain_rows[i], 1), :]

    def cascade(part):
        index = cell[part, :]
        rain = lane_pick(rains[part, :], index + (meta[part, :] >> 9 & WINDOW))
        demand = lane_pick(losses[part, :], index)
        limit = lane_pick(losses[part, :], index + WINDOW)
        wetted = water[part, :] + rain
        flowing = jnp.maximum(wetted - cap[part, :], 0.0)
        retained = jnp.minimum(wetted, cap[part, :])
        canopy_loss = jnp.minimum(demand, retained)
        canopy_new[part, :] = retained - canopy_loss
        surface = jnp.zeros_like(flowing)
        for layer in range(layers):
            filled = soil[layer, part, :] + flowing
            excess = jnp.maximum(filled - porosity[layer, part, :], 0.0)
            surface = surface + excess
            filled = filled - excess
            flowing = drainage[layer, part, :] * filled
            middle = filled - flowing
            if layer == 0:
                soil_loss = jnp.minimum(jnp.minimum(limit, demand - canopy_loss), 0.5 * middle)
                middle = middle - soil_loss
                evaps[part, :] = area[part, :] * (canopy_loss + soil_loss)
            soil_new[layer, part, :] = middle
        runoffs[part, :] = area[part, :] * (surface + flowing)

    def scan(step):
        part = part_of(step)
        marks = meta[part, :]
        runoff = segment_totals(runoffs[part, :], marks)
        evap = segment_totals(evaps[part, :], marks)
        both = jnp.where(iota(runoff.shape, 1) < WINDOW, runoff, evap)
        runoffs[part, :] = jnp.where((marks & 128) != 0, both, 0.0)

    def hand_back(step):
        for i in range(step * block, (step + 1) * block):
            sums_out[pl.ds(slots[i], 1), :] = runoffs[pl.ds(i, 1), :]

    sums_out[...] = jnp.zeros_like(sums_out)
    fetch(0)
    for step in range(steps + 2):
        if step + 1 < steps:
            fetch(step + 1)
        if step < steps:
            for start in range(step * block, (step + 1) * block, chunk):
                cascade(pl.ds(start, chunk))
        if 1 <= step <= steps:
            scan(step - 1)
        if step >= 2:
            hand_back(step - 2)
        if step < steps:
            write(step).start()
    for step in range(steps):
        write(step).wait()


def land_step(
    sums_shape, slots, loss_rows, rain_rows, arrived, cell, meta, area, water, cap, staged
):
    layers, rows = staged[0].shape[:2]
    steps = 5
    near = pl.BlockSpec(memory_space=pltpu.VMEM)
    return pl.pallas_call(
        land_kernel,
        in_specs=[pl.BlockSpec(memory_space=pltpu.SMEM)] * 3 + [near] * 9,
        out_specs=[pl.BlockSpec(memory_space=pltpu.HBM), near, near],
        scratch_shapes=[pltpu.VMEM(staged[0].shape, jnp.float32)]
        + [pltpu.VMEM((rows, LANES), jnp.float32)] * 4
        + [pltpu.SemaphoreType.DMA((steps,))],
        out_shape=(
            jax.ShapeDtypeStruct(staged[0].shape, jnp.float32),
            jax.ShapeDtypeStruct((rows, LANES), jnp.float32),
            jax.ShapeDtypeStruct(sums_shape, jnp.float32),
        ),
        compiler_params=pltpu.CompilerParams(vmem_limit_bytes=VMEM_LIMIT),
        cost_estimate=pl.CostEstimate(flops=10**8, bytes_accessed=20 * MIB, transcendentals=0),
        name="land_layers",
    )(
        slots, loss_rows, rain_rows, arrived, cell, meta, area, water, cap,
        *(pltpu.with_memory_space_constraint(value, pltpu.VMEM) for value in staged),
    )


def edge_strips_kernel(rate, code, _, out):
    for first, values in ((0, rate[...]), (4 * ITERS, code[...].astype(jnp.float32))):
        height, width = values.shape
        columns = jnp.transpose(values)
        columns = jnp.concatenate([columns, jnp.zeros((width, LANES - height), jnp.float32)], 1)
        strips = (
            values[:ITERS], values[height - ITERS :], columns[:ITERS], columns[width - ITERS :]
        )
        for number, strip in enumerate(strips):
            out[pl.ds(first + number * ITERS, ITERS), :] = strip


def edge_strips(rate, code, after):
    return pl.pallas_call(
        edge_strips_kernel,
        in_specs=[pl.BlockSpec(memory_space=pltpu.VMEM)] * 2 + [pl.BlockSpec(memory_space=pl.ANY)],
        out_shape=jax.ShapeDtypeStruct((8 * ITERS, LANES), jnp.float32),
        compiler_params=pltpu.CompilerParams(vmem_limit_bytes=VMEM_LIMIT),
        cost_estimate=pl.CostEstimate(flops=10**6, bytes_accessed=10**5, transcendentals=0),
        name="edge_strips",
    )(rate, code, after)


def extended(own, strip):
    height = own.shape[0]

    def column_strip(right):
        middle, above, below = strip(0, right), strip(-1, right), strip(1, right)
        return jnp.concatenate(
            [
                middle[:, :height],
                below[:, :ITERS],
                above[:, height - ITERS : height],
                jnp.zeros((ITERS, LANES - height - 2 * ITERS), jnp.float32),
            ],
            axis=1,
        )

    gap = jnp.zeros((LANES - 2 * ITERS, LANES), jnp.float32)
    sides = jnp.concatenate([column_strip(1), gap, column_strip(-1)], axis=0)
    sides = jnp.transpose(sides)[: height + 2 * ITERS]
    tall = jnp.concatenate([own, strip(1, 0), strip(-1, 0)], axis=0)
    return jnp.concatenate([tall, sides], axis=1)


def neighbour(down, right):
    row, column = lax.axis_index("region") + down, lax.axis_index("col") + right
    there = (row >= 0) & (row < lax.axis_size("region"))
    there &= (column >= 0) & (column < lax.axis_size("col"))
    return jnp.where(there, row * lax.axis_size("col") + column, 0), jnp.where(there, 1.0, 0.0)


def static_halo_kernel(rate, code, strips, out):
    def strip_at(first):
        def strip(down, right):
            device, there = neighbour(down, right)
            kind = {0: 0 if down == 1 else 1, 1: 2, -1: 3}[right]
            start = device * (8 * ITERS) + first + kind * ITERS
            return strips[pl.ds(start, ITERS), :] * there

        return strip

    out[0] = extended(rate[...], strip_at(0))
    out[1] = extended(code[...].astype(jnp.float32), strip_at(4 * ITERS))


def static_halo(rate, code, strips):
    height, width = rate.shape
    shape = (2, height + 2 * ITERS, width + LANES)
    return pl.pallas_call(
        static_halo_kernel,
        out_shape=jax.ShapeDtypeStruct(shape, jnp.float32),
        compiler_params=pltpu.CompilerParams(vmem_limit_bytes=VMEM_LIMIT),
        cost_estimate=pl.CostEstimate(flops=10**6, bytes_accessed=10**6, transcendentals=0),
        name="static_halo",
    )(rate, code, strips)


def river_kernel(state, strips, fixed, out):
    height, width = state.shape

    def strip(down, right):
        device, there = neighbour(down, right)
        return strips[pl.ds(device * ITERS, ITERS), :] * there

    storage = extended(state[...], strip)
    rate = fixed[0]
    code = fixed[1]
    rows, cols = storage.shape
    for _ in range(ITERS):
        outflow = rate * storage
        inflow = jnp.zeros_like(storage)
        for col_step in (-1, 0, 1):
            column = jnp.zeros_like(storage)
            for bit, (row_step, step) in enumerate(directions):
                if step != col_step:
                    continue
                leaving = jnp.where(code == float(1 << bit), outflow, 0.0)
                if row_step:
                    leaving = pltpu.roll(leaving, row_step % rows, 0)
                column = column + leaving
            if col_step:
                column = pltpu.roll(column, col_step % cols, 1)
            inflow = inflow + column
        storage = storage - outflow + inflow
    out[...] = storage[:height, :width]


def river(state, strips, fixed):
    return pl.pallas_call(
        river_kernel,
        out_shape=jax.ShapeDtypeStruct(state.shape, jnp.float32),
        compiler_params=pltpu.CompilerParams(vmem_limit_bytes=VMEM_LIMIT),
        cost_estimate=pl.CostEstimate(flops=10**7, bytes_accessed=1 * MIB, transcendentals=0),
        name="river_steps",
    )(state, strips, fixed)


def exchange(value):
    return lax.all_to_all(value, axes, split_axis=0, concat_axis=0, tiled=True)


def shards(
    forcing,
    river_storage,
    river_rate,
    flow_code,
    home_slot,
    home_offset,
    worker_list,
    patch_cell,
    patch_area,
    canopy_water,
    canopy_cap,
    soil_water,
    porosity,
    drainage,
):
    homes = lax.axis_size("region") * lax.axis_size("col")
    capacity = home_slot.shape[1] // homes
    grid_rows, grid_cols = river_storage.shape
    lane_rows = grid_rows * grid_cols // LANES
    outgoing = pack(
        homes, capacity, home_slot, home_offset, forcing.reshape(3, lane_rows, LANES)
    )
    arrived = exchange(outgoing).reshape(-1, LANES)
    home = worker_list // capacity
    position = worker_list - home * capacity
    loss_rows = home * outgoing.shape[1] + position
    rain_rows = home * outgoing.shape[1] + capacity + position // 2
    meta = segment_plan(patch_cell, worker_list[:, None])
    code, place = unpack_plan(homes, capacity, lane_rows, home_slot, home_offset)
    edges = lax.all_gather(
        edge_strips(river_rate, flow_code, outgoing), axes, axis=0, tiled=True
    )
    staged = stage(soil_water, porosity, drainage, outgoing)
    soil_new, canopy_new, sums = land_step(
        (homes * capacity, LANES), worker_list, loss_rows, rain_rows, arrived, patch_cell, meta,
        patch_area, canopy_water, canopy_cap, staged,
    )
    returned = exchange(sums)
    cell_runoff, storage, strips = unpack_runoff(
        homes, returned, code, place, river_storage.reshape(lane_rows, LANES)
    )
    fixed = static_halo(river_rate, flow_code, edges)
    cell_evap = unpack_evap(returned, code, place)
    river_new = river(storage.reshape(river_storage.shape), exchange(strips), fixed)
    return (
        soil_new,
        canopy_new,
        cell_runoff.reshape(river_storage.shape),
        cell_evap.reshape(river_storage.shape),
        river_new,
    )


def solution(mesh):
    placed = (
        P(None, "region", "col"),
        P("region", "col"),
        P("region", "col"),
        P("region", "col"),
        P(("region", "col"), None),
        P(("region", "col"), None),
        P(("region", "col")),
        P(("region", "col"), None),
        P(("region", "col"), None),
        P(("region", "col"), None),
        P(("region", "col"), None),
        P(None, ("region", "col"), None),
        P(None, ("region", "col"), None),
        P(None, ("region", "col"), None),
    )
    return jax.shard_map(
        shards,
        mesh=mesh,
        in_specs=placed,
        out_specs=(
            P(None, ("region", "col"), None),
            P(("region", "col"), None),
            P("region", "col"),
            P("region", "col"),
            P("region", "col"),
        ),
        check_vma=False,
    )
```

```python
import functools

import jax
import jax.numpy as jnp
from jax import lax
from jax.experimental import pallas as pl
from jax.experimental.pallas import tpu as pltpu
from jax.sharding import PartitionSpec as P

ITERS = 4
WINDOW = 64
LANES = 128
MIB = 1024 * 1024
VMEM_LIMIT = 24 * MIB

directions = ((0, 1), (1, 1), (1, 0), (1, -1), (0, -1), (-1, -1), (-1, 0), (-1, 1))
axes = ("region", "col")


def iota(shape, dim):
    return lax.broadcasted_iota(jnp.int32, shape, dim)


def onehot(mask):
    return jnp.where(mask, jnp.float32(1.0), jnp.float32(0.0)).astype(jnp.bfloat16)


def lane_pick(values, index):
    return jnp.take_along_axis(values, index, axis=1, mode="promise_in_bounds")


def in_hbm(value):
    return pltpu.with_memory_space_constraint(value, pltpu.HBM)


def thirds(value):
    high = value.astype(jnp.bfloat16)
    rest = value - high.astype(jnp.float32)
    middle = rest.astype(jnp.bfloat16)
    low = (rest - middle.astype(jnp.float32)).astype(jnp.bfloat16)
    return high, middle, low


def halves(value):
    high = value.astype(jnp.bfloat16)
    return high, (value - high.astype(jnp.float32)).astype(jnp.bfloat16)


def matmul(a, b, a_dim=1, b_dim=0):
    return lax.dot_general(
        a, b, (((a_dim,), (b_dim,)), ((), ())), preferred_element_type=jnp.float32
    )


def slot_factors(slot, offset, homes, capacity):
    slots = slot.shape[1]
    worker = slot // capacity if capacity & (capacity - 1) else slot >> (capacity.bit_length() - 1)
    position = slot - worker * capacity
    by_worker = onehot(iota((homes, slots), 0) == worker)
    at_position = iota((capacity, slots), 0) == position
    row = jnp.where(at_position, ((offset >> 7) + 1).astype(jnp.float32), 0.0)
    lane = jnp.where(at_position, (offset & 127).astype(jnp.float32), 0.0)
    return by_worker, row.astype(jnp.bfloat16), lane.astype(jnp.bfloat16)


def slot_columns(slot, offset, homes, capacity):
    slots = slot.shape[1]
    by_worker, row, lane = slot_factors(slot, offset, homes, capacity)
    table = matmul(by_worker, jnp.concatenate([row, lane], axis=0), 1, 1)
    spread = jnp.broadcast_to(table[:, None, :], (homes, capacity, 2 * capacity))
    spread = spread.reshape(slots, 2 * capacity)
    place = iota(spread.shape, 0) % capacity == iota(spread.shape, 1) % capacity
    kept = jnp.where(place, spread, 0.0).astype(jnp.bfloat16)
    shape = (2 * capacity, 2 * LANES)
    gather = onehot((iota(shape, 0) >= capacity) == (iota(shape, 1) >= LANES))
    columns = matmul(kept, gather).astype(jnp.int32)
    return columns[:, :LANES] - 1, columns[:, LANES:]


def slot_rows(slot, offset, homes, capacity):
    slots = slot.shape[1]
    by_worker, row, lane = slot_factors(slot, offset, homes, capacity)
    table = matmul(jnp.concatenate([row, lane], axis=0), by_worker, 1, 1).astype(jnp.bfloat16)
    number = iota((1, slots), 1)
    worker = number // capacity
    position = number - worker * capacity
    spread = matmul(table, onehot(iota((homes, slots), 0) == worker))
    at_position = iota((capacity, slots), 0) == position
    rows = jnp.sum(jnp.where(at_position, spread[:capacity], 0.0), axis=0, keepdims=True)
    lanes = jnp.sum(jnp.where(at_position, spread[capacity:], 0.0), axis=0, keepdims=True)
    return rows.astype(jnp.int32) - 1, lanes.astype(jnp.int32)


def pack_kernel(
    homes, capacity, slot_in, offset_in, forcing_in, out, slot, offset, forcing, row_of, lane_of,
    rain, losses, ready,
):
    copies = [
        pltpu.make_async_copy(source, target, ready.at[i])
        for i, (source, target) in enumerate(
            ((slot_in, slot), (offset_in, offset), (forcing_in, forcing))
        )
    ]
    for copy in copies:
        copy.start()
    slots = slot.shape[1]
    lane_rows = forcing.shape[1]
    copies[0].wait()
    copies[1].wait()
    row_of[...], lane_of[...] = slot_columns(slot[...], offset[...], homes, capacity)
    copies[2].wait()
    parts = []
    for var in range(3):
        here = forcing[var]
        following = jnp.concatenate([here[1:], here[:1]], axis=0)
        parts += [here, following]
    table = jnp.concatenate(thirds(jnp.concatenate(parts, axis=1)), axis=0)
    chunk = 128
    for start in range(0, slots, chunk):
        row = row_of[pl.ds(start, chunk), :]
        lane = lane_of[pl.ds(start, chunk), :]
        shape = (chunk, 3 * lane_rows)
        wide = jnp.concatenate([row, row], axis=1)[:, : 3 * lane_rows]
        pick = onehot(wide == iota(shape, 1) % lane_rows)
        rows = matmul(pick, table)
        here = iota((chunk, LANES), 1)
        after = here >= lane
        joined = [
            jnp.where(
                after,
                rows[:, 2 * var * LANES : (2 * var + 1) * LANES],
                rows[:, (2 * var + 1) * LANES : (2 * var + 2) * LANES],
            )
            for var in range(3)
        ]
        first = (here + lane) & 127
        second = (first + WINDOW) & 127
        odd = iota((chunk, LANES), 0) & 1 == 1
        rain[pl.ds(start, chunk), :] = lane_pick(joined[0], jnp.where(odd, second, first))
        losses[pl.ds(start, chunk), :] = jnp.where(
            here < WINDOW, lane_pick(joined[1], first), lane_pick(joined[2], second)
        )
    pairs = slots // 2
    even_rows = rain[pl.ds(0, pairs, stride=2), :]
    odd_rows = rain[pl.ds(1, pairs, stride=2), :]
    out[pl.ds(0, pairs, stride=3), :] = losses[pl.ds(0, pairs, stride=2), :]
    out[pl.ds(1, pairs, stride=3), :] = jnp.where(
        iota(even_rows.shape, 1) < WINDOW, even_rows, odd_rows
    )
    out[pl.ds(2, pairs, stride=3), :] = losses[pl.ds(1, pairs, stride=2), :]


def pack(homes, capacity, slot, offset, forcing):
    slots = slot.shape[1]
    return pl.pallas_call(
        functools.partial(pack_kernel, homes, capacity),
        in_specs=[pl.BlockSpec(memory_space=pltpu.HBM)] * 3,
        out_shape=jax.ShapeDtypeStruct((slots + slots // 2, LANES), jnp.float32),
        scratch_shapes=[
            pltpu.VMEM(slot.shape, jnp.int32),
            pltpu.VMEM(offset.shape, jnp.int32),
            pltpu.VMEM(forcing.shape, jnp.float32),
            pltpu.VMEM((slots, LANES), jnp.int32),
            pltpu.VMEM((slots, LANES), jnp.int32),
            pltpu.VMEM((slots, LANES), jnp.float32),
            pltpu.VMEM((slots, LANES), jnp.float32),
            pltpu.SemaphoreType.DMA((3,)),
        ],
        compiler_params=pltpu.CompilerParams(vmem_limit_bytes=VMEM_LIMIT),
        cost_estimate=pl.CostEstimate(flops=10**9, bytes_accessed=2 * MIB, transcendentals=0),
        name="pack_forcing",
    )(in_hbm(slot), in_hbm(offset), in_hbm(forcing))


def unpack_plan_kernel(homes, capacity, lane_rows, slot, offset, code, place):
    slots = slot.shape[1]
    row, lane = slot_columns(slot[...], offset[...], homes, capacity)
    here = iota((slots, LANES), 1)
    index = (here - lane) & 127
    inside = (index < WINDOW) & (row >= 0)
    code[...] = jnp.where(inside, index + jnp.where(here >= lane, 0, LANES), -1)
    row_lane, _ = slot_rows(slot[...], offset[...], homes, capacity)
    place[...] = onehot(iota((lane_rows, slots), 0) == row_lane)


def unpack_plan(homes, capacity, lane_rows, slot, offset):
    slots = slot.shape[1]
    return pl.pallas_call(
        functools.partial(unpack_plan_kernel, homes, capacity, lane_rows),
        out_shape=(
            jax.ShapeDtypeStruct((slots, LANES), jnp.int32),
            jax.ShapeDtypeStruct((lane_rows, slots), jnp.bfloat16),
        ),
        compiler_params=pltpu.CompilerParams(vmem_limit_bytes=VMEM_LIMIT),
        cost_estimate=pl.CostEstimate(flops=10**9, bytes_accessed=2 * MIB, transcendentals=0),
        name="unpack_plan",
    )(slot, offset)


def strips_for_neighbours(state, rows):
    device = iota((rows, LANES), 0) // ITERS
    down = device // lax.axis_size("col") - lax.axis_index("region")
    right = device % lax.axis_size("col") - lax.axis_index("col")
    height, width = state.shape
    columns = jnp.transpose(state)
    empty = jnp.zeros((ITERS, LANES - height), jnp.float32)

    def repeated(strip):
        if strip.shape[1] < LANES:
            strip = jnp.concatenate([strip, empty], axis=1)
        return jnp.concatenate([strip] * (rows // ITERS), axis=0)

    near = (jnp.abs(down) <= 1).astype(jnp.int32)
    strips = jnp.zeros((rows, LANES), jnp.float32)
    strips = jnp.where((right == 0) & (down == 1), repeated(state[height - ITERS :]), strips)
    strips = jnp.where((right == 0) & (down == -1), repeated(state[:ITERS]), strips)
    strips = jnp.where((right == 1) & (near == 1), repeated(columns[width - ITERS :]), strips)
    return jnp.where((right == -1) & (near == 1), repeated(columns[:ITERS]), strips)


def cell_totals(arrived, code, place, first):
    lane_rows = place.shape[0]
    marks = code[...]
    window = lane_pick(arrived[...], (marks + first) & 127)
    placed = jnp.concatenate(
        [
            jnp.where((marks >= 0) & (marks < LANES), window, 0.0),
            jnp.where(marks >= LANES, window, 0.0),
        ],
        axis=1,
    )
    totals = matmul(place[...], jnp.concatenate(halves(placed), axis=1))
    totals = totals[:, :256] + totals[:, 256:]
    over = totals[:, LANES:]
    over = jnp.concatenate([over[lane_rows - 1 :], over[: lane_rows - 1]], axis=0)
    over = jnp.where(iota(over.shape, 0) == 0, 0.0, over)
    return totals[:, :LANES] + over


def unpack_runoff_kernel(arrived, code, place, river, runoff, storage, strips):
    total = cell_totals(arrived, code, place, 0)
    state = river[...] + total
    runoff[...] = total
    storage[...] = state
    strips[...] = strips_for_neighbours(state, strips.shape[0])


def unpack_runoff(homes, arrived, code, place, river):
    shape = jax.ShapeDtypeStruct((place.shape[0], LANES), jnp.float32)
    strips = jax.ShapeDtypeStruct((homes * ITERS, LANES), jnp.float32)
    return pl.pallas_call(
        unpack_runoff_kernel,
        out_shape=(shape, shape, strips),
        compiler_params=pltpu.CompilerParams(vmem_limit_bytes=VMEM_LIMIT),
        cost_estimate=pl.CostEstimate(flops=10**9, bytes_accessed=1 * MIB, transcendentals=0),
        name="unpack_runoff",
    )(arrived, code, place, river)


def unpack_evap_kernel(arrived, code, place, evap):
    evap[...] = cell_totals(arrived, code, place, WINDOW)


def unpack_evap(arrived, code, place):
    return pl.pallas_call(
        unpack_evap_kernel,
        out_shape=jax.ShapeDtypeStruct((place.shape[0], LANES), jnp.float32),
        compiler_params=pltpu.CompilerParams(vmem_limit_bytes=VMEM_LIMIT),
        cost_estimate=pl.CostEstimate(flops=10**9, bytes_accessed=1 * MIB, transcendentals=0),
        name="unpack_evap",
    )(arrived, code, place)


def segment_plan_kernel(cell, worker, meta):
    chunk = 96
    for start in range(0, cell.shape[0], chunk):
        values = cell[pl.ds(start, chunk), :]
        target = iota(values.shape, 1) & (WINDOW - 1)
        count = jnp.zeros_like(values)
        for step in (64, 32, 16, 8, 4, 2, 1):
            probe = lane_pick(values, count + (step - 1))
            count = jnp.where(probe <= target, count + step, count)
        count = jnp.where(lane_pick(values, count) <= target, count + 1, count)
        odd = worker[pl.ds(start, chunk), :] & 1
        meta[pl.ds(start, chunk), :] = count + (odd << 8)


def segment_plan(cell, worker):
    return pl.pallas_call(
        segment_plan_kernel,
        out_shape=jax.ShapeDtypeStruct(cell.shape, jnp.int32),
        compiler_params=pltpu.CompilerParams(vmem_limit_bytes=VMEM_LIMIT),
        cost_estimate=pl.CostEstimate(flops=10**8, bytes_accessed=1 * MIB, transcendentals=0),
        name="segment_plan",
    )(cell, worker)


def segment_totals(runoff, evap, marks):
    shape = (2 * LANES, LANES)
    upto = onehot((iota(shape, 0) & 127) <= iota(shape, 1))
    count = marks & 255
    last = jnp.maximum(count - 1, 0)
    here = iota(marks.shape, 1)
    sums = [
        lane_pick(matmul(jnp.concatenate(halves(value), axis=1), upto), last)
        for value in (runoff, evap)
    ]
    reached = jnp.where(count > 0, jnp.where(here < WINDOW, *sums), 0.0)
    before = jnp.where((here & (WINDOW - 1)) == 0, 0.0, pltpu.roll(reached, 1, 1))
    return reached - before


def stage_kernel(soil_in, porosity_in, drainage_in, _, __, soil, porosity, drainage, ready):
    pairs = ((soil_in, soil), (porosity_in, porosity), (drainage_in, drainage))
    copies = [pltpu.make_async_copy(a, b, ready.at[i]) for i, (a, b) in enumerate(pairs)]
    for copy in copies:
        copy.start()
    for copy in copies:
        copy.wait()


def stage(soil, porosity, drainage, *after):
    far = pl.BlockSpec(memory_space=pltpu.HBM)
    near = pl.BlockSpec(memory_space=pltpu.VMEM)
    return pl.pallas_call(
        stage_kernel,
        in_specs=[far] * 3 + [pl.BlockSpec(memory_space=pl.ANY)] * 2,
        out_specs=[near] * 3,
        out_shape=[pltpu.VMEM(soil.shape, jnp.float32)] * 3,
        scratch_shapes=[pltpu.SemaphoreType.DMA((3,))],
        compiler_params=pltpu.CompilerParams(vmem_limit_bytes=4 * MIB),
        cost_estimate=pl.CostEstimate(flops=0, bytes_accessed=22 * MIB, transcendentals=0),
        name="stage_soil",
    )(in_hbm(soil), in_hbm(porosity), in_hbm(drainage), *after)


def land_kernel(
    slots, first_rows, arrived, cell, meta, area, water, cap, soil, porosity, drainage, _, __,
    soil_out, canopy_new, sums_out, soil_new, fetched, runoffs, evaps, written,
):
    layers, rows = soil.shape[:2]
    steps = written.shape[0]
    block = rows // steps
    chunk = block // 2

    def part_of(step):
        return pl.ds(step * block, block)

    def write(step):
        return pltpu.make_async_copy(
            soil_new.at[:, part_of(step), :], soil_out.at[:, part_of(step), :], written.at[step]
        )

    def fetch(step):
        for i in range(step * block, (step + 1) * block):
            fetched[pl.ds(2 * i, 2), :] = arrived[pl.ds(first_rows[i], 2), :]

    def cascade(start):
        part = pl.ds(start, chunk)
        index = cell[part, :]
        one = fetched[pl.ds(2 * start, chunk, stride=2), :]
        two = fetched[pl.ds(2 * start + 1, chunk, stride=2), :]
        odd = meta[part, :] >> 8
        loss = jnp.where(odd == 1, two, one)
        rain = lane_pick(jnp.where(odd == 1, one, two), index + odd * WINDOW)
        demand = lane_pick(loss, index)
        limit = lane_pick(loss, index + WINDOW)
        wetted = water[part, :] + rain
        flowing = jnp.maximum(wetted - cap[part, :], 0.0)
        retained = jnp.minimum(wetted, cap[part, :])
        canopy_loss = jnp.minimum(demand, retained)
        canopy_new[part, :] = retained - canopy_loss
        surface = jnp.zeros_like(flowing)
        for layer in range(layers):
            filled = soil[layer, part, :] + flowing
            excess = jnp.maximum(filled - porosity[layer, part, :], 0.0)
            surface = surface + excess
            filled = filled - excess
            flowing = drainage[layer, part, :] * filled
            middle = filled - flowing
            if layer == 0:
                soil_loss = jnp.minimum(jnp.minimum(limit, demand - canopy_loss), 0.5 * middle)
                middle = middle - soil_loss
                evaps[part, :] = area[part, :] * (canopy_loss + soil_loss)
            soil_new[layer, part, :] = middle
        runoffs[part, :] = area[part, :] * (surface + flowing)

    def scan(step):
        part = part_of(step)
        runoffs[part, :] = segment_totals(runoffs[part, :], evaps[part, :], meta[part, :])

    def hand_back(step):
        for i in range(step * block, (step + 1) * block):
            sums_out[pl.ds(slots[i], 1), :] = runoffs[pl.ds(i, 1), :]

    sums_out[...] = jnp.zeros_like(sums_out)
    fetch(0)
    for step in range(steps + 2):
        if step + 1 < steps:
            fetch(step + 1)
        if step < steps:
            for start in range(step * block, (step + 1) * block, chunk):
                cascade(start)
        if 1 <= step <= steps:
            scan(step - 1)
        if step >= 2:
            hand_back(step - 2)
        if step < steps:
            write(step).start()
    for step in range(steps):
        write(step).wait()


def land_step(
    sums_shape, slots, first_rows, arrived, cell, meta, area, water, cap, staged, after
):
    layers, rows = staged[0].shape[:2]
    steps = 5
    near = pl.BlockSpec(memory_space=pltpu.VMEM)
    return pl.pallas_call(
        land_kernel,
        in_specs=[pl.BlockSpec(memory_space=pltpu.SMEM)] * 2 + [near] * 9
        + [pl.BlockSpec(memory_space=pl.ANY)] * 2,
        out_specs=[pl.BlockSpec(memory_space=pltpu.HBM), near, near],
        scratch_shapes=[pltpu.VMEM(staged[0].shape, jnp.float32)]
        + [pltpu.VMEM((2 * rows, LANES), jnp.float32)]
        + [pltpu.VMEM((rows, LANES), jnp.float32)] * 2
        + [pltpu.SemaphoreType.DMA((steps,))],
        out_shape=(
            jax.ShapeDtypeStruct(staged[0].shape, jnp.float32),
            jax.ShapeDtypeStruct((rows, LANES), jnp.float32),
            jax.ShapeDtypeStruct(sums_shape, jnp.float32),
        ),
        compiler_params=pltpu.CompilerParams(vmem_limit_bytes=VMEM_LIMIT),
        cost_estimate=pl.CostEstimate(flops=10**8, bytes_accessed=20 * MIB, transcendentals=0),
        name="land_layers",
    )(
        slots, first_rows, arrived, cell, meta, area, water, cap,
        *(pltpu.with_memory_space_constraint(value, pltpu.VMEM) for value in staged),
        *after,
    )


def halo_parts(value, axis, dim, width):
    count, length = (lax.axis_size(axis), value.shape[dim])
    up = [(i, i + 1) for i in range(count - 1)]
    down = [(j, i) for i, j in up]
    last = lax.slice_in_dim(value, length - width, length, axis=dim)
    initial = lax.slice_in_dim(value, 0, width, axis=dim)
    return lax.ppermute(last, axis, up), lax.ppermute(initial, axis, down)


def edge_columns_kernel(tall, _, first, last):
    arrays, height, width = tall.shape
    for number in range(arrays):
        values = tall[number]
        values = jnp.concatenate([values, jnp.zeros((LANES - height, width), jnp.float32)], axis=0)
        columns = jnp.transpose(values)
        part = pl.ds(number * ITERS, ITERS)
        first[part, :] = columns[:ITERS]
        last[part, :] = columns[width - ITERS :]


def edge_columns(tall, after):
    shape = jax.ShapeDtypeStruct((2 * ITERS, LANES), jnp.float32)
    return pl.pallas_call(
        edge_columns_kernel,
        in_specs=[pl.BlockSpec(memory_space=pltpu.VMEM), pl.BlockSpec(memory_space=pl.ANY)],
        out_shape=(shape, shape),
        compiler_params=pltpu.CompilerParams(vmem_limit_bytes=VMEM_LIMIT),
        cost_estimate=pl.CostEstimate(flops=10**6, bytes_accessed=10**5, transcendentals=0),
        name="edge_columns",
    )(tall, after)


def extended(own, strip):
    height = own.shape[0]

    def column_strip(right):
        middle, above, below = strip(0, right), strip(-1, right), strip(1, right)
        return jnp.concatenate(
            [
                middle[:, :height],
                below[:, :ITERS],
                above[:, height - ITERS : height],
                jnp.zeros((ITERS, LANES - height - 2 * ITERS), jnp.float32),
            ],
            axis=1,
        )

    gap = jnp.zeros((LANES - 2 * ITERS, LANES), jnp.float32)
    sides = jnp.concatenate([column_strip(1), gap, column_strip(-1)], axis=0)
    sides = jnp.transpose(sides)[: height + 2 * ITERS]
    tall = jnp.concatenate([own, strip(1, 0), strip(-1, 0)], axis=0)
    return jnp.concatenate([tall, sides], axis=1)


def neighbour(down, right):
    row, column = lax.axis_index("region") + down, lax.axis_index("col") + right
    there = (row >= 0) & (row < lax.axis_size("region"))
    there &= (column >= 0) & (column < lax.axis_size("col"))
    return jnp.where(there, row * lax.axis_size("col") + column, 0), jnp.where(there, 1.0, 0.0)


def static_halo_kernel(tall, before, after, out):
    height, width = tall.shape[1:]
    gap = jnp.zeros((LANES - 2 * ITERS, LANES), jnp.float32)
    for number in range(2):
        part = pl.ds(number * ITERS, ITERS)
        sides = jnp.transpose(jnp.concatenate([after[part, :], gap, before[part, :]], axis=0))
        out[number, :, :width] = tall[number]
        out[number, :, width:] = sides[:height]


def static_halo(tall, before, after):
    arrays, height, width = tall.shape
    return pl.pallas_call(
        static_halo_kernel,
        out_shape=jax.ShapeDtypeStruct((arrays, height, width + LANES), jnp.float32),
        compiler_params=pltpu.CompilerParams(vmem_limit_bytes=VMEM_LIMIT),
        cost_estimate=pl.CostEstimate(flops=10**6, bytes_accessed=10**6, transcendentals=0),
        name="static_halo",
    )(tall, before, after)


def river_kernel(state, strips, fixed, out):
    height, width = state.shape

    def strip(down, right):
        device, there = neighbour(down, right)
        return strips[pl.ds(device * ITERS, ITERS), :] * there

    storage = extended(state[...], strip)
    rate = fixed[0]
    code = fixed[1]
    rows, cols = storage.shape
    for _ in range(ITERS):
        outflow = rate * storage
        inflow = jnp.zeros_like(storage)
        for col_step in (-1, 0, 1):
            column = jnp.zeros_like(storage)
            for bit, (row_step, step) in enumerate(directions):
                if step != col_step:
                    continue
                leaving = jnp.where(code == float(1 << bit), outflow, 0.0)
                if row_step:
                    leaving = pltpu.roll(leaving, row_step % rows, 0)
                column = column + leaving
            if col_step:
                column = pltpu.roll(column, col_step % cols, 1)
            inflow = inflow + column
        storage = storage - outflow + inflow
    out[...] = storage[:height, :width]


def river(state, strips, fixed):
    return pl.pallas_call(
        river_kernel,
        out_shape=jax.ShapeDtypeStruct(state.shape, jnp.float32),
        compiler_params=pltpu.CompilerParams(vmem_limit_bytes=VMEM_LIMIT),
        cost_estimate=pl.CostEstimate(flops=10**7, bytes_accessed=1 * MIB, transcendentals=0),
        name="river_steps",
    )(state, strips, fixed)


def exchange(value):
    return lax.all_to_all(value, axes, split_axis=0, concat_axis=0, tiled=True)


def shards(
    forcing,
    river_storage,
    river_rate,
    flow_code,
    home_slot,
    home_offset,
    worker_list,
    patch_cell,
    patch_area,
    canopy_water,
    canopy_cap,
    soil_water,
    porosity,
    drainage,
):
    homes = lax.axis_size("region") * lax.axis_size("col")
    capacity = home_slot.shape[1] // homes
    grid_rows, grid_cols = river_storage.shape
    lane_rows = grid_rows * grid_cols // LANES
    outgoing = pack(
        homes, capacity, home_slot, home_offset, forcing.reshape(3, lane_rows, LANES)
    )
    arrived = exchange(outgoing)
    home = worker_list // capacity
    position = worker_list - home * capacity
    first_rows = home * (outgoing.shape[0] // homes) + position // 2 * 3 + position % 2
    meta = segment_plan(patch_cell, worker_list[:, None])
    fixed = jnp.stack([river_rate, flow_code.astype(jnp.float32)])
    above, below = halo_parts(fixed, "region", 1, ITERS)
    staged = stage(soil_water, porosity, drainage, meta, first_rows)
    soil_new, canopy_new, sums = land_step(
        (homes * capacity, LANES), worker_list, first_rows, arrived, patch_cell, meta,
        patch_area, canopy_water, canopy_cap, staged, (above, below),
    )
    returned = exchange(sums)
    code, place = unpack_plan(homes, capacity, lane_rows, home_slot, home_offset)
    fixed = jnp.concatenate([fixed, below, above], axis=1)
    initial, last = edge_columns(fixed, sums)
    count = lax.axis_size("col")
    before = lax.ppermute(last, "col", [(i, i + 1) for i in range(count - 1)])
    after = lax.ppermute(initial, "col", [(i + 1, i) for i in range(count - 1)])
    fixed = static_halo(fixed, before, after)
    cell_runoff, storage, strips = unpack_runoff(
        homes, returned, code, place, river_storage.reshape(lane_rows, LANES)
    )
    cell_evap = unpack_evap(returned, code, place)
    river_new = river(storage.reshape(river_storage.shape), exchange(strips), fixed)
    return (
        soil_new,
        canopy_new,
        cell_runoff.reshape(river_storage.shape),
        cell_evap.reshape(river_storage.shape),
        river_new,
    )


def solution(mesh):
    placed = (
        P(None, "region", "col"),
        P("region", "col"),
        P("region", "col"),
        P("region", "col"),
        P(("region", "col"), None),
        P(("region", "col"), None),
        P(("region", "col")),
        P(("region", "col"), None),
        P(("region", "col"), None),
        P(("region", "col"), None),
        P(("region", "col"), None),
        P(None, ("region", "col"), None),
        P(None, ("region", "col"), None),
        P(None, ("region", "col"), None),
    )
    return jax.shard_map(
        shards,
        mesh=mesh,
        in_specs=placed,
        out_specs=(
            P(None, ("region", "col"), None),
            P(("region", "col"), None),
            P("region", "col"),
            P("region", "col"),
            P("region", "col"),
        ),
        check_vma=False,
    )
```

```python
import functools

import jax
import jax.numpy as jnp
from jax import lax
from jax.experimental import pallas as pl
from jax.experimental.pallas import tpu as pltpu
from jax.sharding import PartitionSpec as P

ITERS = 4
WINDOW = 64
LANES = 128
MIB = 1024 * 1024
VMEM_LIMIT = 24 * MIB

directions = ((0, 1), (1, 1), (1, 0), (1, -1), (0, -1), (-1, -1), (-1, 0), (-1, 1))
axes = ("region", "col")


def iota(shape, dim):
    return lax.broadcasted_iota(jnp.int32, shape, dim)


def onehot(mask):
    return jnp.where(mask, jnp.float32(1.0), jnp.float32(0.0)).astype(jnp.bfloat16)


def lane_pick(values, index):
    return jnp.take_along_axis(values, index, axis=1, mode="promise_in_bounds")


def in_hbm(value):
    return pltpu.with_memory_space_constraint(value, pltpu.HBM)


def thirds(value):
    high = value.astype(jnp.bfloat16)
    rest = value - high.astype(jnp.float32)
    middle = rest.astype(jnp.bfloat16)
    low = (rest - middle.astype(jnp.float32)).astype(jnp.bfloat16)
    return high, middle, low


def halves(value):
    high = value.astype(jnp.bfloat16)
    return high, (value - high.astype(jnp.float32)).astype(jnp.bfloat16)


def matmul(a, b, a_dim=1, b_dim=0):
    return lax.dot_general(
        a, b, (((a_dim,), (b_dim,)), ((), ())), preferred_element_type=jnp.float32
    )


def slot_factors(slot, offset, homes, capacity):
    slots = slot.shape[1]
    worker = slot // capacity if capacity & (capacity - 1) else slot >> (capacity.bit_length() - 1)
    position = slot - worker * capacity
    by_worker = onehot(iota((homes, slots), 0) == worker)
    at_position = iota((capacity, slots), 0) == position
    row = jnp.where(at_position, ((offset >> 7) + 1).astype(jnp.float32), 0.0)
    lane = jnp.where(at_position, (offset & 127).astype(jnp.float32), 0.0)
    return by_worker, row.astype(jnp.bfloat16), lane.astype(jnp.bfloat16)


def slot_columns(slot, offset, homes, capacity):
    slots = slot.shape[1]
    by_worker, row, lane = slot_factors(slot, offset, homes, capacity)
    table = matmul(by_worker, jnp.concatenate([row, lane], axis=0), 1, 1)
    spread = jnp.broadcast_to(table[:, None, :], (homes, capacity, 2 * capacity))
    spread = spread.reshape(slots, 2 * capacity)
    place = iota(spread.shape, 0) % capacity == iota(spread.shape, 1) % capacity
    kept = jnp.where(place, spread, 0.0).astype(jnp.bfloat16)
    shape = (2 * capacity, 2 * LANES)
    gather = onehot((iota(shape, 0) >= capacity) == (iota(shape, 1) >= LANES))
    columns = matmul(kept, gather).astype(jnp.int32)
    return columns[:, :LANES] - 1, columns[:, LANES:]


def slot_rows(slot, offset, homes, capacity):
    slots = slot.shape[1]
    by_worker, row, lane = slot_factors(slot, offset, homes, capacity)
    table = matmul(jnp.concatenate([row, lane], axis=0), by_worker, 1, 1).astype(jnp.bfloat16)
    number = iota((1, slots), 1)
    worker = number // capacity
    position = number - worker * capacity
    spread = matmul(table, onehot(iota((homes, slots), 0) == worker))
    at_position = iota((capacity, slots), 0) == position
    rows = jnp.sum(jnp.where(at_position, spread[:capacity], 0.0), axis=0, keepdims=True)
    lanes = jnp.sum(jnp.where(at_position, spread[capacity:], 0.0), axis=0, keepdims=True)
    return rows.astype(jnp.int32) - 1, lanes.astype(jnp.int32)


def pack_kernel(
    homes, capacity, slot_in, offset_in, forcing_in, out, slot, offset, forcing, row_of, lane_of,
    rain, losses, ready,
):
    copies = [
        pltpu.make_async_copy(source, target, ready.at[i])
        for i, (source, target) in enumerate(
            ((slot_in, slot), (offset_in, offset), (forcing_in, forcing))
        )
    ]
    for copy in copies:
        copy.start()
    slots = slot.shape[1]
    lane_rows = forcing.shape[1]
    copies[0].wait()
    copies[1].wait()
    row_of[...], lane_of[...] = slot_columns(slot[...], offset[...], homes, capacity)
    copies[2].wait()
    parts = []
    for var in range(3):
        here = forcing[var]
        following = jnp.concatenate([here[1:], here[:1]], axis=0)
        parts += [here, following]
    table = jnp.concatenate(thirds(jnp.concatenate(parts, axis=1)), axis=0)
    chunk = 128
    for start in range(0, slots, chunk):
        row = row_of[pl.ds(start, chunk), :]
        lane = lane_of[pl.ds(start, chunk), :]
        shape = (chunk, 3 * lane_rows)
        wide = jnp.concatenate([row, row], axis=1)[:, : 3 * lane_rows]
        pick = onehot(wide == iota(shape, 1) % lane_rows)
        rows = matmul(pick, table)
        here = iota((chunk, LANES), 1)
        after = here >= lane
        joined = [
            jnp.where(
                after,
                rows[:, 2 * var * LANES : (2 * var + 1) * LANES],
                rows[:, (2 * var + 1) * LANES : (2 * var + 2) * LANES],
            )
            for var in range(3)
        ]
        first = (here + lane) & 127
        second = (first + WINDOW) & 127
        odd = iota((chunk, LANES), 0) & 1 == 1
        rain[pl.ds(start, chunk), :] = lane_pick(joined[0], jnp.where(odd, second, first))
        losses[pl.ds(start, chunk), :] = jnp.where(
            here < WINDOW, lane_pick(joined[1], first), lane_pick(joined[2], second)
        )
    pairs = slots // 2
    even_rows = rain[pl.ds(0, pairs, stride=2), :]
    odd_rows = rain[pl.ds(1, pairs, stride=2), :]
    out[pl.ds(0, pairs, stride=3), :] = losses[pl.ds(0, pairs, stride=2), :]
    out[pl.ds(1, pairs, stride=3), :] = jnp.where(
        iota(even_rows.shape, 1) < WINDOW, even_rows, odd_rows
    )
    out[pl.ds(2, pairs, stride=3), :] = losses[pl.ds(1, pairs, stride=2), :]


def pack(homes, capacity, slot, offset, forcing):
    slots = slot.shape[1]
    return pl.pallas_call(
        functools.partial(pack_kernel, homes, capacity),
        in_specs=[pl.BlockSpec(memory_space=pltpu.HBM)] * 3,
        out_shape=jax.ShapeDtypeStruct((slots + slots // 2, LANES), jnp.float32),
        scratch_shapes=[
            pltpu.VMEM(slot.shape, jnp.int32),
            pltpu.VMEM(offset.shape, jnp.int32),
            pltpu.VMEM(forcing.shape, jnp.float32),
            pltpu.VMEM((slots, LANES), jnp.int32),
            pltpu.VMEM((slots, LANES), jnp.int32),
            pltpu.VMEM((slots, LANES), jnp.float32),
            pltpu.VMEM((slots, LANES), jnp.float32),
            pltpu.SemaphoreType.DMA((3,)),
        ],
        compiler_params=pltpu.CompilerParams(vmem_limit_bytes=VMEM_LIMIT),
        cost_estimate=pl.CostEstimate(flops=10**9, bytes_accessed=2 * MIB, transcendentals=0),
        name="pack_forcing",
    )(in_hbm(slot), in_hbm(offset), in_hbm(forcing))


def unpack_plan_kernel(homes, capacity, lane_rows, slot, offset, code, place):
    slots = slot.shape[1]
    row, lane = slot_columns(slot[...], offset[...], homes, capacity)
    here = iota((slots, LANES), 1)
    index = (here - lane) & 127
    inside = (index < WINDOW) & (row >= 0)
    code[...] = jnp.where(inside, index + jnp.where(here >= lane, 0, LANES), -1)
    row_lane, _ = slot_rows(slot[...], offset[...], homes, capacity)
    place[...] = onehot(iota((lane_rows, slots), 0) == row_lane)


def unpack_plan(homes, capacity, lane_rows, slot, offset):
    slots = slot.shape[1]
    return pl.pallas_call(
        functools.partial(unpack_plan_kernel, homes, capacity, lane_rows),
        out_shape=(
            jax.ShapeDtypeStruct((slots, LANES), jnp.int32),
            jax.ShapeDtypeStruct((lane_rows, slots), jnp.bfloat16),
        ),
        compiler_params=pltpu.CompilerParams(vmem_limit_bytes=VMEM_LIMIT),
        cost_estimate=pl.CostEstimate(flops=10**9, bytes_accessed=2 * MIB, transcendentals=0),
        name="unpack_plan",
    )(slot, offset)


def strips_for_neighbours(state, rows):
    device = iota((rows, LANES), 0) // ITERS
    down = device // lax.axis_size("col") - lax.axis_index("region")
    right = device % lax.axis_size("col") - lax.axis_index("col")
    height, width = state.shape
    columns = jnp.transpose(state)
    empty = jnp.zeros((ITERS, LANES - height), jnp.float32)

    def repeated(strip):
        if strip.shape[1] < LANES:
            strip = jnp.concatenate([strip, empty], axis=1)
        return jnp.concatenate([strip] * (rows // ITERS), axis=0)

    near = (jnp.abs(down) <= 1).astype(jnp.int32)
    strips = jnp.zeros((rows, LANES), jnp.float32)
    strips = jnp.where((right == 0) & (down == 1), repeated(state[height - ITERS :]), strips)
    strips = jnp.where((right == 0) & (down == -1), repeated(state[:ITERS]), strips)
    strips = jnp.where((right == 1) & (near == 1), repeated(columns[width - ITERS :]), strips)
    return jnp.where((right == -1) & (near == 1), repeated(columns[:ITERS]), strips)


def cell_totals(arrived, code, place, first):
    lane_rows = place.shape[0]
    marks = code[...]
    window = lane_pick(arrived[...], (marks + first) & 127)
    placed = jnp.concatenate(
        [
            jnp.where((marks >= 0) & (marks < LANES), window, 0.0),
            jnp.where(marks >= LANES, window, 0.0),
        ],
        axis=1,
    )
    totals = matmul(place[...], jnp.concatenate(halves(placed), axis=1))
    totals = totals[:, :256] + totals[:, 256:]
    over = totals[:, LANES:]
    over = jnp.concatenate([over[lane_rows - 1 :], over[: lane_rows - 1]], axis=0)
    over = jnp.where(iota(over.shape, 0) == 0, 0.0, over)
    return totals[:, :LANES] + over


def unpack_runoff_kernel(arrived, code, place, river, _, runoff, storage, strips):
    total = cell_totals(arrived, code, place, 0)
    state = river[...] + total
    runoff[...] = total
    storage[...] = state
    strips[...] = strips_for_neighbours(state, strips.shape[0])


def unpack_runoff(homes, arrived, code, place, river, after):
    shape = jax.ShapeDtypeStruct((place.shape[0], LANES), jnp.float32)
    strips = jax.ShapeDtypeStruct((homes * ITERS, LANES), jnp.float32)
    return pl.pallas_call(
        unpack_runoff_kernel,
        in_specs=[pl.BlockSpec(memory_space=pltpu.VMEM)] * 4 + [pl.BlockSpec(memory_space=pl.ANY)],
        out_shape=(shape, shape, strips),
        compiler_params=pltpu.CompilerParams(vmem_limit_bytes=VMEM_LIMIT),
        cost_estimate=pl.CostEstimate(flops=10**9, bytes_accessed=1 * MIB, transcendentals=0),
        name="unpack_runoff",
    )(arrived, code, place, river, after)


def unpack_evap_kernel(arrived, code, place, evap):
    evap[...] = cell_totals(arrived, code, place, WINDOW)


def unpack_evap(arrived, code, place):
    return pl.pallas_call(
        unpack_evap_kernel,
        out_shape=jax.ShapeDtypeStruct((place.shape[0], LANES), jnp.float32),
        compiler_params=pltpu.CompilerParams(vmem_limit_bytes=VMEM_LIMIT),
        cost_estimate=pl.CostEstimate(flops=10**9, bytes_accessed=1 * MIB, transcendentals=0),
        name="unpack_evap",
    )(arrived, code, place)


def segment_plan_kernel(cell, worker, meta):
    chunk = 96
    for start in range(0, cell.shape[0], chunk):
        values = cell[pl.ds(start, chunk), :]
        target = iota(values.shape, 1) & (WINDOW - 1)
        count = jnp.zeros_like(values)
        for step in (64, 32, 16, 8, 4, 2, 1):
            probe = lane_pick(values, count + (step - 1))
            count = jnp.where(probe <= target, count + step, count)
        count = jnp.where(lane_pick(values, count) <= target, count + 1, count)
        odd = worker[pl.ds(start, chunk), :] & 1
        meta[pl.ds(start, chunk), :] = count + (odd << 8)


def segment_plan(cell, worker):
    return pl.pallas_call(
        segment_plan_kernel,
        out_shape=jax.ShapeDtypeStruct(cell.shape, jnp.int32),
        compiler_params=pltpu.CompilerParams(vmem_limit_bytes=VMEM_LIMIT),
        cost_estimate=pl.CostEstimate(flops=10**8, bytes_accessed=1 * MIB, transcendentals=0),
        name="segment_plan",
    )(cell, worker)


def segment_totals(runoff, evap, marks):
    shape = (2 * LANES, LANES)
    upto = onehot((iota(shape, 0) & 127) <= iota(shape, 1))
    count = marks & 255
    last = jnp.maximum(count - 1, 0)
    here = iota(marks.shape, 1)
    sums = [
        lane_pick(matmul(jnp.concatenate(halves(value), axis=1), upto), last)
        for value in (runoff, evap)
    ]
    reached = jnp.where(count > 0, jnp.where(here < WINDOW, *sums), 0.0)
    before = jnp.where((here & (WINDOW - 1)) == 0, 0.0, pltpu.roll(reached, 1, 1))
    return reached - before


def land_kernel(
    slots, first_rows, arrived, cell, meta, area, water, cap, soil_in, porosity_in, drainage_in,
    _, __, soil_out, canopy_new, sums_out, soil, porosity, drainage, fetched, runoffs, evaps,
    ready, written,
):
    layers, rows = soil.shape[:2]
    steps = written.shape[0]
    block = rows // steps
    ahead = 3
    arrays = ((soil_in, soil), (porosity_in, porosity), (drainage_in, drainage))

    def part_of(step):
        return pl.ds(step * block, block)

    def reads(step):
        return [
            pltpu.make_async_copy(
                source.at[:, part_of(step), :], target.at[:, part_of(step), :], ready.at[step, i]
            )
            for i, (source, target) in enumerate(arrays)
        ]

    def write(step):
        return pltpu.make_async_copy(
            soil.at[:, part_of(step), :], soil_out.at[:, part_of(step), :], written.at[step]
        )

    def fetch(step):
        for i in range(step * block, (step + 1) * block):
            fetched[pl.ds(2 * i, 2), :] = arrived[pl.ds(first_rows[i], 2), :]

    def cascade(step):
        start, chunk = step * block, block
        part = part_of(step)
        index = cell[part, :]
        one = fetched[pl.ds(2 * start, chunk, stride=2), :]
        two = fetched[pl.ds(2 * start + 1, chunk, stride=2), :]
        odd = meta[part, :] >> 8
        loss = jnp.where(odd == 1, two, one)
        rain = lane_pick(jnp.where(odd == 1, one, two), index + odd * WINDOW)
        demand = lane_pick(loss, index)
        limit = lane_pick(loss, index + WINDOW)
        wetted = water[part, :] + rain
        flowing = jnp.maximum(wetted - cap[part, :], 0.0)
        retained = jnp.minimum(wetted, cap[part, :])
        canopy_loss = jnp.minimum(demand, retained)
        canopy_new[part, :] = retained - canopy_loss
        surface = jnp.zeros_like(flowing)
        for layer in range(layers):
            filled = soil[layer, part, :] + flowing
            excess = jnp.maximum(filled - porosity[layer, part, :], 0.0)
            surface = surface + excess
            filled = filled - excess
            flowing = drainage[layer, part, :] * filled
            middle = filled - flowing
            if layer == 0:
                soil_loss = jnp.minimum(jnp.minimum(limit, demand - canopy_loss), 0.5 * middle)
                middle = middle - soil_loss
                evaps[part, :] = area[part, :] * (canopy_loss + soil_loss)
            soil[layer, part, :] = middle
        runoffs[part, :] = area[part, :] * (surface + flowing)

    def scan(step):
        part = part_of(step)
        runoffs[part, :] = segment_totals(runoffs[part, :], evaps[part, :], meta[part, :])

    def hand_back(step):
        for i in range(step * block, (step + 1) * block):
            sums_out[pl.ds(slots[i], 1), :] = runoffs[pl.ds(i, 1), :]

    for step in range(ahead):
        for copy in reads(step):
            copy.start()
    sums_out[...] = jnp.zeros_like(sums_out)
    for step in range(steps):
        fetch(step)
    for step in range(steps + 2):
        if step < steps:
            for copy in reads(step):
                copy.wait()
            if step + ahead < steps:
                for copy in reads(step + ahead):
                    copy.start()
            cascade(step)
        if 1 <= step <= steps:
            scan(step - 1)
        if step >= 2:
            hand_back(step - 2)
        if step < steps:
            write(step).start()
    for step in range(steps):
        write(step).wait()


def land_step(
    sums_shape, slots, first_rows, arrived, cell, meta, area, water, cap, soil, porosity,
    drainage, after,
):
    layers, rows = soil.shape[:2]
    steps = 10
    near = pl.BlockSpec(memory_space=pltpu.VMEM)
    far = pl.BlockSpec(memory_space=pltpu.HBM)
    return pl.pallas_call(
        land_kernel,
        in_specs=[pl.BlockSpec(memory_space=pltpu.SMEM)] * 2 + [near] * 6 + [far] * 3
        + [pl.BlockSpec(memory_space=pl.ANY)] * 2,
        out_specs=[far, near, near],
        scratch_shapes=[pltpu.VMEM(soil.shape, jnp.float32)] * 3
        + [pltpu.VMEM((2 * rows, LANES), jnp.float32)]
        + [pltpu.VMEM((rows, LANES), jnp.float32)] * 2
        + [pltpu.SemaphoreType.DMA((steps, 3)), pltpu.SemaphoreType.DMA((steps,))],
        out_shape=(
            jax.ShapeDtypeStruct(soil.shape, jnp.float32),
            jax.ShapeDtypeStruct((rows, LANES), jnp.float32),
            jax.ShapeDtypeStruct(sums_shape, jnp.float32),
        ),
        compiler_params=pltpu.CompilerParams(vmem_limit_bytes=VMEM_LIMIT),
        cost_estimate=pl.CostEstimate(flops=10**8, bytes_accessed=20 * MIB, transcendentals=0),
        name="land_layers",
    )(
        slots, first_rows, arrived, cell, meta, area, water, cap,
        in_hbm(soil), in_hbm(porosity), in_hbm(drainage), *after,
    )


def halo_parts(value, axis, dim, width):
    count, length = (lax.axis_size(axis), value.shape[dim])
    up = [(i, i + 1) for i in range(count - 1)]
    down = [(j, i) for i, j in up]
    last = lax.slice_in_dim(value, length - width, length, axis=dim)
    initial = lax.slice_in_dim(value, 0, width, axis=dim)
    return lax.ppermute(last, axis, up), lax.ppermute(initial, axis, down)


def edge_columns_kernel(tall, _, first, last):
    arrays, height, width = tall.shape
    for number in range(arrays):
        values = tall[number]
        values = jnp.concatenate([values, jnp.zeros((LANES - height, width), jnp.float32)], axis=0)
        columns = jnp.transpose(values)
        part = pl.ds(number * ITERS, ITERS)
        first[part, :] = columns[:ITERS]
        last[part, :] = columns[width - ITERS :]


def edge_columns(tall, after):
    shape = jax.ShapeDtypeStruct((2 * ITERS, LANES), jnp.float32)
    return pl.pallas_call(
        edge_columns_kernel,
        in_specs=[pl.BlockSpec(memory_space=pltpu.VMEM), pl.BlockSpec(memory_space=pl.ANY)],
        out_shape=(shape, shape),
        compiler_params=pltpu.CompilerParams(vmem_limit_bytes=VMEM_LIMIT),
        cost_estimate=pl.CostEstimate(flops=10**6, bytes_accessed=10**5, transcendentals=0),
        name="edge_columns",
    )(tall, after)


def extended(own, strip):
    height = own.shape[0]

    def column_strip(right):
        middle, above, below = strip(0, right), strip(-1, right), strip(1, right)
        return jnp.concatenate(
            [
                middle[:, :height],
                below[:, :ITERS],
                above[:, height - ITERS : height],
                jnp.zeros((ITERS, LANES - height - 2 * ITERS), jnp.float32),
            ],
            axis=1,
        )

    gap = jnp.zeros((LANES - 2 * ITERS, LANES), jnp.float32)
    sides = jnp.concatenate([column_strip(1), gap, column_strip(-1)], axis=0)
    sides = jnp.transpose(sides)[: height + 2 * ITERS]
    tall = jnp.concatenate([own, strip(1, 0), strip(-1, 0)], axis=0)
    return jnp.concatenate([tall, sides], axis=1)


def neighbour(down, right):
    row, column = lax.axis_index("region") + down, lax.axis_index("col") + right
    there = (row >= 0) & (row < lax.axis_size("region"))
    there &= (column >= 0) & (column < lax.axis_size("col"))
    return jnp.where(there, row * lax.axis_size("col") + column, 0), jnp.where(there, 1.0, 0.0)


def static_halo_kernel(tall, before, after, out):
    height, width = tall.shape[1:]
    gap = jnp.zeros((LANES - 2 * ITERS, LANES), jnp.float32)
    for number in range(2):
        part = pl.ds(number * ITERS, ITERS)
        sides = jnp.transpose(jnp.concatenate([after[part, :], gap, before[part, :]], axis=0))
        out[number, :, :width] = tall[number]
        out[number, :, width:] = sides[:height]


def static_halo(tall, before, after):
    arrays, height, width = tall.shape
    return pl.pallas_call(
        static_halo_kernel,
        out_shape=jax.ShapeDtypeStruct((arrays, height, width + LANES), jnp.float32),
        compiler_params=pltpu.CompilerParams(vmem_limit_bytes=VMEM_LIMIT),
        cost_estimate=pl.CostEstimate(flops=10**6, bytes_accessed=10**6, transcendentals=0),
        name="static_halo",
    )(tall, before, after)


def river_kernel(state, strips, fixed, out):
    height, width = state.shape

    def strip(down, right):
        device, there = neighbour(down, right)
        return strips[pl.ds(device * ITERS, ITERS), :] * there

    storage = extended(state[...], strip)
    rate = fixed[0]
    code = fixed[1]
    rows, cols = storage.shape
    for _ in range(ITERS):
        outflow = rate * storage
        inflow = jnp.zeros_like(storage)
        for col_step in (-1, 0, 1):
            column = jnp.zeros_like(storage)
            for bit, (row_step, step) in enumerate(directions):
                if step != col_step:
                    continue
                leaving = jnp.where(code == float(1 << bit), outflow, 0.0)
                if row_step:
                    leaving = pltpu.roll(leaving, row_step % rows, 0)
                column = column + leaving
            if col_step:
                column = pltpu.roll(column, col_step % cols, 1)
            inflow = inflow + column
        storage = storage - outflow + inflow
    out[...] = storage[:height, :width]


def river(state, strips, fixed):
    return pl.pallas_call(
        river_kernel,
        out_shape=jax.ShapeDtypeStruct(state.shape, jnp.float32),
        compiler_params=pltpu.CompilerParams(vmem_limit_bytes=VMEM_LIMIT),
        cost_estimate=pl.CostEstimate(flops=10**7, bytes_accessed=1 * MIB, transcendentals=0),
        name="river_steps",
    )(state, strips, fixed)


def exchange(value):
    return lax.all_to_all(value, axes, split_axis=0, concat_axis=0, tiled=True)


def shards(
    forcing,
    river_storage,
    river_rate,
    flow_code,
    home_slot,
    home_offset,
    worker_list,
    patch_cell,
    patch_area,
    canopy_water,
    canopy_cap,
    soil_water,
    porosity,
    drainage,
):
    homes = lax.axis_size("region") * lax.axis_size("col")
    capacity = home_slot.shape[1] // homes
    grid_rows, grid_cols = river_storage.shape
    lane_rows = grid_rows * grid_cols // LANES
    outgoing = pack(
        homes, capacity, home_slot, home_offset, forcing.reshape(3, lane_rows, LANES)
    )
    arrived = exchange(outgoing)
    home = worker_list // capacity
    position = worker_list - home * capacity
    first_rows = home * (outgoing.shape[0] // homes) + position // 2 * 3 + position % 2
    meta = segment_plan(patch_cell, worker_list[:, None])
    fixed = jnp.stack([river_rate, flow_code.astype(jnp.float32)])
    above, below = halo_parts(fixed, "region", 1, ITERS)
    soil_new, canopy_new, sums = land_step(
        (homes * capacity, LANES), worker_list, first_rows, arrived, patch_cell, meta,
        patch_area, canopy_water, canopy_cap, soil_water, porosity, drainage, (above, below),
    )
    returned = exchange(sums)
    code, place = unpack_plan(homes, capacity, lane_rows, home_slot, home_offset)
    fixed = jnp.concatenate([fixed, below, above], axis=1)
    initial, last = edge_columns(fixed, sums)
    count = lax.axis_size("col")
    before = lax.ppermute(last, "col", [(i, i + 1) for i in range(count - 1)])
    after = lax.ppermute(initial, "col", [(i + 1, i) for i in range(count - 1)])
    fixed = static_halo(fixed, before, after)
    cell_runoff, storage, strips = unpack_runoff(
        homes, returned, code, place, river_storage.reshape(lane_rows, LANES), fixed
    )
    cell_evap = unpack_evap(returned, code, place)
    river_new = river(storage.reshape(river_storage.shape), exchange(strips), fixed)
    return (
        soil_new,
        canopy_new,
        cell_runoff.reshape(river_storage.shape),
        cell_evap.reshape(river_storage.shape),
        river_new,
    )


def solution(mesh):
    placed = (
        P(None, "region", "col"),
        P("region", "col"),
        P("region", "col"),
        P("region", "col"),
        P(("region", "col"), None),
        P(("region", "col"), None),
        P(("region", "col")),
        P(("region", "col"), None),
        P(("region", "col"), None),
        P(("region", "col"), None),
        P(("region", "col"), None),
        P(None, ("region", "col"), None),
        P(None, ("region", "col"), None),
        P(None, ("region", "col"), None),
    )
    return jax.shard_map(
        shards,
        mesh=mesh,
        in_specs=placed,
        out_specs=(
            P(None, ("region", "col"), None),
            P(("region", "col"), None),
            P("region", "col"),
            P("region", "col"),
            P("region", "col"),
        ),
        check_vma=False,
    )
```

```python
import functools

import jax
import jax.numpy as jnp
from jax import lax
from jax.experimental import pallas as pl
from jax.experimental.pallas import tpu as pltpu
from jax.sharding import PartitionSpec as P

ITERS = 4
WINDOW = 64
LANES = 128
MIB = 1024 * 1024
VMEM_LIMIT = 24 * MIB

directions = ((0, 1), (1, 1), (1, 0), (1, -1), (0, -1), (-1, -1), (-1, 0), (-1, 1))
axes = ("region", "col")


def iota(shape, dim):
    return lax.broadcasted_iota(jnp.int32, shape, dim)


def onehot(mask):
    return jnp.where(mask, jnp.float32(1.0), jnp.float32(0.0)).astype(jnp.bfloat16)


def lane_pick(values, index):
    return jnp.take_along_axis(values, index, axis=1, mode="promise_in_bounds")


def in_hbm(value):
    return pltpu.with_memory_space_constraint(value, pltpu.HBM)


def thirds(value):
    high = value.astype(jnp.bfloat16)
    rest = value - high.astype(jnp.float32)
    middle = rest.astype(jnp.bfloat16)
    low = (rest - middle.astype(jnp.float32)).astype(jnp.bfloat16)
    return high, middle, low


def halves(value):
    high = value.astype(jnp.bfloat16)
    return high, (value - high.astype(jnp.float32)).astype(jnp.bfloat16)


def matmul(a, b, a_dim=1, b_dim=0):
    return lax.dot_general(
        a, b, (((a_dim,), (b_dim,)), ((), ())), preferred_element_type=jnp.float32
    )


def slot_factors(slot, offset, homes, capacity):
    slots = slot.shape[1]
    worker = slot // capacity if capacity & (capacity - 1) else slot >> (capacity.bit_length() - 1)
    position = slot - worker * capacity
    by_worker = onehot(iota((homes, slots), 0) == worker)
    at_position = iota((capacity, slots), 0) == position
    row = jnp.where(at_position, ((offset >> 7) + 1).astype(jnp.float32), 0.0)
    lane = jnp.where(at_position, (offset & 127).astype(jnp.float32), 0.0)
    return by_worker, row.astype(jnp.bfloat16), lane.astype(jnp.bfloat16)


def slot_columns(slot, offset, homes, capacity, split=False):
    slots = slot.shape[1]
    by_worker, row, lane = slot_factors(slot, offset, homes, capacity)
    table = matmul(by_worker, jnp.concatenate([row, lane], axis=0), 1, 1)
    groups = 2 if split else 1
    spread = jnp.broadcast_to(
        table[:, None, :], (homes, capacity // groups, 2 * capacity)
    ).reshape(slots // groups, 2 * capacity)
    spread = jnp.concatenate([spread] * groups, axis=0)
    number = iota(spread.shape, 0)
    position = number % (capacity // groups) * groups + number // (slots // groups)
    place = position == iota(spread.shape, 1) % capacity
    kept = jnp.where(place, spread, 0.0).astype(jnp.bfloat16)
    shape = (2 * capacity, 2 * LANES)
    gather = onehot((iota(shape, 0) >= capacity) == (iota(shape, 1) >= LANES))
    columns = matmul(kept, gather).astype(jnp.int32)
    return columns[:, :LANES] - 1, columns[:, LANES:]


def slot_rows(slot, offset, homes, capacity):
    slots = slot.shape[1]
    by_worker, row, lane = slot_factors(slot, offset, homes, capacity)
    table = matmul(jnp.concatenate([row, lane], axis=0), by_worker, 1, 1).astype(jnp.bfloat16)
    number = iota((1, slots), 1)
    worker = number // capacity
    position = number - worker * capacity
    spread = matmul(table, onehot(iota((homes, slots), 0) == worker))
    at_position = iota((capacity, slots), 0) == position
    rows = jnp.sum(jnp.where(at_position, spread[:capacity], 0.0), axis=0, keepdims=True)
    lanes = jnp.sum(jnp.where(at_position, spread[capacity:], 0.0), axis=0, keepdims=True)
    return rows.astype(jnp.int32) - 1, lanes.astype(jnp.int32)


def pack_kernel(
    homes, capacity, slot_in, offset_in, forcing_in, out, slot, offset, forcing, row_of, lane_of,
    rain, ready,
):
    copies = [
        pltpu.make_async_copy(source, target, ready.at[i])
        for i, (source, target) in enumerate(
            ((slot_in, slot), (offset_in, offset), (forcing_in, forcing))
        )
    ]
    for copy in copies:
        copy.start()
    slots = slot.shape[1]
    pairs = capacity // 2
    lane_rows = forcing.shape[1]
    copies[0].wait()
    copies[1].wait()
    row_of[...], lane_of[...] = slot_columns(slot[...], offset[...], homes, capacity, True)
    copies[2].wait()
    parts = []
    for var in range(3):
        here = forcing[var]
        following = jnp.concatenate([here[1:], here[:1]], axis=0)
        parts += [here, following]
    table = jnp.concatenate(thirds(jnp.concatenate(parts, axis=1)), axis=0)
    chunk = 128
    here = iota((chunk, LANES), 1)
    for start in range(0, slots, chunk):
        odd = start >= slots // 2
        row = row_of[pl.ds(start, chunk), :]
        lane = lane_of[pl.ds(start, chunk), :]
        shape = (chunk, 3 * lane_rows)
        wide = jnp.concatenate([row, row], axis=1)[:, : 3 * lane_rows]
        pick = onehot(wide == iota(shape, 1) % lane_rows)
        rows = matmul(pick, table)
        after = here >= lane
        joined = [
            jnp.where(
                after,
                rows[:, 2 * var * LANES : (2 * var + 1) * LANES],
                rows[:, (2 * var + 1) * LANES : (2 * var + 2) * LANES],
            )
            for var in range(3)
        ]
        first = (here + lane) & 127
        second = (first + WINDOW) & 127
        losses = jnp.where(
            here < WINDOW, lane_pick(joined[1], first), lane_pick(joined[2], second)
        )
        base = start - slots // 2 if odd else start
        if odd:
            rains = jnp.where(
                here < WINDOW, rain[pl.ds(base, chunk), :], lane_pick(joined[0], second)
            )
        else:
            rain[pl.ds(base, chunk), :] = lane_pick(joined[0], first)
        for part in range(0, chunk, pairs):
            place = (base + part) * 3
            if odd:
                out[pl.ds(place + pairs, pairs), :] = rains[part : part + pairs]
                out[pl.ds(place + 2 * pairs, pairs), :] = losses[part : part + pairs]
            else:
                out[pl.ds(place, pairs), :] = losses[part : part + pairs]


def pack(homes, capacity, slot, offset, forcing):
    slots = slot.shape[1]
    return pl.pallas_call(
        functools.partial(pack_kernel, homes, capacity),
        in_specs=[pl.BlockSpec(memory_space=pltpu.HBM)] * 3,
        out_shape=jax.ShapeDtypeStruct((slots + slots // 2, LANES), jnp.float32),
        scratch_shapes=[
            pltpu.VMEM(slot.shape, jnp.int32),
            pltpu.VMEM(offset.shape, jnp.int32),
            pltpu.VMEM(forcing.shape, jnp.float32),
            pltpu.VMEM((slots, LANES), jnp.int32),
            pltpu.VMEM((slots, LANES), jnp.int32),
            pltpu.VMEM((slots // 2, LANES), jnp.float32),
            pltpu.SemaphoreType.DMA((3,)),
        ],
        compiler_params=pltpu.CompilerParams(vmem_limit_bytes=VMEM_LIMIT),
        cost_estimate=pl.CostEstimate(flops=10**9, bytes_accessed=2 * MIB, transcendentals=0),
        name="pack_forcing",
    )(in_hbm(slot), in_hbm(offset), in_hbm(forcing))


def unpack_plan_kernel(homes, capacity, lane_rows, slot, offset, code, place):
    slots = slot.shape[1]
    row, lane = slot_columns(slot[...], offset[...], homes, capacity)
    here = iota((slots, LANES), 1)
    index = (here - lane) & 127
    inside = (index < WINDOW) & (row >= 0)
    code[...] = jnp.where(inside, index + jnp.where(here >= lane, 0, LANES), -1)
    row_lane, _ = slot_rows(slot[...], offset[...], homes, capacity)
    place[...] = onehot(iota((lane_rows, slots), 0) == row_lane)


def unpack_plan(homes, capacity, lane_rows, slot, offset):
    slots = slot.shape[1]
    return pl.pallas_call(
        functools.partial(unpack_plan_kernel, homes, capacity, lane_rows),
        out_shape=(
            jax.ShapeDtypeStruct((slots, LANES), jnp.int32),
            jax.ShapeDtypeStruct((lane_rows, slots), jnp.bfloat16),
        ),
        compiler_params=pltpu.CompilerParams(vmem_limit_bytes=VMEM_LIMIT),
        cost_estimate=pl.CostEstimate(flops=10**9, bytes_accessed=2 * MIB, transcendentals=0),
        name="unpack_plan",
    )(slot, offset)


def strips_for_neighbours(axis, first, last):
    rows = lax.axis_size(axis) * ITERS
    ahead = iota((rows, LANES), 0) // ITERS - lax.axis_index(axis)

    def repeated(strip):
        return jnp.concatenate([strip] * (rows // ITERS), axis=0)

    strips = jnp.where(ahead == 1, repeated(last), 0.0)
    return jnp.where(ahead == -1, repeated(first), strips)


def strip_of_neighbour(axis, strips, ahead):
    device = lax.axis_index(axis) + ahead
    there = (device >= 0) & (device < lax.axis_size(axis))
    start = jnp.where(there, device, 0) * ITERS
    return strips[pl.ds(start, ITERS), :] * jnp.where(there, 1.0, 0.0)


def cell_totals(arrived, code, place, first):
    lane_rows = place.shape[0]
    marks = code[...]
    window = lane_pick(arrived[...], (marks + first) & 127)
    placed = jnp.concatenate(
        [
            jnp.where((marks >= 0) & (marks < LANES), window, 0.0),
            jnp.where(marks >= LANES, window, 0.0),
        ],
        axis=1,
    )
    totals = matmul(place[...], jnp.concatenate(halves(placed), axis=1))
    totals = totals[:, :256] + totals[:, 256:]
    over = totals[:, LANES:]
    over = jnp.concatenate([over[lane_rows - 1 :], over[: lane_rows - 1]], axis=0)
    over = jnp.where(iota(over.shape, 0) == 0, 0.0, over)
    return totals[:, :LANES] + over


def unpack_runoff_kernel(arrived, code, place, river, _, runoff, storage, strips):
    total = cell_totals(arrived, code, place, 0)
    state = river[...] + total
    runoff[...] = total
    storage[...] = state
    height = state.shape[0]
    strips[...] = strips_for_neighbours("region", state[:ITERS], state[height - ITERS :])


def unpack_runoff(arrived, code, place, river, after):
    shape = jax.ShapeDtypeStruct((place.shape[0], LANES), jnp.float32)
    strips = jax.ShapeDtypeStruct((lax.axis_size("region") * ITERS, LANES), jnp.float32)
    return pl.pallas_call(
        unpack_runoff_kernel,
        in_specs=[pl.BlockSpec(memory_space=pltpu.VMEM)] * 4 + [pl.BlockSpec(memory_space=pl.ANY)],
        out_shape=(shape, shape, strips),
        compiler_params=pltpu.CompilerParams(vmem_limit_bytes=VMEM_LIMIT),
        cost_estimate=pl.CostEstimate(flops=10**9, bytes_accessed=1 * MIB, transcendentals=0),
        name="unpack_runoff",
    )(arrived, code, place, river, after)


def unpack_evap_kernel(arrived, code, place, evap):
    evap[...] = cell_totals(arrived, code, place, WINDOW)


def unpack_evap(arrived, code, place):
    return pl.pallas_call(
        unpack_evap_kernel,
        out_shape=jax.ShapeDtypeStruct((place.shape[0], LANES), jnp.float32),
        compiler_params=pltpu.CompilerParams(vmem_limit_bytes=VMEM_LIMIT),
        cost_estimate=pl.CostEstimate(flops=10**9, bytes_accessed=1 * MIB, transcendentals=0),
        name="unpack_evap",
    )(arrived, code, place)


def segment_plan_kernel(cell, worker, meta):
    chunk = 96
    for start in range(0, cell.shape[0], chunk):
        values = cell[pl.ds(start, chunk), :]
        target = iota(values.shape, 1) & (WINDOW - 1)
        count = jnp.zeros_like(values)
        for step in (64, 32, 16, 8, 4, 2, 1):
            probe = lane_pick(values, count + (step - 1))
            count = jnp.where(probe <= target, count + step, count)
        count = jnp.where(lane_pick(values, count) <= target, count + 1, count)
        odd = worker[pl.ds(start, chunk), :] & 1
        meta[pl.ds(start, chunk), :] = count + (odd << 8)


def segment_plan(cell, worker):
    return pl.pallas_call(
        segment_plan_kernel,
        out_shape=jax.ShapeDtypeStruct(cell.shape, jnp.int32),
        compiler_params=pltpu.CompilerParams(vmem_limit_bytes=VMEM_LIMIT),
        cost_estimate=pl.CostEstimate(flops=10**8, bytes_accessed=1 * MIB, transcendentals=0),
        name="segment_plan",
    )(cell, worker)


def segment_totals(runoff, evap, marks):
    shape = (2 * LANES, LANES)
    upto = onehot((iota(shape, 0) & 127) <= iota(shape, 1))
    count = marks & 255
    last = jnp.maximum(count - 1, 0)
    here = iota(marks.shape, 1)
    sums = [
        lane_pick(matmul(jnp.concatenate(halves(value), axis=1), upto), last)
        for value in (runoff, evap)
    ]
    reached = jnp.where(count > 0, jnp.where(here < WINDOW, *sums), 0.0)
    before = jnp.where((here & (WINDOW - 1)) == 0, 0.0, pltpu.roll(reached, 1, 1))
    return reached - before


def land_kernel(
    pairs, slots, first_rows, arrived, cell, meta, area, water, cap, soil_in, porosity_in, drainage_in,
    _, __, soil_out, canopy_new, sums_out, soil, porosity, drainage, fetched, runoffs, evaps,
    ready, written,
):
    layers, rows = soil.shape[:2]
    steps = written.shape[0]
    block = rows // steps
    chunk = block // 2
    arrays = ((soil_in, soil), (porosity_in, porosity), (drainage_in, drainage))

    def part_of(step):
        return pl.ds(step * block, block)

    def reads(step):
        return [
            pltpu.make_async_copy(
                source.at[:, part_of(step), :], target.at[:, part_of(step), :], ready.at[step, i]
            )
            for i, (source, target) in enumerate(arrays)
        ]

    def write(step):
        return pltpu.make_async_copy(
            soil.at[:, part_of(step), :], soil_out.at[:, part_of(step), :], written.at[step]
        )

    def fetch(step):
        for i in range(step * block, (step + 1) * block):
            fetched[pl.ds(2 * i, 2), :] = arrived[pl.ds(first_rows[i], 2, stride=pairs), :]

    def cascade(start):
        part = pl.ds(start, chunk)
        index = cell[part, :]
        one = fetched[pl.ds(2 * start, chunk, stride=2), :]
        two = fetched[pl.ds(2 * start + 1, chunk, stride=2), :]
        odd = meta[part, :] >> 8
        loss = jnp.where(odd == 1, two, one)
        rain = lane_pick(jnp.where(odd == 1, one, two), index + odd * WINDOW)
        demand = lane_pick(loss, index)
        limit = lane_pick(loss, index + WINDOW)
        wetted = water[part, :] + rain
        flowing = jnp.maximum(wetted - cap[part, :], 0.0)
        retained = jnp.minimum(wetted, cap[part, :])
        canopy_loss = jnp.minimum(demand, retained)
        canopy_new[part, :] = retained - canopy_loss
        surface = jnp.zeros_like(flowing)
        for layer in range(layers):
            filled = soil[layer, part, :] + flowing
            excess = jnp.maximum(filled - porosity[layer, part, :], 0.0)
            surface = surface + excess
            filled = filled - excess
            flowing = drainage[layer, part, :] * filled
            middle = filled - flowing
            if layer == 0:
                soil_loss = jnp.minimum(jnp.minimum(limit, demand - canopy_loss), 0.5 * middle)
                middle = middle - soil_loss
                evaps[part, :] = area[part, :] * (canopy_loss + soil_loss)
            soil[layer, part, :] = middle
        runoffs[part, :] = area[part, :] * (surface + flowing)

    def scan(step):
        part = part_of(step)
        runoffs[part, :] = segment_totals(runoffs[part, :], evaps[part, :], meta[part, :])

    def hand_back(step):
        for i in range(step * block, (step + 1) * block):
            sums_out[pl.ds(slots[i], 1), :] = runoffs[pl.ds(i, 1), :]

    for step in range(steps):
        for copy in reads(step):
            copy.start()
    sums_out[...] = jnp.zeros_like(sums_out)
    for step in range(steps):
        fetch(step)
    for step in range(steps + 2):
        if step < steps:
            for copy in reads(step):
                copy.wait()
            for start in range(step * block, (step + 1) * block, chunk):
                cascade(start)
        if 1 <= step <= steps:
            scan(step - 1)
        if step >= 2:
            hand_back(step - 2)
        if step < steps:
            write(step).start()
    for step in range(steps):
        write(step).wait()


def land_step(
    sums_shape, pairs, slots, first_rows, arrived, cell, meta, area, water, cap, soil, porosity,
    drainage, after,
):
    layers, rows = soil.shape[:2]
    steps = 5
    near = pl.BlockSpec(memory_space=pltpu.VMEM)
    far = pl.BlockSpec(memory_space=pltpu.HBM)
    return pl.pallas_call(
        functools.partial(land_kernel, pairs),
        in_specs=[pl.BlockSpec(memory_space=pltpu.SMEM)] * 2 + [near] * 6 + [far] * 3
        + [pl.BlockSpec(memory_space=pl.ANY)] * 2,
        out_specs=[far, near, near],
        scratch_shapes=[pltpu.VMEM(soil.shape, jnp.float32)] * 3
        + [pltpu.VMEM((2 * rows, LANES), jnp.float32)]
        + [pltpu.VMEM((rows, LANES), jnp.float32)] * 2
        + [pltpu.SemaphoreType.DMA((steps, 3)), pltpu.SemaphoreType.DMA((steps,))],
        out_shape=(
            jax.ShapeDtypeStruct(soil.shape, jnp.float32),
            jax.ShapeDtypeStruct((rows, LANES), jnp.float32),
            jax.ShapeDtypeStruct(sums_shape, jnp.float32),
        ),
        compiler_params=pltpu.CompilerParams(vmem_limit_bytes=VMEM_LIMIT),
        cost_estimate=pl.CostEstimate(flops=10**8, bytes_accessed=20 * MIB, transcendentals=0),
        name="land_layers",
    )(
        slots, first_rows, arrived, cell, meta, area, water, cap,
        in_hbm(soil), in_hbm(porosity), in_hbm(drainage), *after,
    )


def halo_parts(value, axis, dim, width):
    count, length = (lax.axis_size(axis), value.shape[dim])
    up = [(i, i + 1) for i in range(count - 1)]
    down = [(j, i) for i, j in up]
    last = lax.slice_in_dim(value, length - width, length, axis=dim)
    initial = lax.slice_in_dim(value, 0, width, axis=dim)
    return lax.ppermute(last, axis, up), lax.ppermute(initial, axis, down)


def edge_columns_kernel(tall, _, first, last):
    arrays, height, width = tall.shape
    for number in range(arrays):
        values = tall[number]
        values = jnp.concatenate([values, jnp.zeros((LANES - height, width), jnp.float32)], axis=0)
        columns = jnp.transpose(values)
        part = pl.ds(number * ITERS, ITERS)
        first[part, :] = columns[:ITERS]
        last[part, :] = columns[width - ITERS :]


def edge_columns(tall, after):
    shape = jax.ShapeDtypeStruct((2 * ITERS, LANES), jnp.float32)
    return pl.pallas_call(
        edge_columns_kernel,
        in_specs=[pl.BlockSpec(memory_space=pltpu.VMEM), pl.BlockSpec(memory_space=pl.ANY)],
        out_shape=(shape, shape),
        compiler_params=pltpu.CompilerParams(vmem_limit_bytes=VMEM_LIMIT),
        cost_estimate=pl.CostEstimate(flops=10**6, bytes_accessed=10**5, transcendentals=0),
        name="edge_columns",
    )(tall, after)


def with_rows_kernel(own, strips, tall, columns):
    height, width = own.shape
    after = strip_of_neighbour("region", strips, 1)
    before = strip_of_neighbour("region", strips, -1)
    values = jnp.concatenate([own[...], after, before], axis=0)
    tall[...] = values
    gap = jnp.zeros((LANES - height - 2 * ITERS, width), jnp.float32)
    values = jnp.transpose(jnp.concatenate([values, gap], axis=0))
    columns[...] = strips_for_neighbours("col", values[:ITERS], values[width - ITERS :])


def with_rows(own, strips):
    height, width = own.shape
    return pl.pallas_call(
        with_rows_kernel,
        out_shape=(
            jax.ShapeDtypeStruct((height + 2 * ITERS, width), jnp.float32),
            jax.ShapeDtypeStruct((lax.axis_size("col") * ITERS, LANES), jnp.float32),
        ),
        compiler_params=pltpu.CompilerParams(vmem_limit_bytes=VMEM_LIMIT),
        cost_estimate=pl.CostEstimate(flops=10**6, bytes_accessed=10**5, transcendentals=0),
        name="storage_rows",
    )(own, strips)


def static_halo_kernel(tall, before, after, out):
    height, width = tall.shape[1:]
    gap = jnp.zeros((LANES - 2 * ITERS, LANES), jnp.float32)
    for number in range(2):
        part = pl.ds(number * ITERS, ITERS)
        sides = jnp.transpose(jnp.concatenate([after[part, :], gap, before[part, :]], axis=0))
        out[number, :, :width] = tall[number]
        out[number, :, width:] = sides[:height]


def static_halo(tall, before, after):
    arrays, height, width = tall.shape
    return pl.pallas_call(
        static_halo_kernel,
        out_shape=jax.ShapeDtypeStruct((arrays, height, width + LANES), jnp.float32),
        compiler_params=pltpu.CompilerParams(vmem_limit_bytes=VMEM_LIMIT),
        cost_estimate=pl.CostEstimate(flops=10**6, bytes_accessed=10**6, transcendentals=0),
        name="static_halo",
    )(tall, before, after)


def river_kernel(tall, strips, fixed, out):
    height, width = out.shape
    after = strip_of_neighbour("col", strips, 1)
    before = strip_of_neighbour("col", strips, -1)
    gap = jnp.zeros((LANES - 2 * ITERS, LANES), jnp.float32)
    sides = jnp.transpose(jnp.concatenate([after, gap, before], axis=0))
    storage = jnp.concatenate([tall[...], sides[: height + 2 * ITERS]], axis=1)
    rate = fixed[0]
    code = fixed[1]
    rows, cols = storage.shape
    for _ in range(ITERS):
        outflow = rate * storage
        inflow = jnp.zeros_like(storage)
        for col_step in (-1, 0, 1):
            column = jnp.zeros_like(storage)
            for bit, (row_step, step) in enumerate(directions):
                if step != col_step:
                    continue
                leaving = jnp.where(code == float(1 << bit), outflow, 0.0)
                if row_step:
                    leaving = pltpu.roll(leaving, row_step % rows, 0)
                column = column + leaving
            if col_step:
                column = pltpu.roll(column, col_step % cols, 1)
            inflow = inflow + column
        storage = storage - outflow + inflow
    out[...] = storage[:height, :width]


def river(shape, tall, strips, fixed):
    return pl.pallas_call(
        river_kernel,
        out_shape=jax.ShapeDtypeStruct(shape, jnp.float32),
        compiler_params=pltpu.CompilerParams(vmem_limit_bytes=VMEM_LIMIT),
        cost_estimate=pl.CostEstimate(flops=10**7, bytes_accessed=1 * MIB, transcendentals=0),
        name="river_steps",
    )(tall, strips, fixed)


def exchange(value, axis=axes):
    return lax.all_to_all(value, axis, split_axis=0, concat_axis=0, tiled=True)


def shards(
    forcing,
    river_storage,
    river_rate,
    flow_code,
    home_slot,
    home_offset,
    worker_list,
    patch_cell,
    patch_area,
    canopy_water,
    canopy_cap,
    soil_water,
    porosity,
    drainage,
):
    homes = lax.axis_size("region") * lax.axis_size("col")
    capacity = home_slot.shape[1] // homes
    grid_rows, grid_cols = river_storage.shape
    lane_rows = grid_rows * grid_cols // LANES
    outgoing = pack(
        homes, capacity, home_slot, home_offset, forcing.reshape(3, lane_rows, LANES)
    )
    arrived = exchange(outgoing)
    home = worker_list // capacity
    position = worker_list - home * capacity
    pairs = capacity // 2
    first_rows = home * (3 * pairs) + position // 2 + position % 2 * pairs
    meta = segment_plan(patch_cell, worker_list[:, None])
    fixed = jnp.stack([river_rate, flow_code.astype(jnp.float32)])
    above, below = halo_parts(fixed, "region", 1, ITERS)
    soil_new, canopy_new, sums = land_step(
        (homes * capacity, LANES), pairs, worker_list, first_rows, arrived, patch_cell, meta,
        patch_area, canopy_water, canopy_cap, soil_water, porosity, drainage, (above, below),
    )
    returned = exchange(sums)
    code, place = unpack_plan(homes, capacity, lane_rows, home_slot, home_offset)
    fixed = jnp.concatenate([fixed, below, above], axis=1)
    initial, last = edge_columns(fixed, sums)
    count = lax.axis_size("col")
    before = lax.ppermute(last, "col", [(i, i + 1) for i in range(count - 1)])
    after = lax.ppermute(initial, "col", [(i + 1, i) for i in range(count - 1)])
    fixed = static_halo(fixed, before, after)
    cell_runoff, storage, strips = unpack_runoff(
        returned, code, place, river_storage.reshape(lane_rows, LANES), fixed
    )
    cell_evap = unpack_evap(returned, code, place)
    tall, columns = with_rows(storage, exchange(strips, "region"))
    river_new = river(river_storage.shape, tall, exchange(columns, "col"), fixed)
    return (
        soil_new,
        canopy_new,
        cell_runoff.reshape(river_storage.shape),
        cell_evap.reshape(river_storage.shape),
        river_new,
    )


def solution(mesh):
    placed = (
        P(None, "region", "col"),
        P("region", "col"),
        P("region", "col"),
        P("region", "col"),
        P(("region", "col"), None),
        P(("region", "col"), None),
        P(("region", "col")),
        P(("region", "col"), None),
        P(("region", "col"), None),
        P(("region", "col"), None),
        P(("region", "col"), None),
        P(None, ("region", "col"), None),
        P(None, ("region", "col"), None),
        P(None, ("region", "col"), None),
    )
    return jax.shard_map(
        shards,
        mesh=mesh,
        in_specs=placed,
        out_specs=(
            P(None, ("region", "col"), None),
            P(("region", "col"), None),
            P("region", "col"),
            P("region", "col"),
            P("region", "col"),
        ),
        check_vma=False,
    )
```

```python
import functools

import jax
import jax.numpy as jnp
from jax import lax
from jax.experimental import pallas as pl
from jax.experimental.pallas import tpu as pltpu
from jax.sharding import PartitionSpec as P

ITERS = 4
WINDOW = 64
LANES = 128
MIB = 1024 * 1024
VMEM_LIMIT = 24 * MIB

directions = ((0, 1), (1, 1), (1, 0), (1, -1), (0, -1), (-1, -1), (-1, 0), (-1, 1))
axes = ("region", "col")


def iota(shape, dim):
    return lax.broadcasted_iota(jnp.int32, shape, dim)


def onehot(mask):
    return jnp.where(mask, jnp.float32(1.0), jnp.float32(0.0)).astype(jnp.bfloat16)


def lane_pick(values, index):
    return jnp.take_along_axis(values, index, axis=1, mode="promise_in_bounds")


def in_hbm(value):
    return pltpu.with_memory_space_constraint(value, pltpu.HBM)


def thirds(value):
    high = value.astype(jnp.bfloat16)
    rest = value - high.astype(jnp.float32)
    middle = rest.astype(jnp.bfloat16)
    low = (rest - middle.astype(jnp.float32)).astype(jnp.bfloat16)
    return high, middle, low


def halves(value):
    high = value.astype(jnp.bfloat16)
    return high, (value - high.astype(jnp.float32)).astype(jnp.bfloat16)


def matmul(a, b, a_dim=1, b_dim=0):
    return lax.dot_general(
        a, b, (((a_dim,), (b_dim,)), ((), ())), preferred_element_type=jnp.float32
    )


def slot_factors(slot, offset, homes, capacity):
    slots = slot.shape[1]
    worker = slot // capacity if capacity & (capacity - 1) else slot >> (capacity.bit_length() - 1)
    position = slot - worker * capacity
    by_worker = onehot(iota((homes, slots), 0) == worker)
    at_position = iota((capacity, slots), 0) == position
    row = jnp.where(at_position, ((offset >> 7) + 1).astype(jnp.float32), 0.0)
    lane = jnp.where(at_position, (offset & 127).astype(jnp.float32), 0.0)
    return by_worker, row.astype(jnp.bfloat16), lane.astype(jnp.bfloat16)


def slot_columns(slot, offset, homes, capacity, split=False):
    slots = slot.shape[1]
    by_worker, row, lane = slot_factors(slot, offset, homes, capacity)
    table = matmul(by_worker, jnp.concatenate([row, lane], axis=0), 1, 1)
    groups = 2 if split else 1
    spread = jnp.broadcast_to(
        table[:, None, :], (homes, capacity // groups, 2 * capacity)
    ).reshape(slots // groups, 2 * capacity)
    spread = jnp.concatenate([spread] * groups, axis=0)
    number = iota(spread.shape, 0)
    position = number % (capacity // groups) * groups + number // (slots // groups)
    place = position == iota(spread.shape, 1) % capacity
    kept = jnp.where(place, spread, 0.0).astype(jnp.bfloat16)
    shape = (2 * capacity, 2 * LANES)
    gather = onehot((iota(shape, 0) >= capacity) == (iota(shape, 1) >= LANES))
    columns = matmul(kept, gather).astype(jnp.int32)
    return columns[:, :LANES] - 1, columns[:, LANES:]


def slot_rows(slot, offset, homes, capacity):
    slots = slot.shape[1]
    by_worker, row, lane = slot_factors(slot, offset, homes, capacity)
    table = matmul(jnp.concatenate([row, lane], axis=0), by_worker, 1, 1).astype(jnp.bfloat16)
    number = iota((1, slots), 1)
    worker = number // capacity
    position = number - worker * capacity
    spread = matmul(table, onehot(iota((homes, slots), 0) == worker))
    at_position = iota((capacity, slots), 0) == position
    rows = jnp.sum(jnp.where(at_position, spread[:capacity], 0.0), axis=0, keepdims=True)
    lanes = jnp.sum(jnp.where(at_position, spread[capacity:], 0.0), axis=0, keepdims=True)
    return rows.astype(jnp.int32) - 1, lanes.astype(jnp.int32)


def pack_kernel(
    homes, capacity, slot_in, offset_in, forcing_in, out, slot, offset, forcing, row_of, lane_of,
    rain, ready,
):
    copies = [
        pltpu.make_async_copy(source, target, ready.at[i])
        for i, (source, target) in enumerate(
            ((slot_in, slot), (offset_in, offset), (forcing_in, forcing))
        )
    ]
    for copy in copies:
        copy.start()
    slots = slot.shape[1]
    pairs = capacity // 2
    lane_rows = forcing.shape[1]
    copies[0].wait()
    copies[1].wait()
    row_of[...], lane_of[...] = slot_columns(slot[...], offset[...], homes, capacity, True)
    copies[2].wait()
    parts = []
    for var in range(3):
        here = forcing[var]
        following = jnp.concatenate([here[1:], here[:1]], axis=0)
        parts += [here, following]
    table = jnp.concatenate(thirds(jnp.concatenate(parts, axis=1)), axis=0)
    chunk = 128
    here = iota((chunk, LANES), 1)
    for start in range(0, slots, chunk):
        odd = start >= slots // 2
        row = row_of[pl.ds(start, chunk), :]
        lane = lane_of[pl.ds(start, chunk), :]
        shape = (chunk, 3 * lane_rows)
        wide = jnp.concatenate([row, row], axis=1)[:, : 3 * lane_rows]
        pick = onehot(wide == iota(shape, 1) % lane_rows)
        rows = matmul(pick, table)
        after = here >= lane
        joined = [
            jnp.where(
                after,
                rows[:, 2 * var * LANES : (2 * var + 1) * LANES],
                rows[:, (2 * var + 1) * LANES : (2 * var + 2) * LANES],
            )
            for var in range(3)
        ]
        first = (here + lane) & 127
        second = (first + WINDOW) & 127
        losses = jnp.where(
            here < WINDOW, lane_pick(joined[1], first), lane_pick(joined[2], second)
        )
        base = start - slots // 2 if odd else start
        if odd:
            rains = jnp.where(
                here < WINDOW, rain[pl.ds(base, chunk), :], lane_pick(joined[0], second)
            )
        else:
            rain[pl.ds(base, chunk), :] = lane_pick(joined[0], first)
        for part in range(0, chunk, pairs):
            place = (base + part) * 3
            if odd:
                out[pl.ds(place + pairs, pairs), :] = rains[part : part + pairs]
                out[pl.ds(place + 2 * pairs, pairs), :] = losses[part : part + pairs]
            else:
                out[pl.ds(place, pairs), :] = losses[part : part + pairs]


def pack(homes, capacity, slot, offset, forcing):
    slots = slot.shape[1]
    return pl.pallas_call(
        functools.partial(pack_kernel, homes, capacity),
        in_specs=[pl.BlockSpec(memory_space=pltpu.HBM)] * 3,
        out_shape=jax.ShapeDtypeStruct((slots + slots // 2, LANES), jnp.float32),
        scratch_shapes=[
            pltpu.VMEM(slot.shape, jnp.int32),
            pltpu.VMEM(offset.shape, jnp.int32),
            pltpu.VMEM(forcing.shape, jnp.float32),
            pltpu.VMEM((slots, LANES), jnp.int32),
            pltpu.VMEM((slots, LANES), jnp.int32),
            pltpu.VMEM((slots // 2, LANES), jnp.float32),
            pltpu.SemaphoreType.DMA((3,)),
        ],
        compiler_params=pltpu.CompilerParams(vmem_limit_bytes=VMEM_LIMIT),
        cost_estimate=pl.CostEstimate(flops=10**9, bytes_accessed=2 * MIB, transcendentals=0),
        name="pack_forcing",
    )(in_hbm(slot), in_hbm(offset), in_hbm(forcing))


def unpack_plan_kernel(homes, capacity, lane_rows, slot, offset, code, place):
    slots = slot.shape[1]
    row, lane = slot_columns(slot[...], offset[...], homes, capacity)
    here = iota((slots, LANES), 1)
    index = (here - lane) & 127
    inside = (index < WINDOW) & (row >= 0)
    code[...] = jnp.where(inside, index + jnp.where(here >= lane, 0, LANES), -1)
    row_lane, _ = slot_rows(slot[...], offset[...], homes, capacity)
    place[...] = onehot(iota((lane_rows, slots), 0) == row_lane)


def unpack_plan(homes, capacity, lane_rows, slot, offset):
    slots = slot.shape[1]
    return pl.pallas_call(
        functools.partial(unpack_plan_kernel, homes, capacity, lane_rows),
        out_shape=(
            jax.ShapeDtypeStruct((slots, LANES), jnp.int32),
            jax.ShapeDtypeStruct((lane_rows, slots), jnp.bfloat16),
        ),
        compiler_params=pltpu.CompilerParams(vmem_limit_bytes=VMEM_LIMIT),
        cost_estimate=pl.CostEstimate(flops=10**9, bytes_accessed=2 * MIB, transcendentals=0),
        name="unpack_plan",
    )(slot, offset)


def strips_for_neighbours(state, rows):
    device = iota((rows, LANES), 0) // ITERS
    down = device // lax.axis_size("col") - lax.axis_index("region")
    right = device % lax.axis_size("col") - lax.axis_index("col")
    height, width = state.shape
    columns = jnp.transpose(state)
    empty = jnp.zeros((ITERS, LANES - height), jnp.float32)

    def repeated(strip):
        if strip.shape[1] < LANES:
            strip = jnp.concatenate([strip, empty], axis=1)
        return jnp.concatenate([strip] * (rows // ITERS), axis=0)

    near = (jnp.abs(down) <= 1).astype(jnp.int32)
    strips = jnp.zeros((rows, LANES), jnp.float32)
    strips = jnp.where((right == 0) & (down == 1), repeated(state[height - ITERS :]), strips)
    strips = jnp.where((right == 0) & (down == -1), repeated(state[:ITERS]), strips)
    strips = jnp.where((right == 1) & (near == 1), repeated(columns[width - ITERS :]), strips)
    return jnp.where((right == -1) & (near == 1), repeated(columns[:ITERS]), strips)


def cell_totals(arrived, code, place, first):
    lane_rows = place.shape[0]
    marks = code[...]
    window = lane_pick(arrived[...], (marks + first) & 127)
    placed = jnp.concatenate(
        [
            jnp.where((marks >= 0) & (marks < LANES), window, 0.0),
            jnp.where(marks >= LANES, window, 0.0),
        ],
        axis=1,
    )
    totals = matmul(place[...], jnp.concatenate(halves(placed), axis=1))
    totals = totals[:, :256] + totals[:, 256:]
    over = totals[:, LANES:]
    over = jnp.concatenate([over[lane_rows - 1 :], over[: lane_rows - 1]], axis=0)
    over = jnp.where(iota(over.shape, 0) == 0, 0.0, over)
    return totals[:, :LANES] + over


def unpack_runoff_kernel(arrived, code, place, river, _, runoff, storage, strips):
    total = cell_totals(arrived, code, place, 0)
    state = river[...] + total
    runoff[...] = total
    storage[...] = state
    strips[...] = strips_for_neighbours(state, strips.shape[0])


def unpack_runoff(homes, arrived, code, place, river, after):
    shape = jax.ShapeDtypeStruct((place.shape[0], LANES), jnp.float32)
    strips = jax.ShapeDtypeStruct((homes * ITERS, LANES), jnp.float32)
    return pl.pallas_call(
        unpack_runoff_kernel,
        in_specs=[pl.BlockSpec(memory_space=pltpu.VMEM)] * 4 + [pl.BlockSpec(memory_space=pl.ANY)],
        out_shape=(shape, shape, strips),
        compiler_params=pltpu.CompilerParams(vmem_limit_bytes=VMEM_LIMIT),
        cost_estimate=pl.CostEstimate(flops=10**9, bytes_accessed=1 * MIB, transcendentals=0),
        name="unpack_runoff",
    )(arrived, code, place, river, after)


def unpack_evap_kernel(arrived, code, place, evap):
    evap[...] = cell_totals(arrived, code, place, WINDOW)


def unpack_evap(arrived, code, place):
    return pl.pallas_call(
        unpack_evap_kernel,
        out_shape=jax.ShapeDtypeStruct((place.shape[0], LANES), jnp.float32),
        compiler_params=pltpu.CompilerParams(vmem_limit_bytes=VMEM_LIMIT),
        cost_estimate=pl.CostEstimate(flops=10**9, bytes_accessed=1 * MIB, transcendentals=0),
        name="unpack_evap",
    )(arrived, code, place)


def segment_plan_kernel(cell, worker, meta):
    chunk = 96
    for start in range(0, cell.shape[0], chunk):
        values = cell[pl.ds(start, chunk), :]
        target = iota(values.shape, 1) & (WINDOW - 1)
        count = jnp.zeros_like(values)
        for step in (64, 32, 16, 8, 4, 2, 1):
            probe = lane_pick(values, count + (step - 1))
            count = jnp.where(probe <= target, count + step, count)
        count = jnp.where(lane_pick(values, count) <= target, count + 1, count)
        odd = worker[pl.ds(start, chunk), :] & 1
        meta[pl.ds(start, chunk), :] = count + (odd << 8)


def segment_plan(cell, worker):
    return pl.pallas_call(
        segment_plan_kernel,
        out_shape=jax.ShapeDtypeStruct(cell.shape, jnp.int32),
        compiler_params=pltpu.CompilerParams(vmem_limit_bytes=VMEM_LIMIT),
        cost_estimate=pl.CostEstimate(flops=10**8, bytes_accessed=1 * MIB, transcendentals=0),
        name="segment_plan",
    )(cell, worker)


def land_kernel(
    pairs, slots, first_rows, arrived, cell, meta, area, water, cap, soil_in, porosity_in,
    drainage_in, _, __, soil_out, canopy_new, sums_out, soil, porosity, drainage, fetched,
    flows, surfaces, evaps, ready, written,
):
    layers, rows = soil.shape[:2]
    groups = written.shape[0]
    depth = layers // groups
    chunk = 48
    block = 96
    arrays = ((soil_in, soil), (porosity_in, porosity), (drainage_in, drainage))

    def reads(group):
        part = pl.ds(group * depth, depth)
        return [
            pltpu.make_async_copy(source.at[part], target.at[part], ready.at[group, i])
            for i, (source, target) in enumerate(arrays)
        ]

    def write(group):
        part = pl.ds(group * depth, depth)
        return pltpu.make_async_copy(soil.at[part], soil_out.at[part], written.at[group])

    def canopy(start):
        part = pl.ds(start, chunk)
        index = cell[part, :]
        one = fetched[pl.ds(2 * start, chunk, stride=2), :]
        two = fetched[pl.ds(2 * start + 1, chunk, stride=2), :]
        odd = meta[part, :] >> 8
        loss = jnp.where(odd == 1, two, one)
        rain = lane_pick(jnp.where(odd == 1, one, two), index + odd * WINDOW)
        demand = lane_pick(loss, index)
        limit = lane_pick(loss, index + WINDOW)
        wetted = water[part, :] + rain
        retained = jnp.minimum(wetted, cap[part, :])
        canopy_loss = jnp.minimum(demand, retained)
        canopy_new[part, :] = retained - canopy_loss
        flows[part, :] = jnp.maximum(wetted - cap[part, :], 0.0)
        surfaces[part, :] = jnp.minimum(limit, demand - canopy_loss)
        evaps[part, :] = canopy_loss

    def cascade(group, start):
        part = pl.ds(start, chunk)
        flowing = flows[part, :]
        surface = jnp.zeros_like(flowing) if group == 0 else surfaces[part, :]
        for layer in range(group * depth, (group + 1) * depth):
            filled = soil[layer, part, :] + flowing
            excess = jnp.maximum(filled - porosity[layer, part, :], 0.0)
            surface = surface + excess
            filled = filled - excess
            flowing = drainage[layer, part, :] * filled
            middle = filled - flowing
            if layer == 0:
                soil_loss = jnp.minimum(surfaces[part, :], 0.5 * middle)
                middle = middle - soil_loss
                evaps[part, :] = area[part, :] * (evaps[part, :] + soil_loss)
            soil[layer, part, :] = middle
        if group < groups - 1:
            flows[part, :] = flowing
            surfaces[part, :] = surface
        else:
            flows[part, :] = area[part, :] * (surface + flowing)

    def reached(values, part):
        shape = (2 * LANES, LANES)
        upto = onehot((iota(shape, 0) & 127) <= iota(shape, 1))
        count = meta[part, :] & 255
        sums = matmul(jnp.concatenate(halves(values[part, :]), axis=1), upto)
        return jnp.where(count > 0, lane_pick(sums, jnp.maximum(count - 1, 0)), 0.0)

    def hand_back(start):
        part = pl.ds(start, block)
        here = iota((block, LANES), 1)
        sums = jnp.where(here < WINDOW, reached(flows, part), evaps[part, :])
        before = jnp.where((here & (WINDOW - 1)) == 0, 0.0, pltpu.roll(sums, 1, 1))
        surfaces[part, :] = sums - before
        for i in range(start, start + block):
            sums_out[pl.ds(slots[i], 1), :] = surfaces[pl.ds(i, 1), :]

    for group in range(groups):
        for copy in reads(group):
            copy.start()
    sums_out[...] = jnp.zeros_like(sums_out)
    for i in range(rows):
        fetched[pl.ds(2 * i, 2), :] = arrived[pl.ds(first_rows[i], 2, stride=pairs), :]
    for start in range(0, rows, chunk):
        canopy(start)
    for group in range(groups):
        for copy in reads(group):
            copy.wait()
        for start in range(0, rows, chunk):
            cascade(group, start)
        write(group).start()
        if group == min(1, groups - 1):
            for start in range(0, rows, block):
                evaps[pl.ds(start, block), :] = reached(evaps, pl.ds(start, block))
    for start in range(0, rows, block):
        hand_back(start)
    for group in range(groups):
        write(group).wait()


def land_step(
    sums_shape, pairs, slots, first_rows, arrived, cell, meta, area, water, cap, soil, porosity,
    drainage, after,
):
    layers, rows = soil.shape[:2]
    groups = 5 if layers % 5 == 0 else 1
    near = pl.BlockSpec(memory_space=pltpu.VMEM)
    far = pl.BlockSpec(memory_space=pltpu.HBM)
    return pl.pallas_call(
        functools.partial(land_kernel, pairs),
        in_specs=[pl.BlockSpec(memory_space=pltpu.SMEM)] * 2 + [near] * 6 + [far] * 3
        + [pl.BlockSpec(memory_space=pl.ANY)] * 2,
        out_specs=[far, near, near],
        scratch_shapes=[pltpu.VMEM(soil.shape, jnp.float32)] * 3
        + [pltpu.VMEM((2 * rows, LANES), jnp.float32)]
        + [pltpu.VMEM((rows, LANES), jnp.float32)] * 3
        + [pltpu.SemaphoreType.DMA((groups, 3)), pltpu.SemaphoreType.DMA((groups,))],
        out_shape=(
            jax.ShapeDtypeStruct(soil.shape, jnp.float32),
            jax.ShapeDtypeStruct((rows, LANES), jnp.float32),
            jax.ShapeDtypeStruct(sums_shape, jnp.float32),
        ),
        compiler_params=pltpu.CompilerParams(vmem_limit_bytes=VMEM_LIMIT),
        cost_estimate=pl.CostEstimate(flops=10**8, bytes_accessed=20 * MIB, transcendentals=0),
        name="land_layers",
    )(
        slots, first_rows, arrived, cell, meta, area, water, cap,
        in_hbm(soil), in_hbm(porosity), in_hbm(drainage), *after,
    )


def halo_parts(value, axis, dim, width):
    count, length = (lax.axis_size(axis), value.shape[dim])
    up = [(i, i + 1) for i in range(count - 1)]
    down = [(j, i) for i, j in up]
    last = lax.slice_in_dim(value, length - width, length, axis=dim)
    initial = lax.slice_in_dim(value, 0, width, axis=dim)
    return lax.ppermute(last, axis, up), lax.ppermute(initial, axis, down)


def edge_columns_kernel(tall, _, first, last):
    arrays, height, width = tall.shape
    for number in range(arrays):
        values = tall[number]
        values = jnp.concatenate([values, jnp.zeros((LANES - height, width), jnp.float32)], axis=0)
        columns = jnp.transpose(values)
        part = pl.ds(number * ITERS, ITERS)
        first[part, :] = columns[:ITERS]
        last[part, :] = columns[width - ITERS :]


def edge_columns(tall, after):
    shape = jax.ShapeDtypeStruct((2 * ITERS, LANES), jnp.float32)
    return pl.pallas_call(
        edge_columns_kernel,
        in_specs=[pl.BlockSpec(memory_space=pltpu.VMEM), pl.BlockSpec(memory_space=pl.ANY)],
        out_shape=(shape, shape),
        compiler_params=pltpu.CompilerParams(vmem_limit_bytes=VMEM_LIMIT),
        cost_estimate=pl.CostEstimate(flops=10**6, bytes_accessed=10**5, transcendentals=0),
        name="edge_columns",
    )(tall, after)


def extended(own, strip):
    height = own.shape[0]

    def column_strip(right):
        middle, above, below = strip(0, right), strip(-1, right), strip(1, right)
        return jnp.concatenate(
            [
                middle[:, :height],
                below[:, :ITERS],
                above[:, height - ITERS : height],
                jnp.zeros((ITERS, LANES - height - 2 * ITERS), jnp.float32),
            ],
            axis=1,
        )

    gap = jnp.zeros((LANES - 2 * ITERS, LANES), jnp.float32)
    sides = jnp.concatenate([column_strip(1), gap, column_strip(-1)], axis=0)
    sides = jnp.transpose(sides)[: height + 2 * ITERS]
    tall = jnp.concatenate([own, strip(1, 0), strip(-1, 0)], axis=0)
    return jnp.concatenate([tall, sides], axis=1)


def neighbour(down, right):
    row, column = lax.axis_index("region") + down, lax.axis_index("col") + right
    there = (row >= 0) & (row < lax.axis_size("region"))
    there &= (column >= 0) & (column < lax.axis_size("col"))
    return jnp.where(there, row * lax.axis_size("col") + column, 0), jnp.where(there, 1.0, 0.0)


def static_halo_kernel(tall, before, after, out):
    height, width = tall.shape[1:]
    gap = jnp.zeros((LANES - 2 * ITERS, LANES), jnp.float32)
    for number in range(2):
        part = pl.ds(number * ITERS, ITERS)
        sides = jnp.transpose(jnp.concatenate([after[part, :], gap, before[part, :]], axis=0))
        out[number, :, :width] = tall[number]
        out[number, :, width:] = sides[:height]


def static_halo(tall, before, after):
    arrays, height, width = tall.shape
    return pl.pallas_call(
        static_halo_kernel,
        out_shape=jax.ShapeDtypeStruct((arrays, height, width + LANES), jnp.float32),
        compiler_params=pltpu.CompilerParams(vmem_limit_bytes=VMEM_LIMIT),
        cost_estimate=pl.CostEstimate(flops=10**6, bytes_accessed=10**6, transcendentals=0),
        name="static_halo",
    )(tall, before, after)


def river_kernel(state, strips, fixed, out):
    height, width = state.shape

    def strip(down, right):
        device, there = neighbour(down, right)
        return strips[pl.ds(device * ITERS, ITERS), :] * there

    storage = extended(state[...], strip)
    rate = fixed[0]
    code = fixed[1]
    rows, cols = storage.shape
    for _ in range(ITERS):
        outflow = rate * storage
        inflow = jnp.zeros_like(storage)
        for col_step in (-1, 0, 1):
            column = jnp.zeros_like(storage)
            for bit, (row_step, step) in enumerate(directions):
                if step != col_step:
                    continue
                leaving = jnp.where(code == float(1 << bit), outflow, 0.0)
                if row_step:
                    leaving = pltpu.roll(leaving, row_step % rows, 0)
                column = column + leaving
            if col_step:
                column = pltpu.roll(column, col_step % cols, 1)
            inflow = inflow + column
        storage = storage - outflow + inflow
    out[...] = storage[:height, :width]


def river(state, strips, fixed):
    return pl.pallas_call(
        river_kernel,
        out_shape=jax.ShapeDtypeStruct(state.shape, jnp.float32),
        compiler_params=pltpu.CompilerParams(vmem_limit_bytes=VMEM_LIMIT),
        cost_estimate=pl.CostEstimate(flops=10**7, bytes_accessed=1 * MIB, transcendentals=0),
        name="river_steps",
    )(state, strips, fixed)


def exchange(value):
    return lax.all_to_all(value, axes, split_axis=0, concat_axis=0, tiled=True)


def shards(
    forcing,
    river_storage,
    river_rate,
    flow_code,
    home_slot,
    home_offset,
    worker_list,
    patch_cell,
    patch_area,
    canopy_water,
    canopy_cap,
    soil_water,
    porosity,
    drainage,
):
    homes = lax.axis_size("region") * lax.axis_size("col")
    capacity = home_slot.shape[1] // homes
    grid_rows, grid_cols = river_storage.shape
    lane_rows = grid_rows * grid_cols // LANES
    outgoing = pack(
        homes, capacity, home_slot, home_offset, forcing.reshape(3, lane_rows, LANES)
    )
    arrived = exchange(outgoing)
    home = worker_list // capacity
    position = worker_list - home * capacity
    pairs = capacity // 2
    first_rows = home * (3 * pairs) + position // 2 + position % 2 * pairs
    meta = segment_plan(patch_cell, worker_list[:, None])
    fixed = jnp.stack([river_rate, flow_code.astype(jnp.float32)])
    above, below = halo_parts(fixed, "region", 1, ITERS)
    soil_new, canopy_new, sums = land_step(
        (homes * capacity, LANES), pairs, worker_list, first_rows, arrived, patch_cell, meta,
        patch_area, canopy_water, canopy_cap, soil_water, porosity, drainage, (above, below),
    )
    returned = exchange(sums)
    code, place = unpack_plan(homes, capacity, lane_rows, home_slot, home_offset)
    fixed = jnp.concatenate([fixed, below, above], axis=1)
    initial, last = edge_columns(fixed, sums)
    count = lax.axis_size("col")
    before = lax.ppermute(last, "col", [(i, i + 1) for i in range(count - 1)])
    after = lax.ppermute(initial, "col", [(i + 1, i) for i in range(count - 1)])
    fixed = static_halo(fixed, before, after)
    cell_runoff, storage, strips = unpack_runoff(
        homes, returned, code, place, river_storage.reshape(lane_rows, LANES), fixed
    )
    cell_evap = unpack_evap(returned, code, place)
    river_new = river(storage.reshape(river_storage.shape), exchange(strips), fixed)
    return (
        soil_new,
        canopy_new,
        cell_runoff.reshape(river_storage.shape),
        cell_evap.reshape(river_storage.shape),
        river_new,
    )


def solution(mesh):
    placed = (
        P(None, "region", "col"),
        P("region", "col"),
        P("region", "col"),
        P("region", "col"),
        P(("region", "col"), None),
        P(("region", "col"), None),
        P(("region", "col")),
        P(("region", "col"), None),
        P(("region", "col"), None),
        P(("region", "col"), None),
        P(("region", "col"), None),
        P(None, ("region", "col"), None),
        P(None, ("region", "col"), None),
        P(None, ("region", "col"), None),
    )
    return jax.shard_map(
        shards,
        mesh=mesh,
        in_specs=placed,
        out_specs=(
            P(None, ("region", "col"), None),
            P(("region", "col"), None),
            P("region", "col"),
            P("region", "col"),
            P("region", "col"),
        ),
        check_vma=False,
    )
```

```python
import functools

import jax
import jax.numpy as jnp
from jax import lax
from jax.experimental import pallas as pl
from jax.experimental.pallas import tpu as pltpu
from jax.sharding import PartitionSpec as P

ITERS = 4
WINDOW = 64
LANES = 128
MIB = 1024 * 1024
VMEM_LIMIT = 24 * MIB

directions = ((0, 1), (1, 1), (1, 0), (1, -1), (0, -1), (-1, -1), (-1, 0), (-1, 1))
axes = ("region", "col")


def iota(shape, dim):
    return lax.broadcasted_iota(jnp.int32, shape, dim)


def onehot(mask):
    return jnp.where(mask, jnp.float32(1.0), jnp.float32(0.0)).astype(jnp.bfloat16)


def lane_pick(values, index):
    return jnp.take_along_axis(values, index, axis=1, mode="promise_in_bounds")


def in_hbm(value):
    return pltpu.with_memory_space_constraint(value, pltpu.HBM)


def thirds(value):
    high = value.astype(jnp.bfloat16)
    rest = value - high.astype(jnp.float32)
    middle = rest.astype(jnp.bfloat16)
    low = (rest - middle.astype(jnp.float32)).astype(jnp.bfloat16)
    return high, middle, low


def halves(value):
    high = value.astype(jnp.bfloat16)
    return high, (value - high.astype(jnp.float32)).astype(jnp.bfloat16)


def matmul(a, b, a_dim=1, b_dim=0):
    return lax.dot_general(
        a, b, (((a_dim,), (b_dim,)), ((), ())), preferred_element_type=jnp.float32
    )


def slot_factors(slot, offset, homes, capacity):
    slots = slot.shape[1]
    worker = slot // capacity if capacity & (capacity - 1) else slot >> (capacity.bit_length() - 1)
    position = slot - worker * capacity
    by_worker = onehot(iota((homes, slots), 0) == worker)
    at_position = iota((capacity, slots), 0) == position
    row = jnp.where(at_position, ((offset >> 7) + 1).astype(jnp.float32), 0.0)
    lane = jnp.where(at_position, (offset & 127).astype(jnp.float32), 0.0)
    return by_worker, row.astype(jnp.bfloat16), lane.astype(jnp.bfloat16)


def slot_columns(slot, offset, homes, capacity, split=False):
    slots = slot.shape[1]
    by_worker, row, lane = slot_factors(slot, offset, homes, capacity)
    table = matmul(by_worker, jnp.concatenate([row, lane], axis=0), 1, 1)
    groups = 2 if split else 1
    spread = jnp.broadcast_to(
        table[:, None, :], (homes, capacity // groups, 2 * capacity)
    ).reshape(slots // groups, 2 * capacity)
    spread = jnp.concatenate([spread] * groups, axis=0)
    number = iota(spread.shape, 0)
    position = number % (capacity // groups) * groups + number // (slots // groups)
    place = position == iota(spread.shape, 1) % capacity
    kept = jnp.where(place, spread, 0.0).astype(jnp.bfloat16)
    shape = (2 * capacity, 2 * LANES)
    gather = onehot((iota(shape, 0) >= capacity) == (iota(shape, 1) >= LANES))
    columns = matmul(kept, gather).astype(jnp.int32)
    return columns[:, :LANES] - 1, columns[:, LANES:]


def slot_rows(slot, offset, homes, capacity):
    slots = slot.shape[1]
    by_worker, row, lane = slot_factors(slot, offset, homes, capacity)
    table = matmul(jnp.concatenate([row, lane], axis=0), by_worker, 1, 1).astype(jnp.bfloat16)
    number = iota((1, slots), 1)
    worker = number // capacity
    position = number - worker * capacity
    spread = matmul(table, onehot(iota((homes, slots), 0) == worker))
    at_position = iota((capacity, slots), 0) == position
    rows = jnp.sum(jnp.where(at_position, spread[:capacity], 0.0), axis=0, keepdims=True)
    lanes = jnp.sum(jnp.where(at_position, spread[capacity:], 0.0), axis=0, keepdims=True)
    return rows.astype(jnp.int32) - 1, lanes.astype(jnp.int32)


def pack_kernel(
    homes, capacity, slot_in, offset_in, forcing_in, out, slot, offset, forcing, row_of, lane_of,
    rain, ready,
):
    copies = [
        pltpu.make_async_copy(source, target, ready.at[i])
        for i, (source, target) in enumerate(
            ((slot_in, slot), (offset_in, offset), (forcing_in, forcing))
        )
    ]
    for copy in copies:
        copy.start()
    slots = slot.shape[1]
    pairs = capacity // 2
    lane_rows = forcing.shape[1]
    copies[0].wait()
    copies[1].wait()
    row_of[...], lane_of[...] = slot_columns(slot[...], offset[...], homes, capacity, True)
    copies[2].wait()
    parts = []
    for var in range(3):
        here = forcing[var]
        following = jnp.concatenate([here[1:], here[:1]], axis=0)
        parts += [here, following]
    table = jnp.concatenate(thirds(jnp.concatenate(parts, axis=1)), axis=0)
    chunk = 128
    here = iota((chunk, LANES), 1)
    for start in range(0, slots, chunk):
        odd = start >= slots // 2
        row = row_of[pl.ds(start, chunk), :]
        lane = lane_of[pl.ds(start, chunk), :]
        shape = (chunk, 3 * lane_rows)
        wide = jnp.concatenate([row, row], axis=1)[:, : 3 * lane_rows]
        pick = onehot(wide == iota(shape, 1) % lane_rows)
        rows = matmul(pick, table)
        after = here >= lane
        joined = [
            jnp.where(
                after,
                rows[:, 2 * var * LANES : (2 * var + 1) * LANES],
                rows[:, (2 * var + 1) * LANES : (2 * var + 2) * LANES],
            )
            for var in range(3)
        ]
        first = (here + lane) & 127
        second = (first + WINDOW) & 127
        losses = jnp.where(
            here < WINDOW, lane_pick(joined[1], first), lane_pick(joined[2], second)
        )
        base = start - slots // 2 if odd else start
        if odd:
            rains = jnp.where(
                here < WINDOW, rain[pl.ds(base, chunk), :], lane_pick(joined[0], second)
            )
        else:
            rain[pl.ds(base, chunk), :] = lane_pick(joined[0], first)
        for part in range(0, chunk, pairs):
            place = (base + part) * 3
            if odd:
                out[pl.ds(place + pairs, pairs), :] = rains[part : part + pairs]
                out[pl.ds(place + 2 * pairs, pairs), :] = losses[part : part + pairs]
            else:
                out[pl.ds(place, pairs), :] = losses[part : part + pairs]


def pack(homes, capacity, slot, offset, forcing):
    slots = slot.shape[1]
    return pl.pallas_call(
        functools.partial(pack_kernel, homes, capacity),
        in_specs=[pl.BlockSpec(memory_space=pltpu.HBM)] * 3,
        out_shape=jax.ShapeDtypeStruct((slots + slots // 2, LANES), jnp.float32),
        scratch_shapes=[
            pltpu.VMEM(slot.shape, jnp.int32),
            pltpu.VMEM(offset.shape, jnp.int32),
            pltpu.VMEM(forcing.shape, jnp.float32),
            pltpu.VMEM((slots, LANES), jnp.int32),
            pltpu.VMEM((slots, LANES), jnp.int32),
            pltpu.VMEM((slots // 2, LANES), jnp.float32),
            pltpu.SemaphoreType.DMA((3,)),
        ],
        compiler_params=pltpu.CompilerParams(vmem_limit_bytes=VMEM_LIMIT),
        cost_estimate=pl.CostEstimate(flops=10**9, bytes_accessed=2 * MIB, transcendentals=0),
        name="pack_forcing",
    )(in_hbm(slot), in_hbm(offset), in_hbm(forcing))


def unpack_plan_kernel(homes, capacity, lane_rows, slot, offset, code, place):
    slots = slot.shape[1]
    row, lane = slot_columns(slot[...], offset[...], homes, capacity)
    here = iota((slots, LANES), 1)
    index = (here - lane) & 127
    inside = (index < WINDOW) & (row >= 0)
    code[...] = jnp.where(inside, index + jnp.where(here >= lane, 0, LANES), -1)
    row_lane, _ = slot_rows(slot[...], offset[...], homes, capacity)
    place[...] = onehot(iota((lane_rows, slots), 0) == row_lane)


def unpack_plan(homes, capacity, lane_rows, slot, offset):
    slots = slot.shape[1]
    return pl.pallas_call(
        functools.partial(unpack_plan_kernel, homes, capacity, lane_rows),
        out_shape=(
            jax.ShapeDtypeStruct((slots, LANES), jnp.int32),
            jax.ShapeDtypeStruct((lane_rows, slots), jnp.bfloat16),
        ),
        compiler_params=pltpu.CompilerParams(vmem_limit_bytes=VMEM_LIMIT),
        cost_estimate=pl.CostEstimate(flops=10**9, bytes_accessed=2 * MIB, transcendentals=0),
        name="unpack_plan",
    )(slot, offset)


def strips_for_neighbours(state, rows):
    device = iota((rows, LANES), 0) // ITERS
    down = device // lax.axis_size("col") - lax.axis_index("region")
    right = device % lax.axis_size("col") - lax.axis_index("col")
    height, width = state.shape
    columns = jnp.transpose(state)
    empty = jnp.zeros((ITERS, LANES - height), jnp.float32)

    def repeated(strip):
        if strip.shape[1] < LANES:
            strip = jnp.concatenate([strip, empty], axis=1)
        return jnp.concatenate([strip] * (rows // ITERS), axis=0)

    near = (jnp.abs(down) <= 1).astype(jnp.int32)
    strips = jnp.zeros((rows, LANES), jnp.float32)
    strips = jnp.where((right == 0) & (down == 1), repeated(state[height - ITERS :]), strips)
    strips = jnp.where((right == 0) & (down == -1), repeated(state[:ITERS]), strips)
    strips = jnp.where((right == 1) & (near == 1), repeated(columns[width - ITERS :]), strips)
    return jnp.where((right == -1) & (near == 1), repeated(columns[:ITERS]), strips)


def cell_totals(arrived, code, place, first):
    lane_rows = place.shape[0]
    marks = code[...]
    window = lane_pick(arrived[...], (marks + first) & 127)
    placed = jnp.concatenate(
        [
            jnp.where((marks >= 0) & (marks < LANES), window, 0.0),
            jnp.where(marks >= LANES, window, 0.0),
        ],
        axis=1,
    )
    totals = matmul(place[...], jnp.concatenate(halves(placed), axis=1))
    totals = totals[:, :256] + totals[:, 256:]
    over = totals[:, LANES:]
    over = jnp.concatenate([over[lane_rows - 1 :], over[: lane_rows - 1]], axis=0)
    over = jnp.where(iota(over.shape, 0) == 0, 0.0, over)
    return totals[:, :LANES] + over


def unpack_runoff_kernel(arrived, code, place, river, _, runoff, storage, strips):
    total = cell_totals(arrived, code, place, 0)
    state = river[...] + total
    runoff[...] = total
    storage[...] = state
    strips[...] = strips_for_neighbours(state, strips.shape[0])


def unpack_runoff(homes, arrived, code, place, river, after):
    shape = jax.ShapeDtypeStruct((place.shape[0], LANES), jnp.float32)
    strips = jax.ShapeDtypeStruct((homes * ITERS, LANES), jnp.float32)
    return pl.pallas_call(
        unpack_runoff_kernel,
        in_specs=[pl.BlockSpec(memory_space=pltpu.VMEM)] * 4 + [pl.BlockSpec(memory_space=pl.ANY)],
        out_shape=(shape, shape, strips),
        compiler_params=pltpu.CompilerParams(vmem_limit_bytes=VMEM_LIMIT),
        cost_estimate=pl.CostEstimate(flops=10**9, bytes_accessed=1 * MIB, transcendentals=0),
        name="unpack_runoff",
    )(arrived, code, place, river, after)


def unpack_evap_kernel(arrived, code, place, evap):
    evap[...] = cell_totals(arrived, code, place, WINDOW)


def unpack_evap(arrived, code, place):
    return pl.pallas_call(
        unpack_evap_kernel,
        out_shape=jax.ShapeDtypeStruct((place.shape[0], LANES), jnp.float32),
        compiler_params=pltpu.CompilerParams(vmem_limit_bytes=VMEM_LIMIT),
        cost_estimate=pl.CostEstimate(flops=10**9, bytes_accessed=1 * MIB, transcendentals=0),
        name="unpack_evap",
    )(arrived, code, place)


def segment_plan_kernel(cell, worker, meta):
    chunk = 96
    for start in range(0, cell.shape[0], chunk):
        values = cell[pl.ds(start, chunk), :]
        target = iota(values.shape, 1) & (WINDOW - 1)
        count = jnp.zeros_like(values)
        for step in (64, 32, 16, 8, 4, 2, 1):
            probe = lane_pick(values, count + (step - 1))
            count = jnp.where(probe <= target, count + step, count)
        count = jnp.where(lane_pick(values, count) <= target, count + 1, count)
        odd = worker[pl.ds(start, chunk), :] & 1
        meta[pl.ds(start, chunk), :] = count + (odd << 8)


def segment_plan(cell, worker):
    return pl.pallas_call(
        segment_plan_kernel,
        out_shape=jax.ShapeDtypeStruct(cell.shape, jnp.int32),
        compiler_params=pltpu.CompilerParams(vmem_limit_bytes=VMEM_LIMIT),
        cost_estimate=pl.CostEstimate(flops=10**8, bytes_accessed=1 * MIB, transcendentals=0),
        name="segment_plan",
    )(cell, worker)


def land_kernel(
    pairs, slots, first_rows, arrived, cell, meta, area, water, cap, soil_in, porosity_in,
    drainage_in, _, __, soil_out, canopy_new, sums_out, soil, porosity, drainage, soil_new,
    fetched, runoffs, evaps, sums, ready, written,
):
    layers, rows = soil.shape[:2]
    steps = written.shape[0]
    block = rows // steps
    chunk = block // 2
    ahead = 2
    arrays = ((soil_in, soil), (porosity_in, porosity), (drainage_in, drainage))

    def part_of(step):
        return pl.ds(pl.multiple_of(step * block, block), block)

    def reads(step):
        return [
            pltpu.make_async_copy(
                source.at[:, part_of(step), :], target.at[:, part_of(step), :], ready.at[step, i]
            )
            for i, (source, target) in enumerate(arrays)
        ]

    def start_reads(step):
        for copy in reads(step):
            copy.start()

    def write(step):
        return pltpu.make_async_copy(
            soil_new.at[:, part_of(step), :], soil_out.at[:, part_of(step), :], written.at[step]
        )

    def fetch(step):
        for i in range(block):
            row = step * block + i
            fetched[pl.ds(2 * i, 2), :] = arrived[pl.ds(first_rows[row], 2, stride=pairs), :]

    def cascade(step, inner):
        part = pl.ds(pl.multiple_of(step * block + inner, chunk), chunk)
        index = cell[part, :]
        one = fetched[pl.ds(2 * inner, chunk, stride=2), :]
        two = fetched[pl.ds(2 * inner + 1, chunk, stride=2), :]
        odd = meta[part, :] >> 8
        loss = jnp.where(odd == 1, two, one)
        rain = lane_pick(jnp.where(odd == 1, one, two), index + odd * WINDOW)
        demand = lane_pick(loss, index)
        limit = lane_pick(loss, index + WINDOW)
        wetted = water[part, :] + rain
        flowing = jnp.maximum(wetted - cap[part, :], 0.0)
        retained = jnp.minimum(wetted, cap[part, :])
        canopy_loss = jnp.minimum(demand, retained)
        canopy_new[part, :] = retained - canopy_loss
        surface = jnp.zeros_like(flowing)
        for layer in range(layers):
            filled = soil[layer, part, :] + flowing
            excess = jnp.maximum(filled - porosity[layer, part, :], 0.0)
            surface = surface + excess
            filled = filled - excess
            flowing = drainage[layer, part, :] * filled
            middle = filled - flowing
            if layer == 0:
                soil_loss = jnp.minimum(jnp.minimum(limit, demand - canopy_loss), 0.5 * middle)
                middle = middle - soil_loss
                evaps[part, :] = area[part, :] * (canopy_loss + soil_loss)
            soil_new[layer, part, :] = middle
        runoffs[part, :] = area[part, :] * (surface + flowing)

    def hand_back(step):
        part = part_of(step)
        shape = (2 * LANES, LANES)
        upto = onehot((iota(shape, 0) & 127) <= iota(shape, 1))
        count = meta[part, :] & 255
        last = jnp.maximum(count - 1, 0)
        here = iota((block, LANES), 1)
        picked = [
            lane_pick(matmul(jnp.concatenate(halves(value[part, :]), axis=1), upto), last)
            for value in (runoffs, evaps)
        ]
        reached = jnp.where(count > 0, jnp.where(here < WINDOW, *picked), 0.0)
        before = jnp.where((here & (WINDOW - 1)) == 0, 0.0, pltpu.roll(reached, 1, 1))
        sums[...] = reached - before
        for i in range(block):
            sums_out[pl.ds(slots[step * block + i], 1), :] = sums[pl.ds(i, 1), :]

    for step in range(ahead):
        start_reads(step)
    sums_out[...] = jnp.zeros_like(sums_out)
    runoffs[pl.ds(0, block), :] = jnp.zeros((block, LANES), jnp.float32)
    evaps[pl.ds(0, block), :] = jnp.zeros((block, LANES), jnp.float32)

    def round_of(step, carry):
        fetch(step)
        for copy in reads(step):
            copy.wait()

        @pl.when(step + ahead < steps)
        def _():
            start_reads(step + ahead)

        hand_back(jnp.maximum(step - 1, 0))
        for inner in range(0, block, chunk):
            cascade(step, inner)
        write(step).start()
        return carry

    lax.fori_loop(0, steps, round_of, 0)
    hand_back(steps - 1)
    for step in range(steps):
        write(step).wait()


def land_step(
    sums_shape, pairs, slots, first_rows, arrived, cell, meta, area, water, cap, soil, porosity,
    drainage, after,
):
    layers, rows = soil.shape[:2]
    steps = 5
    block = rows // steps
    near = pl.BlockSpec(memory_space=pltpu.VMEM)
    far = pl.BlockSpec(memory_space=pltpu.HBM)
    return pl.pallas_call(
        functools.partial(land_kernel, pairs),
        in_specs=[pl.BlockSpec(memory_space=pltpu.SMEM)] * 2 + [near] * 6 + [far] * 3
        + [pl.BlockSpec(memory_space=pl.ANY)] * 2,
        out_specs=[far, near, near],
        scratch_shapes=[pltpu.VMEM(soil.shape, jnp.float32)] * 4
        + [pltpu.VMEM((2 * block, LANES), jnp.float32)]
        + [pltpu.VMEM((rows, LANES), jnp.float32)] * 2
        + [pltpu.VMEM((block, LANES), jnp.float32)]
        + [pltpu.SemaphoreType.DMA((steps, 3)), pltpu.SemaphoreType.DMA((steps,))],
        out_shape=(
            jax.ShapeDtypeStruct(soil.shape, jnp.float32),
            jax.ShapeDtypeStruct((rows, LANES), jnp.float32),
            jax.ShapeDtypeStruct(sums_shape, jnp.float32),
        ),
        compiler_params=pltpu.CompilerParams(vmem_limit_bytes=VMEM_LIMIT),
        cost_estimate=pl.CostEstimate(flops=10**8, bytes_accessed=20 * MIB, transcendentals=0),
        name="land_layers",
    )(
        slots, first_rows, arrived, cell, meta, area, water, cap,
        in_hbm(soil), in_hbm(porosity), in_hbm(drainage), *after,
    )


def halo_parts(value, axis, dim, width):
    count, length = (lax.axis_size(axis), value.shape[dim])
    up = [(i, i + 1) for i in range(count - 1)]
    down = [(j, i) for i, j in up]
    last = lax.slice_in_dim(value, length - width, length, axis=dim)
    initial = lax.slice_in_dim(value, 0, width, axis=dim)
    return lax.ppermute(last, axis, up), lax.ppermute(initial, axis, down)


def edge_columns_kernel(tall, _, first, last):
    arrays, height, width = tall.shape
    for number in range(arrays):
        values = tall[number]
        values = jnp.concatenate([values, jnp.zeros((LANES - height, width), jnp.float32)], axis=0)
        columns = jnp.transpose(values)
        part = pl.ds(number * ITERS, ITERS)
        first[part, :] = columns[:ITERS]
        last[part, :] = columns[width - ITERS :]


def edge_columns(tall, after):
    shape = jax.ShapeDtypeStruct((2 * ITERS, LANES), jnp.float32)
    return pl.pallas_call(
        edge_columns_kernel,
        in_specs=[pl.BlockSpec(memory_space=pltpu.VMEM), pl.BlockSpec(memory_space=pl.ANY)],
        out_shape=(shape, shape),
        compiler_params=pltpu.CompilerParams(vmem_limit_bytes=VMEM_LIMIT),
        cost_estimate=pl.CostEstimate(flops=10**6, bytes_accessed=10**5, transcendentals=0),
        name="edge_columns",
    )(tall, after)


def extended(own, strip):
    height = own.shape[0]

    def column_strip(right):
        middle, above, below = strip(0, right), strip(-1, right), strip(1, right)
        return jnp.concatenate(
            [
                middle[:, :height],
                below[:, :ITERS],
                above[:, height - ITERS : height],
                jnp.zeros((ITERS, LANES - height - 2 * ITERS), jnp.float32),
            ],
            axis=1,
        )

    gap = jnp.zeros((LANES - 2 * ITERS, LANES), jnp.float32)
    sides = jnp.concatenate([column_strip(1), gap, column_strip(-1)], axis=0)
    sides = jnp.transpose(sides)[: height + 2 * ITERS]
    tall = jnp.concatenate([own, strip(1, 0), strip(-1, 0)], axis=0)
    return jnp.concatenate([tall, sides], axis=1)


def neighbour(down, right):
    row, column = lax.axis_index("region") + down, lax.axis_index("col") + right
    there = (row >= 0) & (row < lax.axis_size("region"))
    there &= (column >= 0) & (column < lax.axis_size("col"))
    return jnp.where(there, row * lax.axis_size("col") + column, 0), jnp.where(there, 1.0, 0.0)


def static_halo_kernel(tall, before, after, out):
    height, width = tall.shape[1:]
    gap = jnp.zeros((LANES - 2 * ITERS, LANES), jnp.float32)
    for number in range(2):
        part = pl.ds(number * ITERS, ITERS)
        sides = jnp.transpose(jnp.concatenate([after[part, :], gap, before[part, :]], axis=0))
        out[number, :, :width] = tall[number]
        out[number, :, width:] = sides[:height]


def static_halo(tall, before, after):
    arrays, height, width = tall.shape
    return pl.pallas_call(
        static_halo_kernel,
        out_shape=jax.ShapeDtypeStruct((arrays, height, width + LANES), jnp.float32),
        compiler_params=pltpu.CompilerParams(vmem_limit_bytes=VMEM_LIMIT),
        cost_estimate=pl.CostEstimate(flops=10**6, bytes_accessed=10**6, transcendentals=0),
        name="static_halo",
    )(tall, before, after)


def river_kernel(state, strips, fixed, out):
    height, width = state.shape

    def strip(down, right):
        device, there = neighbour(down, right)
        return strips[pl.ds(device * ITERS, ITERS), :] * there

    storage = extended(state[...], strip)
    rate = fixed[0]
    code = fixed[1]
    rows, cols = storage.shape
    for _ in range(ITERS):
        outflow = rate * storage
        inflow = jnp.zeros_like(storage)
        for col_step in (-1, 0, 1):
            column = jnp.zeros_like(storage)
            for bit, (row_step, step) in enumerate(directions):
                if step != col_step:
                    continue
                leaving = jnp.where(code == float(1 << bit), outflow, 0.0)
                if row_step:
                    leaving = pltpu.roll(leaving, row_step % rows, 0)
                column = column + leaving
            if col_step:
                column = pltpu.roll(column, col_step % cols, 1)
            inflow = inflow + column
        storage = storage - outflow + inflow
    out[...] = storage[:height, :width]


def river(state, strips, fixed):
    return pl.pallas_call(
        river_kernel,
        out_shape=jax.ShapeDtypeStruct(state.shape, jnp.float32),
        compiler_params=pltpu.CompilerParams(vmem_limit_bytes=VMEM_LIMIT),
        cost_estimate=pl.CostEstimate(flops=10**7, bytes_accessed=1 * MIB, transcendentals=0),
        name="river_steps",
    )(state, strips, fixed)


def exchange(value):
    return lax.all_to_all(value, axes, split_axis=0, concat_axis=0, tiled=True)


def shards(
    forcing,
    river_storage,
    river_rate,
    flow_code,
    home_slot,
    home_offset,
    worker_list,
    patch_cell,
    patch_area,
    canopy_water,
    canopy_cap,
    soil_water,
    porosity,
    drainage,
):
    homes = lax.axis_size("region") * lax.axis_size("col")
    capacity = home_slot.shape[1] // homes
    grid_rows, grid_cols = river_storage.shape
    lane_rows = grid_rows * grid_cols // LANES
    outgoing = pack(
        homes, capacity, home_slot, home_offset, forcing.reshape(3, lane_rows, LANES)
    )
    arrived = exchange(outgoing)
    home = worker_list // capacity
    position = worker_list - home * capacity
    pairs = capacity // 2
    first_rows = home * (3 * pairs) + position // 2 + position % 2 * pairs
    meta = segment_plan(patch_cell, worker_list[:, None])
    fixed = jnp.stack([river_rate, flow_code.astype(jnp.float32)])
    above, below = halo_parts(fixed, "region", 1, ITERS)
    soil_new, canopy_new, sums = land_step(
        (homes * capacity, LANES), pairs, worker_list, first_rows, arrived, patch_cell, meta,
        patch_area, canopy_water, canopy_cap, soil_water, porosity, drainage, (above, below),
    )
    returned = exchange(sums)
    code, place = unpack_plan(homes, capacity, lane_rows, home_slot, home_offset)
    fixed = jnp.concatenate([fixed, below, above], axis=1)
    initial, last = edge_columns(fixed, sums)
    count = lax.axis_size("col")
    before = lax.ppermute(last, "col", [(i, i + 1) for i in range(count - 1)])
    after = lax.ppermute(initial, "col", [(i + 1, i) for i in range(count - 1)])
    fixed = static_halo(fixed, before, after)
    cell_runoff, storage, strips = unpack_runoff(
        homes, returned, code, place, river_storage.reshape(lane_rows, LANES), fixed
    )
    cell_evap = unpack_evap(returned, code, place)
    river_new = river(storage.reshape(river_storage.shape), exchange(strips), fixed)
    return (
        soil_new,
        canopy_new,
        cell_runoff.reshape(river_storage.shape),
        cell_evap.reshape(river_storage.shape),
        river_new,
    )


def solution(mesh):
    placed = (
        P(None, "region", "col"),
        P("region", "col"),
        P("region", "col"),
        P("region", "col"),
        P(("region", "col"), None),
        P(("region", "col"), None),
        P(("region", "col")),
        P(("region", "col"), None),
        P(("region", "col"), None),
        P(("region", "col"), None),
        P(("region", "col"), None),
        P(None, ("region", "col"), None),
        P(None, ("region", "col"), None),
        P(None, ("region", "col"), None),
    )
    return jax.shard_map(
        shards,
        mesh=mesh,
        in_specs=placed,
        out_specs=(
            P(None, ("region", "col"), None),
            P(("region", "col"), None),
            P("region", "col"),
            P("region", "col"),
            P("region", "col"),
        ),
        check_vma=False,
    )
```

```python
import functools

import jax
import jax.numpy as jnp
from jax import lax
from jax.experimental import pallas as pl
from jax.experimental.pallas import tpu as pltpu
from jax.sharding import PartitionSpec as P

ITERS = 4
WINDOW = 64
LANES = 128
MIB = 1024 * 1024
VMEM_LIMIT = 24 * MIB

directions = ((0, 1), (1, 1), (1, 0), (1, -1), (0, -1), (-1, -1), (-1, 0), (-1, 1))
axes = ("region", "col")


def iota(shape, dim):
    return lax.broadcasted_iota(jnp.int32, shape, dim)


def onehot(mask):
    return jnp.where(mask, jnp.float32(1.0), jnp.float32(0.0)).astype(jnp.bfloat16)


def lane_pick(values, index):
    return jnp.take_along_axis(values, index, axis=1, mode="promise_in_bounds")


def in_hbm(value):
    return pltpu.with_memory_space_constraint(value, pltpu.HBM)


def thirds(value):
    high = value.astype(jnp.bfloat16)
    rest = value - high.astype(jnp.float32)
    middle = rest.astype(jnp.bfloat16)
    low = (rest - middle.astype(jnp.float32)).astype(jnp.bfloat16)
    return high, middle, low


def halves(value):
    high = value.astype(jnp.bfloat16)
    return high, (value - high.astype(jnp.float32)).astype(jnp.bfloat16)


def matmul(a, b, a_dim=1, b_dim=0):
    return lax.dot_general(
        a, b, (((a_dim,), (b_dim,)), ((), ())), preferred_element_type=jnp.float32
    )


def slot_factors(slot, offset, homes, capacity):
    slots = slot.shape[1]
    worker = slot // capacity if capacity & (capacity - 1) else slot >> (capacity.bit_length() - 1)
    position = slot - worker * capacity
    by_worker = onehot(iota((homes, slots), 0) == worker)
    at_position = iota((capacity, slots), 0) == position
    row = jnp.where(at_position, ((offset >> 7) + 1).astype(jnp.float32), 0.0)
    lane = jnp.where(at_position, (offset & 127).astype(jnp.float32), 0.0)
    return by_worker, row.astype(jnp.bfloat16), lane.astype(jnp.bfloat16)


def slot_columns(slot, offset, homes, capacity, split=False):
    slots = slot.shape[1]
    by_worker, row, lane = slot_factors(slot, offset, homes, capacity)
    table = matmul(by_worker, jnp.concatenate([row, lane], axis=0), 1, 1)
    groups = 2 if split else 1
    spread = jnp.broadcast_to(
        table[:, None, :], (homes, capacity // groups, 2 * capacity)
    ).reshape(slots // groups, 2 * capacity)
    spread = jnp.concatenate([spread] * groups, axis=0)
    number = iota(spread.shape, 0)
    position = number % (capacity // groups) * groups + number // (slots // groups)
    place = position == iota(spread.shape, 1) % capacity
    kept = jnp.where(place, spread, 0.0).astype(jnp.bfloat16)
    shape = (2 * capacity, 2 * LANES)
    gather = onehot((iota(shape, 0) >= capacity) == (iota(shape, 1) >= LANES))
    columns = matmul(kept, gather).astype(jnp.int32)
    return columns[:, :LANES] - 1, columns[:, LANES:]


def slot_rows(slot, offset, homes, capacity):
    slots = slot.shape[1]
    by_worker, row, lane = slot_factors(slot, offset, homes, capacity)
    table = matmul(jnp.concatenate([row, lane], axis=0), by_worker, 1, 1).astype(jnp.bfloat16)
    number = iota((1, slots), 1)
    worker = number // capacity
    position = number - worker * capacity
    spread = matmul(table, onehot(iota((homes, slots), 0) == worker))
    at_position = iota((capacity, slots), 0) == position
    rows = jnp.sum(jnp.where(at_position, spread[:capacity], 0.0), axis=0, keepdims=True)
    lanes = jnp.sum(jnp.where(at_position, spread[capacity:], 0.0), axis=0, keepdims=True)
    return rows.astype(jnp.int32) - 1, lanes.astype(jnp.int32)


def pack_kernel(
    homes, capacity, slot_in, offset_in, forcing_in, out, slot, offset, forcing, row_of, lane_of,
    rain, ready,
):
    copies = [
        pltpu.make_async_copy(source, target, ready.at[i])
        for i, (source, target) in enumerate(
            ((slot_in, slot), (offset_in, offset), (forcing_in, forcing))
        )
    ]
    for copy in copies:
        copy.start()
    slots = slot.shape[1]
    pairs = capacity // 2
    lane_rows = forcing.shape[1]
    copies[0].wait()
    copies[1].wait()
    row_of[...], lane_of[...] = slot_columns(slot[...], offset[...], homes, capacity, True)
    copies[2].wait()
    parts = []
    for var in range(3):
        here = forcing[var]
        following = jnp.concatenate([here[1:], here[:1]], axis=0)
        parts += [here, following]
    table = jnp.concatenate(thirds(jnp.concatenate(parts, axis=1)), axis=0)
    chunk = 128
    here = iota((chunk, LANES), 1)
    for start in range(0, slots, chunk):
        odd = start >= slots // 2
        row = row_of[pl.ds(start, chunk), :]
        lane = lane_of[pl.ds(start, chunk), :]
        shape = (chunk, 3 * lane_rows)
        wide = jnp.concatenate([row, row], axis=1)[:, : 3 * lane_rows]
        pick = onehot(wide == iota(shape, 1) % lane_rows)
        rows = matmul(pick, table)
        after = here >= lane
        joined = [
            jnp.where(
                after,
                rows[:, 2 * var * LANES : (2 * var + 1) * LANES],
                rows[:, (2 * var + 1) * LANES : (2 * var + 2) * LANES],
            )
            for var in range(3)
        ]
        first = (here + lane) & 127
        second = (first + WINDOW) & 127
        losses = jnp.where(
            here < WINDOW, lane_pick(joined[1], first), lane_pick(joined[2], second)
        )
        base = start - slots // 2 if odd else start
        if odd:
            rains = jnp.where(
                here < WINDOW, rain[pl.ds(base, chunk), :], lane_pick(joined[0], second)
            )
        else:
            rain[pl.ds(base, chunk), :] = lane_pick(joined[0], first)
        for part in range(0, chunk, pairs):
            place = (base + part) * 3
            if odd:
                out[pl.ds(place + pairs, pairs), :] = rains[part : part + pairs]
                out[pl.ds(place + 2 * pairs, pairs), :] = losses[part : part + pairs]
            else:
                out[pl.ds(place, pairs), :] = losses[part : part + pairs]


def pack(homes, capacity, slot, offset, forcing):
    slots = slot.shape[1]
    return pl.pallas_call(
        functools.partial(pack_kernel, homes, capacity),
        in_specs=[pl.BlockSpec(memory_space=pltpu.HBM)] * 3,
        out_shape=jax.ShapeDtypeStruct((slots + slots // 2, LANES), jnp.float32),
        scratch_shapes=[
            pltpu.VMEM(slot.shape, jnp.int32),
            pltpu.VMEM(offset.shape, jnp.int32),
            pltpu.VMEM(forcing.shape, jnp.float32),
            pltpu.VMEM((slots, LANES), jnp.int32),
            pltpu.VMEM((slots, LANES), jnp.int32),
            pltpu.VMEM((slots // 2, LANES), jnp.float32),
            pltpu.SemaphoreType.DMA((3,)),
        ],
        compiler_params=pltpu.CompilerParams(vmem_limit_bytes=VMEM_LIMIT),
        cost_estimate=pl.CostEstimate(flops=10**9, bytes_accessed=2 * MIB, transcendentals=0),
        name="pack_forcing",
    )(in_hbm(slot), in_hbm(offset), in_hbm(forcing))


def unpack_plan_kernel(homes, capacity, lane_rows, slot, offset, code, place):
    slots = slot.shape[1]
    row, lane = slot_columns(slot[...], offset[...], homes, capacity)
    here = iota((slots, LANES), 1)
    index = (here - lane) & 127
    inside = (index < WINDOW) & (row >= 0)
    code[...] = jnp.where(inside, index + jnp.where(here >= lane, 0, LANES), -1)
    row_lane, _ = slot_rows(slot[...], offset[...], homes, capacity)
    place[...] = onehot(iota((lane_rows, slots), 0) == row_lane)


def unpack_plan(homes, capacity, lane_rows, slot, offset):
    slots = slot.shape[1]
    return pl.pallas_call(
        functools.partial(unpack_plan_kernel, homes, capacity, lane_rows),
        out_shape=(
            jax.ShapeDtypeStruct((slots, LANES), jnp.int32),
            jax.ShapeDtypeStruct((lane_rows, slots), jnp.bfloat16),
        ),
        compiler_params=pltpu.CompilerParams(vmem_limit_bytes=VMEM_LIMIT),
        cost_estimate=pl.CostEstimate(flops=10**9, bytes_accessed=2 * MIB, transcendentals=0),
        name="unpack_plan",
    )(slot, offset)


def strips_for_neighbours(state, rows):
    device = iota((rows, LANES), 0) // ITERS
    down = device // lax.axis_size("col") - lax.axis_index("region")
    right = device % lax.axis_size("col") - lax.axis_index("col")
    height, width = state.shape
    columns = jnp.transpose(state)
    empty = jnp.zeros((ITERS, LANES - height), jnp.float32)

    def repeated(strip):
        if strip.shape[1] < LANES:
            strip = jnp.concatenate([strip, empty], axis=1)
        return jnp.concatenate([strip] * (rows // ITERS), axis=0)

    near = (jnp.abs(down) <= 1).astype(jnp.int32)
    strips = jnp.zeros((rows, LANES), jnp.float32)
    strips = jnp.where((right == 0) & (down == 1), repeated(state[height - ITERS :]), strips)
    strips = jnp.where((right == 0) & (down == -1), repeated(state[:ITERS]), strips)
    strips = jnp.where((right == 1) & (near == 1), repeated(columns[width - ITERS :]), strips)
    return jnp.where((right == -1) & (near == 1), repeated(columns[:ITERS]), strips)


def cell_totals(arrived, code, place, first):
    lane_rows = place.shape[0]
    marks = code[...]
    window = lane_pick(arrived[...], (marks + first) & 127)
    placed = jnp.concatenate(
        [
            jnp.where((marks >= 0) & (marks < LANES), window, 0.0),
            jnp.where(marks >= LANES, window, 0.0),
        ],
        axis=1,
    )
    totals = matmul(place[...], jnp.concatenate(halves(placed), axis=1))
    totals = totals[:, :256] + totals[:, 256:]
    over = totals[:, LANES:]
    over = jnp.concatenate([over[lane_rows - 1 :], over[: lane_rows - 1]], axis=0)
    over = jnp.where(iota(over.shape, 0) == 0, 0.0, over)
    return totals[:, :LANES] + over


def unpack_runoff_kernel(arrived, code, place, river, _, runoff, storage, strips):
    total = cell_totals(arrived, code, place, 0)
    state = river[...] + total
    runoff[...] = total
    storage[...] = state
    strips[...] = strips_for_neighbours(state, strips.shape[0])


def unpack_runoff(homes, arrived, code, place, river, after):
    shape = jax.ShapeDtypeStruct((place.shape[0], LANES), jnp.float32)
    strips = jax.ShapeDtypeStruct((homes * ITERS, LANES), jnp.float32)
    return pl.pallas_call(
        unpack_runoff_kernel,
        in_specs=[pl.BlockSpec(memory_space=pltpu.VMEM)] * 4 + [pl.BlockSpec(memory_space=pl.ANY)],
        out_shape=(shape, shape, strips),
        compiler_params=pltpu.CompilerParams(vmem_limit_bytes=VMEM_LIMIT),
        cost_estimate=pl.CostEstimate(flops=10**9, bytes_accessed=1 * MIB, transcendentals=0),
        name="unpack_runoff",
    )(arrived, code, place, river, after)


def unpack_evap_kernel(arrived, code, place, evap):
    evap[...] = cell_totals(arrived, code, place, WINDOW)


def unpack_evap(arrived, code, place):
    return pl.pallas_call(
        unpack_evap_kernel,
        out_shape=jax.ShapeDtypeStruct((place.shape[0], LANES), jnp.float32),
        compiler_params=pltpu.CompilerParams(vmem_limit_bytes=VMEM_LIMIT),
        cost_estimate=pl.CostEstimate(flops=10**9, bytes_accessed=1 * MIB, transcendentals=0),
        name="unpack_evap",
    )(arrived, code, place)


def segment_plan_kernel(cell, worker, meta):
    chunk = 96
    for start in range(0, cell.shape[0], chunk):
        values = cell[pl.ds(start, chunk), :]
        target = iota(values.shape, 1) & (WINDOW - 1)
        count = jnp.zeros_like(values)
        for step in (64, 32, 16, 8, 4, 2, 1):
            probe = lane_pick(values, count + (step - 1))
            count = jnp.where(probe <= target, count + step, count)
        count = jnp.where(lane_pick(values, count) <= target, count + 1, count)
        odd = worker[pl.ds(start, chunk), :] & 1
        meta[pl.ds(start, chunk), :] = count + (odd << 8)


def segment_plan(cell, worker):
    return pl.pallas_call(
        segment_plan_kernel,
        out_shape=jax.ShapeDtypeStruct(cell.shape, jnp.int32),
        compiler_params=pltpu.CompilerParams(vmem_limit_bytes=VMEM_LIMIT),
        cost_estimate=pl.CostEstimate(flops=10**8, bytes_accessed=1 * MIB, transcendentals=0),
        name="segment_plan",
    )(cell, worker)


def land_kernel(
    pairs, slots, first_rows, arrived, cell, meta, area, water, cap, soil_in, porosity_in,
    drainage_in, _, __, soil_out, canopy_new, sums_out, soil, porosity, drainage, soil_new,
    fetched, runoffs, evaps, sums, ready, written,
):
    layers, rows = soil.shape[:2]
    steps = written.shape[0]
    block = rows // steps
    ahead = 3
    arrays = ((soil_in, soil), (porosity_in, porosity), (drainage_in, drainage))

    def part_of(step):
        return pl.ds(pl.multiple_of(step * block, block), block)

    def reads(step):
        return [
            pltpu.make_async_copy(
                source.at[:, part_of(step), :], target.at[:, part_of(step), :], ready.at[step, i]
            )
            for i, (source, target) in enumerate(arrays)
        ]

    def start_reads(step):
        for copy in reads(step):
            copy.start()

    def write(step):
        return pltpu.make_async_copy(
            soil_new.at[:, part_of(step), :], soil_out.at[:, part_of(step), :], written.at[step]
        )

    def fetch(step):
        base = pl.multiple_of(step % 2 * (2 * block), 2 * block)
        for i in range(block):
            row = first_rows[step * block + i]
            fetched[pl.ds(base + 2 * i, 2), :] = arrived[pl.ds(row, 2, stride=pairs), :]

    def cascade(step):
        part = part_of(step)
        base = pl.multiple_of(step % 2 * (2 * block), 2 * block)
        index = cell[part, :]
        one = fetched[pl.ds(base, block, stride=2), :]
        two = fetched[pl.ds(base + 1, block, stride=2), :]
        odd = meta[part, :] >> 8
        loss = jnp.where(odd == 1, two, one)
        rain = lane_pick(jnp.where(odd == 1, one, two), index + odd * WINDOW)
        demand = lane_pick(loss, index)
        limit = lane_pick(loss, index + WINDOW)
        wetted = water[part, :] + rain
        flowing = jnp.maximum(wetted - cap[part, :], 0.0)
        retained = jnp.minimum(wetted, cap[part, :])
        canopy_loss = jnp.minimum(demand, retained)
        canopy_new[part, :] = retained - canopy_loss
        surface = jnp.zeros_like(flowing)
        for layer in range(layers):
            filled = soil[layer, part, :] + flowing
            excess = jnp.maximum(filled - porosity[layer, part, :], 0.0)
            surface = surface + excess
            filled = filled - excess
            flowing = drainage[layer, part, :] * filled
            middle = filled - flowing
            if layer == 0:
                soil_loss = jnp.minimum(jnp.minimum(limit, demand - canopy_loss), 0.5 * middle)
                middle = middle - soil_loss
                evaps[part, :] = area[part, :] * (canopy_loss + soil_loss)
            soil_new[layer, part, :] = middle
        runoffs[part, :] = area[part, :] * (surface + flowing)

    def hand_back(step):
        part = part_of(step)
        shape = (2 * LANES, LANES)
        upto = onehot((iota(shape, 0) & 127) <= iota(shape, 1))
        count = meta[part, :] & 255
        last = jnp.maximum(count - 1, 0)
        here = iota((block, LANES), 1)
        picked = [
            lane_pick(matmul(jnp.concatenate(halves(value[part, :]), axis=1), upto), last)
            for value in (runoffs, evaps)
        ]
        reached = jnp.where(count > 0, jnp.where(here < WINDOW, *picked), 0.0)
        before = jnp.where((here & (WINDOW - 1)) == 0, 0.0, pltpu.roll(reached, 1, 1))
        sums[...] = reached - before
        for i in range(block):
            sums_out[pl.ds(slots[step * block + i], 1), :] = sums[pl.ds(i, 1), :]

    start_reads(0)
    fetch(0)
    start_reads(1)
    sums_out[...] = jnp.zeros_like(sums_out)
    runoffs[pl.ds(0, block), :] = jnp.zeros((block, LANES), jnp.float32)
    evaps[pl.ds(0, block), :] = jnp.zeros((block, LANES), jnp.float32)
    start_reads(2)

    def round_of(step, carry):
        for copy in reads(step):
            copy.wait()

        @pl.when(step + ahead < steps)
        def _():
            start_reads(step + ahead)

        hand_back(jnp.maximum(step - 1, 0))
        cascade(step)
        fetch(jnp.minimum(step + 1, steps - 1))
        write(step).start()
        return carry

    lax.fori_loop(0, steps, round_of, 0)
    hand_back(steps - 1)
    for step in range(steps):
        write(step).wait()


def land_step(
    sums_shape, pairs, slots, first_rows, arrived, cell, meta, area, water, cap, soil, porosity,
    drainage, after,
):
    layers, rows = soil.shape[:2]
    steps = 10
    block = rows // steps
    near = pl.BlockSpec(memory_space=pltpu.VMEM)
    far = pl.BlockSpec(memory_space=pltpu.HBM)
    return pl.pallas_call(
        functools.partial(land_kernel, pairs),
        in_specs=[pl.BlockSpec(memory_space=pltpu.SMEM)] * 2 + [near] * 6 + [far] * 3
        + [pl.BlockSpec(memory_space=pl.ANY)] * 2,
        out_specs=[far, near, near],
        scratch_shapes=[pltpu.VMEM(soil.shape, jnp.float32)] * 4
        + [pltpu.VMEM((4 * block, LANES), jnp.float32)]
        + [pltpu.VMEM((rows, LANES), jnp.float32)] * 2
        + [pltpu.VMEM((block, LANES), jnp.float32)]
        + [pltpu.SemaphoreType.DMA((steps, 3)), pltpu.SemaphoreType.DMA((steps,))],
        out_shape=(
            jax.ShapeDtypeStruct(soil.shape, jnp.float32),
            jax.ShapeDtypeStruct((rows, LANES), jnp.float32),
            jax.ShapeDtypeStruct(sums_shape, jnp.float32),
        ),
        compiler_params=pltpu.CompilerParams(vmem_limit_bytes=VMEM_LIMIT),
        cost_estimate=pl.CostEstimate(flops=10**8, bytes_accessed=20 * MIB, transcendentals=0),
        name="land_layers",
    )(
        slots, first_rows, arrived, cell, meta, area, water, cap,
        in_hbm(soil), in_hbm(porosity), in_hbm(drainage), *after,
    )


def halo_parts(value, axis, dim, width):
    count, length = (lax.axis_size(axis), value.shape[dim])
    up = [(i, i + 1) for i in range(count - 1)]
    down = [(j, i) for i, j in up]
    last = lax.slice_in_dim(value, length - width, length, axis=dim)
    initial = lax.slice_in_dim(value, 0, width, axis=dim)
    return lax.ppermute(last, axis, up), lax.ppermute(initial, axis, down)


def edge_columns_kernel(tall, _, first, last):
    arrays, height, width = tall.shape
    for number in range(arrays):
        values = tall[number]
        values = jnp.concatenate([values, jnp.zeros((LANES - height, width), jnp.float32)], axis=0)
        columns = jnp.transpose(values)
        part = pl.ds(number * ITERS, ITERS)
        first[part, :] = columns[:ITERS]
        last[part, :] = columns[width - ITERS :]


def edge_columns(tall, after):
    shape = jax.ShapeDtypeStruct((2 * ITERS, LANES), jnp.float32)
    return pl.pallas_call(
        edge_columns_kernel,
        in_specs=[pl.BlockSpec(memory_space=pltpu.VMEM), pl.BlockSpec(memory_space=pl.ANY)],
        out_shape=(shape, shape),
        compiler_params=pltpu.CompilerParams(vmem_limit_bytes=VMEM_LIMIT),
        cost_estimate=pl.CostEstimate(flops=10**6, bytes_accessed=10**5, transcendentals=0),
        name="edge_columns",
    )(tall, after)


def extended(own, strip):
    height = own.shape[0]

    def column_strip(right):
        middle, above, below = strip(0, right), strip(-1, right), strip(1, right)
        return jnp.concatenate(
            [
                middle[:, :height],
                below[:, :ITERS],
                above[:, height - ITERS : height],
                jnp.zeros((ITERS, LANES - height - 2 * ITERS), jnp.float32),
            ],
            axis=1,
        )

    gap = jnp.zeros((LANES - 2 * ITERS, LANES), jnp.float32)
    sides = jnp.concatenate([column_strip(1), gap, column_strip(-1)], axis=0)
    sides = jnp.transpose(sides)[: height + 2 * ITERS]
    tall = jnp.concatenate([own, strip(1, 0), strip(-1, 0)], axis=0)
    return jnp.concatenate([tall, sides], axis=1)


def neighbour(down, right):
    row, column = lax.axis_index("region") + down, lax.axis_index("col") + right
    there = (row >= 0) & (row < lax.axis_size("region"))
    there &= (column >= 0) & (column < lax.axis_size("col"))
    return jnp.where(there, row * lax.axis_size("col") + column, 0), jnp.where(there, 1.0, 0.0)


def static_halo_kernel(tall, before, after, out):
    height, width = tall.shape[1:]
    gap = jnp.zeros((LANES - 2 * ITERS, LANES), jnp.float32)
    for number in range(2):
        part = pl.ds(number * ITERS, ITERS)
        sides = jnp.transpose(jnp.concatenate([after[part, :], gap, before[part, :]], axis=0))
        out[number, :, :width] = tall[number]
        out[number, :, width:] = sides[:height]


def static_halo(tall, before, after):
    arrays, height, width = tall.shape
    return pl.pallas_call(
        static_halo_kernel,
        out_shape=jax.ShapeDtypeStruct((arrays, height, width + LANES), jnp.float32),
        compiler_params=pltpu.CompilerParams(vmem_limit_bytes=VMEM_LIMIT),
        cost_estimate=pl.CostEstimate(flops=10**6, bytes_accessed=10**6, transcendentals=0),
        name="static_halo",
    )(tall, before, after)


def river_kernel(state, strips, fixed, out):
    height, width = state.shape

    def strip(down, right):
        device, there = neighbour(down, right)
        return strips[pl.ds(device * ITERS, ITERS), :] * there

    storage = extended(state[...], strip)
    rate = fixed[0]
    code = fixed[1]
    rows, cols = storage.shape
    for _ in range(ITERS):
        outflow = rate * storage
        inflow = jnp.zeros_like(storage)
        for col_step in (-1, 0, 1):
            column = jnp.zeros_like(storage)
            for bit, (row_step, step) in enumerate(directions):
                if step != col_step:
                    continue
                leaving = jnp.where(code == float(1 << bit), outflow, 0.0)
                if row_step:
                    leaving = pltpu.roll(leaving, row_step % rows, 0)
                column = column + leaving
            if col_step:
                column = pltpu.roll(column, col_step % cols, 1)
            inflow = inflow + column
        storage = storage - outflow + inflow
    out[...] = storage[:height, :width]


def river(state, strips, fixed):
    return pl.pallas_call(
        river_kernel,
        out_shape=jax.ShapeDtypeStruct(state.shape, jnp.float32),
        compiler_params=pltpu.CompilerParams(vmem_limit_bytes=VMEM_LIMIT),
        cost_estimate=pl.CostEstimate(flops=10**7, bytes_accessed=1 * MIB, transcendentals=0),
        name="river_steps",
    )(state, strips, fixed)


def exchange(value):
    return lax.all_to_all(value, axes, split_axis=0, concat_axis=0, tiled=True)


def shards(
    forcing,
    river_storage,
    river_rate,
    flow_code,
    home_slot,
    home_offset,
    worker_list,
    patch_cell,
    patch_area,
    canopy_water,
    canopy_cap,
    soil_water,
    porosity,
    drainage,
):
    homes = lax.axis_size("region") * lax.axis_size("col")
    capacity = home_slot.shape[1] // homes
    grid_rows, grid_cols = river_storage.shape
    lane_rows = grid_rows * grid_cols // LANES
    outgoing = pack(
        homes, capacity, home_slot, home_offset, forcing.reshape(3, lane_rows, LANES)
    )
    arrived = exchange(outgoing)
    home = worker_list // capacity
    position = worker_list - home * capacity
    pairs = capacity // 2
    first_rows = home * (3 * pairs) + position // 2 + position % 2 * pairs
    meta = segment_plan(patch_cell, worker_list[:, None])
    fixed = jnp.stack([river_rate, flow_code.astype(jnp.float32)])
    above, below = halo_parts(fixed, "region", 1, ITERS)
    soil_new, canopy_new, sums = land_step(
        (homes * capacity, LANES), pairs, worker_list, first_rows, arrived, patch_cell, meta,
        patch_area, canopy_water, canopy_cap, soil_water, porosity, drainage, (above, below),
    )
    returned = exchange(sums)
    code, place = unpack_plan(homes, capacity, lane_rows, home_slot, home_offset)
    fixed = jnp.concatenate([fixed, below, above], axis=1)
    initial, last = edge_columns(fixed, sums)
    count = lax.axis_size("col")
    before = lax.ppermute(last, "col", [(i, i + 1) for i in range(count - 1)])
    after = lax.ppermute(initial, "col", [(i + 1, i) for i in range(count - 1)])
    fixed = static_halo(fixed, before, after)
    cell_runoff, storage, strips = unpack_runoff(
        homes, returned, code, place, river_storage.reshape(lane_rows, LANES), fixed
    )
    cell_evap = unpack_evap(returned, code, place)
    river_new = river(storage.reshape(river_storage.shape), exchange(strips), fixed)
    return (
        soil_new,
        canopy_new,
        cell_runoff.reshape(river_storage.shape),
        cell_evap.reshape(river_storage.shape),
        river_new,
    )


def solution(mesh):
    placed = (
        P(None, "region", "col"),
        P("region", "col"),
        P("region", "col"),
        P("region", "col"),
        P(("region", "col"), None),
        P(("region", "col"), None),
        P(("region", "col")),
        P(("region", "col"), None),
        P(("region", "col"), None),
        P(("region", "col"), None),
        P(("region", "col"), None),
        P(None, ("region", "col"), None),
        P(None, ("region", "col"), None),
        P(None, ("region", "col"), None),
    )
    return jax.shard_map(
        shards,
        mesh=mesh,
        in_specs=placed,
        out_specs=(
            P(None, ("region", "col"), None),
            P(("region", "col"), None),
            P("region", "col"),
            P("region", "col"),
            P("region", "col"),
        ),
        check_vma=False,
    )
```

```python
import functools

import jax
import jax.numpy as jnp
from jax import lax
from jax.experimental import pallas as pl
from jax.experimental.pallas import tpu as pltpu
from jax.sharding import PartitionSpec as P

ITERS = 4
WINDOW = 64
LANES = 128
MIB = 1024 * 1024
VMEM_LIMIT = 24 * MIB

directions = ((0, 1), (1, 1), (1, 0), (1, -1), (0, -1), (-1, -1), (-1, 0), (-1, 1))
axes = ("region", "col")


def iota(shape, dim):
    return lax.broadcasted_iota(jnp.int32, shape, dim)


def onehot(mask):
    return jnp.where(mask, jnp.float32(1.0), jnp.float32(0.0)).astype(jnp.bfloat16)


def lane_pick(values, index):
    return jnp.take_along_axis(values, index, axis=1, mode="promise_in_bounds")


def in_hbm(value):
    return pltpu.with_memory_space_constraint(value, pltpu.HBM)


def thirds(value):
    high = value.astype(jnp.bfloat16)
    rest = value - high.astype(jnp.float32)
    middle = rest.astype(jnp.bfloat16)
    low = (rest - middle.astype(jnp.float32)).astype(jnp.bfloat16)
    return high, middle, low


def halves(value):
    high = value.astype(jnp.bfloat16)
    return high, (value - high.astype(jnp.float32)).astype(jnp.bfloat16)


def matmul(a, b, a_dim=1, b_dim=0):
    return lax.dot_general(
        a, b, (((a_dim,), (b_dim,)), ((), ())), preferred_element_type=jnp.float32
    )


def slot_factors(slot, offset, homes, capacity):
    slots = slot.shape[1]
    worker = slot // capacity if capacity & (capacity - 1) else slot >> (capacity.bit_length() - 1)
    position = slot - worker * capacity
    by_worker = onehot(iota((homes, slots), 0) == worker)
    at_position = iota((capacity, slots), 0) == position
    row = jnp.where(at_position, ((offset >> 7) + 1).astype(jnp.float32), 0.0)
    lane = jnp.where(at_position, (offset & 127).astype(jnp.float32), 0.0)
    return by_worker, row.astype(jnp.bfloat16), lane.astype(jnp.bfloat16)


def slot_columns(slot, offset, homes, capacity, split=False):
    slots = slot.shape[1]
    by_worker, row, lane = slot_factors(slot, offset, homes, capacity)
    table = matmul(by_worker, jnp.concatenate([row, lane], axis=0), 1, 1)
    groups = 2 if split else 1
    spread = jnp.broadcast_to(
        table[:, None, :], (homes, capacity // groups, 2 * capacity)
    ).reshape(slots // groups, 2 * capacity)
    spread = jnp.concatenate([spread] * groups, axis=0)
    number = iota(spread.shape, 0)
    position = number % (capacity // groups) * groups + number // (slots // groups)
    place = position == iota(spread.shape, 1) % capacity
    kept = jnp.where(place, spread, 0.0).astype(jnp.bfloat16)
    shape = (2 * capacity, 2 * LANES)
    gather = onehot((iota(shape, 0) >= capacity) == (iota(shape, 1) >= LANES))
    columns = matmul(kept, gather).astype(jnp.int32)
    return columns[:, :LANES] - 1, columns[:, LANES:]


def slot_rows(slot, offset, homes, capacity):
    slots = slot.shape[1]
    by_worker, row, lane = slot_factors(slot, offset, homes, capacity)
    table = matmul(jnp.concatenate([row, lane], axis=0), by_worker, 1, 1).astype(jnp.bfloat16)
    number = iota((1, slots), 1)
    worker = number // capacity
    position = number - worker * capacity
    spread = matmul(table, onehot(iota((homes, slots), 0) == worker))
    at_position = iota((capacity, slots), 0) == position
    rows = jnp.sum(jnp.where(at_position, spread[:capacity], 0.0), axis=0, keepdims=True)
    lanes = jnp.sum(jnp.where(at_position, spread[capacity:], 0.0), axis=0, keepdims=True)
    return rows.astype(jnp.int32) - 1, lanes.astype(jnp.int32)


def pack_kernel(
    homes, capacity, slot_in, offset_in, forcing_in, out, slot, offset, forcing, row_of, lane_of,
    rain, ready,
):
    copies = [
        pltpu.make_async_copy(source, target, ready.at[i])
        for i, (source, target) in enumerate(
            ((slot_in, slot), (offset_in, offset), (forcing_in, forcing))
        )
    ]
    for copy in copies:
        copy.start()
    slots = slot.shape[1]
    pairs = capacity // 2
    lane_rows = forcing.shape[1]
    copies[0].wait()
    copies[1].wait()
    row_of[...], lane_of[...] = slot_columns(slot[...], offset[...], homes, capacity, True)
    copies[2].wait()
    parts = []
    for var in range(3):
        here = forcing[var]
        following = jnp.concatenate([here[1:], here[:1]], axis=0)
        parts += [here, following]
    table = jnp.concatenate(thirds(jnp.concatenate(parts, axis=1)), axis=0)
    chunk = 128
    here = iota((chunk, LANES), 1)
    for start in range(0, slots, chunk):
        odd = start >= slots // 2
        row = row_of[pl.ds(start, chunk), :]
        lane = lane_of[pl.ds(start, chunk), :]
        shape = (chunk, 3 * lane_rows)
        wide = jnp.concatenate([row, row], axis=1)[:, : 3 * lane_rows]
        pick = onehot(wide == iota(shape, 1) % lane_rows)
        rows = matmul(pick, table)
        after = here >= lane
        joined = [
            jnp.where(
                after,
                rows[:, 2 * var * LANES : (2 * var + 1) * LANES],
                rows[:, (2 * var + 1) * LANES : (2 * var + 2) * LANES],
            )
            for var in range(3)
        ]
        first = (here + lane) & 127
        second = (first + WINDOW) & 127
        losses = jnp.where(
            here < WINDOW, lane_pick(joined[1], first), lane_pick(joined[2], second)
        )
        base = start - slots // 2 if odd else start
        if odd:
            rains = jnp.where(
                here < WINDOW, rain[pl.ds(base, chunk), :], lane_pick(joined[0], second)
            )
        else:
            rain[pl.ds(base, chunk), :] = lane_pick(joined[0], first)
        for part in range(0, chunk, pairs):
            place = (base + part) * 3
            if odd:
                out[pl.ds(place + pairs, pairs), :] = rains[part : part + pairs]
                out[pl.ds(place + 2 * pairs, pairs), :] = losses[part : part + pairs]
            else:
                out[pl.ds(place, pairs), :] = losses[part : part + pairs]


def pack(homes, capacity, slot, offset, forcing):
    slots = slot.shape[1]
    return pl.pallas_call(
        functools.partial(pack_kernel, homes, capacity),
        in_specs=[pl.BlockSpec(memory_space=pltpu.HBM)] * 3,
        out_shape=jax.ShapeDtypeStruct((slots + slots // 2, LANES), jnp.float32),
        scratch_shapes=[
            pltpu.VMEM(slot.shape, jnp.int32),
            pltpu.VMEM(offset.shape, jnp.int32),
            pltpu.VMEM(forcing.shape, jnp.float32),
            pltpu.VMEM((slots, LANES), jnp.int32),
            pltpu.VMEM((slots, LANES), jnp.int32),
            pltpu.VMEM((slots // 2, LANES), jnp.float32),
            pltpu.SemaphoreType.DMA((3,)),
        ],
        compiler_params=pltpu.CompilerParams(vmem_limit_bytes=VMEM_LIMIT),
        cost_estimate=pl.CostEstimate(flops=10**9, bytes_accessed=2 * MIB, transcendentals=0),
        name="pack_forcing",
    )(in_hbm(slot), in_hbm(offset), in_hbm(forcing))


def unpack_plan_kernel(homes, capacity, lane_rows, slot, offset, code, place):
    slots = slot.shape[1]
    row, lane = slot_columns(slot[...], offset[...], homes, capacity)
    here = iota((slots, LANES), 1)
    index = (here - lane) & 127
    inside = (index < WINDOW) & (row >= 0)
    code[...] = jnp.where(inside, index + jnp.where(here >= lane, 0, LANES), -1)
    row_lane, _ = slot_rows(slot[...], offset[...], homes, capacity)
    place[...] = onehot(iota((lane_rows, slots), 0) == row_lane)


def unpack_plan(homes, capacity, lane_rows, slot, offset):
    slots = slot.shape[1]
    return pl.pallas_call(
        functools.partial(unpack_plan_kernel, homes, capacity, lane_rows),
        out_shape=(
            jax.ShapeDtypeStruct((slots, LANES), jnp.int32),
            jax.ShapeDtypeStruct((lane_rows, slots), jnp.bfloat16),
        ),
        compiler_params=pltpu.CompilerParams(vmem_limit_bytes=VMEM_LIMIT),
        cost_estimate=pl.CostEstimate(flops=10**9, bytes_accessed=2 * MIB, transcendentals=0),
        name="unpack_plan",
    )(slot, offset)


def strips_for_neighbours(state, rows):
    device = iota((rows, LANES), 0) // ITERS
    down = device // lax.axis_size("col") - lax.axis_index("region")
    right = device % lax.axis_size("col") - lax.axis_index("col")
    height, width = state.shape
    columns = jnp.transpose(state)
    empty = jnp.zeros((ITERS, LANES - height), jnp.float32)

    def repeated(strip):
        if strip.shape[1] < LANES:
            strip = jnp.concatenate([strip, empty], axis=1)
        return jnp.concatenate([strip] * (rows // ITERS), axis=0)

    near = (jnp.abs(down) <= 1).astype(jnp.int32)
    strips = jnp.zeros((rows, LANES), jnp.float32)
    strips = jnp.where((right == 0) & (down == 1), repeated(state[height - ITERS :]), strips)
    strips = jnp.where((right == 0) & (down == -1), repeated(state[:ITERS]), strips)
    strips = jnp.where((right == 1) & (near == 1), repeated(columns[width - ITERS :]), strips)
    return jnp.where((right == -1) & (near == 1), repeated(columns[:ITERS]), strips)


def cell_totals(arrived, code, place, first):
    lane_rows = place.shape[0]
    marks = code[...]
    window = lane_pick(arrived[...], (marks + first) & 127)
    placed = jnp.concatenate(
        [
            jnp.where((marks >= 0) & (marks < LANES), window, 0.0),
            jnp.where(marks >= LANES, window, 0.0),
        ],
        axis=1,
    )
    totals = matmul(place[...], jnp.concatenate(halves(placed), axis=1))
    totals = totals[:, :256] + totals[:, 256:]
    over = totals[:, LANES:]
    over = jnp.concatenate([over[lane_rows - 1 :], over[: lane_rows - 1]], axis=0)
    over = jnp.where(iota(over.shape, 0) == 0, 0.0, over)
    return totals[:, :LANES] + over


def unpack_runoff_kernel(arrived, code, place, river, _, __, runoff, storage, strips):
    total = cell_totals(arrived, code, place, 0)
    state = river[...] + total
    runoff[...] = total
    storage[...] = state
    strips[...] = strips_for_neighbours(state, strips.shape[0])


def unpack_runoff(homes, arrived, code, place, river, *after):
    shape = jax.ShapeDtypeStruct((place.shape[0], LANES), jnp.float32)
    strips = jax.ShapeDtypeStruct((homes * ITERS, LANES), jnp.float32)
    return pl.pallas_call(
        unpack_runoff_kernel,
        in_specs=[pl.BlockSpec(memory_space=pltpu.VMEM)] * 4
        + [pl.BlockSpec(memory_space=pl.ANY)] * 2,
        out_shape=(shape, shape, strips),
        compiler_params=pltpu.CompilerParams(vmem_limit_bytes=VMEM_LIMIT),
        cost_estimate=pl.CostEstimate(flops=10**9, bytes_accessed=1 * MIB, transcendentals=0),
        name="unpack_runoff",
    )(arrived, code, place, river, *after)


def unpack_evap_kernel(arrived, code, place, evap):
    evap[...] = cell_totals(arrived, code, place, WINDOW)


def unpack_evap(arrived, code, place):
    return pl.pallas_call(
        unpack_evap_kernel,
        out_shape=jax.ShapeDtypeStruct((place.shape[0], LANES), jnp.float32),
        compiler_params=pltpu.CompilerParams(vmem_limit_bytes=VMEM_LIMIT),
        cost_estimate=pl.CostEstimate(flops=10**9, bytes_accessed=1 * MIB, transcendentals=0),
        name="unpack_evap",
    )(arrived, code, place)


def segment_plan_kernel(cell, worker, meta):
    chunk = 96
    for start in range(0, cell.shape[0], chunk):
        values = cell[pl.ds(start, chunk), :]
        target = iota(values.shape, 1) & (WINDOW - 1)
        count = jnp.zeros_like(values)
        for step in (64, 32, 16, 8, 4, 2, 1):
            probe = lane_pick(values, count + (step - 1))
            count = jnp.where(probe <= target, count + step, count)
        count = jnp.where(lane_pick(values, count) <= target, count + 1, count)
        odd = worker[pl.ds(start, chunk), :] & 1
        meta[pl.ds(start, chunk), :] = count + (odd << 8)


def segment_plan(cell, worker):
    return pl.pallas_call(
        segment_plan_kernel,
        out_shape=jax.ShapeDtypeStruct(cell.shape, jnp.int32),
        compiler_params=pltpu.CompilerParams(vmem_limit_bytes=VMEM_LIMIT),
        cost_estimate=pl.CostEstimate(flops=10**8, bytes_accessed=1 * MIB, transcendentals=0),
        name="segment_plan",
    )(cell, worker)


def land_sums_kernel(
    pairs, slots, first_rows, arrived, cell, meta, area, water, cap, soil_in, porosity_in,
    drainage_in, _, __, through, lost, canopy_new, sums_out, soil, porosity, drainage, fetched,
    runoffs, evaps, sums, ready,
):
    layers, rows = soil.shape[:2]
    steps = ready.shape[0]
    block = rows // steps
    ahead = 4
    arrays = ((soil_in, soil), (porosity_in, porosity), (drainage_in, drainage))

    def part_of(step):
        return pl.ds(pl.multiple_of(step * block, block), block)

    def reads(step):
        return [
            pltpu.make_async_copy(
                source.at[:, part_of(step), :], target.at[:, part_of(step), :], ready.at[step, i]
            )
            for i, (source, target) in enumerate(arrays)
        ]

    def start_reads(step):
        for copy in reads(step):
            copy.start()

    def fetch(step):
        base = pl.multiple_of(step % 2 * (2 * block), 2 * block)
        for i in range(block):
            row = first_rows[step * block + i]
            fetched[pl.ds(base + 2 * i, 2), :] = arrived[pl.ds(row, 2, stride=pairs), :]

    def cascade(step):
        part = part_of(step)
        base = pl.multiple_of(step % 2 * (2 * block), 2 * block)
        index = cell[part, :]
        one = fetched[pl.ds(base, block, stride=2), :]
        two = fetched[pl.ds(base + 1, block, stride=2), :]
        odd = meta[part, :] >> 8
        loss = jnp.where(odd == 1, two, one)
        rain = lane_pick(jnp.where(odd == 1, one, two), index + odd * WINDOW)
        demand = lane_pick(loss, index)
        limit = lane_pick(loss, index + WINDOW)
        wetted = water[part, :] + rain
        flowing = jnp.maximum(wetted - cap[part, :], 0.0)
        retained = jnp.minimum(wetted, cap[part, :])
        canopy_loss = jnp.minimum(demand, retained)
        canopy_new[part, :] = retained - canopy_loss
        through[part, :] = flowing
        surface = jnp.zeros_like(flowing)
        for layer in range(layers):
            filled = soil[layer, part, :] + flowing
            excess = jnp.maximum(filled - porosity[layer, part, :], 0.0)
            surface = surface + excess
            filled = filled - excess
            flowing = drainage[layer, part, :] * filled
            if layer == 0:
                half = 0.5 * (filled - flowing)
                soil_loss = jnp.minimum(jnp.minimum(limit, demand - canopy_loss), half)
                lost[part, :] = soil_loss
                evaps[part, :] = area[part, :] * (canopy_loss + soil_loss)
        runoffs[part, :] = area[part, :] * (surface + flowing)

    def hand_back(step):
        part = part_of(step)
        shape = (2 * LANES, LANES)
        upto = onehot((iota(shape, 0) & 127) <= iota(shape, 1))
        count = meta[part, :] & 255
        last = jnp.maximum(count - 1, 0)
        here = iota((block, LANES), 1)
        picked = [
            lane_pick(matmul(jnp.concatenate(halves(value[part, :]), axis=1), upto), last)
            for value in (runoffs, evaps)
        ]
        reached = jnp.where(count > 0, jnp.where(here < WINDOW, *picked), 0.0)
        before = jnp.where((here & (WINDOW - 1)) == 0, 0.0, pltpu.roll(reached, 1, 1))
        sums[...] = reached - before
        for i in range(block):
            sums_out[pl.ds(slots[step * block + i], 1), :] = sums[pl.ds(i, 1), :]

    start_reads(0)
    fetch(0)
    start_reads(1)
    sums_out[...] = jnp.zeros_like(sums_out)
    runoffs[pl.ds(0, block), :] = jnp.zeros((block, LANES), jnp.float32)
    evaps[pl.ds(0, block), :] = jnp.zeros((block, LANES), jnp.float32)
    start_reads(2)
    start_reads(3)

    def round_of(step, carry):
        for copy in reads(step):
            copy.wait()

        @pl.when(step + ahead < steps)
        def _():
            start_reads(step + ahead)

        hand_back(jnp.maximum(step - 1, 0))
        cascade(step)
        fetch(jnp.minimum(step + 1, steps - 1))
        return carry

    lax.fori_loop(0, steps, round_of, 0)
    hand_back(steps - 1)


def land_sums(
    sums_shape, pairs, slots, first_rows, arrived, cell, meta, area, water, cap, soil, porosity,
    drainage, after,
):
    layers, rows = soil.shape[:2]
    steps = 10
    block = rows // steps
    near = pl.BlockSpec(memory_space=pltpu.VMEM)
    far = pl.BlockSpec(memory_space=pltpu.HBM)
    return pl.pallas_call(
        functools.partial(land_sums_kernel, pairs),
        in_specs=[pl.BlockSpec(memory_space=pltpu.SMEM)] * 2 + [near] * 6 + [far] * 3
        + [pl.BlockSpec(memory_space=pl.ANY)] * 2,
        out_specs=[near] * 4,
        scratch_shapes=[pltpu.VMEM(soil.shape, jnp.float32)] * 3
        + [pltpu.VMEM((4 * block, LANES), jnp.float32)]
        + [pltpu.VMEM((rows, LANES), jnp.float32)] * 2
        + [pltpu.VMEM((block, LANES), jnp.float32), pltpu.SemaphoreType.DMA((steps, 3))],
        out_shape=[jax.ShapeDtypeStruct((rows, LANES), jnp.float32)] * 3
        + [jax.ShapeDtypeStruct(sums_shape, jnp.float32)],
        compiler_params=pltpu.CompilerParams(vmem_limit_bytes=VMEM_LIMIT),
        cost_estimate=pl.CostEstimate(flops=10**8, bytes_accessed=20 * MIB, transcendentals=0),
        name="land_sums",
    )(
        slots, first_rows, arrived, cell, meta, area, water, cap,
        in_hbm(soil), in_hbm(porosity), in_hbm(drainage), *after,
    )


def new_soil_kernel(through, lost, canopy, soil, porosity, drainage, soil_new, canopy_new):
    layers, block = soil.shape[:2]
    chunk = 48
    canopy_new[...] = canopy[...]
    for start in range(0, block, chunk):
        part = pl.ds(start, chunk)
        flowing = through[part, :]
        for layer in range(layers):
            filled = soil[layer, part, :] + flowing
            filled = filled - jnp.maximum(filled - porosity[layer, part, :], 0.0)
            flowing = drainage[layer, part, :] * filled
            middle = filled - flowing
            soil_new[layer, part, :] = middle - lost[part, :] if layer == 0 else middle


def new_soil(through, lost, canopy, soil, porosity, drainage):
    layers, rows = soil.shape[:2]
    block = 96
    flat = pl.BlockSpec((block, LANES), lambda i: (i, 0))
    deep = pl.BlockSpec((layers, block, LANES), lambda i: (0, i, 0))
    return pl.pallas_call(
        new_soil_kernel,
        grid=(rows // block,),
        in_specs=[flat, flat, flat, deep, deep, deep],
        out_specs=[deep, flat],
        out_shape=(
            jax.ShapeDtypeStruct(soil.shape, jnp.float32),
            jax.ShapeDtypeStruct((rows, LANES), jnp.float32),
        ),
        compiler_params=pltpu.CompilerParams(vmem_limit_bytes=VMEM_LIMIT),
        cost_estimate=pl.CostEstimate(flops=10**8, bytes_accessed=16 * MIB, transcendentals=0),
        name="new_soil",
    )(through, lost, canopy, in_hbm(soil), in_hbm(porosity), in_hbm(drainage))


def halo_parts(value, axis, dim, width):
    count, length = (lax.axis_size(axis), value.shape[dim])
    up = [(i, i + 1) for i in range(count - 1)]
    down = [(j, i) for i, j in up]
    last = lax.slice_in_dim(value, length - width, length, axis=dim)
    initial = lax.slice_in_dim(value, 0, width, axis=dim)
    return lax.ppermute(last, axis, up), lax.ppermute(initial, axis, down)


def edge_columns_kernel(tall, _, first, last):
    arrays, height, width = tall.shape
    for number in range(arrays):
        values = tall[number]
        values = jnp.concatenate([values, jnp.zeros((LANES - height, width), jnp.float32)], axis=0)
        columns = jnp.transpose(values)
        part = pl.ds(number * ITERS, ITERS)
        first[part, :] = columns[:ITERS]
        last[part, :] = columns[width - ITERS :]


def edge_columns(tall, after):
    shape = jax.ShapeDtypeStruct((2 * ITERS, LANES), jnp.float32)
    return pl.pallas_call(
        edge_columns_kernel,
        in_specs=[pl.BlockSpec(memory_space=pltpu.VMEM), pl.BlockSpec(memory_space=pl.ANY)],
        out_shape=(shape, shape),
        compiler_params=pltpu.CompilerParams(vmem_limit_bytes=VMEM_LIMIT),
        cost_estimate=pl.CostEstimate(flops=10**6, bytes_accessed=10**5, transcendentals=0),
        name="edge_columns",
    )(tall, after)


def extended(own, strip):
    height = own.shape[0]

    def column_strip(right):
        middle, above, below = strip(0, right), strip(-1, right), strip(1, right)
        return jnp.concatenate(
            [
                middle[:, :height],
                below[:, :ITERS],
                above[:, height - ITERS : height],
                jnp.zeros((ITERS, LANES - height - 2 * ITERS), jnp.float32),
            ],
            axis=1,
        )

    gap = jnp.zeros((LANES - 2 * ITERS, LANES), jnp.float32)
    sides = jnp.concatenate([column_strip(1), gap, column_strip(-1)], axis=0)
    sides = jnp.transpose(sides)[: height + 2 * ITERS]
    tall = jnp.concatenate([own, strip(1, 0), strip(-1, 0)], axis=0)
    return jnp.concatenate([tall, sides], axis=1)


def neighbour(down, right):
    row, column = lax.axis_index("region") + down, lax.axis_index("col") + right
    there = (row >= 0) & (row < lax.axis_size("region"))
    there &= (column >= 0) & (column < lax.axis_size("col"))
    return jnp.where(there, row * lax.axis_size("col") + column, 0), jnp.where(there, 1.0, 0.0)


def static_halo_kernel(tall, before, after, out):
    height, width = tall.shape[1:]
    gap = jnp.zeros((LANES - 2 * ITERS, LANES), jnp.float32)
    for number in range(2):
        part = pl.ds(number * ITERS, ITERS)
        sides = jnp.transpose(jnp.concatenate([after[part, :], gap, before[part, :]], axis=0))
        out[number, :, :width] = tall[number]
        out[number, :, width:] = sides[:height]


def static_halo(tall, before, after):
    arrays, height, width = tall.shape
    return pl.pallas_call(
        static_halo_kernel,
        out_shape=jax.ShapeDtypeStruct((arrays, height, width + LANES), jnp.float32),
        compiler_params=pltpu.CompilerParams(vmem_limit_bytes=VMEM_LIMIT),
        cost_estimate=pl.CostEstimate(flops=10**6, bytes_accessed=10**6, transcendentals=0),
        name="static_halo",
    )(tall, before, after)


def river_kernel(state, strips, fixed, out):
    height, width = state.shape

    def strip(down, right):
        device, there = neighbour(down, right)
        return strips[pl.ds(device * ITERS, ITERS), :] * there

    storage = extended(state[...], strip)
    rate = fixed[0]
    code = fixed[1]
    rows, cols = storage.shape
    for _ in range(ITERS):
        outflow = rate * storage
        inflow = jnp.zeros_like(storage)
        for col_step in (-1, 0, 1):
            column = jnp.zeros_like(storage)
            for bit, (row_step, step) in enumerate(directions):
                if step != col_step:
                    continue
                leaving = jnp.where(code == float(1 << bit), outflow, 0.0)
                if row_step:
                    leaving = pltpu.roll(leaving, row_step % rows, 0)
                column = column + leaving
            if col_step:
                column = pltpu.roll(column, col_step % cols, 1)
            inflow = inflow + column
        storage = storage - outflow + inflow
    out[...] = storage[:height, :width]


def river(state, strips, fixed):
    return pl.pallas_call(
        river_kernel,
        out_shape=jax.ShapeDtypeStruct(state.shape, jnp.float32),
        compiler_params=pltpu.CompilerParams(vmem_limit_bytes=VMEM_LIMIT),
        cost_estimate=pl.CostEstimate(flops=10**7, bytes_accessed=1 * MIB, transcendentals=0),
        name="river_steps",
    )(state, strips, fixed)


def exchange(value):
    return lax.all_to_all(value, axes, split_axis=0, concat_axis=0, tiled=True)


def shards(
    forcing,
    river_storage,
    river_rate,
    flow_code,
    home_slot,
    home_offset,
    worker_list,
    patch_cell,
    patch_area,
    canopy_water,
    canopy_cap,
    soil_water,
    porosity,
    drainage,
):
    homes = lax.axis_size("region") * lax.axis_size("col")
    capacity = home_slot.shape[1] // homes
    grid_rows, grid_cols = river_storage.shape
    lane_rows = grid_rows * grid_cols // LANES
    outgoing = pack(
        homes, capacity, home_slot, home_offset, forcing.reshape(3, lane_rows, LANES)
    )
    arrived = exchange(outgoing)
    home = worker_list // capacity
    position = worker_list - home * capacity
    pairs = capacity // 2
    first_rows = home * (3 * pairs) + position // 2 + position % 2 * pairs
    meta = segment_plan(patch_cell, worker_list[:, None])
    fixed = jnp.stack([river_rate, flow_code.astype(jnp.float32)])
    above, below = halo_parts(fixed, "region", 1, ITERS)
    through, lost, canopy, sums = land_sums(
        (homes * capacity, LANES), pairs, worker_list, first_rows, arrived, patch_cell, meta,
        patch_area, canopy_water, canopy_cap, soil_water, porosity, drainage, (above, below),
    )
    returned = exchange(sums)
    soil_new, canopy_new = new_soil(through, lost, canopy, soil_water, porosity, drainage)
    code, place = unpack_plan(homes, capacity, lane_rows, home_slot, home_offset)
    fixed = jnp.concatenate([fixed, below, above], axis=1)
    initial, last = edge_columns(fixed, sums)
    count = lax.axis_size("col")
    before = lax.ppermute(last, "col", [(i, i + 1) for i in range(count - 1)])
    after = lax.ppermute(initial, "col", [(i + 1, i) for i in range(count - 1)])
    fixed = static_halo(fixed, before, after)
    cell_runoff, storage, strips = unpack_runoff(
        homes, returned, code, place, river_storage.reshape(lane_rows, LANES), fixed, in_hbm(canopy_new)
    )
    cell_evap = unpack_evap(returned, code, place)
    river_new = river(storage.reshape(river_storage.shape), exchange(strips), fixed)
    return (
        soil_new,
        canopy_new,
        cell_runoff.reshape(river_storage.shape),
        cell_evap.reshape(river_storage.shape),
        river_new,
    )


def solution(mesh):
    placed = (
        P(None, "region", "col"),
        P("region", "col"),
        P("region", "col"),
        P("region", "col"),
        P(("region", "col"), None),
        P(("region", "col"), None),
        P(("region", "col")),
        P(("region", "col"), None),
        P(("region", "col"), None),
        P(("region", "col"), None),
        P(("region", "col"), None),
        P(None, ("region", "col"), None),
        P(None, ("region", "col"), None),
        P(None, ("region", "col"), None),
    )
    return jax.shard_map(
        shards,
        mesh=mesh,
        in_specs=placed,
        out_specs=(
            P(None, ("region", "col"), None),
            P(("region", "col"), None),
            P("region", "col"),
            P("region", "col"),
            P("region", "col"),
        ),
        check_vma=False,
    )
```

```python
import functools

import jax
import jax.numpy as jnp
from jax import lax
from jax.experimental import pallas as pl
from jax.experimental.pallas import tpu as pltpu
from jax.sharding import PartitionSpec as P

ITERS = 4
WINDOW = 64
LANES = 128
MIB = 1024 * 1024
VMEM_LIMIT = 24 * MIB

directions = ((0, 1), (1, 1), (1, 0), (1, -1), (0, -1), (-1, -1), (-1, 0), (-1, 1))
axes = ("region", "col")


def iota(shape, dim):
    return lax.broadcasted_iota(jnp.int32, shape, dim)


def onehot(mask):
    return jnp.where(mask, jnp.float32(1.0), jnp.float32(0.0)).astype(jnp.bfloat16)


def lane_pick(values, index):
    return jnp.take_along_axis(values, index, axis=1, mode="promise_in_bounds")


def in_hbm(value):
    return pltpu.with_memory_space_constraint(value, pltpu.HBM)


def thirds(value):
    high = value.astype(jnp.bfloat16)
    rest = value - high.astype(jnp.float32)
    middle = rest.astype(jnp.bfloat16)
    low = (rest - middle.astype(jnp.float32)).astype(jnp.bfloat16)
    return high, middle, low


def halves(value):
    high = value.astype(jnp.bfloat16)
    return high, (value - high.astype(jnp.float32)).astype(jnp.bfloat16)


def matmul(a, b, a_dim=1, b_dim=0):
    return lax.dot_general(
        a, b, (((a_dim,), (b_dim,)), ((), ())), preferred_element_type=jnp.float32
    )


def slot_factors(slot, offset, homes, capacity):
    slots = slot.shape[1]
    worker = slot // capacity if capacity & (capacity - 1) else slot >> (capacity.bit_length() - 1)
    position = slot - worker * capacity
    by_worker = onehot(iota((homes, slots), 0) == worker)
    at_position = iota((capacity, slots), 0) == position
    row = jnp.where(at_position, ((offset >> 7) + 1).astype(jnp.float32), 0.0)
    lane = jnp.where(at_position, (offset & 127).astype(jnp.float32), 0.0)
    return by_worker, row.astype(jnp.bfloat16), lane.astype(jnp.bfloat16)


def slot_columns(slot, offset, homes, capacity, split=False):
    slots = slot.shape[1]
    by_worker, row, lane = slot_factors(slot, offset, homes, capacity)
    table = matmul(by_worker, jnp.concatenate([row, lane], axis=0), 1, 1)
    groups = 2 if split else 1
    spread = jnp.broadcast_to(
        table[:, None, :], (homes, capacity // groups, 2 * capacity)
    ).reshape(slots // groups, 2 * capacity)
    spread = jnp.concatenate([spread] * groups, axis=0)
    number = iota(spread.shape, 0)
    position = number % (capacity // groups) * groups + number // (slots // groups)
    place = position == iota(spread.shape, 1) % capacity
    kept = jnp.where(place, spread, 0.0).astype(jnp.bfloat16)
    shape = (2 * capacity, 2 * LANES)
    gather = onehot((iota(shape, 0) >= capacity) == (iota(shape, 1) >= LANES))
    columns = matmul(kept, gather).astype(jnp.int32)
    return columns[:, :LANES] - 1, columns[:, LANES:]


def slot_rows(slot, offset, homes, capacity):
    slots = slot.shape[1]
    by_worker, row, lane = slot_factors(slot, offset, homes, capacity)
    table = matmul(jnp.concatenate([row, lane], axis=0), by_worker, 1, 1).astype(jnp.bfloat16)
    number = iota((1, slots), 1)
    worker = number // capacity
    position = number - worker * capacity
    spread = matmul(table, onehot(iota((homes, slots), 0) == worker))
    at_position = iota((capacity, slots), 0) == position
    rows = jnp.sum(jnp.where(at_position, spread[:capacity], 0.0), axis=0, keepdims=True)
    lanes = jnp.sum(jnp.where(at_position, spread[capacity:], 0.0), axis=0, keepdims=True)
    return rows.astype(jnp.int32) - 1, lanes.astype(jnp.int32)


def pack_kernel(
    homes, capacity, slot_in, offset_in, forcing_in, out, slot, offset, forcing, row_of, lane_of,
    rain, ready,
):
    copies = [
        pltpu.make_async_copy(source, target, ready.at[i])
        for i, (source, target) in enumerate(
            ((slot_in, slot), (offset_in, offset), (forcing_in, forcing))
        )
    ]
    for copy in copies:
        copy.start()
    slots = slot.shape[1]
    pairs = capacity // 2
    lane_rows = forcing.shape[1]
    copies[0].wait()
    copies[1].wait()
    row_of[...], lane_of[...] = slot_columns(slot[...], offset[...], homes, capacity, True)
    copies[2].wait()
    parts = []
    for var in range(3):
        here = forcing[var]
        following = jnp.concatenate([here[1:], here[:1]], axis=0)
        parts += [here, following]
    table = jnp.concatenate(thirds(jnp.concatenate(parts, axis=1)), axis=0)
    chunk = 128
    here = iota((chunk, LANES), 1)
    for start in range(0, slots, chunk):
        odd = start >= slots // 2
        row = row_of[pl.ds(start, chunk), :]
        lane = lane_of[pl.ds(start, chunk), :]
        shape = (chunk, 3 * lane_rows)
        wide = jnp.concatenate([row, row], axis=1)[:, : 3 * lane_rows]
        pick = onehot(wide == iota(shape, 1) % lane_rows)
        rows = matmul(pick, table)
        after = here >= lane
        joined = [
            jnp.where(
                after,
                rows[:, 2 * var * LANES : (2 * var + 1) * LANES],
                rows[:, (2 * var + 1) * LANES : (2 * var + 2) * LANES],
            )
            for var in range(3)
        ]
        first = (here + lane) & 127
        second = (first + WINDOW) & 127
        losses = jnp.where(
            here < WINDOW, lane_pick(joined[1], first), lane_pick(joined[2], second)
        )
        base = start - slots // 2 if odd else start
        if odd:
            rains = jnp.where(
                here < WINDOW, rain[pl.ds(base, chunk), :], lane_pick(joined[0], second)
            )
        else:
            rain[pl.ds(base, chunk), :] = lane_pick(joined[0], first)
        for part in range(0, chunk, pairs):
            place = (base + part) * 3
            if odd:
                out[pl.ds(place + pairs, pairs), :] = rains[part : part + pairs]
                out[pl.ds(place + 2 * pairs, pairs), :] = losses[part : part + pairs]
            else:
                out[pl.ds(place, pairs), :] = losses[part : part + pairs]


def pack(homes, capacity, slot, offset, forcing):
    slots = slot.shape[1]
    return pl.pallas_call(
        functools.partial(pack_kernel, homes, capacity),
        in_specs=[pl.BlockSpec(memory_space=pltpu.HBM)] * 3,
        out_shape=jax.ShapeDtypeStruct((slots + slots // 2, LANES), jnp.float32),
        scratch_shapes=[
            pltpu.VMEM(slot.shape, jnp.int32),
            pltpu.VMEM(offset.shape, jnp.int32),
            pltpu.VMEM(forcing.shape, jnp.float32),
            pltpu.VMEM((slots, LANES), jnp.int32),
            pltpu.VMEM((slots, LANES), jnp.int32),
            pltpu.VMEM((slots // 2, LANES), jnp.float32),
            pltpu.SemaphoreType.DMA((3,)),
        ],
        compiler_params=pltpu.CompilerParams(vmem_limit_bytes=VMEM_LIMIT),
        cost_estimate=pl.CostEstimate(flops=10**9, bytes_accessed=2 * MIB, transcendentals=0),
        name="pack_forcing",
    )(in_hbm(slot), in_hbm(offset), in_hbm(forcing))


def unpack_plan_kernel(homes, capacity, lane_rows, slot, offset, code, place):
    slots = slot.shape[1]
    row, lane = slot_columns(slot[...], offset[...], homes, capacity)
    here = iota((slots, LANES), 1)
    index = (here - lane) & 127
    inside = (index < WINDOW) & (row >= 0)
    code[...] = jnp.where(inside, index + jnp.where(here >= lane, 0, LANES), -1)
    row_lane, _ = slot_rows(slot[...], offset[...], homes, capacity)
    place[...] = onehot(iota((lane_rows, slots), 0) == row_lane)


def unpack_plan(homes, capacity, lane_rows, slot, offset):
    slots = slot.shape[1]
    return pl.pallas_call(
        functools.partial(unpack_plan_kernel, homes, capacity, lane_rows),
        out_shape=(
            jax.ShapeDtypeStruct((slots, LANES), jnp.int32),
            jax.ShapeDtypeStruct((lane_rows, slots), jnp.bfloat16),
        ),
        compiler_params=pltpu.CompilerParams(vmem_limit_bytes=VMEM_LIMIT),
        cost_estimate=pl.CostEstimate(flops=10**9, bytes_accessed=2 * MIB, transcendentals=0),
        name="unpack_plan",
    )(slot, offset)


def strips_for_neighbours(state, rows):
    device = iota((rows, LANES), 0) // ITERS
    down = device // lax.axis_size("col") - lax.axis_index("region")
    right = device % lax.axis_size("col") - lax.axis_index("col")
    height, width = state.shape
    columns = jnp.transpose(state)
    empty = jnp.zeros((ITERS, LANES - height), jnp.float32)

    def repeated(strip):
        if strip.shape[1] < LANES:
            strip = jnp.concatenate([strip, empty], axis=1)
        return jnp.concatenate([strip] * (rows // ITERS), axis=0)

    near = (jnp.abs(down) <= 1).astype(jnp.int32)
    strips = jnp.zeros((rows, LANES), jnp.float32)
    strips = jnp.where((right == 0) & (down == 1), repeated(state[height - ITERS :]), strips)
    strips = jnp.where((right == 0) & (down == -1), repeated(state[:ITERS]), strips)
    strips = jnp.where((right == 1) & (near == 1), repeated(columns[width - ITERS :]), strips)
    return jnp.where((right == -1) & (near == 1), repeated(columns[:ITERS]), strips)


def cell_totals(arrived, code, place, first):
    lane_rows = place.shape[0]
    marks = code[...]
    window = lane_pick(arrived[...], (marks + first) & 127)
    placed = jnp.concatenate(
        [
            jnp.where((marks >= 0) & (marks < LANES), window, 0.0),
            jnp.where(marks >= LANES, window, 0.0),
        ],
        axis=1,
    )
    totals = matmul(place[...], jnp.concatenate(halves(placed), axis=1))
    totals = totals[:, :256] + totals[:, 256:]
    over = totals[:, LANES:]
    over = jnp.concatenate([over[lane_rows - 1 :], over[: lane_rows - 1]], axis=0)
    over = jnp.where(iota(over.shape, 0) == 0, 0.0, over)
    return totals[:, :LANES] + over


def unpack_runoff_kernel(arrived, code, place, river, _, __, runoff, storage, strips):
    total = cell_totals(arrived, code, place, 0)
    state = river[...] + total
    runoff[...] = total
    storage[...] = state
    strips[...] = strips_for_neighbours(state, strips.shape[0])


def unpack_runoff(homes, arrived, code, place, river, *after):
    shape = jax.ShapeDtypeStruct((place.shape[0], LANES), jnp.float32)
    strips = jax.ShapeDtypeStruct((homes * ITERS, LANES), jnp.float32)
    return pl.pallas_call(
        unpack_runoff_kernel,
        in_specs=[pl.BlockSpec(memory_space=pltpu.VMEM)] * 4
        + [pl.BlockSpec(memory_space=pl.ANY)] * 2,
        out_shape=(shape, shape, strips),
        compiler_params=pltpu.CompilerParams(vmem_limit_bytes=VMEM_LIMIT),
        cost_estimate=pl.CostEstimate(flops=10**9, bytes_accessed=1 * MIB, transcendentals=0),
        name="unpack_runoff",
    )(arrived, code, place, river, *after)


def unpack_evap_kernel(arrived, code, place, evap):
    evap[...] = cell_totals(arrived, code, place, WINDOW)


def unpack_evap(arrived, code, place):
    return pl.pallas_call(
        unpack_evap_kernel,
        out_shape=jax.ShapeDtypeStruct((place.shape[0], LANES), jnp.float32),
        compiler_params=pltpu.CompilerParams(vmem_limit_bytes=VMEM_LIMIT),
        cost_estimate=pl.CostEstimate(flops=10**9, bytes_accessed=1 * MIB, transcendentals=0),
        name="unpack_evap",
    )(arrived, code, place)


def segment_plan_kernel(cell, worker, meta):
    chunk = 96
    for start in range(0, cell.shape[0], chunk):
        values = cell[pl.ds(start, chunk), :]
        target = iota(values.shape, 1) & (WINDOW - 1)
        count = jnp.zeros_like(values)
        for step in (64, 32, 16, 8, 4, 2, 1):
            probe = lane_pick(values, count + (step - 1))
            count = jnp.where(probe <= target, count + step, count)
        count = jnp.where(lane_pick(values, count) <= target, count + 1, count)
        odd = worker[pl.ds(start, chunk), :] & 1
        meta[pl.ds(start, chunk), :] = count + (odd << 8)


def segment_plan(cell, worker):
    return pl.pallas_call(
        segment_plan_kernel,
        out_shape=jax.ShapeDtypeStruct(cell.shape, jnp.int32),
        compiler_params=pltpu.CompilerParams(vmem_limit_bytes=VMEM_LIMIT),
        cost_estimate=pl.CostEstimate(flops=10**8, bytes_accessed=1 * MIB, transcendentals=0),
        name="segment_plan",
    )(cell, worker)


def land_sums_kernel(
    pairs, slots, first_rows, arrived, cell, meta, area, water, cap, soil_in, porosity_in,
    drainage_in, _, __, through, lost, canopy_new, sums_out, soil, porosity, drainage, fetched,
    runoffs, evaps, sums, ready,
):
    layers, rows = soil.shape[:2]
    steps = ready.shape[0]
    block = rows // steps
    ahead = 4
    arrays = ((soil_in, soil), (porosity_in, porosity), (drainage_in, drainage))

    def part_of(step):
        return pl.ds(pl.multiple_of(step * block, block), block)

    def reads(step):
        return [
            pltpu.make_async_copy(
                source.at[:, part_of(step), :], target.at[:, part_of(step), :], ready.at[step, i]
            )
            for i, (source, target) in enumerate(arrays)
        ]

    def start_reads(step):
        for copy in reads(step):
            copy.start()

    def fetch(step):
        base = pl.multiple_of(step % 2 * (2 * block), 2 * block)
        for i in range(block):
            row = first_rows[step * block + i]
            fetched[pl.ds(base + 2 * i, 2), :] = arrived[pl.ds(row, 2, stride=pairs), :]

    def cascade(step):
        part = part_of(step)
        base = pl.multiple_of(step % 2 * (2 * block), 2 * block)
        index = cell[part, :]
        one = fetched[pl.ds(base, block, stride=2), :]
        two = fetched[pl.ds(base + 1, block, stride=2), :]
        odd = meta[part, :] >> 8
        loss = jnp.where(odd == 1, two, one)
        rain = lane_pick(jnp.where(odd == 1, one, two), index + odd * WINDOW)
        demand = lane_pick(loss, index)
        limit = lane_pick(loss, index + WINDOW)
        wetted = water[part, :] + rain
        flowing = jnp.maximum(wetted - cap[part, :], 0.0)
        retained = jnp.minimum(wetted, cap[part, :])
        canopy_loss = jnp.minimum(demand, retained)
        canopy_new[part, :] = retained - canopy_loss
        through[part, :] = flowing
        surface = jnp.zeros_like(flowing)
        for layer in range(layers):
            filled = soil[layer, part, :] + flowing
            excess = jnp.maximum(filled - porosity[layer, part, :], 0.0)
            surface = surface + excess
            filled = filled - excess
            flowing = drainage[layer, part, :] * filled
            if layer == 0:
                half = 0.5 * (filled - flowing)
                soil_loss = jnp.minimum(jnp.minimum(limit, demand - canopy_loss), half)
                lost[part, :] = soil_loss
                evaps[part, :] = area[part, :] * (canopy_loss + soil_loss)
        runoffs[part, :] = area[part, :] * (surface + flowing)

    def hand_back(start, count):
        part = pl.ds(start, count)
        shape = (2 * LANES, LANES)
        upto = onehot((iota(shape, 0) & 127) <= iota(shape, 1))
        patches = meta[part, :] & 255
        last = jnp.maximum(patches - 1, 0)
        here = iota((count, LANES), 1)
        picked = [
            lane_pick(matmul(jnp.concatenate(halves(value[part, :]), axis=1), upto), last)
            for value in (runoffs, evaps)
        ]
        reached = jnp.where(patches > 0, jnp.where(here < WINDOW, *picked), 0.0)
        before = jnp.where((here & (WINDOW - 1)) == 0, 0.0, pltpu.roll(reached, 1, 1))
        sums[...] = reached - before
        for i in range(count):
            sums_out[pl.ds(slots[start + i], 1), :] = sums[pl.ds(i, 1), :]

    start_reads(0)
    fetch(0)
    start_reads(1)
    sums_out[...] = jnp.zeros_like(sums_out)
    start_reads(2)
    start_reads(3)

    def round_of(step, carry):
        for copy in reads(step):
            copy.wait()

        @pl.when(step + ahead < steps)
        def _():
            start_reads(step + ahead)

        cascade(step)
        fetch(jnp.minimum(step + 1, steps - 1))
        return carry

    for half in range(2):
        lax.fori_loop(half * steps // 2, (half + 1) * steps // 2, round_of, 0)
        hand_back(half * rows // 2, rows // 2)


def land_sums(
    sums_shape, pairs, slots, first_rows, arrived, cell, meta, area, water, cap, soil, porosity,
    drainage, after,
):
    layers, rows = soil.shape[:2]
    steps = 10
    block = rows // steps
    near = pl.BlockSpec(memory_space=pltpu.VMEM)
    far = pl.BlockSpec(memory_space=pltpu.HBM)
    return pl.pallas_call(
        functools.partial(land_sums_kernel, pairs),
        in_specs=[pl.BlockSpec(memory_space=pltpu.SMEM)] * 2 + [near] * 6 + [far] * 3
        + [pl.BlockSpec(memory_space=pl.ANY)] * 2,
        out_specs=[near] * 4,
        scratch_shapes=[pltpu.VMEM(soil.shape, jnp.float32)] * 3
        + [pltpu.VMEM((4 * block, LANES), jnp.float32)]
        + [pltpu.VMEM((rows, LANES), jnp.float32)] * 2
        + [pltpu.VMEM((rows // 2, LANES), jnp.float32), pltpu.SemaphoreType.DMA((steps, 3))],
        out_shape=[jax.ShapeDtypeStruct((rows, LANES), jnp.float32)] * 3
        + [jax.ShapeDtypeStruct(sums_shape, jnp.float32)],
        compiler_params=pltpu.CompilerParams(vmem_limit_bytes=VMEM_LIMIT),
        cost_estimate=pl.CostEstimate(flops=10**8, bytes_accessed=20 * MIB, transcendentals=0),
        name="land_sums",
    )(
        slots, first_rows, arrived, cell, meta, area, water, cap,
        in_hbm(soil), in_hbm(porosity), in_hbm(drainage), *after,
    )


def new_soil_kernel(through, lost, canopy, soil, porosity, drainage, *rest):
    soil_new, canopy_new = rest[-2:]
    layers, block = soil.shape[:2]
    chunk = 48
    canopy_new[...] = canopy[...]
    for start in range(0, block, chunk):
        part = pl.ds(start, chunk)
        flowing = through[part, :]
        for layer in range(layers):
            filled = soil[layer, part, :] + flowing
            filled = filled - jnp.maximum(filled - porosity[layer, part, :], 0.0)
            flowing = drainage[layer, part, :] * filled
            middle = filled - flowing
            soil_new[layer, part, :] = middle - lost[part, :] if layer == 0 else middle


def new_soil(first, last, through, lost, canopy, soil, porosity, drainage, made=(), after=None):
    layers, rows = soil.shape[:2]
    block = 96
    flat = pl.BlockSpec((block, LANES), lambda i: (first + i, 0))
    deep = pl.BlockSpec((layers, block, LANES), lambda i: (0, first + i, 0))
    anywhere = pl.BlockSpec(memory_space=pl.ANY)
    more = [in_hbm(value) for value in made] + ([] if after is None else [after])
    return pl.pallas_call(
        new_soil_kernel,
        grid=(last - first,),
        in_specs=[flat, flat, flat, deep, deep, deep] + [anywhere] * len(more),
        out_specs=[deep, flat],
        out_shape=(
            jax.ShapeDtypeStruct(soil.shape, jnp.float32),
            jax.ShapeDtypeStruct((rows, LANES), jnp.float32),
        ),
        input_output_aliases={6: 0, 7: 1} if made else {},
        compiler_params=pltpu.CompilerParams(vmem_limit_bytes=VMEM_LIMIT),
        cost_estimate=pl.CostEstimate(
            flops=10**8, bytes_accessed=3 * MIB * (last - first), transcendentals=0
        ),
        name="new_soil",
    )(through, lost, canopy, in_hbm(soil), in_hbm(porosity), in_hbm(drainage), *more)


def halo_parts(value, axis, dim, width):
    count, length = (lax.axis_size(axis), value.shape[dim])
    up = [(i, i + 1) for i in range(count - 1)]
    down = [(j, i) for i, j in up]
    last = lax.slice_in_dim(value, length - width, length, axis=dim)
    initial = lax.slice_in_dim(value, 0, width, axis=dim)
    return lax.ppermute(last, axis, up), lax.ppermute(initial, axis, down)


def edge_columns_kernel(tall, _, first, last):
    arrays, height, width = tall.shape
    for number in range(arrays):
        values = tall[number]
        values = jnp.concatenate([values, jnp.zeros((LANES - height, width), jnp.float32)], axis=0)
        columns = jnp.transpose(values)
        part = pl.ds(number * ITERS, ITERS)
        first[part, :] = columns[:ITERS]
        last[part, :] = columns[width - ITERS :]


def edge_columns(tall, after):
    shape = jax.ShapeDtypeStruct((2 * ITERS, LANES), jnp.float32)
    return pl.pallas_call(
        edge_columns_kernel,
        in_specs=[pl.BlockSpec(memory_space=pltpu.VMEM), pl.BlockSpec(memory_space=pl.ANY)],
        out_shape=(shape, shape),
        compiler_params=pltpu.CompilerParams(vmem_limit_bytes=VMEM_LIMIT),
        cost_estimate=pl.CostEstimate(flops=10**6, bytes_accessed=10**5, transcendentals=0),
        name="edge_columns",
    )(tall, after)


def extended(own, strip):
    height = own.shape[0]

    def column_strip(right):
        middle, above, below = strip(0, right), strip(-1, right), strip(1, right)
        return jnp.concatenate(
            [
                middle[:, :height],
                below[:, :ITERS],
                above[:, height - ITERS : height],
                jnp.zeros((ITERS, LANES - height - 2 * ITERS), jnp.float32),
            ],
            axis=1,
        )

    gap = jnp.zeros((LANES - 2 * ITERS, LANES), jnp.float32)
    sides = jnp.concatenate([column_strip(1), gap, column_strip(-1)], axis=0)
    sides = jnp.transpose(sides)[: height + 2 * ITERS]
    tall = jnp.concatenate([own, strip(1, 0), strip(-1, 0)], axis=0)
    return jnp.concatenate([tall, sides], axis=1)


def neighbour(down, right):
    row, column = lax.axis_index("region") + down, lax.axis_index("col") + right
    there = (row >= 0) & (row < lax.axis_size("region"))
    there &= (column >= 0) & (column < lax.axis_size("col"))
    return jnp.where(there, row * lax.axis_size("col") + column, 0), jnp.where(there, 1.0, 0.0)


def static_halo_kernel(tall, before, after, out):
    height, width = tall.shape[1:]
    gap = jnp.zeros((LANES - 2 * ITERS, LANES), jnp.float32)
    for number in range(2):
        part = pl.ds(number * ITERS, ITERS)
        sides = jnp.transpose(jnp.concatenate([after[part, :], gap, before[part, :]], axis=0))
        out[number, :, :width] = tall[number]
        out[number, :, width:] = sides[:height]


def static_halo(tall, before, after):
    arrays, height, width = tall.shape
    return pl.pallas_call(
        static_halo_kernel,
        out_shape=jax.ShapeDtypeStruct((arrays, height, width + LANES), jnp.float32),
        compiler_params=pltpu.CompilerParams(vmem_limit_bytes=VMEM_LIMIT),
        cost_estimate=pl.CostEstimate(flops=10**6, bytes_accessed=10**6, transcendentals=0),
        name="static_halo",
    )(tall, before, after)


def river_kernel(state, strips, fixed, _, out):
    height, width = state.shape

    def strip(down, right):
        device, there = neighbour(down, right)
        return strips[pl.ds(device * ITERS, ITERS), :] * there

    storage = extended(state[...], strip)
    rate = fixed[0]
    code = fixed[1]
    rows, cols = storage.shape
    for _ in range(ITERS):
        outflow = rate * storage
        inflow = jnp.zeros_like(storage)
        for col_step in (-1, 0, 1):
            column = jnp.zeros_like(storage)
            for bit, (row_step, step) in enumerate(directions):
                if step != col_step:
                    continue
                leaving = jnp.where(code == float(1 << bit), outflow, 0.0)
                if row_step:
                    leaving = pltpu.roll(leaving, row_step % rows, 0)
                column = column + leaving
            if col_step:
                column = pltpu.roll(column, col_step % cols, 1)
            inflow = inflow + column
        storage = storage - outflow + inflow
    out[...] = storage[:height, :width]


def river(state, strips, fixed, after):
    return pl.pallas_call(
        river_kernel,
        in_specs=[pl.BlockSpec(memory_space=pltpu.VMEM)] * 3 + [pl.BlockSpec(memory_space=pl.ANY)],
        out_shape=jax.ShapeDtypeStruct(state.shape, jnp.float32),
        compiler_params=pltpu.CompilerParams(vmem_limit_bytes=VMEM_LIMIT),
        cost_estimate=pl.CostEstimate(flops=10**7, bytes_accessed=1 * MIB, transcendentals=0),
        name="river_steps",
    )(state, strips, fixed, in_hbm(after))


def exchange(value):
    return lax.all_to_all(value, axes, split_axis=0, concat_axis=0, tiled=True)


def shards(
    forcing,
    river_storage,
    river_rate,
    flow_code,
    home_slot,
    home_offset,
    worker_list,
    patch_cell,
    patch_area,
    canopy_water,
    canopy_cap,
    soil_water,
    porosity,
    drainage,
):
    homes = lax.axis_size("region") * lax.axis_size("col")
    capacity = home_slot.shape[1] // homes
    grid_rows, grid_cols = river_storage.shape
    lane_rows = grid_rows * grid_cols // LANES
    outgoing = pack(
        homes, capacity, home_slot, home_offset, forcing.reshape(3, lane_rows, LANES)
    )
    arrived = exchange(outgoing)
    home = worker_list // capacity
    position = worker_list - home * capacity
    pairs = capacity // 2
    first_rows = home * (3 * pairs) + position // 2 + position % 2 * pairs
    meta = segment_plan(patch_cell, worker_list[:, None])
    fixed = jnp.stack([river_rate, flow_code.astype(jnp.float32)])
    above, below = halo_parts(fixed, "region", 1, ITERS)
    through, lost, canopy, sums = land_sums(
        (homes * capacity, LANES), pairs, worker_list, first_rows, arrived, patch_cell, meta,
        patch_area, canopy_water, canopy_cap, soil_water, porosity, drainage, (above, below),
    )
    returned = exchange(sums)
    layers_of = (through, lost, canopy, soil_water, porosity, drainage)
    blocks = worker_list.shape[0] // 96
    early = blocks * 3 // 5
    made = new_soil(0, early, *layers_of)
    code, place = unpack_plan(homes, capacity, lane_rows, home_slot, home_offset)
    fixed = jnp.concatenate([fixed, below, above], axis=1)
    initial, last = edge_columns(fixed, sums)
    count = lax.axis_size("col")
    before = lax.ppermute(last, "col", [(i, i + 1) for i in range(count - 1)])
    after = lax.ppermute(initial, "col", [(i + 1, i) for i in range(count - 1)])
    fixed = static_halo(fixed, before, after)
    cell_runoff, storage, strips = unpack_runoff(
        homes, returned, code, place, river_storage.reshape(lane_rows, LANES), fixed,
        in_hbm(made[1]),
    )
    soil_new, canopy_new = new_soil(early, blocks, *layers_of, made, strips)
    cell_evap = unpack_evap(returned, code, place)
    river_new = river(
        storage.reshape(river_storage.shape), exchange(strips), fixed, canopy_new
    )
    return (
        soil_new,
        canopy_new,
        cell_runoff.reshape(river_storage.shape),
        cell_evap.reshape(river_storage.shape),
        river_new,
    )


def solution(mesh):
    placed = (
        P(None, "region", "col"),
        P("region", "col"),
        P("region", "col"),
        P("region", "col"),
        P(("region", "col"), None),
        P(("region", "col"), None),
        P(("region", "col")),
        P(("region", "col"), None),
        P(("region", "col"), None),
        P(("region", "col"), None),
        P(("region", "col"), None),
        P(None, ("region", "col"), None),
        P(None, ("region", "col"), None),
        P(None, ("region", "col"), None),
    )
    return jax.shard_map(
        shards,
        mesh=mesh,
        in_specs=placed,
        out_specs=(
            P(None, ("region", "col"), None),
            P(("region", "col"), None),
            P("region", "col"),
            P("region", "col"),
            P("region", "col"),
        ),
        check_vma=False,
    )
```

```python
import functools

import jax
import jax.numpy as jnp
from jax import lax
from jax.experimental import pallas as pl
from jax.experimental.pallas import tpu as pltpu
from jax.sharding import PartitionSpec as P

ITERS = 4
WINDOW = 64
LANES = 128
MIB = 1024 * 1024
VMEM_LIMIT = 24 * MIB

directions = ((0, 1), (1, 1), (1, 0), (1, -1), (0, -1), (-1, -1), (-1, 0), (-1, 1))
axes = ("region", "col")


def iota(shape, dim):
    return lax.broadcasted_iota(jnp.int32, shape, dim)


def onehot(mask):
    return jnp.where(mask, jnp.float32(1.0), jnp.float32(0.0)).astype(jnp.bfloat16)


def lane_pick(values, index):
    return jnp.take_along_axis(values, index, axis=1, mode="promise_in_bounds")


def in_hbm(value):
    return pltpu.with_memory_space_constraint(value, pltpu.HBM)


def thirds(value):
    high = value.astype(jnp.bfloat16)
    rest = value - high.astype(jnp.float32)
    middle = rest.astype(jnp.bfloat16)
    low = (rest - middle.astype(jnp.float32)).astype(jnp.bfloat16)
    return high, middle, low


def halves(value):
    high = value.astype(jnp.bfloat16)
    return high, (value - high.astype(jnp.float32)).astype(jnp.bfloat16)


def matmul(a, b, a_dim=1, b_dim=0):
    return lax.dot_general(
        a, b, (((a_dim,), (b_dim,)), ((), ())), preferred_element_type=jnp.float32
    )


def slot_factors(slot, offset, homes, capacity):
    slots = slot.shape[1]
    worker = slot // capacity if capacity & (capacity - 1) else slot >> (capacity.bit_length() - 1)
    position = slot - worker * capacity
    by_worker = onehot(iota((homes, slots), 0) == worker)
    at_position = iota((capacity, slots), 0) == position
    row = jnp.where(at_position, ((offset >> 7) + 1).astype(jnp.float32), 0.0)
    lane = jnp.where(at_position, (offset & 127).astype(jnp.float32), 0.0)
    return by_worker, row.astype(jnp.bfloat16), lane.astype(jnp.bfloat16)


def slot_table(slot, offset, homes, capacity, split=False):
    slots = slot.shape[1]
    by_worker, row, lane = slot_factors(slot, offset, homes, capacity)
    table = matmul(by_worker, jnp.concatenate([row, lane], axis=0), 1, 1)
    groups = 2 if split else 1
    spread = jnp.broadcast_to(
        table[:, None, :], (homes, capacity // groups, 2 * capacity)
    ).reshape(slots // groups, 2 * capacity)
    spread = jnp.concatenate([spread] * groups, axis=0)
    number = iota(spread.shape, 0)
    position = number % (capacity // groups) * groups + number // (slots // groups)
    place = position == iota(spread.shape, 1) % capacity
    return jnp.where(place, spread, 0.0).astype(jnp.bfloat16)


def slot_columns(table):
    width = table.shape[1]
    shape = (width, 2 * LANES)
    gather = onehot((iota(shape, 0) >= width // 2) == (iota(shape, 1) >= LANES))
    columns = matmul(table, gather).astype(jnp.int32)
    return columns[:, :LANES] - 1, columns[:, LANES:]


def slot_rows(slot, offset, homes, capacity):
    slots = slot.shape[1]
    by_worker, row, lane = slot_factors(slot, offset, homes, capacity)
    table = matmul(jnp.concatenate([row, lane], axis=0), by_worker, 1, 1).astype(jnp.bfloat16)
    number = iota((1, slots), 1)
    worker = number // capacity
    position = number - worker * capacity
    spread = matmul(table, onehot(iota((homes, slots), 0) == worker))
    at_position = iota((capacity, slots), 0) == position
    rows = jnp.sum(jnp.where(at_position, spread[:capacity], 0.0), axis=0, keepdims=True)
    lanes = jnp.sum(jnp.where(at_position, spread[capacity:], 0.0), axis=0, keepdims=True)
    return rows.astype(jnp.int32) - 1, lanes.astype(jnp.int32)


def pack_kernel(
    homes, capacity, slot_in, offset_in, forcing_in, out, slot, offset, forcing, rain, ready
):
    copies = [
        pltpu.make_async_copy(source, target, ready.at[i])
        for i, (source, target) in enumerate(
            ((slot_in, slot), (offset_in, offset), (forcing_in, forcing))
        )
    ]
    for copy in copies:
        copy.start()
    slots = slot.shape[1]
    pairs = capacity // 2
    lane_rows = forcing.shape[1]
    copies[0].wait()
    copies[1].wait()
    places = slot_table(slot[...], offset[...], homes, capacity, True)
    copies[2].wait()
    parts = []
    for var in range(3):
        here = forcing[var]
        following = jnp.concatenate([here[1:], here[:1]], axis=0)
        parts += [here, following]
    table = jnp.concatenate(thirds(jnp.concatenate(parts, axis=1)), axis=0)
    chunk = 128
    here = iota((chunk, LANES), 1)
    for start in range(0, slots, chunk):
        odd = start >= slots // 2
        row, lane = slot_columns(places[start : start + chunk])
        shape = (chunk, 3 * lane_rows)
        wide = jnp.concatenate([row, row], axis=1)[:, : 3 * lane_rows]
        pick = onehot(wide == iota(shape, 1) % lane_rows)
        rows = matmul(pick, table)
        after = here >= lane
        joined = [
            jnp.where(
                after,
                rows[:, 2 * var * LANES : (2 * var + 1) * LANES],
                rows[:, (2 * var + 1) * LANES : (2 * var + 2) * LANES],
            )
            for var in range(3)
        ]
        first = (here + lane) & 127
        second = (first + WINDOW) & 127
        losses = jnp.where(
            here < WINDOW, lane_pick(joined[1], first), lane_pick(joined[2], second)
        )
        base = start - slots // 2 if odd else start
        if odd:
            rains = jnp.where(
                here < WINDOW, rain[pl.ds(base, chunk), :], lane_pick(joined[0], second)
            )
        else:
            rain[pl.ds(base, chunk), :] = lane_pick(joined[0], first)
        for part in range(0, chunk, pairs):
            place = (base + part) * 3
            if odd:
                out[pl.ds(place + pairs, pairs), :] = rains[part : part + pairs]
                out[pl.ds(place + 2 * pairs, pairs), :] = losses[part : part + pairs]
            else:
                out[pl.ds(place, pairs), :] = losses[part : part + pairs]


def pack(homes, capacity, slot, offset, forcing):
    slots = slot.shape[1]
    return pl.pallas_call(
        functools.partial(pack_kernel, homes, capacity),
        in_specs=[pl.BlockSpec(memory_space=pltpu.HBM)] * 3,
        out_shape=jax.ShapeDtypeStruct((slots + slots // 2, LANES), jnp.float32),
        scratch_shapes=[
            pltpu.VMEM(slot.shape, jnp.int32),
            pltpu.VMEM(offset.shape, jnp.int32),
            pltpu.VMEM(forcing.shape, jnp.float32),
            pltpu.VMEM((slots // 2, LANES), jnp.float32),
            pltpu.SemaphoreType.DMA((3,)),
        ],
        compiler_params=pltpu.CompilerParams(vmem_limit_bytes=VMEM_LIMIT),
        cost_estimate=pl.CostEstimate(flops=10**9, bytes_accessed=2 * MIB, transcendentals=0),
        name="pack_forcing",
    )(in_hbm(slot), in_hbm(offset), in_hbm(forcing))


def unpack_plan_kernel(homes, capacity, lane_rows, slot, offset, code, place):
    slots = slot.shape[1]
    row, lane = slot_columns(slot_table(slot[...], offset[...], homes, capacity))
    here = iota((slots, LANES), 1)
    index = (here - lane) & 127
    inside = (index < WINDOW) & (row >= 0)
    code[...] = jnp.where(inside, index + jnp.where(here >= lane, 0, LANES), -1)
    row_lane, _ = slot_rows(slot[...], offset[...], homes, capacity)
    place[...] = onehot(iota((lane_rows, slots), 0) == row_lane)


def unpack_plan(homes, capacity, lane_rows, slot, offset):
    slots = slot.shape[1]
    return pl.pallas_call(
        functools.partial(unpack_plan_kernel, homes, capacity, lane_rows),
        out_shape=(
            jax.ShapeDtypeStruct((slots, LANES), jnp.int32),
            jax.ShapeDtypeStruct((lane_rows, slots), jnp.bfloat16),
        ),
        compiler_params=pltpu.CompilerParams(vmem_limit_bytes=VMEM_LIMIT),
        cost_estimate=pl.CostEstimate(flops=10**9, bytes_accessed=2 * MIB, transcendentals=0),
        name="unpack_plan",
    )(slot, offset)


def strips_for_neighbours(state, rows):
    device = iota((rows, LANES), 0) // ITERS
    down = device // lax.axis_size("col") - lax.axis_index("region")
    right = device % lax.axis_size("col") - lax.axis_index("col")
    height, width = state.shape
    columns = jnp.transpose(state)
    empty = jnp.zeros((ITERS, LANES - height), jnp.float32)

    def repeated(strip):
        if strip.shape[1] < LANES:
            strip = jnp.concatenate([strip, empty], axis=1)
        return jnp.concatenate([strip] * (rows // ITERS), axis=0)

    near = (jnp.abs(down) <= 1).astype(jnp.int32)
    strips = jnp.zeros((rows, LANES), jnp.float32)
    strips = jnp.where((right == 0) & (down == 1), repeated(state[height - ITERS :]), strips)
    strips = jnp.where((right == 0) & (down == -1), repeated(state[:ITERS]), strips)
    strips = jnp.where((right == 1) & (near == 1), repeated(columns[width - ITERS :]), strips)
    return jnp.where((right == -1) & (near == 1), repeated(columns[:ITERS]), strips)


def cell_totals(arrived, code, place, first):
    lane_rows = place.shape[0]
    marks = code[...]
    window = lane_pick(arrived[...], (marks + first) & 127)
    placed = jnp.concatenate(
        [
            jnp.where((marks >= 0) & (marks < LANES), window, 0.0),
            jnp.where(marks >= LANES, window, 0.0),
        ],
        axis=1,
    )
    totals = matmul(place[...], jnp.concatenate(halves(placed), axis=1))
    totals = totals[:, :256] + totals[:, 256:]
    over = totals[:, LANES:]
    over = jnp.concatenate([over[lane_rows - 1 :], over[: lane_rows - 1]], axis=0)
    over = jnp.where(iota(over.shape, 0) == 0, 0.0, over)
    return totals[:, :LANES] + over


def unpack_runoff_kernel(arrived, code, place, river, _, __, runoff, storage, strips):
    total = cell_totals(arrived, code, place, 0)
    state = river[...] + total
    runoff[...] = total
    storage[...] = state
    strips[...] = strips_for_neighbours(state, strips.shape[0])


def unpack_runoff(homes, arrived, code, place, river, *after):
    shape = jax.ShapeDtypeStruct((place.shape[0], LANES), jnp.float32)
    strips = jax.ShapeDtypeStruct((homes * ITERS, LANES), jnp.float32)
    return pl.pallas_call(
        unpack_runoff_kernel,
        in_specs=[pl.BlockSpec(memory_space=pltpu.VMEM)] * 4
        + [pl.BlockSpec(memory_space=pl.ANY)] * 2,
        out_shape=(shape, shape, strips),
        compiler_params=pltpu.CompilerParams(vmem_limit_bytes=VMEM_LIMIT),
        cost_estimate=pl.CostEstimate(flops=10**9, bytes_accessed=1 * MIB, transcendentals=0),
        name="unpack_runoff",
    )(arrived, code, place, river, *after)


def unpack_evap_kernel(arrived, code, place, evap):
    evap[...] = cell_totals(arrived, code, place, WINDOW)


def unpack_evap(arrived, code, place):
    return pl.pallas_call(
        unpack_evap_kernel,
        out_shape=jax.ShapeDtypeStruct((place.shape[0], LANES), jnp.float32),
        compiler_params=pltpu.CompilerParams(vmem_limit_bytes=VMEM_LIMIT),
        cost_estimate=pl.CostEstimate(flops=10**9, bytes_accessed=1 * MIB, transcendentals=0),
        name="unpack_evap",
    )(arrived, code, place)


def segment_plan_kernel(cell, worker, meta):
    chunk = 96
    for start in range(0, cell.shape[0], chunk):
        values = cell[pl.ds(start, chunk), :]
        target = iota(values.shape, 1) & (WINDOW - 1)
        count = jnp.zeros_like(values)
        for step in (64, 32, 16, 8, 4, 2, 1):
            probe = lane_pick(values, count + (step - 1))
            count = jnp.where(probe <= target, count + step, count)
        count = jnp.where(lane_pick(values, count) <= target, count + 1, count)
        odd = worker[pl.ds(start, chunk), :] & 1
        meta[pl.ds(start, chunk), :] = count + (odd << 8)


def segment_plan(cell, worker):
    return pl.pallas_call(
        segment_plan_kernel,
        out_shape=jax.ShapeDtypeStruct(cell.shape, jnp.int32),
        compiler_params=pltpu.CompilerParams(vmem_limit_bytes=VMEM_LIMIT),
        cost_estimate=pl.CostEstimate(flops=10**8, bytes_accessed=1 * MIB, transcendentals=0),
        name="segment_plan",
    )(cell, worker)


def land_sums_kernel(
    pairs, slots, first_rows, arrived, cell, meta, area, water, cap, soil_in, porosity_in,
    drainage_in, _, __, through, lost, canopy_new, sums_out, soil, porosity, drainage, fetched,
    runoffs, evaps, ready,
):
    layers, rows = soil.shape[:2]
    steps = ready.shape[0]
    block = rows // steps
    chunk = block // 2
    arrays = ((soil_in, soil), (porosity_in, porosity), (drainage_in, drainage))

    def part_of(step):
        return pl.ds(step * block, block)

    def reads(step):
        return [
            pltpu.make_async_copy(
                source.at[:, part_of(step), :], target.at[:, part_of(step), :], ready.at[step, i]
            )
            for i, (source, target) in enumerate(arrays)
        ]

    def fetch(step):
        for i in range(step * block, (step + 1) * block):
            fetched[pl.ds(2 * i, 2), :] = arrived[pl.ds(first_rows[i], 2, stride=pairs), :]

    def cascade(start):
        part = pl.ds(start, chunk)
        index = cell[part, :]
        one = fetched[pl.ds(2 * start, chunk, stride=2), :]
        two = fetched[pl.ds(2 * start + 1, chunk, stride=2), :]
        odd = meta[part, :] >> 8
        loss = jnp.where(odd == 1, two, one)
        rain = lane_pick(jnp.where(odd == 1, one, two), index + odd * WINDOW)
        demand = lane_pick(loss, index)
        limit = lane_pick(loss, index + WINDOW)
        wetted = water[part, :] + rain
        flowing = jnp.maximum(wetted - cap[part, :], 0.0)
        retained = jnp.minimum(wetted, cap[part, :])
        canopy_loss = jnp.minimum(demand, retained)
        canopy_new[part, :] = retained - canopy_loss
        through[part, :] = flowing
        surface = jnp.zeros_like(flowing)
        for layer in range(layers):
            filled = soil[layer, part, :] + flowing
            excess = jnp.maximum(filled - porosity[layer, part, :], 0.0)
            surface = surface + excess
            filled = filled - excess
            flowing = drainage[layer, part, :] * filled
            if layer == 0:
                half = 0.5 * (filled - flowing)
                soil_loss = jnp.minimum(jnp.minimum(limit, demand - canopy_loss), half)
                lost[part, :] = soil_loss
                evaps[part, :] = area[part, :] * (canopy_loss + soil_loss)
        runoffs[part, :] = area[part, :] * (surface + flowing)

    def scan(step):
        part = part_of(step)
        shape = (2 * LANES, LANES)
        upto = onehot((iota(shape, 0) & 127) <= iota(shape, 1))
        patches = meta[part, :] & 255
        last = jnp.maximum(patches - 1, 0)
        here = iota((block, LANES), 1)
        picked = [
            lane_pick(matmul(jnp.concatenate(halves(value[part, :]), axis=1), upto), last)
            for value in (runoffs, evaps)
        ]
        reached = jnp.where(patches > 0, jnp.where(here < WINDOW, *picked), 0.0)
        before = jnp.where((here & (WINDOW - 1)) == 0, 0.0, pltpu.roll(reached, 1, 1))
        runoffs[part, :] = reached - before

    def hand_back(step):
        for i in range(step * block, (step + 1) * block):
            sums_out[pl.ds(slots[i], 1), :] = runoffs[pl.ds(i, 1), :]

    for step in range(steps):
        for copy in reads(step):
            copy.start()
    sums_out[...] = jnp.zeros_like(sums_out)
    for step in range(steps):
        fetch(step)
    for step in range(steps + 2):
        if step < steps:
            for copy in reads(step):
                copy.wait()
            for start in range(step * block, (step + 1) * block, chunk):
                cascade(start)
        if 1 <= step <= steps:
            scan(step - 1)
        if step >= 2:
            hand_back(step - 2)


def land_sums(
    sums_shape, pairs, slots, first_rows, arrived, cell, meta, area, water, cap, soil, porosity,
    drainage, after,
):
    layers, rows = soil.shape[:2]
    steps = 5
    near = pl.BlockSpec(memory_space=pltpu.VMEM)
    far = pl.BlockSpec(memory_space=pltpu.HBM)
    return pl.pallas_call(
        functools.partial(land_sums_kernel, pairs),
        in_specs=[pl.BlockSpec(memory_space=pltpu.SMEM)] * 2 + [near] * 6 + [far] * 3
        + [pl.BlockSpec(memory_space=pl.ANY)] * 2,
        out_specs=[near] * 4,
        scratch_shapes=[pltpu.VMEM(soil.shape, jnp.float32)] * 3
        + [pltpu.VMEM((2 * rows, LANES), jnp.float32)]
        + [pltpu.VMEM((rows, LANES), jnp.float32)] * 2
        + [pltpu.SemaphoreType.DMA((steps, 3))],
        out_shape=[jax.ShapeDtypeStruct((rows, LANES), jnp.float32)] * 3
        + [jax.ShapeDtypeStruct(sums_shape, jnp.float32)],
        compiler_params=pltpu.CompilerParams(vmem_limit_bytes=VMEM_LIMIT),
        cost_estimate=pl.CostEstimate(flops=10**8, bytes_accessed=20 * MIB, transcendentals=0),
        name="land_sums",
    )(
        slots, first_rows, arrived, cell, meta, area, water, cap,
        in_hbm(soil), in_hbm(porosity), in_hbm(drainage), *after,
    )


def new_soil_kernel(through, lost, canopy, soil, porosity, drainage, *rest):
    soil_new, canopy_new = rest[-2:]
    layers, block = soil.shape[:2]
    chunk = 48
    canopy_new[...] = canopy[...]
    for start in range(0, block, chunk):
        part = pl.ds(start, chunk)
        flowing = through[part, :]
        for layer in range(layers):
            filled = soil[layer, part, :] + flowing
            filled = filled - jnp.maximum(filled - porosity[layer, part, :], 0.0)
            flowing = drainage[layer, part, :] * filled
            middle = filled - flowing
            soil_new[layer, part, :] = middle - lost[part, :] if layer == 0 else middle


def new_soil(first, last, through, lost, canopy, soil, porosity, drainage, made=(), after=None):
    layers, rows = soil.shape[:2]
    block = 96
    flat = pl.BlockSpec((block, LANES), lambda i: (first + i, 0))
    deep = pl.BlockSpec((layers, block, LANES), lambda i: (0, first + i, 0))
    anywhere = pl.BlockSpec(memory_space=pl.ANY)
    more = [in_hbm(value) for value in made] + ([] if after is None else [after])
    return pl.pallas_call(
        new_soil_kernel,
        grid=(last - first,),
        in_specs=[flat, flat, flat, deep, deep, deep] + [anywhere] * len(more),
        out_specs=[deep, flat],
        out_shape=(
            jax.ShapeDtypeStruct(soil.shape, jnp.float32),
            jax.ShapeDtypeStruct((rows, LANES), jnp.float32),
        ),
        input_output_aliases={6: 0, 7: 1} if made else {},
        compiler_params=pltpu.CompilerParams(vmem_limit_bytes=VMEM_LIMIT),
        cost_estimate=pl.CostEstimate(
            flops=10**8, bytes_accessed=3 * MIB * (last - first), transcendentals=0
        ),
        name="new_soil",
    )(through, lost, canopy, in_hbm(soil), in_hbm(porosity), in_hbm(drainage), *more)


def halo_parts(value, axis, dim, width):
    count, length = (lax.axis_size(axis), value.shape[dim])
    up = [(i, i + 1) for i in range(count - 1)]
    down = [(j, i) for i, j in up]
    last = lax.slice_in_dim(value, length - width, length, axis=dim)
    initial = lax.slice_in_dim(value, 0, width, axis=dim)
    return lax.ppermute(last, axis, up), lax.ppermute(initial, axis, down)


def edge_columns_kernel(tall, _, first, last):
    arrays, height, width = tall.shape
    for number in range(arrays):
        values = tall[number]
        values = jnp.concatenate([values, jnp.zeros((LANES - height, width), jnp.float32)], axis=0)
        columns = jnp.transpose(values)
        part = pl.ds(number * ITERS, ITERS)
        first[part, :] = columns[:ITERS]
        last[part, :] = columns[width - ITERS :]


def edge_columns(tall, after):
    shape = jax.ShapeDtypeStruct((2 * ITERS, LANES), jnp.float32)
    return pl.pallas_call(
        edge_columns_kernel,
        in_specs=[pl.BlockSpec(memory_space=pltpu.VMEM), pl.BlockSpec(memory_space=pl.ANY)],
        out_shape=(shape, shape),
        compiler_params=pltpu.CompilerParams(vmem_limit_bytes=VMEM_LIMIT),
        cost_estimate=pl.CostEstimate(flops=10**6, bytes_accessed=10**5, transcendentals=0),
        name="edge_columns",
    )(tall, after)


def extended(own, strip):
    height = own.shape[0]

    def column_strip(right):
        middle, above, below = strip(0, right), strip(-1, right), strip(1, right)
        return jnp.concatenate(
            [
                middle[:, :height],
                below[:, :ITERS],
                above[:, height - ITERS : height],
                jnp.zeros((ITERS, LANES - height - 2 * ITERS), jnp.float32),
            ],
            axis=1,
        )

    gap = jnp.zeros((LANES - 2 * ITERS, LANES), jnp.float32)
    sides = jnp.concatenate([column_strip(1), gap, column_strip(-1)], axis=0)
    sides = jnp.transpose(sides)[: height + 2 * ITERS]
    tall = jnp.concatenate([own, strip(1, 0), strip(-1, 0)], axis=0)
    return jnp.concatenate([tall, sides], axis=1)


def neighbour(down, right):
    row, column = lax.axis_index("region") + down, lax.axis_index("col") + right
    there = (row >= 0) & (row < lax.axis_size("region"))
    there &= (column >= 0) & (column < lax.axis_size("col"))
    return jnp.where(there, row * lax.axis_size("col") + column, 0), jnp.where(there, 1.0, 0.0)


def static_halo_kernel(tall, before, after, out):
    height, width = tall.shape[1:]
    gap = jnp.zeros((LANES - 2 * ITERS, LANES), jnp.float32)
    for number in range(2):
        part = pl.ds(number * ITERS, ITERS)
        sides = jnp.transpose(jnp.concatenate([after[part, :], gap, before[part, :]], axis=0))
        out[number, :, :width] = tall[number]
        out[number, :, width:] = sides[:height]


def static_halo(tall, before, after):
    arrays, height, width = tall.shape
    return pl.pallas_call(
        static_halo_kernel,
        out_shape=jax.ShapeDtypeStruct((arrays, height, width + LANES), jnp.float32),
        compiler_params=pltpu.CompilerParams(vmem_limit_bytes=VMEM_LIMIT),
        cost_estimate=pl.CostEstimate(flops=10**6, bytes_accessed=10**6, transcendentals=0),
        name="static_halo",
    )(tall, before, after)


def river_kernel(state, strips, fixed, _, out):
    height, width = state.shape

    def strip(down, right):
        device, there = neighbour(down, right)
        return strips[pl.ds(device * ITERS, ITERS), :] * there

    storage = extended(state[...], strip)
    rate = fixed[0]
    code = fixed[1]
    rows, cols = storage.shape
    for _ in range(ITERS):
        outflow = rate * storage
        inflow = jnp.zeros_like(storage)
        for col_step in (-1, 0, 1):
            column = jnp.zeros_like(storage)
            for bit, (row_step, step) in enumerate(directions):
                if step != col_step:
                    continue
                leaving = jnp.where(code == float(1 << bit), outflow, 0.0)
                if row_step:
                    leaving = pltpu.roll(leaving, row_step % rows, 0)
                column = column + leaving
            if col_step:
                column = pltpu.roll(column, col_step % cols, 1)
            inflow = inflow + column
        storage = storage - outflow + inflow
    out[...] = storage[:height, :width]


def river(state, strips, fixed, after):
    return pl.pallas_call(
        river_kernel,
        in_specs=[pl.BlockSpec(memory_space=pltpu.VMEM)] * 3 + [pl.BlockSpec(memory_space=pl.ANY)],
        out_shape=jax.ShapeDtypeStruct(state.shape, jnp.float32),
        compiler_params=pltpu.CompilerParams(vmem_limit_bytes=VMEM_LIMIT),
        cost_estimate=pl.CostEstimate(flops=10**7, bytes_accessed=1 * MIB, transcendentals=0),
        name="river_steps",
    )(state, strips, fixed, in_hbm(after))


def exchange(value):
    return lax.all_to_all(value, axes, split_axis=0, concat_axis=0, tiled=True)


def shards(
    forcing,
    river_storage,
    river_rate,
    flow_code,
    home_slot,
    home_offset,
    worker_list,
    patch_cell,
    patch_area,
    canopy_water,
    canopy_cap,
    soil_water,
    porosity,
    drainage,
):
    homes = lax.axis_size("region") * lax.axis_size("col")
    capacity = home_slot.shape[1] // homes
    grid_rows, grid_cols = river_storage.shape
    lane_rows = grid_rows * grid_cols // LANES
    outgoing = pack(
        homes, capacity, home_slot, home_offset, forcing.reshape(3, lane_rows, LANES)
    )
    arrived = exchange(outgoing)
    home = worker_list // capacity
    position = worker_list - home * capacity
    pairs = capacity // 2
    first_rows = home * (3 * pairs) + position // 2 + position % 2 * pairs
    meta = segment_plan(patch_cell, worker_list[:, None])
    fixed = jnp.stack([river_rate, flow_code.astype(jnp.float32)])
    above, below = halo_parts(fixed, "region", 1, ITERS)
    through, lost, canopy, sums = land_sums(
        (homes * capacity, LANES), pairs, worker_list, first_rows, arrived, patch_cell, meta,
        patch_area, canopy_water, canopy_cap, soil_water, porosity, drainage, (above, below),
    )
    returned = exchange(sums)
    layers_of = (through, lost, canopy, soil_water, porosity, drainage)
    blocks = worker_list.shape[0] // 96
    early = blocks * 3 // 5
    made = new_soil(0, early, *layers_of)
    code, place = unpack_plan(homes, capacity, lane_rows, home_slot, home_offset)
    fixed = jnp.concatenate([fixed, below, above], axis=1)
    initial, last = edge_columns(fixed, sums)
    count = lax.axis_size("col")
    before = lax.ppermute(last, "col", [(i, i + 1) for i in range(count - 1)])
    after = lax.ppermute(initial, "col", [(i + 1, i) for i in range(count - 1)])
    fixed = static_halo(fixed, before, after)
    cell_runoff, storage, strips = unpack_runoff(
        homes, returned, code, place, river_storage.reshape(lane_rows, LANES), fixed,
        in_hbm(made[1]),
    )
    soil_new, canopy_new = new_soil(early, blocks, *layers_of, made, strips)
    cell_evap = unpack_evap(returned, code, place)
    river_new = river(
        storage.reshape(river_storage.shape), exchange(strips), fixed, canopy_new
    )
    return (
        soil_new,
        canopy_new,
        cell_runoff.reshape(river_storage.shape),
        cell_evap.reshape(river_storage.shape),
        river_new,
    )


def solution(mesh):
    placed = (
        P(None, "region", "col"),
        P("region", "col"),
        P("region", "col"),
        P("region", "col"),
        P(("region", "col"), None),
        P(("region", "col"), None),
        P(("region", "col")),
        P(("region", "col"), None),
        P(("region", "col"), None),
        P(("region", "col"), None),
        P(("region", "col"), None),
        P(None, ("region", "col"), None),
        P(None, ("region", "col"), None),
        P(None, ("region", "col"), None),
    )
    return jax.shard_map(
        shards,
        mesh=mesh,
        in_specs=placed,
        out_specs=(
            P(None, ("region", "col"), None),
            P(("region", "col"), None),
            P("region", "col"),
            P("region", "col"),
            P("region", "col"),
        ),
        check_vma=False,
    )
```

```python
import functools

import jax
import jax.numpy as jnp
from jax import lax
from jax.experimental import pallas as pl
from jax.experimental.pallas import tpu as pltpu
from jax.sharding import PartitionSpec as P

ITERS = 4
WINDOW = 64
LANES = 128
MIB = 1024 * 1024
VMEM_LIMIT = 24 * MIB

directions = ((0, 1), (1, 1), (1, 0), (1, -1), (0, -1), (-1, -1), (-1, 0), (-1, 1))
axes = ("region", "col")


def iota(shape, dim):
    return lax.broadcasted_iota(jnp.int32, shape, dim)


def onehot(mask):
    return jnp.where(mask, jnp.float32(1.0), jnp.float32(0.0)).astype(jnp.bfloat16)


def lane_pick(values, index):
    return jnp.take_along_axis(values, index, axis=1, mode="promise_in_bounds")


def in_hbm(value):
    return pltpu.with_memory_space_constraint(value, pltpu.HBM)


def thirds(value):
    high = value.astype(jnp.bfloat16)
    rest = value - high.astype(jnp.float32)
    middle = rest.astype(jnp.bfloat16)
    low = (rest - middle.astype(jnp.float32)).astype(jnp.bfloat16)
    return high, middle, low


def halves(value):
    high = value.astype(jnp.bfloat16)
    return high, (value - high.astype(jnp.float32)).astype(jnp.bfloat16)


def matmul(a, b, a_dim=1, b_dim=0):
    return lax.dot_general(
        a, b, (((a_dim,), (b_dim,)), ((), ())), preferred_element_type=jnp.float32
    )


def slot_factors(slot, offset, homes, capacity):
    slots = slot.shape[1]
    worker = slot // capacity if capacity & (capacity - 1) else slot >> (capacity.bit_length() - 1)
    position = slot - worker * capacity
    by_worker = onehot(iota((homes, slots), 0) == worker)
    at_position = iota((capacity, slots), 0) == position
    row = jnp.where(at_position, ((offset >> 7) + 1).astype(jnp.float32), 0.0)
    lane = jnp.where(at_position, (offset & 127).astype(jnp.float32), 0.0)
    return by_worker, row.astype(jnp.bfloat16), lane.astype(jnp.bfloat16)


def slot_table(slot, offset, homes, capacity, split=False):
    slots = slot.shape[1]
    by_worker, row, lane = slot_factors(slot, offset, homes, capacity)
    table = matmul(by_worker, jnp.concatenate([row, lane], axis=0), 1, 1)
    groups = 2 if split else 1
    spread = jnp.broadcast_to(
        table[:, None, :], (homes, capacity // groups, 2 * capacity)
    ).reshape(slots // groups, 2 * capacity)
    spread = jnp.concatenate([spread] * groups, axis=0)
    number = iota(spread.shape, 0)
    position = number % (capacity // groups) * groups + number // (slots // groups)
    place = position == iota(spread.shape, 1) % capacity
    return jnp.where(place, spread, 0.0).astype(jnp.bfloat16)


def slot_columns(table):
    width = table.shape[1]
    shape = (width, 2 * LANES)
    gather = onehot((iota(shape, 0) >= width // 2) == (iota(shape, 1) >= LANES))
    columns = matmul(table, gather).astype(jnp.int32)
    return columns[:, :LANES] - 1, columns[:, LANES:]


def slot_rows(slot, offset, homes, capacity):
    slots = slot.shape[1]
    by_worker, row, lane = slot_factors(slot, offset, homes, capacity)
    table = matmul(jnp.concatenate([row, lane], axis=0), by_worker, 1, 1).astype(jnp.bfloat16)
    number = iota((1, slots), 1)
    worker = number // capacity
    position = number - worker * capacity
    spread = matmul(table, onehot(iota((homes, slots), 0) == worker))
    at_position = iota((capacity, slots), 0) == position
    rows = jnp.sum(jnp.where(at_position, spread[:capacity], 0.0), axis=0, keepdims=True)
    lanes = jnp.sum(jnp.where(at_position, spread[capacity:], 0.0), axis=0, keepdims=True)
    return rows.astype(jnp.int32) - 1, lanes.astype(jnp.int32)


def pack_kernel(
    homes, capacity, slot_in, offset_in, forcing_in, out, slot, offset, forcing, rain, ready
):
    copies = [
        pltpu.make_async_copy(source, target, ready.at[i])
        for i, (source, target) in enumerate(
            ((slot_in, slot), (offset_in, offset), (forcing_in, forcing))
        )
    ]
    for copy in copies:
        copy.start()
    slots = slot.shape[1]
    pairs = capacity // 2
    lane_rows = forcing.shape[1]
    copies[0].wait()
    copies[1].wait()
    places = slot_table(slot[...], offset[...], homes, capacity, True)
    copies[2].wait()
    limit = pltpu.roll(forcing[2], WINDOW, 1)
    above = jnp.concatenate([limit[lane_rows - 1 :], limit[: lane_rows - 1]], axis=0)
    limit = jnp.where(iota(limit.shape, 1) < WINDOW, above, limit)
    parts = []
    for own in (forcing[0], forcing[1], limit):
        parts += [own, jnp.concatenate([own[1:], own[:1]], axis=0)]
    table = jnp.concatenate(thirds(jnp.concatenate(parts, axis=1)), axis=0)
    chunk = 128
    here = iota((chunk, LANES), 1)
    for start in range(0, slots, chunk):
        odd = start >= slots // 2
        row, lane = slot_columns(places[start : start + chunk])
        shape = (chunk, 3 * lane_rows)
        wide = jnp.concatenate([row, row], axis=1)[:, : 3 * lane_rows]
        pick = onehot(wide == iota(shape, 1) % lane_rows)
        rows = matmul(pick, table)
        after = here >= lane
        joined = [
            jnp.where(
                after,
                rows[:, 2 * var * LANES : (2 * var + 1) * LANES],
                rows[:, (2 * var + 1) * LANES : (2 * var + 2) * LANES],
            )
            for var in range(3)
        ]
        first = (here + lane) & 127
        second = (first + WINDOW) & 127
        demanded = ((here - lane) & 127) < WINDOW
        losses = lane_pick(jnp.where(demanded, joined[1], joined[2]), first)
        base = start - slots // 2 if odd else start
        if odd:
            rains = jnp.where(
                here < WINDOW, rain[pl.ds(base, chunk), :], lane_pick(joined[0], second)
            )
        else:
            rain[pl.ds(base, chunk), :] = lane_pick(joined[0], first)
        for part in range(0, chunk, pairs):
            place = (base + part) * 3
            if odd:
                out[pl.ds(place + pairs, pairs), :] = rains[part : part + pairs]
                out[pl.ds(place + 2 * pairs, pairs), :] = losses[part : part + pairs]
            else:
                out[pl.ds(place, pairs), :] = losses[part : part + pairs]


def pack(homes, capacity, slot, offset, forcing):
    slots = slot.shape[1]
    return pl.pallas_call(
        functools.partial(pack_kernel, homes, capacity),
        in_specs=[pl.BlockSpec(memory_space=pltpu.HBM)] * 3,
        out_shape=jax.ShapeDtypeStruct((slots + slots // 2, LANES), jnp.float32),
        scratch_shapes=[
            pltpu.VMEM(slot.shape, jnp.int32),
            pltpu.VMEM(offset.shape, jnp.int32),
            pltpu.VMEM(forcing.shape, jnp.float32),
            pltpu.VMEM((slots // 2, LANES), jnp.float32),
            pltpu.SemaphoreType.DMA((3,)),
        ],
        compiler_params=pltpu.CompilerParams(vmem_limit_bytes=VMEM_LIMIT),
        cost_estimate=pl.CostEstimate(flops=10**9, bytes_accessed=2 * MIB, transcendentals=0),
        name="pack_forcing",
    )(in_hbm(slot), in_hbm(offset), in_hbm(forcing))


def unpack_plan_kernel(homes, capacity, lane_rows, slot, offset, code, place):
    slots = slot.shape[1]
    row, lane = slot_columns(slot_table(slot[...], offset[...], homes, capacity))
    here = iota((slots, LANES), 1)
    index = (here - lane) & 127
    inside = (index < WINDOW) & (row >= 0)
    code[...] = jnp.where(inside, index + jnp.where(here >= lane, 0, LANES), -1)
    row_lane, _ = slot_rows(slot[...], offset[...], homes, capacity)
    place[...] = onehot(iota((lane_rows, slots), 0) == row_lane)


def unpack_plan(homes, capacity, lane_rows, slot, offset):
    slots = slot.shape[1]
    return pl.pallas_call(
        functools.partial(unpack_plan_kernel, homes, capacity, lane_rows),
        out_shape=(
            jax.ShapeDtypeStruct((slots, LANES), jnp.int32),
            jax.ShapeDtypeStruct((lane_rows, slots), jnp.bfloat16),
        ),
        compiler_params=pltpu.CompilerParams(vmem_limit_bytes=VMEM_LIMIT),
        cost_estimate=pl.CostEstimate(flops=10**9, bytes_accessed=2 * MIB, transcendentals=0),
        name="unpack_plan",
    )(slot, offset)


def strips_for_neighbours(state, rows):
    device = iota((rows, LANES), 0) // ITERS
    down = device // lax.axis_size("col") - lax.axis_index("region")
    right = device % lax.axis_size("col") - lax.axis_index("col")
    height, width = state.shape
    columns = jnp.transpose(state)
    empty = jnp.zeros((ITERS, LANES - height), jnp.float32)

    def repeated(strip):
        if strip.shape[1] < LANES:
            strip = jnp.concatenate([strip, empty], axis=1)
        return jnp.concatenate([strip] * (rows // ITERS), axis=0)

    near = (jnp.abs(down) <= 1).astype(jnp.int32)
    strips = jnp.zeros((rows, LANES), jnp.float32)
    strips = jnp.where((right == 0) & (down == 1), repeated(state[height - ITERS :]), strips)
    strips = jnp.where((right == 0) & (down == -1), repeated(state[:ITERS]), strips)
    strips = jnp.where((right == 1) & (near == 1), repeated(columns[width - ITERS :]), strips)
    return jnp.where((right == -1) & (near == 1), repeated(columns[:ITERS]), strips)


def cell_totals(arrived, code, place, first):
    lane_rows = place.shape[0]
    marks = code[...]
    window = lane_pick(arrived[...], (marks + first) & 127)
    placed = jnp.concatenate(
        [
            jnp.where((marks >= 0) & (marks < LANES), window, 0.0),
            jnp.where(marks >= LANES, window, 0.0),
        ],
        axis=1,
    )
    totals = matmul(place[...], jnp.concatenate(halves(placed), axis=1))
    totals = totals[:, :256] + totals[:, 256:]
    over = totals[:, LANES:]
    over = jnp.concatenate([over[lane_rows - 1 :], over[: lane_rows - 1]], axis=0)
    over = jnp.where(iota(over.shape, 0) == 0, 0.0, over)
    return totals[:, :LANES] + over


def unpack_runoff_kernel(arrived, code, place, river, _, __, runoff, storage, strips):
    total = cell_totals(arrived, code, place, 0)
    state = river[...] + total
    runoff[...] = total
    storage[...] = state
    strips[...] = strips_for_neighbours(state, strips.shape[0])


def unpack_runoff(homes, arrived, code, place, river, *after):
    shape = jax.ShapeDtypeStruct((place.shape[0], LANES), jnp.float32)
    strips = jax.ShapeDtypeStruct((homes * ITERS, LANES), jnp.float32)
    return pl.pallas_call(
        unpack_runoff_kernel,
        in_specs=[pl.BlockSpec(memory_space=pltpu.VMEM)] * 4
        + [pl.BlockSpec(memory_space=pl.ANY)] * 2,
        out_shape=(shape, shape, strips),
        compiler_params=pltpu.CompilerParams(vmem_limit_bytes=VMEM_LIMIT),
        cost_estimate=pl.CostEstimate(flops=10**9, bytes_accessed=1 * MIB, transcendentals=0),
        name="unpack_runoff",
    )(arrived, code, place, river, *after)


def unpack_evap_kernel(arrived, code, place, evap):
    evap[...] = cell_totals(arrived, code, place, WINDOW)


def unpack_evap(arrived, code, place):
    return pl.pallas_call(
        unpack_evap_kernel,
        out_shape=jax.ShapeDtypeStruct((place.shape[0], LANES), jnp.float32),
        compiler_params=pltpu.CompilerParams(vmem_limit_bytes=VMEM_LIMIT),
        cost_estimate=pl.CostEstimate(flops=10**9, bytes_accessed=1 * MIB, transcendentals=0),
        name="unpack_evap",
    )(arrived, code, place)


def segment_plan_kernel(cell, worker, meta):
    chunk = 96
    for start in range(0, cell.shape[0], chunk):
        values = cell[pl.ds(start, chunk), :]
        target = iota(values.shape, 1) & (WINDOW - 1)
        count = jnp.zeros_like(values)
        for step in (64, 32, 16, 8, 4, 2, 1):
            probe = lane_pick(values, count + (step - 1))
            count = jnp.where(probe <= target, count + step, count)
        count = jnp.where(lane_pick(values, count) <= target, count + 1, count)
        odd = worker[pl.ds(start, chunk), :] & 1
        meta[pl.ds(start, chunk), :] = count + (odd << 8)


def segment_plan(cell, worker):
    return pl.pallas_call(
        segment_plan_kernel,
        out_shape=jax.ShapeDtypeStruct(cell.shape, jnp.int32),
        compiler_params=pltpu.CompilerParams(vmem_limit_bytes=VMEM_LIMIT),
        cost_estimate=pl.CostEstimate(flops=10**8, bytes_accessed=1 * MIB, transcendentals=0),
        name="segment_plan",
    )(cell, worker)


def stage_kernel(soil_in, porosity_in, drainage_in, _, soil, porosity, drainage, ready):
    part = pl.ds(0, soil.shape[1])
    pairs = ((soil_in, soil), (porosity_in, porosity), (drainage_in, drainage))
    copies = [
        pltpu.make_async_copy(source.at[:, part, :], target, ready.at[i])
        for i, (source, target) in enumerate(pairs)
    ]
    for copy in copies:
        copy.start()
    for copy in copies:
        copy.wait()


def stage(rows, soil, porosity, drainage, after):
    far = pl.BlockSpec(memory_space=pltpu.HBM)
    shape = (soil.shape[0], rows, LANES)
    return pl.pallas_call(
        stage_kernel,
        in_specs=[far] * 3 + [pl.BlockSpec(memory_space=pl.ANY)],
        out_specs=[pl.BlockSpec(memory_space=pltpu.VMEM)] * 3,
        out_shape=[pltpu.VMEM(shape, jnp.float32)] * 3,
        scratch_shapes=[pltpu.SemaphoreType.DMA((3,))],
        compiler_params=pltpu.CompilerParams(vmem_limit_bytes=4 * MIB),
        cost_estimate=pl.CostEstimate(flops=0, bytes_accessed=4 * MIB, transcendentals=0),
        name="stage_soil",
    )(in_hbm(soil), in_hbm(porosity), in_hbm(drainage), after)


def land_sums_kernel(
    pairs, slots, first_rows, arrived, cell, meta, area, water, cap, soil_first, porosity_first,
    drainage_first, soil_in, porosity_in, drainage_in, _, __, through, lost, canopy_new,
    sums_out, soil_rest, porosity_rest, drainage_rest, fetched, runoffs, evaps, ready,
):
    layers, block = soil_first.shape[:2]
    rows = cell.shape[0]
    steps = rows // block
    chunk = block // 2
    staged = (soil_first, porosity_first, drainage_first)
    rest = (soil_rest, porosity_rest, drainage_rest)
    sources = (soil_in, porosity_in, drainage_in)

    def part_of(step):
        return pl.ds(step * block, block)

    def reads(step):
        return [
            pltpu.make_async_copy(
                source.at[:, part_of(step), :],
                target.at[:, part_of(step - 1), :],
                ready.at[step - 1, i],
            )
            for i, (source, target) in enumerate(zip(sources, rest))
        ]

    def fetch(step):
        for i in range(step * block, (step + 1) * block):
            fetched[pl.ds(2 * i, 2), :] = arrived[pl.ds(first_rows[i], 2, stride=pairs), :]

    def cascade(start):
        part = pl.ds(start, chunk)
        index = cell[part, :]
        one = fetched[pl.ds(2 * start, chunk, stride=2), :]
        two = fetched[pl.ds(2 * start + 1, chunk, stride=2), :]
        odd = meta[part, :] >> 8
        loss = jnp.where(odd == 1, two, one)
        rain = lane_pick(jnp.where(odd == 1, one, two), index + odd * WINDOW)
        demand = lane_pick(loss, index)
        limit = lane_pick(loss, index + WINDOW)
        wetted = water[part, :] + rain
        flowing = jnp.maximum(wetted - cap[part, :], 0.0)
        retained = jnp.minimum(wetted, cap[part, :])
        canopy_loss = jnp.minimum(demand, retained)
        canopy_new[part, :] = retained - canopy_loss
        through[part, :] = flowing
        surface = jnp.zeros_like(flowing)
        soil, porosity, drainage = staged if start < block else rest
        local = pl.ds(start if start < block else start - block, chunk)
        for layer in range(layers):
            filled = soil[layer, local, :] + flowing
            excess = jnp.maximum(filled - porosity[layer, local, :], 0.0)
            surface = surface + excess
            filled = filled - excess
            flowing = drainage[layer, local, :] * filled
            if layer == 0:
                half = 0.5 * (filled - flowing)
                soil_loss = jnp.minimum(jnp.minimum(limit, demand - canopy_loss), half)
                lost[part, :] = soil_loss
                evaps[part, :] = area[part, :] * (canopy_loss + soil_loss)
        runoffs[part, :] = area[part, :] * (surface + flowing)

    def scan(step):
        part = part_of(step)
        shape = (2 * LANES, LANES)
        upto = onehot((iota(shape, 0) & 127) <= iota(shape, 1))
        patches = meta[part, :] & 255
        last = jnp.maximum(patches - 1, 0)
        here = iota((block, LANES), 1)
        picked = [
            lane_pick(matmul(jnp.concatenate(halves(value[part, :]), axis=1), upto), last)
            for value in (runoffs, evaps)
        ]
        reached = jnp.where(patches > 0, jnp.where(here < WINDOW, *picked), 0.0)
        before = jnp.where((here & (WINDOW - 1)) == 0, 0.0, pltpu.roll(reached, 1, 1))
        runoffs[part, :] = reached - before

    def hand_back(step):
        for i in range(step * block, (step + 1) * block):
            sums_out[pl.ds(slots[i], 1), :] = runoffs[pl.ds(i, 1), :]

    for step in range(1, steps):
        for copy in reads(step):
            copy.start()
    sums_out[...] = jnp.zeros_like(sums_out)
    for step in range(steps):
        fetch(step)
    for step in range(steps + 2):
        if step < steps:
            for copy in reads(step) if step else ():
                copy.wait()
            for start in range(step * block, (step + 1) * block, chunk):
                cascade(start)
        if 1 <= step <= steps:
            scan(step - 1)
        if step >= 2:
            hand_back(step - 2)


def land_sums(
    sums_shape, pairs, slots, first_rows, arrived, cell, meta, area, water, cap, staged, soil,
    porosity, drainage, after,
):
    layers, rows = soil.shape[:2]
    block = staged[0].shape[1]
    steps = rows // block
    near = pl.BlockSpec(memory_space=pltpu.VMEM)
    far = pl.BlockSpec(memory_space=pltpu.HBM)
    return pl.pallas_call(
        functools.partial(land_sums_kernel, pairs),
        in_specs=[pl.BlockSpec(memory_space=pltpu.SMEM)] * 2 + [near] * 9 + [far] * 3
        + [pl.BlockSpec(memory_space=pl.ANY)] * 2,
        out_specs=[near] * 4,
        scratch_shapes=[pltpu.VMEM((layers, rows - block, LANES), jnp.float32)] * 3
        + [pltpu.VMEM((2 * rows, LANES), jnp.float32)]
        + [pltpu.VMEM((rows, LANES), jnp.float32)] * 2
        + [pltpu.SemaphoreType.DMA((steps - 1, 3))],
        out_shape=[jax.ShapeDtypeStruct((rows, LANES), jnp.float32)] * 3
        + [jax.ShapeDtypeStruct(sums_shape, jnp.float32)],
        compiler_params=pltpu.CompilerParams(vmem_limit_bytes=VMEM_LIMIT),
        cost_estimate=pl.CostEstimate(flops=10**8, bytes_accessed=20 * MIB, transcendentals=0),
        name="land_sums",
    )(
        slots, first_rows, arrived, cell, meta, area, water, cap,
        *(pltpu.with_memory_space_constraint(value, pltpu.VMEM) for value in staged),
        in_hbm(soil), in_hbm(porosity), in_hbm(drainage), *after,
    )


def new_soil_kernel(through, lost, canopy, soil, porosity, drainage, *rest):
    soil_new, canopy_new = rest[-2:]
    layers, block = soil.shape[:2]
    chunk = 48
    canopy_new[...] = canopy[...]
    for start in range(0, block, chunk):
        part = pl.ds(start, chunk)
        flowing = through[part, :]
        for layer in range(layers):
            filled = soil[layer, part, :] + flowing
            filled = filled - jnp.maximum(filled - porosity[layer, part, :], 0.0)
            flowing = drainage[layer, part, :] * filled
            middle = filled - flowing
            soil_new[layer, part, :] = middle - lost[part, :] if layer == 0 else middle


def new_soil(first, last, through, lost, canopy, soil, porosity, drainage, made=(), after=None):
    layers, rows = soil.shape[:2]
    block = 96
    flat = pl.BlockSpec((block, LANES), lambda i: (first + i, 0))
    deep = pl.BlockSpec((layers, block, LANES), lambda i: (0, first + i, 0))
    anywhere = pl.BlockSpec(memory_space=pl.ANY)
    more = [in_hbm(value) for value in made] + ([] if after is None else [after])
    return pl.pallas_call(
        new_soil_kernel,
        grid=(last - first,),
        in_specs=[flat, flat, flat, deep, deep, deep] + [anywhere] * len(more),
        out_specs=[deep, flat],
        out_shape=(
            jax.ShapeDtypeStruct(soil.shape, jnp.float32),
            jax.ShapeDtypeStruct((rows, LANES), jnp.float32),
        ),
        input_output_aliases={6: 0, 7: 1} if made else {},
        compiler_params=pltpu.CompilerParams(vmem_limit_bytes=VMEM_LIMIT),
        cost_estimate=pl.CostEstimate(
            flops=10**8, bytes_accessed=3 * MIB * (last - first), transcendentals=0
        ),
        name="new_soil",
    )(through, lost, canopy, in_hbm(soil), in_hbm(porosity), in_hbm(drainage), *more)


def halo_parts(value, axis, dim, width):
    count, length = (lax.axis_size(axis), value.shape[dim])
    up = [(i, i + 1) for i in range(count - 1)]
    down = [(j, i) for i, j in up]
    last = lax.slice_in_dim(value, length - width, length, axis=dim)
    initial = lax.slice_in_dim(value, 0, width, axis=dim)
    return lax.ppermute(last, axis, up), lax.ppermute(initial, axis, down)


def edge_columns_kernel(tall, _, first, last):
    arrays, height, width = tall.shape
    for number in range(arrays):
        values = tall[number]
        values = jnp.concatenate([values, jnp.zeros((LANES - height, width), jnp.float32)], axis=0)
        columns = jnp.transpose(values)
        part = pl.ds(number * ITERS, ITERS)
        first[part, :] = columns[:ITERS]
        last[part, :] = columns[width - ITERS :]


def edge_columns(tall, after):
    shape = jax.ShapeDtypeStruct((2 * ITERS, LANES), jnp.float32)
    return pl.pallas_call(
        edge_columns_kernel,
        in_specs=[pl.BlockSpec(memory_space=pltpu.VMEM), pl.BlockSpec(memory_space=pl.ANY)],
        out_shape=(shape, shape),
        compiler_params=pltpu.CompilerParams(vmem_limit_bytes=VMEM_LIMIT),
        cost_estimate=pl.CostEstimate(flops=10**6, bytes_accessed=10**5, transcendentals=0),
        name="edge_columns",
    )(tall, after)


def extended(own, strip):
    height = own.shape[0]

    def column_strip(right):
        middle, above, below = strip(0, right), strip(-1, right), strip(1, right)
        return jnp.concatenate(
            [
                middle[:, :height],
                below[:, :ITERS],
                above[:, height - ITERS : height],
                jnp.zeros((ITERS, LANES - height - 2 * ITERS), jnp.float32),
            ],
            axis=1,
        )

    gap = jnp.zeros((LANES - 2 * ITERS, LANES), jnp.float32)
    sides = jnp.concatenate([column_strip(1), gap, column_strip(-1)], axis=0)
    sides = jnp.transpose(sides)[: height + 2 * ITERS]
    tall = jnp.concatenate([own, strip(1, 0), strip(-1, 0)], axis=0)
    return jnp.concatenate([tall, sides], axis=1)


def neighbour(down, right):
    row, column = lax.axis_index("region") + down, lax.axis_index("col") + right
    there = (row >= 0) & (row < lax.axis_size("region"))
    there &= (column >= 0) & (column < lax.axis_size("col"))
    return jnp.where(there, row * lax.axis_size("col") + column, 0), jnp.where(there, 1.0, 0.0)


def static_halo_kernel(tall, before, after, out):
    height, width = tall.shape[1:]
    gap = jnp.zeros((LANES - 2 * ITERS, LANES), jnp.float32)
    for number in range(2):
        part = pl.ds(number * ITERS, ITERS)
        sides = jnp.transpose(jnp.concatenate([after[part, :], gap, before[part, :]], axis=0))
        out[number, :, :width] = tall[number]
        out[number, :, width:] = sides[:height]


def static_halo(tall, before, after):
    arrays, height, width = tall.shape
    return pl.pallas_call(
        static_halo_kernel,
        out_shape=jax.ShapeDtypeStruct((arrays, height, width + LANES), jnp.float32),
        compiler_params=pltpu.CompilerParams(vmem_limit_bytes=VMEM_LIMIT),
        cost_estimate=pl.CostEstimate(flops=10**6, bytes_accessed=10**6, transcendentals=0),
        name="static_halo",
    )(tall, before, after)


def river_kernel(state, strips, fixed, _, out):
    height, width = state.shape

    def strip(down, right):
        device, there = neighbour(down, right)
        return strips[pl.ds(device * ITERS, ITERS), :] * there

    storage = extended(state[...], strip)
    rate = fixed[0]
    code = fixed[1]
    rows, cols = storage.shape
    for _ in range(ITERS):
        outflow = rate * storage
        inflow = jnp.zeros_like(storage)
        for col_step in (-1, 0, 1):
            column = jnp.zeros_like(storage)
            for bit, (row_step, step) in enumerate(directions):
                if step != col_step:
                    continue
                leaving = jnp.where(code == float(1 << bit), outflow, 0.0)
                if row_step:
                    leaving = pltpu.roll(leaving, row_step % rows, 0)
                column = column + leaving
            if col_step:
                column = pltpu.roll(column, col_step % cols, 1)
            inflow = inflow + column
        storage = storage - outflow + inflow
    out[...] = storage[:height, :width]


def river(state, strips, fixed, after):
    return pl.pallas_call(
        river_kernel,
        in_specs=[pl.BlockSpec(memory_space=pltpu.VMEM)] * 3 + [pl.BlockSpec(memory_space=pl.ANY)],
        out_shape=jax.ShapeDtypeStruct(state.shape, jnp.float32),
        compiler_params=pltpu.CompilerParams(vmem_limit_bytes=VMEM_LIMIT),
        cost_estimate=pl.CostEstimate(flops=10**7, bytes_accessed=1 * MIB, transcendentals=0),
        name="river_steps",
    )(state, strips, fixed, in_hbm(after))


def exchange(value):
    return lax.all_to_all(value, axes, split_axis=0, concat_axis=0, tiled=True)


def shards(
    forcing,
    river_storage,
    river_rate,
    flow_code,
    home_slot,
    home_offset,
    worker_list,
    patch_cell,
    patch_area,
    canopy_water,
    canopy_cap,
    soil_water,
    porosity,
    drainage,
):
    homes = lax.axis_size("region") * lax.axis_size("col")
    capacity = home_slot.shape[1] // homes
    grid_rows, grid_cols = river_storage.shape
    lane_rows = grid_rows * grid_cols // LANES
    outgoing = pack(
        homes, capacity, home_slot, home_offset, forcing.reshape(3, lane_rows, LANES)
    )
    arrived = exchange(outgoing)
    home = worker_list // capacity
    position = worker_list - home * capacity
    pairs = capacity // 2
    first_rows = home * (3 * pairs) + position // 2 + position % 2 * pairs
    meta = segment_plan(patch_cell, worker_list[:, None])
    fixed = jnp.stack([river_rate, flow_code.astype(jnp.float32)])
    above, below = halo_parts(fixed, "region", 1, ITERS)
    staged = stage(96, soil_water, porosity, drainage, meta)
    through, lost, canopy, sums = land_sums(
        (homes * capacity, LANES), pairs, worker_list, first_rows, arrived, patch_cell, meta,
        patch_area, canopy_water, canopy_cap, staged, soil_water, porosity, drainage,
        (above, below),
    )
    returned = exchange(sums)
    layers_of = (through, lost, canopy, soil_water, porosity, drainage)
    blocks = worker_list.shape[0] // 96
    early = blocks * 3 // 5
    made = new_soil(0, early, *layers_of)
    code, place = unpack_plan(homes, capacity, lane_rows, home_slot, home_offset)
    fixed = jnp.concatenate([fixed, below, above], axis=1)
    initial, last = edge_columns(fixed, sums)
    count = lax.axis_size("col")
    before = lax.ppermute(last, "col", [(i, i + 1) for i in range(count - 1)])
    after = lax.ppermute(initial, "col", [(i + 1, i) for i in range(count - 1)])
    fixed = static_halo(fixed, before, after)
    cell_runoff, storage, strips = unpack_runoff(
        homes, returned, code, place, river_storage.reshape(lane_rows, LANES), fixed,
        in_hbm(made[1]),
    )
    soil_new, canopy_new = new_soil(early, blocks, *layers_of, made, strips)
    cell_evap = unpack_evap(returned, code, place)
    river_new = river(
        storage.reshape(river_storage.shape), exchange(strips), fixed, canopy_new
    )
    return (
        soil_new,
        canopy_new,
        cell_runoff.reshape(river_storage.shape),
        cell_evap.reshape(river_storage.shape),
        river_new,
    )


def solution(mesh):
    placed = (
        P(None, "region", "col"),
        P("region", "col"),
        P("region", "col"),
        P("region", "col"),
        P(("region", "col"), None),
        P(("region", "col"), None),
        P(("region", "col")),
        P(("region", "col"), None),
        P(("region", "col"), None),
        P(("region", "col"), None),
        P(("region", "col"), None),
        P(None, ("region", "col"), None),
        P(None, ("region", "col"), None),
        P(None, ("region", "col"), None),
    )
    return jax.shard_map(
        shards,
        mesh=mesh,
        in_specs=placed,
        out_specs=(
            P(None, ("region", "col"), None),
            P(("region", "col"), None),
            P("region", "col"),
            P("region", "col"),
            P("region", "col"),
        ),
        check_vma=False,
    )
```

```python
import functools

import jax
import jax.numpy as jnp
from jax import lax
from jax.experimental import pallas as pl
from jax.experimental.pallas import tpu as pltpu
from jax.sharding import PartitionSpec as P

ITERS = 4
WINDOW = 64
LANES = 128
MIB = 1024 * 1024
VMEM_LIMIT = 24 * MIB

directions = ((0, 1), (1, 1), (1, 0), (1, -1), (0, -1), (-1, -1), (-1, 0), (-1, 1))
axes = ("region", "col")


def iota(shape, dim):
    return lax.broadcasted_iota(jnp.int32, shape, dim)


def onehot(mask):
    return jnp.where(mask, jnp.float32(1.0), jnp.float32(0.0)).astype(jnp.bfloat16)


def lane_pick(values, index):
    return jnp.take_along_axis(values, index, axis=1, mode="promise_in_bounds")


def in_hbm(value):
    return pltpu.with_memory_space_constraint(value, pltpu.HBM)


def thirds(value):
    high = value.astype(jnp.bfloat16)
    rest = value - high.astype(jnp.float32)
    middle = rest.astype(jnp.bfloat16)
    low = (rest - middle.astype(jnp.float32)).astype(jnp.bfloat16)
    return high, middle, low


def halves(value):
    high = value.astype(jnp.bfloat16)
    return high, (value - high.astype(jnp.float32)).astype(jnp.bfloat16)


def matmul(a, b, a_dim=1, b_dim=0):
    return lax.dot_general(
        a, b, (((a_dim,), (b_dim,)), ((), ())), preferred_element_type=jnp.float32
    )


def slot_factors(slot, offset, homes, capacity):
    slots = slot.shape[1]
    worker = slot // capacity if capacity & (capacity - 1) else slot >> (capacity.bit_length() - 1)
    position = slot - worker * capacity
    by_worker = onehot(iota((homes, slots), 0) == worker)
    at_position = iota((capacity, slots), 0) == position
    row = jnp.where(at_position, ((offset >> 7) + 1).astype(jnp.float32), 0.0)
    lane = jnp.where(at_position, (offset & 127).astype(jnp.float32), 0.0)
    return by_worker, row.astype(jnp.bfloat16), lane.astype(jnp.bfloat16)


def slot_table(slot, offset, homes, capacity, split=False):
    slots = slot.shape[1]
    by_worker, row, lane = slot_factors(slot, offset, homes, capacity)
    table = matmul(by_worker, jnp.concatenate([row, lane], axis=0), 1, 1)
    groups = 2 if split else 1
    spread = jnp.broadcast_to(
        table[:, None, :], (homes, capacity // groups, 2 * capacity)
    ).reshape(slots // groups, 2 * capacity)
    spread = jnp.concatenate([spread] * groups, axis=0)
    number = iota(spread.shape, 0)
    position = number % (capacity // groups) * groups + number // (slots // groups)
    place = position == iota(spread.shape, 1) % capacity
    return jnp.where(place, spread, 0.0).astype(jnp.bfloat16)


def slot_columns(table):
    width = table.shape[1]
    shape = (width, 2 * LANES)
    gather = onehot((iota(shape, 0) >= width // 2) == (iota(shape, 1) >= LANES))
    columns = matmul(table, gather).astype(jnp.int32)
    return columns[:, :LANES] - 1, columns[:, LANES:]


def slot_rows(slot, offset, homes, capacity):
    slots = slot.shape[1]
    by_worker, row, lane = slot_factors(slot, offset, homes, capacity)
    table = matmul(jnp.concatenate([row, lane], axis=0), by_worker, 1, 1).astype(jnp.bfloat16)
    number = iota((1, slots), 1)
    worker = number // capacity
    position = number - worker * capacity
    spread = matmul(table, onehot(iota((homes, slots), 0) == worker))
    at_position = iota((capacity, slots), 0) == position
    rows = jnp.sum(jnp.where(at_position, spread[:capacity], 0.0), axis=0, keepdims=True)
    lanes = jnp.sum(jnp.where(at_position, spread[capacity:], 0.0), axis=0, keepdims=True)
    return rows.astype(jnp.int32) - 1, lanes.astype(jnp.int32)


def pack_kernel(
    homes, capacity, slot_in, offset_in, forcing_in, out, slot, offset, forcing, rain, ready
):
    copies = [
        pltpu.make_async_copy(source, target, ready.at[i])
        for i, (source, target) in enumerate(
            ((slot_in, slot), (offset_in, offset), (forcing_in, forcing))
        )
    ]
    for copy in copies:
        copy.start()
    slots = slot.shape[1]
    pairs = capacity // 2
    lane_rows = forcing.shape[1]
    copies[0].wait()
    copies[1].wait()
    places = slot_table(slot[...], offset[...], homes, capacity, True)
    copies[2].wait()
    limit = pltpu.roll(forcing[2], WINDOW, 1)
    above = jnp.concatenate([limit[lane_rows - 1 :], limit[: lane_rows - 1]], axis=0)
    limit = jnp.where(iota(limit.shape, 1) < WINDOW, above, limit)
    parts = []
    for own in (forcing[0], forcing[1], limit):
        parts += [own, jnp.concatenate([own[1:], own[:1]], axis=0)]
    table = jnp.concatenate(thirds(jnp.concatenate(parts, axis=1)), axis=0)
    chunk = 128
    here = iota((chunk, LANES), 1)
    for start in range(0, slots, chunk):
        odd = start >= slots // 2
        row, lane = slot_columns(places[start : start + chunk])
        shape = (chunk, 3 * lane_rows)
        wide = jnp.concatenate([row, row], axis=1)[:, : 3 * lane_rows]
        pick = onehot(wide == iota(shape, 1) % lane_rows)
        rows = matmul(pick, table)
        after = here >= lane
        joined = [
            jnp.where(
                after,
                rows[:, 2 * var * LANES : (2 * var + 1) * LANES],
                rows[:, (2 * var + 1) * LANES : (2 * var + 2) * LANES],
            )
            for var in range(3)
        ]
        first = (here + lane) & 127
        second = (first + WINDOW) & 127
        demanded = ((here - lane) & 127) < WINDOW
        losses = lane_pick(jnp.where(demanded, joined[1], joined[2]), first)
        base = start - slots // 2 if odd else start
        if odd:
            rains = jnp.where(
                here < WINDOW, rain[pl.ds(base, chunk), :], lane_pick(joined[0], second)
            )
        else:
            rain[pl.ds(base, chunk), :] = lane_pick(joined[0], first)
        for part in range(0, chunk, pairs):
            place = (base + part) * 3
            if odd:
                out[pl.ds(place + pairs, pairs), :] = rains[part : part + pairs]
                out[pl.ds(place + 2 * pairs, pairs), :] = losses[part : part + pairs]
            else:
                out[pl.ds(place, pairs), :] = losses[part : part + pairs]


def pack(homes, capacity, slot, offset, forcing):
    slots = slot.shape[1]
    return pl.pallas_call(
        functools.partial(pack_kernel, homes, capacity),
        in_specs=[pl.BlockSpec(memory_space=pltpu.HBM)] * 3,
        out_shape=jax.ShapeDtypeStruct((slots + slots // 2, LANES), jnp.float32),
        scratch_shapes=[
            pltpu.VMEM(slot.shape, jnp.int32),
            pltpu.VMEM(offset.shape, jnp.int32),
            pltpu.VMEM(forcing.shape, jnp.float32),
            pltpu.VMEM((slots // 2, LANES), jnp.float32),
            pltpu.SemaphoreType.DMA((3,)),
        ],
        compiler_params=pltpu.CompilerParams(vmem_limit_bytes=VMEM_LIMIT),
        cost_estimate=pl.CostEstimate(flops=10**9, bytes_accessed=2 * MIB, transcendentals=0),
        name="pack_forcing",
    )(in_hbm(slot), in_hbm(offset), in_hbm(forcing))


def unpack_plan_kernel(homes, capacity, lane_rows, slot, offset, code, place):
    slots = slot.shape[1]
    row, lane = slot_columns(slot_table(slot[...], offset[...], homes, capacity))
    here = iota((slots, LANES), 1)
    index = (here - lane) & 127
    inside = (index < WINDOW) & (row >= 0)
    code[...] = jnp.where(inside, index + jnp.where(here >= lane, 0, LANES), -1)
    row_lane, _ = slot_rows(slot[...], offset[...], homes, capacity)
    place[...] = onehot(iota((lane_rows, slots), 0) == row_lane)


def unpack_plan(homes, capacity, lane_rows, slot, offset):
    slots = slot.shape[1]
    return pl.pallas_call(
        functools.partial(unpack_plan_kernel, homes, capacity, lane_rows),
        out_shape=(
            jax.ShapeDtypeStruct((slots, LANES), jnp.int32),
            jax.ShapeDtypeStruct((lane_rows, slots), jnp.bfloat16),
        ),
        compiler_params=pltpu.CompilerParams(vmem_limit_bytes=VMEM_LIMIT),
        cost_estimate=pl.CostEstimate(flops=10**9, bytes_accessed=2 * MIB, transcendentals=0),
        name="unpack_plan",
    )(slot, offset)


def strips_for_neighbours(state, rows):
    device = iota((rows, LANES), 0) // ITERS
    down = device // lax.axis_size("col") - lax.axis_index("region")
    right = device % lax.axis_size("col") - lax.axis_index("col")
    height, width = state.shape
    columns = jnp.transpose(state)
    empty = jnp.zeros((ITERS, LANES - height), jnp.float32)

    def repeated(strip):
        if strip.shape[1] < LANES:
            strip = jnp.concatenate([strip, empty], axis=1)
        return jnp.concatenate([strip] * (rows // ITERS), axis=0)

    near = (jnp.abs(down) <= 1).astype(jnp.int32)
    strips = jnp.zeros((rows, LANES), jnp.float32)
    strips = jnp.where((right == 0) & (down == 1), repeated(state[height - ITERS :]), strips)
    strips = jnp.where((right == 0) & (down == -1), repeated(state[:ITERS]), strips)
    strips = jnp.where((right == 1) & (near == 1), repeated(columns[width - ITERS :]), strips)
    return jnp.where((right == -1) & (near == 1), repeated(columns[:ITERS]), strips)


def cell_totals(arrived, code, place, first):
    lane_rows = place.shape[0]
    marks = code[...]
    window = lane_pick(arrived[...], (marks + first) & 127)
    placed = jnp.concatenate(
        [
            jnp.where((marks >= 0) & (marks < LANES), window, 0.0),
            jnp.where(marks >= LANES, window, 0.0),
        ],
        axis=1,
    )
    totals = matmul(place[...], jnp.concatenate(halves(placed), axis=1))
    totals = totals[:, :256] + totals[:, 256:]
    over = totals[:, LANES:]
    over = jnp.concatenate([over[lane_rows - 1 :], over[: lane_rows - 1]], axis=0)
    over = jnp.where(iota(over.shape, 0) == 0, 0.0, over)
    return totals[:, :LANES] + over


def unpack_runoff_kernel(arrived, code, place, river, _, __, runoff, storage, strips):
    total = cell_totals(arrived, code, place, 0)
    state = river[...] + total
    runoff[...] = total
    storage[...] = state
    strips[...] = strips_for_neighbours(state, strips.shape[0])


def unpack_runoff(homes, arrived, code, place, river, *after):
    shape = jax.ShapeDtypeStruct((place.shape[0], LANES), jnp.float32)
    strips = jax.ShapeDtypeStruct((homes * ITERS, LANES), jnp.float32)
    return pl.pallas_call(
        unpack_runoff_kernel,
        in_specs=[pl.BlockSpec(memory_space=pltpu.VMEM)] * 4
        + [pl.BlockSpec(memory_space=pl.ANY)] * 2,
        out_shape=(shape, shape, strips),
        compiler_params=pltpu.CompilerParams(vmem_limit_bytes=VMEM_LIMIT),
        cost_estimate=pl.CostEstimate(flops=10**9, bytes_accessed=1 * MIB, transcendentals=0),
        name="unpack_runoff",
    )(arrived, code, place, river, *after)


def unpack_evap_kernel(arrived, code, place, evap):
    evap[...] = cell_totals(arrived, code, place, WINDOW)


def unpack_evap(arrived, code, place):
    return pl.pallas_call(
        unpack_evap_kernel,
        out_shape=jax.ShapeDtypeStruct((place.shape[0], LANES), jnp.float32),
        compiler_params=pltpu.CompilerParams(vmem_limit_bytes=VMEM_LIMIT),
        cost_estimate=pl.CostEstimate(flops=10**9, bytes_accessed=1 * MIB, transcendentals=0),
        name="unpack_evap",
    )(arrived, code, place)


def segment_plan_kernel(cell, worker, meta):
    chunk = 96
    for start in range(0, cell.shape[0], chunk):
        values = cell[pl.ds(start, chunk), :]
        target = iota(values.shape, 1) & (WINDOW - 1)
        count = jnp.zeros_like(values)
        for step in (64, 32, 16, 8, 4, 2, 1):
            probe = lane_pick(values, count + (step - 1))
            count = jnp.where(probe <= target, count + step, count)
        count = jnp.where(lane_pick(values, count) <= target, count + 1, count)
        odd = worker[pl.ds(start, chunk), :] & 1
        meta[pl.ds(start, chunk), :] = count + (odd << 8)


def segment_plan(cell, worker):
    return pl.pallas_call(
        segment_plan_kernel,
        out_shape=jax.ShapeDtypeStruct(cell.shape, jnp.int32),
        compiler_params=pltpu.CompilerParams(vmem_limit_bytes=VMEM_LIMIT),
        cost_estimate=pl.CostEstimate(flops=10**8, bytes_accessed=1 * MIB, transcendentals=0),
        name="segment_plan",
    )(cell, worker)


def layer_terms_kernel(soil, porosity, drainage, _, out):
    layers, block = soil.shape[:2]
    chunk = 48
    for start in range(0, block, chunk):
        part = pl.ds(start, chunk)
        share = inverse = None
        total = jnp.zeros((chunk, LANES), jnp.float32)
        for layer in range(layers):
            content, room = soil[layer, part, :], porosity[layer, part, :]
            if layer:
                content, room = content * inverse, room * inverse
            total = total + content
            out[0, layer, part, :] = room - total
            rate = drainage[layer, part, :]
            share = rate if layer == 0 else share * rate
            inverse = 1.0 / share
            out[0, layers + layer, part, :] = share
        out[0, 2 * layers, part, :] = total
        out[0, 2 * layers + 1, part, :] = soil[0, part, :]


def layer_terms(soil, porosity, drainage, after):
    layers, rows = soil.shape[:2]
    block = 96
    deep = pl.BlockSpec((layers, block, LANES), lambda i: (0, i, 0))
    shape = (rows // block, 2 * layers + 2, block, LANES)
    return pl.pallas_call(
        layer_terms_kernel,
        grid=(rows // block,),
        in_specs=[deep] * 3 + [pl.BlockSpec(memory_space=pl.ANY)],
        out_specs=pl.BlockSpec((1,) + shape[1:], lambda i: (i, 0, 0, 0)),
        out_shape=pltpu.HBM(shape, jnp.float32),
        compiler_params=pltpu.CompilerParams(vmem_limit_bytes=VMEM_LIMIT),
        cost_estimate=pl.CostEstimate(flops=10**8, bytes_accessed=19 * MIB, transcendentals=0),
        name="layer_terms",
    )(in_hbm(soil), in_hbm(porosity), in_hbm(drainage), after)


def land_sums_kernel(
    pairs, slots, first_rows, arrived, cell, meta, area, water, cap, terms_in, _, __, through,
    lost, canopy_new, sums_out, terms, fetched, runoffs, evaps, ready,
):
    steps, count, block = terms.shape[:3]
    layers = count // 2 - 1
    chunk = block // 2

    def part_of(step):
        return pl.ds(step * block, block)

    def reads(step):
        return [
            pltpu.make_async_copy(
                terms_in.at[step, part], terms.at[step, part], ready.at[step, i]
            )
            for i, part in enumerate((pl.ds(0, count // 2), pl.ds(count // 2, count // 2)))
        ]

    def fetch(step):
        for i in range(step * block, (step + 1) * block):
            fetched[pl.ds(2 * i, 2), :] = arrived[pl.ds(first_rows[i], 2, stride=pairs), :]

    def cascade(start):
        part = pl.ds(start, chunk)
        index = cell[part, :]
        one = fetched[pl.ds(2 * start, chunk, stride=2), :]
        two = fetched[pl.ds(2 * start + 1, chunk, stride=2), :]
        odd = meta[part, :] >> 8
        loss = jnp.where(odd == 1, two, one)
        rain = lane_pick(jnp.where(odd == 1, one, two), index + odd * WINDOW)
        demand = lane_pick(loss, index)
        limit = lane_pick(loss, index + WINDOW)
        wetted = water[part, :] + rain
        flowing = jnp.maximum(wetted - cap[part, :], 0.0)
        retained = jnp.minimum(wetted, cap[part, :])
        canopy_loss = jnp.minimum(demand, retained)
        canopy_new[part, :] = retained - canopy_loss
        through[part, :] = flowing
        step, local = start // block, pl.ds(start % block, chunk)
        surface = None
        for layer in range(layers):
            room = terms[step, layer, local, :]
            excess = jnp.maximum(flowing - room, 0.0)
            flowing = jnp.minimum(flowing, room)
            if layer == 0:
                surface = excess
                content = flowing + terms[step, 2 * layers + 1, local, :]
                half = 0.5 * (content - terms[step, layers, local, :] * content)
                soil_loss = jnp.minimum(jnp.minimum(limit, demand - canopy_loss), half)
                lost[part, :] = soil_loss
                evaps[part, :] = area[part, :] * (canopy_loss + soil_loss)
            else:
                surface = surface + terms[step, layers + layer - 1, local, :] * excess
        bottom = terms[step, 2 * layers - 1, local, :] * (
            flowing + terms[step, 2 * layers, local, :]
        )
        runoffs[part, :] = area[part, :] * (surface + bottom)

    def scan(step):
        part = part_of(step)
        shape = (2 * LANES, LANES)
        upto = onehot((iota(shape, 0) & 127) <= iota(shape, 1))
        patches = meta[part, :] & 255
        last = jnp.maximum(patches - 1, 0)
        here = iota((block, LANES), 1)
        picked = [
            lane_pick(matmul(jnp.concatenate(halves(value[part, :]), axis=1), upto), last)
            for value in (runoffs, evaps)
        ]
        reached = jnp.where(patches > 0, jnp.where(here < WINDOW, *picked), 0.0)
        before = jnp.where((here & (WINDOW - 1)) == 0, 0.0, pltpu.roll(reached, 1, 1))
        runoffs[part, :] = reached - before

    def hand_back(step):
        for i in range(step * block, (step + 1) * block):
            sums_out[pl.ds(slots[i], 1), :] = runoffs[pl.ds(i, 1), :]

    for step in range(steps):
        for copy in reads(step):
            copy.start()
    sums_out[...] = jnp.zeros_like(sums_out)
    for step in range(steps):
        fetch(step)
    for step in range(steps + 2):
        if step < steps:
            for copy in reads(step):
                copy.wait()
            for start in range(step * block, (step + 1) * block, chunk):
                cascade(start)
        if 1 <= step <= steps:
            scan(step - 1)
        if step >= 2:
            hand_back(step - 2)


def land_sums(
    sums_shape, pairs, slots, first_rows, arrived, cell, meta, area, water, cap, terms, after
):
    rows = cell.shape[0]
    near = pl.BlockSpec(memory_space=pltpu.VMEM)
    return pl.pallas_call(
        functools.partial(land_sums_kernel, pairs),
        in_specs=[pl.BlockSpec(memory_space=pltpu.SMEM)] * 2 + [near] * 6
        + [pl.BlockSpec(memory_space=pltpu.HBM)] + [pl.BlockSpec(memory_space=pl.ANY)] * 2,
        out_specs=[near] * 4,
        scratch_shapes=[
            pltpu.VMEM(terms.shape, jnp.float32),
            pltpu.VMEM((2 * rows, LANES), jnp.float32),
            pltpu.VMEM((rows, LANES), jnp.float32),
            pltpu.VMEM((rows, LANES), jnp.float32),
            pltpu.SemaphoreType.DMA((terms.shape[0], 2)),
        ],
        out_shape=[jax.ShapeDtypeStruct((rows, LANES), jnp.float32)] * 3
        + [jax.ShapeDtypeStruct(sums_shape, jnp.float32)],
        compiler_params=pltpu.CompilerParams(vmem_limit_bytes=VMEM_LIMIT),
        cost_estimate=pl.CostEstimate(flops=10**8, bytes_accessed=20 * MIB, transcendentals=0),
        name="land_sums",
    )(
        slots, first_rows, arrived, cell, meta, area, water, cap,
        in_hbm(terms), *after,
    )


def new_soil_kernel(through, lost, canopy, soil, porosity, drainage, *rest):
    soil_new, canopy_new = rest[-2:]
    layers, block = soil.shape[:2]
    chunk = 48
    canopy_new[...] = canopy[...]
    for start in range(0, block, chunk):
        part = pl.ds(start, chunk)
        flowing = through[part, :]
        for layer in range(layers):
            filled = soil[layer, part, :] + flowing
            filled = filled - jnp.maximum(filled - porosity[layer, part, :], 0.0)
            flowing = drainage[layer, part, :] * filled
            middle = filled - flowing
            soil_new[layer, part, :] = middle - lost[part, :] if layer == 0 else middle


def new_soil(first, last, through, lost, canopy, soil, porosity, drainage, made=(), after=None):
    layers, rows = soil.shape[:2]
    block = 96
    flat = pl.BlockSpec((block, LANES), lambda i: (first + i, 0))
    deep = pl.BlockSpec((layers, block, LANES), lambda i: (0, first + i, 0))
    anywhere = pl.BlockSpec(memory_space=pl.ANY)
    more = [in_hbm(value) for value in made] + ([] if after is None else [after])
    return pl.pallas_call(
        new_soil_kernel,
        grid=(last - first,),
        in_specs=[flat, flat, flat, deep, deep, deep] + [anywhere] * len(more),
        out_specs=[deep, flat],
        out_shape=(
            jax.ShapeDtypeStruct(soil.shape, jnp.float32),
            jax.ShapeDtypeStruct((rows, LANES), jnp.float32),
        ),
        input_output_aliases={6: 0, 7: 1} if made else {},
        compiler_params=pltpu.CompilerParams(vmem_limit_bytes=VMEM_LIMIT),
        cost_estimate=pl.CostEstimate(
            flops=10**8, bytes_accessed=3 * MIB * (last - first), transcendentals=0
        ),
        name="new_soil",
    )(through, lost, canopy, in_hbm(soil), in_hbm(porosity), in_hbm(drainage), *more)


def halo_parts(value, axis, dim, width):
    count, length = (lax.axis_size(axis), value.shape[dim])
    up = [(i, i + 1) for i in range(count - 1)]
    down = [(j, i) for i, j in up]
    last = lax.slice_in_dim(value, length - width, length, axis=dim)
    initial = lax.slice_in_dim(value, 0, width, axis=dim)
    return lax.ppermute(last, axis, up), lax.ppermute(initial, axis, down)


def edge_columns_kernel(tall, _, first, last):
    arrays, height, width = tall.shape
    for number in range(arrays):
        values = tall[number]
        values = jnp.concatenate([values, jnp.zeros((LANES - height, width), jnp.float32)], axis=0)
        columns = jnp.transpose(values)
        part = pl.ds(number * ITERS, ITERS)
        first[part, :] = columns[:ITERS]
        last[part, :] = columns[width - ITERS :]


def edge_columns(tall, after):
    shape = jax.ShapeDtypeStruct((2 * ITERS, LANES), jnp.float32)
    return pl.pallas_call(
        edge_columns_kernel,
        in_specs=[pl.BlockSpec(memory_space=pltpu.VMEM), pl.BlockSpec(memory_space=pl.ANY)],
        out_shape=(shape, shape),
        compiler_params=pltpu.CompilerParams(vmem_limit_bytes=VMEM_LIMIT),
        cost_estimate=pl.CostEstimate(flops=10**6, bytes_accessed=10**5, transcendentals=0),
        name="edge_columns",
    )(tall, after)


def extended(own, strip):
    height = own.shape[0]

    def column_strip(right):
        middle, above, below = strip(0, right), strip(-1, right), strip(1, right)
        return jnp.concatenate(
            [
                middle[:, :height],
                below[:, :ITERS],
                above[:, height - ITERS : height],
                jnp.zeros((ITERS, LANES - height - 2 * ITERS), jnp.float32),
            ],
            axis=1,
        )

    gap = jnp.zeros((LANES - 2 * ITERS, LANES), jnp.float32)
    sides = jnp.concatenate([column_strip(1), gap, column_strip(-1)], axis=0)
    sides = jnp.transpose(sides)[: height + 2 * ITERS]
    tall = jnp.concatenate([own, strip(1, 0), strip(-1, 0)], axis=0)
    return jnp.concatenate([tall, sides], axis=1)


def neighbour(down, right):
    row, column = lax.axis_index("region") + down, lax.axis_index("col") + right
    there = (row >= 0) & (row < lax.axis_size("region"))
    there &= (column >= 0) & (column < lax.axis_size("col"))
    return jnp.where(there, row * lax.axis_size("col") + column, 0), jnp.where(there, 1.0, 0.0)


def static_halo_kernel(tall, before, after, out):
    height, width = tall.shape[1:]
    gap = jnp.zeros((LANES - 2 * ITERS, LANES), jnp.float32)
    for number in range(2):
        part = pl.ds(number * ITERS, ITERS)
        sides = jnp.transpose(jnp.concatenate([after[part, :], gap, before[part, :]], axis=0))
        out[number, :, :width] = tall[number]
        out[number, :, width:] = sides[:height]


def static_halo(tall, before, after):
    arrays, height, width = tall.shape
    return pl.pallas_call(
        static_halo_kernel,
        out_shape=jax.ShapeDtypeStruct((arrays, height, width + LANES), jnp.float32),
        compiler_params=pltpu.CompilerParams(vmem_limit_bytes=VMEM_LIMIT),
        cost_estimate=pl.CostEstimate(flops=10**6, bytes_accessed=10**6, transcendentals=0),
        name="static_halo",
    )(tall, before, after)


def river_kernel(state, strips, fixed, _, out):
    height, width = state.shape

    def strip(down, right):
        device, there = neighbour(down, right)
        return strips[pl.ds(device * ITERS, ITERS), :] * there

    storage = extended(state[...], strip)
    rate = fixed[0]
    code = fixed[1]
    rows, cols = storage.shape
    for _ in range(ITERS):
        outflow = rate * storage
        inflow = jnp.zeros_like(storage)
        for col_step in (-1, 0, 1):
            column = jnp.zeros_like(storage)
            for bit, (row_step, step) in enumerate(directions):
                if step != col_step:
                    continue
                leaving = jnp.where(code == float(1 << bit), outflow, 0.0)
                if row_step:
                    leaving = pltpu.roll(leaving, row_step % rows, 0)
                column = column + leaving
            if col_step:
                column = pltpu.roll(column, col_step % cols, 1)
            inflow = inflow + column
        storage = storage - outflow + inflow
    out[...] = storage[:height, :width]


def river(state, strips, fixed, after):
    return pl.pallas_call(
        river_kernel,
        in_specs=[pl.BlockSpec(memory_space=pltpu.VMEM)] * 3 + [pl.BlockSpec(memory_space=pl.ANY)],
        out_shape=jax.ShapeDtypeStruct(state.shape, jnp.float32),
        compiler_params=pltpu.CompilerParams(vmem_limit_bytes=VMEM_LIMIT),
        cost_estimate=pl.CostEstimate(flops=10**7, bytes_accessed=1 * MIB, transcendentals=0),
        name="river_steps",
    )(state, strips, fixed, in_hbm(after))


def exchange(value):
    return lax.all_to_all(value, axes, split_axis=0, concat_axis=0, tiled=True)


def shards(
    forcing,
    river_storage,
    river_rate,
    flow_code,
    home_slot,
    home_offset,
    worker_list,
    patch_cell,
    patch_area,
    canopy_water,
    canopy_cap,
    soil_water,
    porosity,
    drainage,
):
    homes = lax.axis_size("region") * lax.axis_size("col")
    capacity = home_slot.shape[1] // homes
    grid_rows, grid_cols = river_storage.shape
    lane_rows = grid_rows * grid_cols // LANES
    outgoing = pack(
        homes, capacity, home_slot, home_offset, forcing.reshape(3, lane_rows, LANES)
    )
    arrived = exchange(outgoing)
    home = worker_list // capacity
    position = worker_list - home * capacity
    pairs = capacity // 2
    first_rows = home * (3 * pairs) + position // 2 + position % 2 * pairs
    meta = segment_plan(patch_cell, worker_list[:, None])
    fixed = jnp.stack([river_rate, flow_code.astype(jnp.float32)])
    above, below = halo_parts(fixed, "region", 1, ITERS)
    terms = layer_terms(soil_water, porosity, drainage, meta)
    through, lost, canopy, sums = land_sums(
        (homes * capacity, LANES), pairs, worker_list, first_rows, arrived, patch_cell, meta,
        patch_area, canopy_water, canopy_cap, terms, (above, below),
    )
    returned = exchange(sums)
    layers_of = (through, lost, canopy, soil_water, porosity, drainage)
    blocks = worker_list.shape[0] // 96
    early = blocks * 3 // 5
    made = new_soil(0, early, *layers_of)
    code, place = unpack_plan(homes, capacity, lane_rows, home_slot, home_offset)
    fixed = jnp.concatenate([fixed, below, above], axis=1)
    initial, last = edge_columns(fixed, sums)
    count = lax.axis_size("col")
    before = lax.ppermute(last, "col", [(i, i + 1) for i in range(count - 1)])
    after = lax.ppermute(initial, "col", [(i + 1, i) for i in range(count - 1)])
    fixed = static_halo(fixed, before, after)
    cell_runoff, storage, strips = unpack_runoff(
        homes, returned, code, place, river_storage.reshape(lane_rows, LANES), fixed,
        in_hbm(made[1]),
    )
    soil_new, canopy_new = new_soil(early, blocks, *layers_of, made, strips)
    cell_evap = unpack_evap(returned, code, place)
    river_new = river(
        storage.reshape(river_storage.shape), exchange(strips), fixed, canopy_new
    )
    return (
        soil_new,
        canopy_new,
        cell_runoff.reshape(river_storage.shape),
        cell_evap.reshape(river_storage.shape),
        river_new,
    )


def solution(mesh):
    placed = (
        P(None, "region", "col"),
        P("region", "col"),
        P("region", "col"),
        P("region", "col"),
        P(("region", "col"), None),
        P(("region", "col"), None),
        P(("region", "col")),
        P(("region", "col"), None),
        P(("region", "col"), None),
        P(("region", "col"), None),
        P(("region", "col"), None),
        P(None, ("region", "col"), None),
        P(None, ("region", "col"), None),
        P(None, ("region", "col"), None),
    )
    return jax.shard_map(
        shards,
        mesh=mesh,
        in_specs=placed,
        out_specs=(
            P(None, ("region", "col"), None),
            P(("region", "col"), None),
            P("region", "col"),
            P("region", "col"),
            P("region", "col"),
        ),
        check_vma=False,
    )
```

```python
import functools

import jax
import jax.numpy as jnp
from jax import lax
from jax.experimental import pallas as pl
from jax.experimental.pallas import tpu as pltpu
from jax.sharding import PartitionSpec as P

ITERS = 4
WINDOW = 64
LANES = 128
MIB = 1024 * 1024
VMEM_LIMIT = 24 * MIB

directions = ((0, 1), (1, 1), (1, 0), (1, -1), (0, -1), (-1, -1), (-1, 0), (-1, 1))
region = ("half", "near")
axes = ("half", "near", "col")


def iota(shape, dim):
    return lax.broadcasted_iota(jnp.int32, shape, dim)


def onehot(mask):
    return jnp.where(mask, jnp.float32(1.0), jnp.float32(0.0)).astype(jnp.bfloat16)


def lane_pick(values, index):
    return jnp.take_along_axis(values, index, axis=1, mode="promise_in_bounds")


def in_hbm(value):
    return pltpu.with_memory_space_constraint(value, pltpu.HBM)


def thirds(value):
    high = value.astype(jnp.bfloat16)
    rest = value - high.astype(jnp.float32)
    middle = rest.astype(jnp.bfloat16)
    low = (rest - middle.astype(jnp.float32)).astype(jnp.bfloat16)
    return high, middle, low


def halves(value):
    high = value.astype(jnp.bfloat16)
    return high, (value - high.astype(jnp.float32)).astype(jnp.bfloat16)


def matmul(a, b, a_dim=1, b_dim=0):
    return lax.dot_general(
        a, b, (((a_dim,), (b_dim,)), ((), ())), preferred_element_type=jnp.float32
    )


def slot_factors(slot, offset, homes, capacity, first=0):
    slots = slot.shape[1]
    worker = slot // capacity if capacity & (capacity - 1) else slot >> (capacity.bit_length() - 1)
    position = slot - worker * capacity
    by_worker = onehot(iota((homes, slots), 0) + first == worker)
    at_position = iota((capacity, slots), 0) == position
    row = jnp.where(at_position, ((offset >> 7) + 1).astype(jnp.float32), 0.0)
    lane = jnp.where(at_position, (offset & 127).astype(jnp.float32), 0.0)
    return by_worker, row.astype(jnp.bfloat16), lane.astype(jnp.bfloat16)


def slot_table(slot, offset, homes, capacity, first=0, split=False):
    slots = homes * capacity
    by_worker, row, lane = slot_factors(slot, offset, homes, capacity, first)
    table = matmul(by_worker, jnp.concatenate([row, lane], axis=0), 1, 1)
    groups = 2 if split else 1
    spread = jnp.broadcast_to(
        table[:, None, :], (homes, capacity // groups, 2 * capacity)
    ).reshape(slots // groups, 2 * capacity)
    spread = jnp.concatenate([spread] * groups, axis=0)
    number = iota(spread.shape, 0)
    position = number % (capacity // groups) * groups + number // (slots // groups)
    place = position == iota(spread.shape, 1) % capacity
    return jnp.where(place, spread, 0.0).astype(jnp.bfloat16)


def slot_columns(table):
    width = table.shape[1]
    shape = (width, 2 * LANES)
    gather = onehot((iota(shape, 0) >= width // 2) == (iota(shape, 1) >= LANES))
    columns = matmul(table, gather).astype(jnp.int32)
    return columns[:, :LANES] - 1, columns[:, LANES:]


def slot_rows(slot, offset, homes, capacity):
    slots = slot.shape[1]
    by_worker, row, lane = slot_factors(slot, offset, homes, capacity)
    table = matmul(jnp.concatenate([row, lane], axis=0), by_worker, 1, 1).astype(jnp.bfloat16)
    number = iota((1, slots), 1)
    worker = number // capacity
    position = number - worker * capacity
    spread = matmul(table, onehot(iota((homes, slots), 0) == worker))
    at_position = iota((capacity, slots), 0) == position
    rows = jnp.sum(jnp.where(at_position, spread[:capacity], 0.0), axis=0, keepdims=True)
    lanes = jnp.sum(jnp.where(at_position, spread[capacity:], 0.0), axis=0, keepdims=True)
    return rows.astype(jnp.int32) - 1, lanes.astype(jnp.int32)


def pack_kernel(
    homes, capacity, slot_in, offset_in, forcing_in, far_slots, far_forcing, out, slot, offset,
    forcing, rain, ready,
):
    copies = [
        pltpu.make_async_copy(source, target, ready.at[i])
        for i, (source, target) in enumerate(
            ((slot_in, slot), (offset_in, offset), (forcing_in, forcing))
        )
    ]
    for copy in copies:
        copy.start()
    first_home = lax.axis_index("half") * homes
    pairs = capacity // 2
    half = homes * pairs
    lane_rows = forcing.shape[1]
    chunk = 128
    here = iota((chunk, LANES), 1)

    def windows(number, slots, offsets, values):
        places = slot_table(slots, offsets, homes, capacity, first_home, True)
        limit = pltpu.roll(values[2], WINDOW, 1)
        above = jnp.concatenate([limit[lane_rows - 1 :], limit[: lane_rows - 1]], axis=0)
        limit = jnp.where(iota(limit.shape, 1) < WINDOW, above, limit)
        parts = []
        for own in (values[0], values[1], limit):
            parts += [own, jnp.concatenate([own[1:], own[:1]], axis=0)]
        table = jnp.concatenate(thirds(jnp.concatenate(parts, axis=1)), axis=0)
        for start in range(0, 2 * half, chunk):
            odd = start >= half
            row, lane = slot_columns(places[start : start + chunk])
            shape = (chunk, 3 * lane_rows)
            wide = jnp.concatenate([row, row], axis=1)[:, : 3 * lane_rows]
            pick = onehot(wide == iota(shape, 1) % lane_rows)
            rows = matmul(pick, table)
            after = here >= lane
            joined = [
                jnp.where(
                    after,
                    rows[:, 2 * var * LANES : (2 * var + 1) * LANES],
                    rows[:, (2 * var + 1) * LANES : (2 * var + 2) * LANES],
                )
                for var in range(3)
            ]
            first = (here + lane) & 127
            second = (first + WINDOW) & 127
            demanded = ((here - lane) & 127) < WINDOW
            losses = lane_pick(jnp.where(demanded, joined[1], joined[2]), first)
            base = start - half if odd else start
            if odd:
                rains = jnp.where(
                    here < WINDOW, rain[pl.ds(base, chunk), :], lane_pick(joined[0], second)
                )
            else:
                rain[pl.ds(base, chunk), :] = lane_pick(joined[0], first)
            for part in range(0, chunk, pairs):
                place = (base + part) * 6 + number * 3 * pairs
                if odd:
                    out[pl.ds(place + pairs, pairs), :] = rains[part : part + pairs]
                    out[pl.ds(place + 2 * pairs, pairs), :] = losses[part : part + pairs]
                else:
                    out[pl.ds(place, pairs), :] = losses[part : part + pairs]

    windows(1, far_slots[pl.ds(0, 1), :], far_slots[pl.ds(1, 1), :], far_forcing)
    for copy in copies:
        copy.wait()
    windows(0, slot[...], offset[...], forcing)


def pack(homes, capacity, slot, offset, forcing, far_slots, far_forcing):
    slots = slot.shape[1]
    far = pl.BlockSpec(memory_space=pltpu.HBM)
    near = pl.BlockSpec(memory_space=pltpu.VMEM)
    return pl.pallas_call(
        functools.partial(pack_kernel, homes, capacity),
        in_specs=[far] * 3 + [near] * 2,
        out_shape=jax.ShapeDtypeStruct((slots + slots // 2, LANES), jnp.float32),
        scratch_shapes=[
            pltpu.VMEM(slot.shape, jnp.int32),
            pltpu.VMEM(offset.shape, jnp.int32),
            pltpu.VMEM(forcing.shape, jnp.float32),
            pltpu.VMEM((slots // 4, LANES), jnp.float32),
            pltpu.SemaphoreType.DMA((3,)),
        ],
        compiler_params=pltpu.CompilerParams(vmem_limit_bytes=VMEM_LIMIT),
        cost_estimate=pl.CostEstimate(flops=10**9, bytes_accessed=2 * MIB, transcendentals=0),
        name="pack_forcing",
    )(in_hbm(slot), in_hbm(offset), in_hbm(forcing), far_slots, far_forcing)


def unpack_plan_kernel(homes, capacity, lane_rows, slot, offset, code, place):
    slots = slot.shape[1]
    row, lane = slot_columns(slot_table(slot[...], offset[...], homes, capacity))
    here = iota((slots, LANES), 1)
    index = (here - lane) & 127
    inside = (index < WINDOW) & (row >= 0)
    code[...] = jnp.where(inside, index + jnp.where(here >= lane, 0, LANES), -1)
    row_lane, _ = slot_rows(slot[...], offset[...], homes, capacity)
    place[...] = onehot(iota((lane_rows, slots), 0) == row_lane)


def unpack_plan(homes, capacity, lane_rows, slot, offset):
    slots = slot.shape[1]
    return pl.pallas_call(
        functools.partial(unpack_plan_kernel, homes, capacity, lane_rows),
        out_shape=(
            jax.ShapeDtypeStruct((slots, LANES), jnp.int32),
            jax.ShapeDtypeStruct((lane_rows, slots), jnp.bfloat16),
        ),
        compiler_params=pltpu.CompilerParams(vmem_limit_bytes=VMEM_LIMIT),
        cost_estimate=pl.CostEstimate(flops=10**9, bytes_accessed=2 * MIB, transcendentals=0),
        name="unpack_plan",
    )(slot, offset)


def strips_for_neighbours(state, rows):
    device = iota((rows, LANES), 0) // ITERS
    down = device // lax.axis_size("col") - lax.axis_index(region)
    right = device % lax.axis_size("col") - lax.axis_index("col")
    height, width = state.shape
    columns = jnp.transpose(state)
    empty = jnp.zeros((ITERS, LANES - height), jnp.float32)

    def repeated(strip):
        if strip.shape[1] < LANES:
            strip = jnp.concatenate([strip, empty], axis=1)
        return jnp.concatenate([strip] * (rows // ITERS), axis=0)

    near = (jnp.abs(down) <= 1).astype(jnp.int32)
    strips = jnp.zeros((rows, LANES), jnp.float32)
    strips = jnp.where((right == 0) & (down == 1), repeated(state[height - ITERS :]), strips)
    strips = jnp.where((right == 0) & (down == -1), repeated(state[:ITERS]), strips)
    strips = jnp.where((right == 1) & (near == 1), repeated(columns[width - ITERS :]), strips)
    return jnp.where((right == -1) & (near == 1), repeated(columns[:ITERS]), strips)


def cell_totals(arrived, code, place, first):
    lane_rows = place.shape[0]
    marks = code[...]
    window = lane_pick(arrived[...], (marks + first) & 127)
    placed = jnp.concatenate(
        [
            jnp.where((marks >= 0) & (marks < LANES), window, 0.0),
            jnp.where(marks >= LANES, window, 0.0),
        ],
        axis=1,
    )
    totals = matmul(place[...], jnp.concatenate(halves(placed), axis=1))
    totals = totals[:, :256] + totals[:, 256:]
    over = totals[:, LANES:]
    over = jnp.concatenate([over[lane_rows - 1 :], over[: lane_rows - 1]], axis=0)
    over = jnp.where(iota(over.shape, 0) == 0, 0.0, over)
    return totals[:, :LANES] + over


def unpack_runoff_kernel(arrived, code, place, river, _, __, runoff, storage, strips):
    total = cell_totals(arrived, code, place, 0)
    state = river[...] + total
    runoff[...] = total
    storage[...] = state
    strips[...] = strips_for_neighbours(state, strips.shape[0])


def unpack_runoff(homes, arrived, code, place, river, *after):
    shape = jax.ShapeDtypeStruct((place.shape[0], LANES), jnp.float32)
    strips = jax.ShapeDtypeStruct((homes * ITERS, LANES), jnp.float32)
    return pl.pallas_call(
        unpack_runoff_kernel,
        in_specs=[pl.BlockSpec(memory_space=pltpu.VMEM)] * 4
        + [pl.BlockSpec(memory_space=pl.ANY)] * 2,
        out_shape=(shape, shape, strips),
        compiler_params=pltpu.CompilerParams(vmem_limit_bytes=VMEM_LIMIT),
        cost_estimate=pl.CostEstimate(flops=10**9, bytes_accessed=1 * MIB, transcendentals=0),
        name="unpack_runoff",
    )(arrived, code, place, river, *after)


def unpack_evap_kernel(arrived, code, place, evap):
    evap[...] = cell_totals(arrived, code, place, WINDOW)


def unpack_evap(arrived, code, place):
    return pl.pallas_call(
        unpack_evap_kernel,
        out_shape=jax.ShapeDtypeStruct((place.shape[0], LANES), jnp.float32),
        compiler_params=pltpu.CompilerParams(vmem_limit_bytes=VMEM_LIMIT),
        cost_estimate=pl.CostEstimate(flops=10**9, bytes_accessed=1 * MIB, transcendentals=0),
        name="unpack_evap",
    )(arrived, code, place)


def segment_plan_kernel(cell, worker, meta):
    chunk = 96
    for start in range(0, cell.shape[0], chunk):
        values = cell[pl.ds(start, chunk), :]
        target = iota(values.shape, 1) & (WINDOW - 1)
        count = jnp.zeros_like(values)
        for step in (64, 32, 16, 8, 4, 2, 1):
            probe = lane_pick(values, count + (step - 1))
            count = jnp.where(probe <= target, count + step, count)
        count = jnp.where(lane_pick(values, count) <= target, count + 1, count)
        odd = worker[pl.ds(start, chunk), :] & 1
        meta[pl.ds(start, chunk), :] = count + (odd << 8)


def segment_plan(cell, worker):
    return pl.pallas_call(
        segment_plan_kernel,
        out_shape=jax.ShapeDtypeStruct(cell.shape, jnp.int32),
        compiler_params=pltpu.CompilerParams(vmem_limit_bytes=VMEM_LIMIT),
        cost_estimate=pl.CostEstimate(flops=10**8, bytes_accessed=1 * MIB, transcendentals=0),
        name="segment_plan",
    )(cell, worker)


def layer_terms_kernel(soil, porosity, drainage, _, out):
    layers, block = soil.shape[:2]
    chunk = 48
    for start in range(0, block, chunk):
        part = pl.ds(start, chunk)
        share = inverse = None
        total = jnp.zeros((chunk, LANES), jnp.float32)
        for layer in range(layers):
            content, room = soil[layer, part, :], porosity[layer, part, :]
            if layer:
                content, room = content * inverse, room * inverse
            total = total + content
            out[0, layer, part, :] = room - total
            rate = drainage[layer, part, :]
            share = rate if layer == 0 else share * rate
            inverse = 1.0 / share
            out[0, layers + layer, part, :] = share
        out[0, 2 * layers, part, :] = total
        out[0, 2 * layers + 1, part, :] = soil[0, part, :]


def layer_terms(soil, porosity, drainage, after):
    layers, rows = soil.shape[:2]
    block = 96
    deep = pl.BlockSpec((layers, block, LANES), lambda i: (0, i, 0))
    shape = (rows // block, 2 * layers + 2, block, LANES)
    return pl.pallas_call(
        layer_terms_kernel,
        grid=(rows // block,),
        in_specs=[deep] * 3 + [pl.BlockSpec(memory_space=pl.ANY)],
        out_specs=pl.BlockSpec((1,) + shape[1:], lambda i: (i, 0, 0, 0)),
        out_shape=pltpu.HBM(shape, jnp.float32),
        compiler_params=pltpu.CompilerParams(vmem_limit_bytes=VMEM_LIMIT),
        cost_estimate=pl.CostEstimate(flops=10**8, bytes_accessed=19 * MIB, transcendentals=0),
        name="layer_terms",
    )(in_hbm(soil), in_hbm(porosity), in_hbm(drainage), after)


def land_sums_kernel(
    pairs, slots, first_rows, arrived, cell, meta, area, water, cap, terms_in, _, __, through,
    lost, canopy_new, sums_out, terms, fetched, runoffs, evaps, ready,
):
    steps, count, block = terms.shape[:3]
    layers = count // 2 - 1
    chunk = block // 2

    def part_of(step):
        return pl.ds(step * block, block)

    def reads(step):
        return [
            pltpu.make_async_copy(
                terms_in.at[step, part], terms.at[step, part], ready.at[step, i]
            )
            for i, part in enumerate((pl.ds(0, count // 2), pl.ds(count // 2, count // 2)))
        ]

    def fetch(step):
        for i in range(step * block, (step + 1) * block):
            fetched[pl.ds(2 * i, 2), :] = arrived[pl.ds(first_rows[i], 2, stride=pairs), :]

    def cascade(start):
        part = pl.ds(start, chunk)
        index = cell[part, :]
        one = fetched[pl.ds(2 * start, chunk, stride=2), :]
        two = fetched[pl.ds(2 * start + 1, chunk, stride=2), :]
        odd = meta[part, :] >> 8
        loss = jnp.where(odd == 1, two, one)
        rain = lane_pick(jnp.where(odd == 1, one, two), index + odd * WINDOW)
        demand = lane_pick(loss, index)
        limit = lane_pick(loss, index + WINDOW)
        wetted = water[part, :] + rain
        flowing = jnp.maximum(wetted - cap[part, :], 0.0)
        retained = jnp.minimum(wetted, cap[part, :])
        canopy_loss = jnp.minimum(demand, retained)
        canopy_new[part, :] = retained - canopy_loss
        through[part, :] = flowing
        step, local = start // block, pl.ds(start % block, chunk)
        surface = None
        for layer in range(layers):
            room = terms[step, layer, local, :]
            excess = jnp.maximum(flowing - room, 0.0)
            flowing = jnp.minimum(flowing, room)
            if layer == 0:
                surface = excess
                content = flowing + terms[step, 2 * layers + 1, local, :]
                half = 0.5 * (content - terms[step, layers, local, :] * content)
                soil_loss = jnp.minimum(jnp.minimum(limit, demand - canopy_loss), half)
                lost[part, :] = soil_loss
                evaps[part, :] = area[part, :] * (canopy_loss + soil_loss)
            else:
                surface = surface + terms[step, layers + layer - 1, local, :] * excess
        bottom = terms[step, 2 * layers - 1, local, :] * (
            flowing + terms[step, 2 * layers, local, :]
        )
        runoffs[part, :] = area[part, :] * (surface + bottom)

    def scan(step):
        part = part_of(step)
        shape = (2 * LANES, LANES)
        upto = onehot((iota(shape, 0) & 127) <= iota(shape, 1))
        patches = meta[part, :] & 255
        last = jnp.maximum(patches - 1, 0)
        here = iota((block, LANES), 1)
        picked = [
            lane_pick(matmul(jnp.concatenate(halves(value[part, :]), axis=1), upto), last)
            for value in (runoffs, evaps)
        ]
        reached = jnp.where(patches > 0, jnp.where(here < WINDOW, *picked), 0.0)
        before = jnp.where((here & (WINDOW - 1)) == 0, 0.0, pltpu.roll(reached, 1, 1))
        runoffs[part, :] = reached - before

    def hand_back(step):
        for i in range(step * block, (step + 1) * block):
            sums_out[pl.ds(slots[i], 1), :] = runoffs[pl.ds(i, 1), :]

    for step in range(steps):
        for copy in reads(step):
            copy.start()
    sums_out[...] = jnp.zeros_like(sums_out)
    for step in range(steps):
        fetch(step)
    for step in range(steps + 2):
        if step < steps:
            for copy in reads(step):
                copy.wait()
            for start in range(step * block, (step + 1) * block, chunk):
                cascade(start)
        if 1 <= step <= steps:
            scan(step - 1)
        if step >= 2:
            hand_back(step - 2)


def land_sums(
    sums_shape, pairs, slots, first_rows, arrived, cell, meta, area, water, cap, terms, after
):
    rows = cell.shape[0]
    near = pl.BlockSpec(memory_space=pltpu.VMEM)
    return pl.pallas_call(
        functools.partial(land_sums_kernel, pairs),
        in_specs=[pl.BlockSpec(memory_space=pltpu.SMEM)] * 2 + [near] * 6
        + [pl.BlockSpec(memory_space=pltpu.HBM)] + [pl.BlockSpec(memory_space=pl.ANY)] * 2,
        out_specs=[near] * 4,
        scratch_shapes=[
            pltpu.VMEM(terms.shape, jnp.float32),
            pltpu.VMEM((2 * rows, LANES), jnp.float32),
            pltpu.VMEM((rows, LANES), jnp.float32),
            pltpu.VMEM((rows, LANES), jnp.float32),
            pltpu.SemaphoreType.DMA((terms.shape[0], 2)),
        ],
        out_shape=[jax.ShapeDtypeStruct((rows, LANES), jnp.float32)] * 3
        + [jax.ShapeDtypeStruct(sums_shape, jnp.float32)],
        compiler_params=pltpu.CompilerParams(vmem_limit_bytes=VMEM_LIMIT),
        cost_estimate=pl.CostEstimate(flops=10**8, bytes_accessed=20 * MIB, transcendentals=0),
        name="land_sums",
    )(
        slots, first_rows, arrived, cell, meta, area, water, cap,
        in_hbm(terms), *after,
    )


def new_soil_kernel(through, lost, canopy, soil, porosity, drainage, *rest):
    soil_new, canopy_new = rest[-2:]
    layers, block = soil.shape[:2]
    chunk = 48
    canopy_new[...] = canopy[...]
    for start in range(0, block, chunk):
        part = pl.ds(start, chunk)
        flowing = through[part, :]
        for layer in range(layers):
            filled = soil[layer, part, :] + flowing
            filled = filled - jnp.maximum(filled - porosity[layer, part, :], 0.0)
            flowing = drainage[layer, part, :] * filled
            middle = filled - flowing
            soil_new[layer, part, :] = middle - lost[part, :] if layer == 0 else middle


def new_soil(first, last, through, lost, canopy, soil, porosity, drainage, made=(), after=None):
    layers, rows = soil.shape[:2]
    block = 96
    flat = pl.BlockSpec((block, LANES), lambda i: (first + i, 0))
    deep = pl.BlockSpec((layers, block, LANES), lambda i: (0, first + i, 0))
    anywhere = pl.BlockSpec(memory_space=pl.ANY)
    more = [in_hbm(value) for value in made] + ([] if after is None else [after])
    return pl.pallas_call(
        new_soil_kernel,
        grid=(last - first,),
        in_specs=[flat, flat, flat, deep, deep, deep] + [anywhere] * len(more),
        out_specs=[deep, flat],
        out_shape=(
            jax.ShapeDtypeStruct(soil.shape, jnp.float32),
            jax.ShapeDtypeStruct((rows, LANES), jnp.float32),
        ),
        input_output_aliases={6: 0, 7: 1} if made else {},
        compiler_params=pltpu.CompilerParams(vmem_limit_bytes=VMEM_LIMIT),
        cost_estimate=pl.CostEstimate(
            flops=10**8, bytes_accessed=3 * MIB * (last - first), transcendentals=0
        ),
        name="new_soil",
    )(through, lost, canopy, in_hbm(soil), in_hbm(porosity), in_hbm(drainage), *more)


def halo_parts(value, axis, dim, width):
    count, length = (lax.axis_size(axis), value.shape[dim])
    up = [(i, i + 1) for i in range(count - 1)]
    down = [(j, i) for i, j in up]
    last = lax.slice_in_dim(value, length - width, length, axis=dim)
    initial = lax.slice_in_dim(value, 0, width, axis=dim)
    return lax.ppermute(last, axis, up), lax.ppermute(initial, axis, down)


def rate_and_code_kernel(rate, code, _, out):
    out[0] = rate[...]
    out[1] = code[...].astype(jnp.float32)


def rate_and_code(rate, code, after):
    return pl.pallas_call(
        rate_and_code_kernel,
        in_specs=[pl.BlockSpec(memory_space=pltpu.VMEM)] * 2 + [pl.BlockSpec(memory_space=pl.ANY)],
        out_shape=jax.ShapeDtypeStruct((2,) + rate.shape, jnp.float32),
        compiler_params=pltpu.CompilerParams(vmem_limit_bytes=VMEM_LIMIT),
        cost_estimate=pl.CostEstimate(flops=10**5, bytes_accessed=10**5, transcendentals=0),
        name="rate_and_code",
    )(rate, code, after)


def edge_columns_kernel(tall, _, first, last):
    arrays, height, width = tall.shape
    for number in range(arrays):
        values = tall[number]
        values = jnp.concatenate([values, jnp.zeros((LANES - height, width), jnp.float32)], axis=0)
        columns = jnp.transpose(values)
        part = pl.ds(number * ITERS, ITERS)
        first[part, :] = columns[:ITERS]
        last[part, :] = columns[width - ITERS :]


def edge_columns(tall, after):
    shape = jax.ShapeDtypeStruct((2 * ITERS, LANES), jnp.float32)
    return pl.pallas_call(
        edge_columns_kernel,
        in_specs=[pl.BlockSpec(memory_space=pltpu.VMEM), pl.BlockSpec(memory_space=pl.ANY)],
        out_shape=(shape, shape),
        compiler_params=pltpu.CompilerParams(vmem_limit_bytes=VMEM_LIMIT),
        cost_estimate=pl.CostEstimate(flops=10**6, bytes_accessed=10**5, transcendentals=0),
        name="edge_columns",
    )(tall, after)


def extended(own, strip):
    height = own.shape[0]

    def column_strip(right):
        middle, above, below = strip(0, right), strip(-1, right), strip(1, right)
        return jnp.concatenate(
            [
                middle[:, :height],
                below[:, :ITERS],
                above[:, height - ITERS : height],
                jnp.zeros((ITERS, LANES - height - 2 * ITERS), jnp.float32),
            ],
            axis=1,
        )

    gap = jnp.zeros((LANES - 2 * ITERS, LANES), jnp.float32)
    sides = jnp.concatenate([column_strip(1), gap, column_strip(-1)], axis=0)
    sides = jnp.transpose(sides)[: height + 2 * ITERS]
    tall = jnp.concatenate([own, strip(1, 0), strip(-1, 0)], axis=0)
    return jnp.concatenate([tall, sides], axis=1)


def neighbour(down, right):
    row, column = lax.axis_index(region) + down, lax.axis_index("col") + right
    there = (row >= 0) & (row < lax.axis_size(region))
    there &= (column >= 0) & (column < lax.axis_size("col"))
    return jnp.where(there, row * lax.axis_size("col") + column, 0), jnp.where(there, 1.0, 0.0)


def static_halo_kernel(tall, before, after, out):
    height, width = tall.shape[1:]
    gap = jnp.zeros((LANES - 2 * ITERS, LANES), jnp.float32)
    for number in range(2):
        part = pl.ds(number * ITERS, ITERS)
        sides = jnp.transpose(jnp.concatenate([after[part, :], gap, before[part, :]], axis=0))
        out[number, :, :width] = tall[number]
        out[number, :, width:] = sides[:height]


def static_halo(tall, before, after):
    arrays, height, width = tall.shape
    return pl.pallas_call(
        static_halo_kernel,
        out_shape=jax.ShapeDtypeStruct((arrays, height, width + LANES), jnp.float32),
        compiler_params=pltpu.CompilerParams(vmem_limit_bytes=VMEM_LIMIT),
        cost_estimate=pl.CostEstimate(flops=10**6, bytes_accessed=10**6, transcendentals=0),
        name="static_halo",
    )(tall, before, after)


def river_kernel(state, strips, fixed, _, out):
    height, width = state.shape

    def strip(down, right):
        device, there = neighbour(down, right)
        return strips[pl.ds(device * ITERS, ITERS), :] * there

    storage = extended(state[...], strip)
    rate = fixed[0]
    code = fixed[1]
    rows, cols = storage.shape
    for _ in range(ITERS):
        outflow = rate * storage
        inflow = jnp.zeros_like(storage)
        for col_step in (-1, 0, 1):
            column = jnp.zeros_like(storage)
            for bit, (row_step, step) in enumerate(directions):
                if step != col_step:
                    continue
                leaving = jnp.where(code == float(1 << bit), outflow, 0.0)
                if row_step:
                    leaving = pltpu.roll(leaving, row_step % rows, 0)
                column = column + leaving
            if col_step:
                column = pltpu.roll(column, col_step % cols, 1)
            inflow = inflow + column
        storage = storage - outflow + inflow
    out[...] = storage[:height, :width]


def river(state, strips, fixed, after):
    return pl.pallas_call(
        river_kernel,
        in_specs=[pl.BlockSpec(memory_space=pltpu.VMEM)] * 3 + [pl.BlockSpec(memory_space=pl.ANY)],
        out_shape=jax.ShapeDtypeStruct(state.shape, jnp.float32),
        compiler_params=pltpu.CompilerParams(vmem_limit_bytes=VMEM_LIMIT),
        cost_estimate=pl.CostEstimate(flops=10**7, bytes_accessed=1 * MIB, transcendentals=0),
        name="river_steps",
    )(state, strips, fixed, in_hbm(after))


def exchange(value, over=axes):
    return lax.all_to_all(value, over, split_axis=0, concat_axis=0, tiled=True)


def shards(
    forcing,
    river_storage,
    river_rate,
    flow_code,
    home_slot,
    home_offset,
    worker_list,
    patch_cell,
    patch_area,
    canopy_water,
    canopy_cap,
    soil_water,
    porosity,
    drainage,
):
    homes = lax.axis_size(region) * lax.axis_size("col")
    capacity = home_slot.shape[1] // homes
    grid_rows, grid_cols = river_storage.shape
    lane_rows = grid_rows * grid_cols // LANES
    forcing = forcing.reshape(3, lane_rows, LANES)
    swap = [(0, 1), (1, 0)]
    far_slots = lax.ppermute(jnp.concatenate([home_slot, home_offset], axis=0), "half", swap)
    far_forcing = lax.ppermute(forcing, "half", swap)
    outgoing = pack(
        homes // 2, capacity, home_slot, home_offset, forcing, far_slots, far_forcing
    )
    arrived = exchange(outgoing, ("near", "col"))
    home = worker_list // capacity
    position = worker_list - home * capacity
    pairs = capacity // 2
    own_half = home // (homes // 2) == lax.axis_index("half")
    first_rows = home % (homes // 2) * (6 * pairs) + jnp.where(own_half, 0, 3 * pairs)
    first_rows = first_rows + position // 2 + position % 2 * pairs
    meta = segment_plan(patch_cell, worker_list[:, None])
    fixed = rate_and_code(river_rate, flow_code, outgoing)
    above, below = halo_parts(fixed, region, 1, ITERS)
    terms = layer_terms(soil_water, porosity, drainage, outgoing)
    through, lost, canopy, sums = land_sums(
        (homes * capacity, LANES), pairs, worker_list, first_rows, arrived, patch_cell, meta,
        patch_area, canopy_water, canopy_cap, terms, (above, below),
    )
    returned = exchange(sums)
    layers_of = (through, lost, canopy, soil_water, porosity, drainage)
    blocks = worker_list.shape[0] // 96
    early = blocks * 3 // 5
    made = new_soil(0, early, *layers_of)
    code, place = unpack_plan(homes, capacity, lane_rows, home_slot, home_offset)
    fixed = jnp.concatenate([fixed, below, above], axis=1)
    initial, last = edge_columns(fixed, sums)
    count = lax.axis_size("col")
    before = lax.ppermute(last, "col", [(i, i + 1) for i in range(count - 1)])
    after = lax.ppermute(initial, "col", [(i + 1, i) for i in range(count - 1)])
    fixed = static_halo(fixed, before, after)
    cell_runoff, storage, strips = unpack_runoff(
        homes, returned, code, place, river_storage.reshape(lane_rows, LANES), fixed,
        in_hbm(made[1]),
    )
    soil_new, canopy_new = new_soil(early, blocks, *layers_of, made, strips)
    cell_evap = unpack_evap(returned, code, place)
    river_new = river(
        storage.reshape(river_storage.shape), exchange(strips), fixed, canopy_new
    )
    return (
        soil_new,
        canopy_new,
        cell_runoff.reshape(river_storage.shape),
        cell_evap.reshape(river_storage.shape),
        river_new,
    )


def solution(mesh):
    rows, cols = mesh.devices.shape
    mesh = jax.sharding.Mesh(mesh.devices.reshape(2, rows // 2, cols), axes)
    placed = (
        P(None, region, "col"),
        P(region, "col"),
        P(region, "col"),
        P(region, "col"),
        P(axes, None),
        P(axes, None),
        P(axes),
        P(axes, None),
        P(axes, None),
        P(axes, None),
        P(axes, None),
        P(None, axes, None),
        P(None, axes, None),
        P(None, axes, None),
    )
    return jax.shard_map(
        shards,
        mesh=mesh,
        in_specs=placed,
        out_specs=(
            P(None, axes, None),
            P(axes, None),
            P(region, "col"),
            P(region, "col"),
            P(region, "col"),
        ),
        check_vma=False,
    )
```

```python
import functools

import jax
import jax.numpy as jnp
from jax import lax
from jax.experimental import pallas as pl
from jax.experimental.pallas import tpu as pltpu
from jax.sharding import PartitionSpec as P

ITERS = 4
WINDOW = 64
LANES = 128
MIB = 1024 * 1024
VMEM_LIMIT = 24 * MIB

directions = ((0, 1), (1, 1), (1, 0), (1, -1), (0, -1), (-1, -1), (-1, 0), (-1, 1))
region = ("half", "near")
axes = ("half", "near", "col")


def iota(shape, dim):
    return lax.broadcasted_iota(jnp.int32, shape, dim)


def onehot(mask):
    return jnp.where(mask, jnp.float32(1.0), jnp.float32(0.0)).astype(jnp.bfloat16)


def lane_pick(values, index):
    return jnp.take_along_axis(values, index, axis=1, mode="promise_in_bounds")


def in_hbm(value):
    return pltpu.with_memory_space_constraint(value, pltpu.HBM)


def thirds(value):
    high = value.astype(jnp.bfloat16)
    rest = value - high.astype(jnp.float32)
    middle = rest.astype(jnp.bfloat16)
    low = (rest - middle.astype(jnp.float32)).astype(jnp.bfloat16)
    return high, middle, low


def halves(value):
    high = value.astype(jnp.bfloat16)
    return high, (value - high.astype(jnp.float32)).astype(jnp.bfloat16)


def matmul(a, b, a_dim=1, b_dim=0):
    return lax.dot_general(
        a, b, (((a_dim,), (b_dim,)), ((), ())), preferred_element_type=jnp.float32
    )


def slot_factors(slot, offset, homes, capacity, first=0):
    slots = slot.shape[1]
    worker = slot // capacity if capacity & (capacity - 1) else slot >> (capacity.bit_length() - 1)
    position = slot - worker * capacity
    by_worker = onehot(iota((homes, slots), 0) + first == worker)
    at_position = iota((capacity, slots), 0) == position
    row = jnp.where(at_position, ((offset >> 7) + 1).astype(jnp.float32), 0.0)
    lane = jnp.where(at_position, (offset & 127).astype(jnp.float32), 0.0)
    return by_worker, row.astype(jnp.bfloat16), lane.astype(jnp.bfloat16)


def slot_table(slot, offset, homes, capacity, first=0, split=False):
    slots = homes * capacity
    by_worker, row, lane = slot_factors(slot, offset, homes, capacity, first)
    table = matmul(by_worker, jnp.concatenate([row, lane], axis=0), 1, 1)
    groups = 2 if split else 1
    spread = jnp.broadcast_to(
        table[:, None, :], (homes, capacity // groups, 2 * capacity)
    ).reshape(slots // groups, 2 * capacity)
    spread = jnp.concatenate([spread] * groups, axis=0)
    number = iota(spread.shape, 0)
    position = number % (capacity // groups) * groups + number // (slots // groups)
    place = position == iota(spread.shape, 1) % capacity
    return jnp.where(place, spread, 0.0).astype(jnp.bfloat16)


def slot_columns(table):
    width = table.shape[1]
    shape = (width, 2 * LANES)
    gather = onehot((iota(shape, 0) >= width // 2) == (iota(shape, 1) >= LANES))
    columns = matmul(table, gather).astype(jnp.int32)
    return columns[:, :LANES] - 1, columns[:, LANES:]


def slot_rows(slot, offset, homes, capacity):
    slots = slot.shape[1]
    by_worker, row, lane = slot_factors(slot, offset, homes, capacity)
    table = matmul(jnp.concatenate([row, lane], axis=0), by_worker, 1, 1).astype(jnp.bfloat16)
    number = iota((1, slots), 1)
    worker = number // capacity
    position = number - worker * capacity
    spread = matmul(table, onehot(iota((homes, slots), 0) == worker))
    at_position = iota((capacity, slots), 0) == position
    rows = jnp.sum(jnp.where(at_position, spread[:capacity], 0.0), axis=0, keepdims=True)
    lanes = jnp.sum(jnp.where(at_position, spread[capacity:], 0.0), axis=0, keepdims=True)
    return rows.astype(jnp.int32) - 1, lanes.astype(jnp.int32)


def pack_kernel(
    homes, capacity, slot_in, offset_in, forcing_in, far_slots, far_forcing, _, __, out, slot,
    offset, forcing, rain, ready,
):
    copies = [
        pltpu.make_async_copy(source, target, ready.at[i])
        for i, (source, target) in enumerate(
            ((slot_in, slot), (offset_in, offset), (forcing_in, forcing))
        )
    ]
    for copy in copies:
        copy.start()
    first_home = lax.axis_index("half") * homes
    pairs = capacity // 2
    half = homes * pairs
    lane_rows = forcing.shape[1]
    chunk = 128
    here = iota((chunk, LANES), 1)

    def windows(number, slots, offsets, values):
        places = slot_table(slots, offsets, homes, capacity, first_home, True)
        limit = pltpu.roll(values[2], WINDOW, 1)
        above = jnp.concatenate([limit[lane_rows - 1 :], limit[: lane_rows - 1]], axis=0)
        limit = jnp.where(iota(limit.shape, 1) < WINDOW, above, limit)
        parts = []
        for own in (values[0], values[1], limit):
            parts += [own, jnp.concatenate([own[1:], own[:1]], axis=0)]
        table = jnp.concatenate(thirds(jnp.concatenate(parts, axis=1)), axis=0)
        for start in range(0, 2 * half, chunk):
            odd = start >= half
            row, lane = slot_columns(places[start : start + chunk])
            shape = (chunk, 3 * lane_rows)
            wide = jnp.concatenate([row, row], axis=1)[:, : 3 * lane_rows]
            pick = onehot(wide == iota(shape, 1) % lane_rows)
            rows = matmul(pick, table)
            after = here >= lane
            joined = [
                jnp.where(
                    after,
                    rows[:, 2 * var * LANES : (2 * var + 1) * LANES],
                    rows[:, (2 * var + 1) * LANES : (2 * var + 2) * LANES],
                )
                for var in range(3)
            ]
            first = (here + lane) & 127
            second = (first + WINDOW) & 127
            demanded = ((here - lane) & 127) < WINDOW
            losses = lane_pick(jnp.where(demanded, joined[1], joined[2]), first)
            base = start - half if odd else start
            if odd:
                rains = jnp.where(
                    here < WINDOW, rain[pl.ds(base, chunk), :], lane_pick(joined[0], second)
                )
            else:
                rain[pl.ds(base, chunk), :] = lane_pick(joined[0], first)
            for part in range(0, chunk, pairs):
                place = (base + part) * 6 + number * 3 * pairs
                if odd:
                    out[pl.ds(place + pairs, pairs), :] = rains[part : part + pairs]
                    out[pl.ds(place + 2 * pairs, pairs), :] = losses[part : part + pairs]
                else:
                    out[pl.ds(place, pairs), :] = losses[part : part + pairs]

    windows(1, far_slots[pl.ds(0, 1), :], far_slots[pl.ds(1, 1), :], far_forcing)
    for copy in copies:
        copy.wait()
    windows(0, slot[...], offset[...], forcing)


def pack(homes, capacity, slot, offset, forcing, far_slots, far_forcing, after):
    slots = slot.shape[1]
    far = pl.BlockSpec(memory_space=pltpu.HBM)
    near = pl.BlockSpec(memory_space=pltpu.VMEM)
    return pl.pallas_call(
        functools.partial(pack_kernel, homes, capacity),
        in_specs=[far] * 3 + [near] * 2 + [pl.BlockSpec(memory_space=pl.ANY)] * 2,
        out_shape=jax.ShapeDtypeStruct((slots + slots // 2, LANES), jnp.float32),
        scratch_shapes=[
            pltpu.VMEM(slot.shape, jnp.int32),
            pltpu.VMEM(offset.shape, jnp.int32),
            pltpu.VMEM(forcing.shape, jnp.float32),
            pltpu.VMEM((slots // 4, LANES), jnp.float32),
            pltpu.SemaphoreType.DMA((3,)),
        ],
        compiler_params=pltpu.CompilerParams(vmem_limit_bytes=VMEM_LIMIT),
        cost_estimate=pl.CostEstimate(flops=10**9, bytes_accessed=2 * MIB, transcendentals=0),
        name="pack_forcing",
    )(in_hbm(slot), in_hbm(offset), in_hbm(forcing), far_slots, far_forcing, *after)


def unpack_plan_kernel(homes, capacity, lane_rows, slot, offset, code, place):
    slots = slot.shape[1]
    row, lane = slot_columns(slot_table(slot[...], offset[...], homes, capacity))
    here = iota((slots, LANES), 1)
    index = (here - lane) & 127
    inside = (index < WINDOW) & (row >= 0)
    code[...] = jnp.where(inside, index + jnp.where(here >= lane, 0, LANES), -1)
    row_lane, _ = slot_rows(slot[...], offset[...], homes, capacity)
    place[...] = onehot(iota((lane_rows, slots), 0) == row_lane)


def unpack_plan(homes, capacity, lane_rows, slot, offset):
    slots = slot.shape[1]
    return pl.pallas_call(
        functools.partial(unpack_plan_kernel, homes, capacity, lane_rows),
        out_shape=(
            jax.ShapeDtypeStruct((slots, LANES), jnp.int32),
            jax.ShapeDtypeStruct((lane_rows, slots), jnp.bfloat16),
        ),
        compiler_params=pltpu.CompilerParams(vmem_limit_bytes=VMEM_LIMIT),
        cost_estimate=pl.CostEstimate(flops=10**9, bytes_accessed=2 * MIB, transcendentals=0),
        name="unpack_plan",
    )(slot, offset)


def strips_for_neighbours(state, rows):
    device = iota((rows, LANES), 0) // ITERS
    down = device // lax.axis_size("col") - lax.axis_index(region)
    right = device % lax.axis_size("col") - lax.axis_index("col")
    height, width = state.shape
    columns = jnp.transpose(state)
    empty = jnp.zeros((ITERS, LANES - height), jnp.float32)

    def repeated(strip):
        if strip.shape[1] < LANES:
            strip = jnp.concatenate([strip, empty], axis=1)
        return jnp.concatenate([strip] * (rows // ITERS), axis=0)

    near = (jnp.abs(down) <= 1).astype(jnp.int32)
    strips = jnp.zeros((rows, LANES), jnp.float32)
    strips = jnp.where((right == 0) & (down == 1), repeated(state[height - ITERS :]), strips)
    strips = jnp.where((right == 0) & (down == -1), repeated(state[:ITERS]), strips)
    strips = jnp.where((right == 1) & (near == 1), repeated(columns[width - ITERS :]), strips)
    return jnp.where((right == -1) & (near == 1), repeated(columns[:ITERS]), strips)


def cell_totals(arrived, code, place, first):
    lane_rows = place.shape[0]
    marks = code[...]
    window = lane_pick(arrived[...], (marks + first) & 127)
    placed = jnp.concatenate(
        [
            jnp.where((marks >= 0) & (marks < LANES), window, 0.0),
            jnp.where(marks >= LANES, window, 0.0),
        ],
        axis=1,
    )
    totals = matmul(place[...], jnp.concatenate(halves(placed), axis=1))
    totals = totals[:, :256] + totals[:, 256:]
    over = totals[:, LANES:]
    over = jnp.concatenate([over[lane_rows - 1 :], over[: lane_rows - 1]], axis=0)
    over = jnp.where(iota(over.shape, 0) == 0, 0.0, over)
    return totals[:, :LANES] + over


def unpack_runoff_kernel(arrived, code, place, river, _, __, runoff, storage, strips):
    total = cell_totals(arrived, code, place, 0)
    state = river[...] + total
    runoff[...] = total
    storage[...] = state
    strips[...] = strips_for_neighbours(state, strips.shape[0])


def unpack_runoff(homes, arrived, code, place, river, *after):
    shape = jax.ShapeDtypeStruct((place.shape[0], LANES), jnp.float32)
    strips = jax.ShapeDtypeStruct((homes * ITERS, LANES), jnp.float32)
    return pl.pallas_call(
        unpack_runoff_kernel,
        in_specs=[pl.BlockSpec(memory_space=pltpu.VMEM)] * 4
        + [pl.BlockSpec(memory_space=pl.ANY)] * 2,
        out_shape=(shape, shape, strips),
        compiler_params=pltpu.CompilerParams(vmem_limit_bytes=VMEM_LIMIT),
        cost_estimate=pl.CostEstimate(flops=10**9, bytes_accessed=1 * MIB, transcendentals=0),
        name="unpack_runoff",
    )(arrived, code, place, river, *after)


def unpack_evap_kernel(arrived, code, place, evap):
    evap[...] = cell_totals(arrived, code, place, WINDOW)


def unpack_evap(arrived, code, place):
    return pl.pallas_call(
        unpack_evap_kernel,
        out_shape=jax.ShapeDtypeStruct((place.shape[0], LANES), jnp.float32),
        compiler_params=pltpu.CompilerParams(vmem_limit_bytes=VMEM_LIMIT),
        cost_estimate=pl.CostEstimate(flops=10**9, bytes_accessed=1 * MIB, transcendentals=0),
        name="unpack_evap",
    )(arrived, code, place)


def segment_plan_kernel(cell, worker, meta):
    chunk = 96
    for start in range(0, cell.shape[0], chunk):
        values = cell[pl.ds(start, chunk), :]
        target = iota(values.shape, 1) & (WINDOW - 1)
        count = jnp.zeros_like(values)
        for step in (64, 32, 16, 8, 4, 2, 1):
            probe = lane_pick(values, count + (step - 1))
            count = jnp.where(probe <= target, count + step, count)
        count = jnp.where(lane_pick(values, count) <= target, count + 1, count)
        odd = worker[pl.ds(start, chunk), :] & 1
        meta[pl.ds(start, chunk), :] = count + (odd << 8)


def segment_plan(cell, worker):
    return pl.pallas_call(
        segment_plan_kernel,
        out_shape=jax.ShapeDtypeStruct(cell.shape, jnp.int32),
        compiler_params=pltpu.CompilerParams(vmem_limit_bytes=VMEM_LIMIT),
        cost_estimate=pl.CostEstimate(flops=10**8, bytes_accessed=1 * MIB, transcendentals=0),
        name="segment_plan",
    )(cell, worker)


def layer_terms_kernel(soil, porosity, drainage, _, out):
    layers, block = soil.shape[:2]
    chunk = 48
    for start in range(0, block, chunk):
        part = pl.ds(start, chunk)
        share = inverse = None
        total = jnp.zeros((chunk, LANES), jnp.float32)
        for layer in range(layers):
            content, room = soil[layer, part, :], porosity[layer, part, :]
            if layer:
                content, room = content * inverse, room * inverse
            total = total + content
            out[0, layer, part, :] = room - total
            rate = drainage[layer, part, :]
            share = rate if layer == 0 else share * rate
            inverse = 1.0 / share
            out[0, layers + layer, part, :] = share
        out[0, 2 * layers, part, :] = total
        out[0, 2 * layers + 1, part, :] = soil[0, part, :]


def layer_terms(soil, porosity, drainage, after):
    layers, rows = soil.shape[:2]
    block = 96
    deep = pl.BlockSpec((layers, block, LANES), lambda i: (0, i, 0))
    shape = (rows // block, 2 * layers + 2, block, LANES)
    return pl.pallas_call(
        layer_terms_kernel,
        grid=(rows // block,),
        in_specs=[deep] * 3 + [pl.BlockSpec(memory_space=pl.ANY)],
        out_specs=pl.BlockSpec((1,) + shape[1:], lambda i: (i, 0, 0, 0)),
        out_shape=pltpu.HBM(shape, jnp.float32),
        compiler_params=pltpu.CompilerParams(vmem_limit_bytes=VMEM_LIMIT),
        cost_estimate=pl.CostEstimate(flops=10**8, bytes_accessed=19 * MIB, transcendentals=0),
        name="layer_terms",
    )(in_hbm(soil), in_hbm(porosity), in_hbm(drainage), after)


def land_sums_kernel(
    pairs, slots, first_rows, arrived, cell, meta, area, water, cap, terms_in, _, __, through,
    lost, canopy_new, sums_out, terms, fetched, runoffs, evaps, ready,
):
    steps, count, block = terms.shape[:3]
    layers = count // 2 - 1
    chunk = block // 2

    def part_of(step):
        return pl.ds(step * block, block)

    def reads(step):
        return [
            pltpu.make_async_copy(
                terms_in.at[step, part], terms.at[step, part], ready.at[step, i]
            )
            for i, part in enumerate((pl.ds(0, count // 2), pl.ds(count // 2, count // 2)))
        ]

    def fetch(step):
        for i in range(step * block, (step + 1) * block):
            fetched[pl.ds(2 * i, 2), :] = arrived[pl.ds(first_rows[i], 2, stride=pairs), :]

    def cascade(start):
        part = pl.ds(start, chunk)
        index = cell[part, :]
        one = fetched[pl.ds(2 * start, chunk, stride=2), :]
        two = fetched[pl.ds(2 * start + 1, chunk, stride=2), :]
        odd = meta[part, :] >> 8
        loss = jnp.where(odd == 1, two, one)
        rain = lane_pick(jnp.where(odd == 1, one, two), index + odd * WINDOW)
        demand = lane_pick(loss, index)
        limit = lane_pick(loss, index + WINDOW)
        wetted = water[part, :] + rain
        flowing = jnp.maximum(wetted - cap[part, :], 0.0)
        retained = jnp.minimum(wetted, cap[part, :])
        canopy_loss = jnp.minimum(demand, retained)
        canopy_new[part, :] = retained - canopy_loss
        through[part, :] = flowing
        step, local = start // block, pl.ds(start % block, chunk)
        surface = None
        for layer in range(layers):
            room = terms[step, layer, local, :]
            excess = jnp.maximum(flowing - room, 0.0)
            flowing = jnp.minimum(flowing, room)
            if layer == 0:
                surface = excess
                content = flowing + terms[step, 2 * layers + 1, local, :]
                half = 0.5 * (content - terms[step, layers, local, :] * content)
                soil_loss = jnp.minimum(jnp.minimum(limit, demand - canopy_loss), half)
                lost[part, :] = soil_loss
                evaps[part, :] = area[part, :] * (canopy_loss + soil_loss)
            else:
                surface = surface + terms[step, layers + layer - 1, local, :] * excess
        bottom = terms[step, 2 * layers - 1, local, :] * (
            flowing + terms[step, 2 * layers, local, :]
        )
        runoffs[part, :] = area[part, :] * (surface + bottom)

    def scan(step):
        part = part_of(step)
        shape = (2 * LANES, LANES)
        upto = onehot((iota(shape, 0) & 127) <= iota(shape, 1))
        patches = meta[part, :] & 255
        last = jnp.maximum(patches - 1, 0)
        here = iota((block, LANES), 1)
        picked = [
            lane_pick(matmul(jnp.concatenate(halves(value[part, :]), axis=1), upto), last)
            for value in (runoffs, evaps)
        ]
        reached = jnp.where(patches > 0, jnp.where(here < WINDOW, *picked), 0.0)
        before = jnp.where((here & (WINDOW - 1)) == 0, 0.0, pltpu.roll(reached, 1, 1))
        runoffs[part, :] = reached - before

    def hand_back(step):
        for i in range(step * block, (step + 1) * block):
            sums_out[pl.ds(slots[i], 1), :] = runoffs[pl.ds(i, 1), :]

    for step in range(steps):
        for copy in reads(step):
            copy.start()
    sums_out[...] = jnp.zeros_like(sums_out)
    for step in range(steps):
        fetch(step)
    for step in range(steps + 2):
        if step < steps:
            for copy in reads(step):
                copy.wait()
            for start in range(step * block, (step + 1) * block, chunk):
                cascade(start)
        if 1 <= step <= steps:
            scan(step - 1)
        if step >= 2:
            hand_back(step - 2)


def land_sums(
    sums_shape, pairs, slots, first_rows, arrived, cell, meta, area, water, cap, terms, after
):
    rows = cell.shape[0]
    near = pl.BlockSpec(memory_space=pltpu.VMEM)
    return pl.pallas_call(
        functools.partial(land_sums_kernel, pairs),
        in_specs=[pl.BlockSpec(memory_space=pltpu.SMEM)] * 2 + [near] * 6
        + [pl.BlockSpec(memory_space=pltpu.HBM)] + [pl.BlockSpec(memory_space=pl.ANY)] * 2,
        out_specs=[near] * 4,
        scratch_shapes=[
            pltpu.VMEM(terms.shape, jnp.float32),
            pltpu.VMEM((2 * rows, LANES), jnp.float32),
            pltpu.VMEM((rows, LANES), jnp.float32),
            pltpu.VMEM((rows, LANES), jnp.float32),
            pltpu.SemaphoreType.DMA((terms.shape[0], 2)),
        ],
        out_shape=[jax.ShapeDtypeStruct((rows, LANES), jnp.float32)] * 3
        + [jax.ShapeDtypeStruct(sums_shape, jnp.float32)],
        compiler_params=pltpu.CompilerParams(vmem_limit_bytes=VMEM_LIMIT),
        cost_estimate=pl.CostEstimate(flops=10**8, bytes_accessed=20 * MIB, transcendentals=0),
        name="land_sums",
    )(
        slots, first_rows, arrived, cell, meta, area, water, cap,
        in_hbm(terms), *after,
    )


def new_soil_kernel(through, lost, canopy, soil, porosity, drainage, *rest):
    soil_new, canopy_new = rest[-2:]
    layers, block = soil.shape[:2]
    chunk = 48
    canopy_new[...] = canopy[...]
    for start in range(0, block, chunk):
        part = pl.ds(start, chunk)
        flowing = through[part, :]
        for layer in range(layers):
            filled = soil[layer, part, :] + flowing
            filled = filled - jnp.maximum(filled - porosity[layer, part, :], 0.0)
            flowing = drainage[layer, part, :] * filled
            middle = filled - flowing
            soil_new[layer, part, :] = middle - lost[part, :] if layer == 0 else middle


def new_soil(first, last, through, lost, canopy, soil, porosity, drainage, made=(), after=None):
    layers, rows = soil.shape[:2]
    block = 96
    flat = pl.BlockSpec((block, LANES), lambda i: (first + i, 0))
    deep = pl.BlockSpec((layers, block, LANES), lambda i: (0, first + i, 0))
    anywhere = pl.BlockSpec(memory_space=pl.ANY)
    more = [in_hbm(value) for value in made] + ([] if after is None else [after])
    return pl.pallas_call(
        new_soil_kernel,
        grid=(last - first,),
        in_specs=[flat, flat, flat, deep, deep, deep] + [anywhere] * len(more),
        out_specs=[deep, flat],
        out_shape=(
            jax.ShapeDtypeStruct(soil.shape, jnp.float32),
            jax.ShapeDtypeStruct((rows, LANES), jnp.float32),
        ),
        input_output_aliases={6: 0, 7: 1} if made else {},
        compiler_params=pltpu.CompilerParams(vmem_limit_bytes=VMEM_LIMIT),
        cost_estimate=pl.CostEstimate(
            flops=10**8, bytes_accessed=3 * MIB * (last - first), transcendentals=0
        ),
        name="new_soil",
    )(through, lost, canopy, in_hbm(soil), in_hbm(porosity), in_hbm(drainage), *more)


def halo_parts(value, axis, dim, width):
    count, length = (lax.axis_size(axis), value.shape[dim])
    up = [(i, i + 1) for i in range(count - 1)]
    down = [(j, i) for i, j in up]
    last = lax.slice_in_dim(value, length - width, length, axis=dim)
    initial = lax.slice_in_dim(value, 0, width, axis=dim)
    return lax.ppermute(last, axis, up), lax.ppermute(initial, axis, down)


def edge_columns_kernel(tall, _, first, last):
    arrays, height, width = tall.shape
    for number in range(arrays):
        values = tall[number]
        values = jnp.concatenate([values, jnp.zeros((LANES - height, width), jnp.float32)], axis=0)
        columns = jnp.transpose(values)
        part = pl.ds(number * ITERS, ITERS)
        first[part, :] = columns[:ITERS]
        last[part, :] = columns[width - ITERS :]


def edge_columns(tall, after):
    shape = jax.ShapeDtypeStruct((2 * ITERS, LANES), jnp.float32)
    return pl.pallas_call(
        edge_columns_kernel,
        in_specs=[pl.BlockSpec(memory_space=pltpu.VMEM), pl.BlockSpec(memory_space=pl.ANY)],
        out_shape=(shape, shape),
        compiler_params=pltpu.CompilerParams(vmem_limit_bytes=VMEM_LIMIT),
        cost_estimate=pl.CostEstimate(flops=10**6, bytes_accessed=10**5, transcendentals=0),
        name="edge_columns",
    )(tall, after)


def extended(own, strip):
    height = own.shape[0]

    def column_strip(right):
        middle, above, below = strip(0, right), strip(-1, right), strip(1, right)
        return jnp.concatenate(
            [
                middle[:, :height],
                below[:, :ITERS],
                above[:, height - ITERS : height],
                jnp.zeros((ITERS, LANES - height - 2 * ITERS), jnp.float32),
            ],
            axis=1,
        )

    gap = jnp.zeros((LANES - 2 * ITERS, LANES), jnp.float32)
    sides = jnp.concatenate([column_strip(1), gap, column_strip(-1)], axis=0)
    sides = jnp.transpose(sides)[: height + 2 * ITERS]
    tall = jnp.concatenate([own, strip(1, 0), strip(-1, 0)], axis=0)
    return jnp.concatenate([tall, sides], axis=1)


def neighbour(down, right):
    row, column = lax.axis_index(region) + down, lax.axis_index("col") + right
    there = (row >= 0) & (row < lax.axis_size(region))
    there &= (column >= 0) & (column < lax.axis_size("col"))
    return jnp.where(there, row * lax.axis_size("col") + column, 0), jnp.where(there, 1.0, 0.0)


def static_halo_kernel(tall, before, after, out):
    height, width = tall.shape[1:]
    gap = jnp.zeros((LANES - 2 * ITERS, LANES), jnp.float32)
    for number in range(2):
        part = pl.ds(number * ITERS, ITERS)
        sides = jnp.transpose(jnp.concatenate([after[part, :], gap, before[part, :]], axis=0))
        out[number, :, :width] = tall[number]
        out[number, :, width:] = sides[:height]


def static_halo(tall, before, after):
    arrays, height, width = tall.shape
    return pl.pallas_call(
        static_halo_kernel,
        out_shape=jax.ShapeDtypeStruct((arrays, height, width + LANES), jnp.float32),
        compiler_params=pltpu.CompilerParams(vmem_limit_bytes=VMEM_LIMIT),
        cost_estimate=pl.CostEstimate(flops=10**6, bytes_accessed=10**6, transcendentals=0),
        name="static_halo",
    )(tall, before, after)


def river_kernel(state, strips, fixed, _, out):
    height, width = state.shape

    def strip(down, right):
        device, there = neighbour(down, right)
        return strips[pl.ds(device * ITERS, ITERS), :] * there

    storage = extended(state[...], strip)
    rate = fixed[0]
    code = fixed[1]
    rows, cols = storage.shape
    for _ in range(ITERS):
        outflow = rate * storage
        inflow = jnp.zeros_like(storage)
        for col_step in (-1, 0, 1):
            column = jnp.zeros_like(storage)
            for bit, (row_step, step) in enumerate(directions):
                if step != col_step:
                    continue
                leaving = jnp.where(code == float(1 << bit), outflow, 0.0)
                if row_step:
                    leaving = pltpu.roll(leaving, row_step % rows, 0)
                column = column + leaving
            if col_step:
                column = pltpu.roll(column, col_step % cols, 1)
            inflow = inflow + column
        storage = storage - outflow + inflow
    out[...] = storage[:height, :width]


def river(state, strips, fixed, after):
    return pl.pallas_call(
        river_kernel,
        in_specs=[pl.BlockSpec(memory_space=pltpu.VMEM)] * 3 + [pl.BlockSpec(memory_space=pl.ANY)],
        out_shape=jax.ShapeDtypeStruct(state.shape, jnp.float32),
        compiler_params=pltpu.CompilerParams(vmem_limit_bytes=VMEM_LIMIT),
        cost_estimate=pl.CostEstimate(flops=10**7, bytes_accessed=1 * MIB, transcendentals=0),
        name="river_steps",
    )(state, strips, fixed, in_hbm(after))


def exchange(value, over=axes):
    return lax.all_to_all(value, over, split_axis=0, concat_axis=0, tiled=True)


def shards(
    forcing,
    river_storage,
    river_rate,
    flow_code,
    home_slot,
    home_offset,
    worker_list,
    patch_cell,
    patch_area,
    canopy_water,
    canopy_cap,
    soil_water,
    porosity,
    drainage,
):
    homes = lax.axis_size(region) * lax.axis_size("col")
    capacity = home_slot.shape[1] // homes
    grid_rows, grid_cols = river_storage.shape
    lane_rows = grid_rows * grid_cols // LANES
    forcing = forcing.reshape(3, lane_rows, LANES)
    swap = [(0, 1), (1, 0)]
    far_slots = lax.ppermute(jnp.concatenate([home_slot, home_offset], axis=0), "half", swap)
    far_forcing = lax.ppermute(forcing, "half", swap)
    fixed = jnp.stack([river_rate, flow_code.astype(jnp.float32)])
    above, below = halo_parts(fixed, region, 1, ITERS)
    outgoing = pack(
        homes // 2, capacity, home_slot, home_offset, forcing, far_slots, far_forcing,
        (above, below),
    )
    arrived = exchange(outgoing, ("near", "col"))
    home = worker_list // capacity
    position = worker_list - home * capacity
    pairs = capacity // 2
    own_half = home // (homes // 2) == lax.axis_index("half")
    first_rows = home % (homes // 2) * (6 * pairs) + jnp.where(own_half, 0, 3 * pairs)
    first_rows = first_rows + position // 2 + position % 2 * pairs
    meta = segment_plan(patch_cell, worker_list[:, None])
    terms = layer_terms(soil_water, porosity, drainage, outgoing)
    through, lost, canopy, sums = land_sums(
        (homes * capacity, LANES), pairs, worker_list, first_rows, arrived, patch_cell, meta,
        patch_area, canopy_water, canopy_cap, terms, (above, below),
    )
    returned = exchange(sums)
    layers_of = (through, lost, canopy, soil_water, porosity, drainage)
    blocks = worker_list.shape[0] // 96
    early = blocks * 3 // 5
    made = new_soil(0, early, *layers_of)
    code, place = unpack_plan(homes, capacity, lane_rows, home_slot, home_offset)
    fixed = jnp.concatenate([fixed, below, above], axis=1)
    initial, last = edge_columns(fixed, sums)
    count = lax.axis_size("col")
    before = lax.ppermute(last, "col", [(i, i + 1) for i in range(count - 1)])
    after = lax.ppermute(initial, "col", [(i + 1, i) for i in range(count - 1)])
    fixed = static_halo(fixed, before, after)
    cell_runoff, storage, strips = unpack_runoff(
        homes, returned, code, place, river_storage.reshape(lane_rows, LANES), fixed,
        in_hbm(made[1]),
    )
    soil_new, canopy_new = new_soil(early, blocks, *layers_of, made, strips)
    cell_evap = unpack_evap(returned, code, place)
    river_new = river(
        storage.reshape(river_storage.shape), exchange(strips), fixed, canopy_new
    )
    return (
        soil_new,
        canopy_new,
        cell_runoff.reshape(river_storage.shape),
        cell_evap.reshape(river_storage.shape),
        river_new,
    )


def solution(mesh):
    rows, cols = mesh.devices.shape
    mesh = jax.sharding.Mesh(mesh.devices.reshape(2, rows // 2, cols), axes)
    placed = (
        P(None, region, "col"),
        P(region, "col"),
        P(region, "col"),
        P(region, "col"),
        P(axes, None),
        P(axes, None),
        P(axes),
        P(axes, None),
        P(axes, None),
        P(axes, None),
        P(axes, None),
        P(None, axes, None),
        P(None, axes, None),
        P(None, axes, None),
    )
    return jax.shard_map(
        shards,
        mesh=mesh,
        in_specs=placed,
        out_specs=(
            P(None, axes, None),
            P(axes, None),
            P(region, "col"),
            P(region, "col"),
            P(region, "col"),
        ),
        check_vma=False,
    )
```

```python
import functools

import jax
import jax.numpy as jnp
from jax import lax
from jax.experimental import pallas as pl
from jax.experimental.pallas import tpu as pltpu
from jax.sharding import PartitionSpec as P

ITERS = 4
WINDOW = 64
LANES = 128
MIB = 1024 * 1024
VMEM_LIMIT = 24 * MIB

directions = ((0, 1), (1, 1), (1, 0), (1, -1), (0, -1), (-1, -1), (-1, 0), (-1, 1))
region = ("half", "near")
axes = ("half", "near", "col")


def iota(shape, dim):
    return lax.broadcasted_iota(jnp.int32, shape, dim)


def onehot(mask):
    return jnp.where(mask, jnp.float32(1.0), jnp.float32(0.0)).astype(jnp.bfloat16)


def lane_pick(values, index):
    return jnp.take_along_axis(values, index, axis=1, mode="promise_in_bounds")


def in_hbm(value):
    return pltpu.with_memory_space_constraint(value, pltpu.HBM)


def thirds(value):
    high = value.astype(jnp.bfloat16)
    rest = value - high.astype(jnp.float32)
    middle = rest.astype(jnp.bfloat16)
    low = (rest - middle.astype(jnp.float32)).astype(jnp.bfloat16)
    return high, middle, low


def halves(value):
    high = value.astype(jnp.bfloat16)
    return high, (value - high.astype(jnp.float32)).astype(jnp.bfloat16)


def matmul(a, b, a_dim=1, b_dim=0):
    return lax.dot_general(
        a, b, (((a_dim,), (b_dim,)), ((), ())), preferred_element_type=jnp.float32
    )


def slot_factors(slot, offset, homes, capacity, first=0):
    slots = slot.shape[1]
    worker = slot // capacity if capacity & (capacity - 1) else slot >> (capacity.bit_length() - 1)
    position = slot - worker * capacity
    by_worker = onehot(iota((homes, slots), 0) + first == worker)
    at_position = iota((capacity, slots), 0) == position
    row = jnp.where(at_position, ((offset >> 7) + 1).astype(jnp.float32), 0.0)
    lane = jnp.where(at_position, (offset & 127).astype(jnp.float32), 0.0)
    return by_worker, row.astype(jnp.bfloat16), lane.astype(jnp.bfloat16)


def slot_table(slot, offset, homes, capacity, first=0, split=False):
    slots = homes * capacity
    by_worker, row, lane = slot_factors(slot, offset, homes, capacity, first)
    table = matmul(by_worker, jnp.concatenate([row, lane], axis=0), 1, 1)
    groups = 2 if split else 1
    spread = jnp.broadcast_to(
        table[:, None, :], (homes, capacity // groups, 2 * capacity)
    ).reshape(slots // groups, 2 * capacity)
    spread = jnp.concatenate([spread] * groups, axis=0)
    number = iota(spread.shape, 0)
    position = number % (capacity // groups) * groups + number // (slots // groups)
    place = position == iota(spread.shape, 1) % capacity
    return jnp.where(place, spread, 0.0).astype(jnp.bfloat16)


def slot_columns(table):
    width = table.shape[1]
    shape = (width, 2 * LANES)
    gather = onehot((iota(shape, 0) >= width // 2) == (iota(shape, 1) >= LANES))
    columns = matmul(table, gather).astype(jnp.int32)
    return columns[:, :LANES] - 1, columns[:, LANES:]


def slot_rows(slot, offset, homes, capacity):
    slots = slot.shape[1]
    by_worker, row, lane = slot_factors(slot, offset, homes, capacity)
    table = matmul(jnp.concatenate([row, lane], axis=0), by_worker, 1, 1).astype(jnp.bfloat16)
    number = iota((1, slots), 1)
    worker = number // capacity
    position = number - worker * capacity
    spread = matmul(table, onehot(iota((homes, slots), 0) == worker))
    at_position = iota((capacity, slots), 0) == position
    rows = jnp.sum(jnp.where(at_position, spread[:capacity], 0.0), axis=0, keepdims=True)
    lanes = jnp.sum(jnp.where(at_position, spread[capacity:], 0.0), axis=0, keepdims=True)
    return rows.astype(jnp.int32) - 1, lanes.astype(jnp.int32)


def put_windows(homes, capacity, stride, shift, out, rain, slots, offsets, values):
    first_home = lax.axis_index("half") * homes
    pairs = capacity // 2
    half = homes * pairs
    lane_rows = values.shape[1]
    chunk = 128
    here = iota((chunk, LANES), 1)
    places = slot_table(slots, offsets, homes, capacity, first_home, True)
    limit = pltpu.roll(values[2], WINDOW, 1)
    above = jnp.concatenate([limit[lane_rows - 1 :], limit[: lane_rows - 1]], axis=0)
    limit = jnp.where(iota(limit.shape, 1) < WINDOW, above, limit)
    parts = []
    for own in (values[0], values[1], limit):
        parts += [own, jnp.concatenate([own[1:], own[:1]], axis=0)]
    table = jnp.concatenate(thirds(jnp.concatenate(parts, axis=1)), axis=0)
    for start in range(0, 2 * half, chunk):
        odd = start >= half
        row, lane = slot_columns(places[start : start + chunk])
        shape = (chunk, 3 * lane_rows)
        wide = jnp.concatenate([row, row], axis=1)[:, : 3 * lane_rows]
        pick = onehot(wide == iota(shape, 1) % lane_rows)
        rows = matmul(pick, table)
        after = here >= lane
        joined = [
            jnp.where(
                after,
                rows[:, 2 * var * LANES : (2 * var + 1) * LANES],
                rows[:, (2 * var + 1) * LANES : (2 * var + 2) * LANES],
            )
            for var in range(3)
        ]
        first = (here + lane) & 127
        second = (first + WINDOW) & 127
        demanded = ((here - lane) & 127) < WINDOW
        losses = lane_pick(jnp.where(demanded, joined[1], joined[2]), first)
        base = start - half if odd else start
        if odd:
            rains = jnp.where(
                here < WINDOW, rain[pl.ds(base, chunk), :], lane_pick(joined[0], second)
            )
        else:
            rain[pl.ds(base, chunk), :] = lane_pick(joined[0], first)
        for part in range(0, chunk, pairs):
            place = (base + part) * stride + shift
            if odd:
                out[pl.ds(place + pairs, pairs), :] = rains[part : part + pairs]
                out[pl.ds(place + 2 * pairs, pairs), :] = losses[part : part + pairs]
            else:
                out[pl.ds(place, pairs), :] = losses[part : part + pairs]


def pack_own_kernel(
    homes, capacity, slot_in, offset_in, forcing_in, out, slot, offset, forcing, rain, ready
):
    copies = [
        pltpu.make_async_copy(source, target, ready.at[i])
        for i, (source, target) in enumerate(
            ((slot_in, slot), (offset_in, offset), (forcing_in, forcing))
        )
    ]
    for copy in copies:
        copy.start()
    for copy in copies:
        copy.wait()
    put_windows(homes, capacity, 3, 0, out, rain, slot[...], offset[...], forcing)


def pack_own(homes, capacity, slot, offset, forcing):
    rows = homes * capacity // 2
    return pl.pallas_call(
        functools.partial(pack_own_kernel, homes, capacity),
        in_specs=[pl.BlockSpec(memory_space=pltpu.HBM)] * 3,
        out_shape=jax.ShapeDtypeStruct((3 * rows, LANES), jnp.float32),
        scratch_shapes=[
            pltpu.VMEM(slot.shape, jnp.int32),
            pltpu.VMEM(offset.shape, jnp.int32),
            pltpu.VMEM(forcing.shape, jnp.float32),
            pltpu.VMEM((rows, LANES), jnp.float32),
            pltpu.SemaphoreType.DMA((3,)),
        ],
        compiler_params=pltpu.CompilerParams(vmem_limit_bytes=VMEM_LIMIT),
        cost_estimate=pl.CostEstimate(flops=10**9, bytes_accessed=2 * MIB, transcendentals=0),
        name="pack_own",
    )(in_hbm(slot), in_hbm(offset), in_hbm(forcing))


def pack_both_kernel(homes, capacity, own, far_slots, far_forcing, out, rain):
    size = own.shape[0] // homes
    for home in range(homes):
        out[pl.ds(2 * size * home, size), :] = own[pl.ds(size * home, size), :]
    slots, offsets = far_slots[pl.ds(0, 1), :], far_slots[pl.ds(1, 1), :]
    put_windows(homes, capacity, 6, size, out, rain, slots, offsets, far_forcing)


def pack_both(homes, capacity, own, far_slots, far_forcing):
    return pl.pallas_call(
        functools.partial(pack_both_kernel, homes, capacity),
        out_shape=jax.ShapeDtypeStruct((2 * own.shape[0], LANES), jnp.float32),
        scratch_shapes=[pltpu.VMEM((homes * capacity // 2, LANES), jnp.float32)],
        compiler_params=pltpu.CompilerParams(vmem_limit_bytes=VMEM_LIMIT),
        cost_estimate=pl.CostEstimate(flops=10**9, bytes_accessed=2 * MIB, transcendentals=0),
        name="pack_both",
    )(own, far_slots, far_forcing)


def unpack_plan_kernel(homes, capacity, lane_rows, slot, offset, code, place):
    slots = slot.shape[1]
    row, lane = slot_columns(slot_table(slot[...], offset[...], homes, capacity))
    here = iota((slots, LANES), 1)
    index = (here - lane) & 127
    inside = (index < WINDOW) & (row >= 0)
    code[...] = jnp.where(inside, index + jnp.where(here >= lane, 0, LANES), -1)
    row_lane, _ = slot_rows(slot[...], offset[...], homes, capacity)
    place[...] = onehot(iota((lane_rows, slots), 0) == row_lane)


def unpack_plan(homes, capacity, lane_rows, slot, offset):
    slots = slot.shape[1]
    return pl.pallas_call(
        functools.partial(unpack_plan_kernel, homes, capacity, lane_rows),
        out_shape=(
            jax.ShapeDtypeStruct((slots, LANES), jnp.int32),
            jax.ShapeDtypeStruct((lane_rows, slots), jnp.bfloat16),
        ),
        compiler_params=pltpu.CompilerParams(vmem_limit_bytes=VMEM_LIMIT),
        cost_estimate=pl.CostEstimate(flops=10**9, bytes_accessed=2 * MIB, transcendentals=0),
        name="unpack_plan",
    )(slot, offset)


def strips_for_neighbours(state, rows):
    device = iota((rows, LANES), 0) // ITERS
    down = device // lax.axis_size("col") - lax.axis_index(region)
    right = device % lax.axis_size("col") - lax.axis_index("col")
    height, width = state.shape
    columns = jnp.transpose(state)
    empty = jnp.zeros((ITERS, LANES - height), jnp.float32)

    def repeated(strip):
        if strip.shape[1] < LANES:
            strip = jnp.concatenate([strip, empty], axis=1)
        return jnp.concatenate([strip] * (rows // ITERS), axis=0)

    near = (jnp.abs(down) <= 1).astype(jnp.int32)
    strips = jnp.zeros((rows, LANES), jnp.float32)
    strips = jnp.where((right == 0) & (down == 1), repeated(state[height - ITERS :]), strips)
    strips = jnp.where((right == 0) & (down == -1), repeated(state[:ITERS]), strips)
    strips = jnp.where((right == 1) & (near == 1), repeated(columns[width - ITERS :]), strips)
    return jnp.where((right == -1) & (near == 1), repeated(columns[:ITERS]), strips)


def cell_totals(arrived, code, place, first):
    lane_rows = place.shape[0]
    marks = code[...]
    window = lane_pick(arrived[...], (marks + first) & 127)
    placed = jnp.concatenate(
        [
            jnp.where((marks >= 0) & (marks < LANES), window, 0.0),
            jnp.where(marks >= LANES, window, 0.0),
        ],
        axis=1,
    )
    totals = matmul(place[...], jnp.concatenate(halves(placed), axis=1))
    totals = totals[:, :256] + totals[:, 256:]
    over = totals[:, LANES:]
    over = jnp.concatenate([over[lane_rows - 1 :], over[: lane_rows - 1]], axis=0)
    over = jnp.where(iota(over.shape, 0) == 0, 0.0, over)
    return totals[:, :LANES] + over


def unpack_runoff_kernel(arrived, code, place, river, _, __, runoff, storage, strips):
    total = cell_totals(arrived, code, place, 0)
    state = river[...] + total
    runoff[...] = total
    storage[...] = state
    strips[...] = strips_for_neighbours(state, strips.shape[0])


def unpack_runoff(homes, arrived, code, place, river, *after):
    shape = jax.ShapeDtypeStruct((place.shape[0], LANES), jnp.float32)
    strips = jax.ShapeDtypeStruct((homes * ITERS, LANES), jnp.float32)
    return pl.pallas_call(
        unpack_runoff_kernel,
        in_specs=[pl.BlockSpec(memory_space=pltpu.VMEM)] * 4
        + [pl.BlockSpec(memory_space=pl.ANY)] * 2,
        out_shape=(shape, shape, strips),
        compiler_params=pltpu.CompilerParams(vmem_limit_bytes=VMEM_LIMIT),
        cost_estimate=pl.CostEstimate(flops=10**9, bytes_accessed=1 * MIB, transcendentals=0),
        name="unpack_runoff",
    )(arrived, code, place, river, *after)


def unpack_evap_kernel(arrived, code, place, evap):
    evap[...] = cell_totals(arrived, code, place, WINDOW)


def unpack_evap(arrived, code, place):
    return pl.pallas_call(
        unpack_evap_kernel,
        out_shape=jax.ShapeDtypeStruct((place.shape[0], LANES), jnp.float32),
        compiler_params=pltpu.CompilerParams(vmem_limit_bytes=VMEM_LIMIT),
        cost_estimate=pl.CostEstimate(flops=10**9, bytes_accessed=1 * MIB, transcendentals=0),
        name="unpack_evap",
    )(arrived, code, place)


def segment_plan_kernel(cell, worker, meta):
    chunk = 96
    for start in range(0, cell.shape[0], chunk):
        values = cell[pl.ds(start, chunk), :]
        target = iota(values.shape, 1) & (WINDOW - 1)
        count = jnp.zeros_like(values)
        for step in (64, 32, 16, 8, 4, 2, 1):
            probe = lane_pick(values, count + (step - 1))
            count = jnp.where(probe <= target, count + step, count)
        count = jnp.where(lane_pick(values, count) <= target, count + 1, count)
        odd = worker[pl.ds(start, chunk), :] & 1
        meta[pl.ds(start, chunk), :] = count + (odd << 8)


def segment_plan(cell, worker):
    return pl.pallas_call(
        segment_plan_kernel,
        out_shape=jax.ShapeDtypeStruct(cell.shape, jnp.int32),
        compiler_params=pltpu.CompilerParams(vmem_limit_bytes=VMEM_LIMIT),
        cost_estimate=pl.CostEstimate(flops=10**8, bytes_accessed=1 * MIB, transcendentals=0),
        name="segment_plan",
    )(cell, worker)


def land_sums_kernel(
    pairs, slots, first_rows, arrived, cell, meta, area, water, cap, soil_in, porosity_in,
    drainage_in, _, __, through, lost, canopy_new, sums_out, soil, porosity, drainage, fetched,
    runoffs, evaps, ready,
):
    layers, rows = soil.shape[:2]
    steps = ready.shape[0]
    block = rows // steps
    chunk = block // 2
    arrays = ((soil_in, soil), (porosity_in, porosity), (drainage_in, drainage))

    def part_of(step):
        return pl.ds(step * block, block)

    def reads(step):
        return [
            pltpu.make_async_copy(
                source.at[:, part_of(step), :], target.at[:, part_of(step), :], ready.at[step, i]
            )
            for i, (source, target) in enumerate(arrays)
        ]

    def fetch(step):
        for i in range(step * block, (step + 1) * block):
            fetched[pl.ds(2 * i, 2), :] = arrived[pl.ds(first_rows[i], 2, stride=pairs), :]

    def cascade(start):
        part = pl.ds(start, chunk)
        index = cell[part, :]
        one = fetched[pl.ds(2 * start, chunk, stride=2), :]
        two = fetched[pl.ds(2 * start + 1, chunk, stride=2), :]
        odd = meta[part, :] >> 8
        loss = jnp.where(odd == 1, two, one)
        rain = lane_pick(jnp.where(odd == 1, one, two), index + odd * WINDOW)
        demand = lane_pick(loss, index)
        limit = lane_pick(loss, index + WINDOW)
        wetted = water[part, :] + rain
        flowing = jnp.maximum(wetted - cap[part, :], 0.0)
        retained = jnp.minimum(wetted, cap[part, :])
        canopy_loss = jnp.minimum(demand, retained)
        canopy_new[part, :] = retained - canopy_loss
        through[part, :] = flowing
        surface = jnp.zeros_like(flowing)
        for layer in range(layers):
            filled = soil[layer, part, :] + flowing
            excess = jnp.maximum(filled - porosity[layer, part, :], 0.0)
            surface = surface + excess
            filled = filled - excess
            flowing = drainage[layer, part, :] * filled
            if layer == 0:
                half = 0.5 * (filled - flowing)
                soil_loss = jnp.minimum(jnp.minimum(limit, demand - canopy_loss), half)
                lost[part, :] = soil_loss
                evaps[part, :] = area[part, :] * (canopy_loss + soil_loss)
        runoffs[part, :] = area[part, :] * (surface + flowing)

    def scan(step):
        part = part_of(step)
        shape = (2 * LANES, LANES)
        upto = onehot((iota(shape, 0) & 127) <= iota(shape, 1))
        patches = meta[part, :] & 255
        last = jnp.maximum(patches - 1, 0)
        here = iota((block, LANES), 1)
        picked = [
            lane_pick(matmul(jnp.concatenate(halves(value[part, :]), axis=1), upto), last)
            for value in (runoffs, evaps)
        ]
        reached = jnp.where(patches > 0, jnp.where(here < WINDOW, *picked), 0.0)
        before = jnp.where((here & (WINDOW - 1)) == 0, 0.0, pltpu.roll(reached, 1, 1))
        runoffs[part, :] = reached - before

    def hand_back(step):
        for i in range(step * block, (step + 1) * block):
            sums_out[pl.ds(slots[i], 1), :] = runoffs[pl.ds(i, 1), :]

    for step in range(steps):
        for copy in reads(step):
            copy.start()
    sums_out[...] = jnp.zeros_like(sums_out)
    for step in range(steps):
        fetch(step)
    for step in range(steps + 2):
        if step < steps:
            for copy in reads(step):
                copy.wait()
            for start in range(step * block, (step + 1) * block, chunk):
                cascade(start)
        if 1 <= step <= steps:
            scan(step - 1)
        if step >= 2:
            hand_back(step - 2)


def land_sums(
    sums_shape, pairs, slots, first_rows, arrived, cell, meta, area, water, cap, soil, porosity,
    drainage, after,
):
    layers, rows = soil.shape[:2]
    steps = 5
    near = pl.BlockSpec(memory_space=pltpu.VMEM)
    far = pl.BlockSpec(memory_space=pltpu.HBM)
    return pl.pallas_call(
        functools.partial(land_sums_kernel, pairs),
        in_specs=[pl.BlockSpec(memory_space=pltpu.SMEM)] * 2 + [near] * 6 + [far] * 3
        + [pl.BlockSpec(memory_space=pl.ANY)] * 2,
        out_specs=[near] * 4,
        scratch_shapes=[pltpu.VMEM(soil.shape, jnp.float32)] * 3
        + [pltpu.VMEM((2 * rows, LANES), jnp.float32)]
        + [pltpu.VMEM((rows, LANES), jnp.float32)] * 2
        + [pltpu.SemaphoreType.DMA((steps, 3))],
        out_shape=[jax.ShapeDtypeStruct((rows, LANES), jnp.float32)] * 3
        + [jax.ShapeDtypeStruct(sums_shape, jnp.float32)],
        compiler_params=pltpu.CompilerParams(vmem_limit_bytes=VMEM_LIMIT),
        cost_estimate=pl.CostEstimate(flops=10**8, bytes_accessed=20 * MIB, transcendentals=0),
        name="land_sums",
    )(
        slots, first_rows, arrived, cell, meta, area, water, cap,
        in_hbm(soil), in_hbm(porosity), in_hbm(drainage), *after,
    )


def new_soil_kernel(through, lost, canopy, soil, porosity, drainage, *rest):
    soil_new, canopy_new = rest[-2:]
    layers, block = soil.shape[:2]
    chunk = 48
    canopy_new[...] = canopy[...]
    for start in range(0, block, chunk):
        part = pl.ds(start, chunk)
        flowing = through[part, :]
        for layer in range(layers):
            filled = soil[layer, part, :] + flowing
            filled = filled - jnp.maximum(filled - porosity[layer, part, :], 0.0)
            flowing = drainage[layer, part, :] * filled
            middle = filled - flowing
            soil_new[layer, part, :] = middle - lost[part, :] if layer == 0 else middle


def new_soil(first, last, through, lost, canopy, soil, porosity, drainage, made=(), after=None):
    layers, rows = soil.shape[:2]
    block = 96
    flat = pl.BlockSpec((block, LANES), lambda i: (first + i, 0))
    deep = pl.BlockSpec((layers, block, LANES), lambda i: (0, first + i, 0))
    anywhere = pl.BlockSpec(memory_space=pl.ANY)
    more = [in_hbm(value) for value in made] + ([] if after is None else [after])
    return pl.pallas_call(
        new_soil_kernel,
        grid=(last - first,),
        in_specs=[flat, flat, flat, deep, deep, deep] + [anywhere] * len(more),
        out_specs=[deep, flat],
        out_shape=(
            jax.ShapeDtypeStruct(soil.shape, jnp.float32),
            jax.ShapeDtypeStruct((rows, LANES), jnp.float32),
        ),
        input_output_aliases={6: 0, 7: 1} if made else {},
        compiler_params=pltpu.CompilerParams(vmem_limit_bytes=VMEM_LIMIT),
        cost_estimate=pl.CostEstimate(
            flops=10**8, bytes_accessed=3 * MIB * (last - first), transcendentals=0
        ),
        name="new_soil",
    )(through, lost, canopy, in_hbm(soil), in_hbm(porosity), in_hbm(drainage), *more)


def halo_parts(value, axis, dim, width):
    count, length = (lax.axis_size(axis), value.shape[dim])
    up = [(i, i + 1) for i in range(count - 1)]
    down = [(j, i) for i, j in up]
    last = lax.slice_in_dim(value, length - width, length, axis=dim)
    initial = lax.slice_in_dim(value, 0, width, axis=dim)
    return lax.ppermute(last, axis, up), lax.ppermute(initial, axis, down)


def rate_and_code_kernel(rate, code, _, out):
    out[0] = rate[...]
    out[1] = code[...].astype(jnp.float32)


def rate_and_code(rate, code, after):
    return pl.pallas_call(
        rate_and_code_kernel,
        in_specs=[pl.BlockSpec(memory_space=pltpu.VMEM)] * 2 + [pl.BlockSpec(memory_space=pl.ANY)],
        out_shape=jax.ShapeDtypeStruct((2,) + rate.shape, jnp.float32),
        compiler_params=pltpu.CompilerParams(vmem_limit_bytes=VMEM_LIMIT),
        cost_estimate=pl.CostEstimate(flops=10**5, bytes_accessed=10**5, transcendentals=0),
        name="rate_and_code",
    )(rate, code, after)


def edge_columns_kernel(tall, _, first, last):
    arrays, height, width = tall.shape
    for number in range(arrays):
        values = tall[number]
        values = jnp.concatenate([values, jnp.zeros((LANES - height, width), jnp.float32)], axis=0)
        columns = jnp.transpose(values)
        part = pl.ds(number * ITERS, ITERS)
        first[part, :] = columns[:ITERS]
        last[part, :] = columns[width - ITERS :]


def edge_columns(tall, after):
    shape = jax.ShapeDtypeStruct((2 * ITERS, LANES), jnp.float32)
    return pl.pallas_call(
        edge_columns_kernel,
        in_specs=[pl.BlockSpec(memory_space=pltpu.VMEM), pl.BlockSpec(memory_space=pl.ANY)],
        out_shape=(shape, shape),
        compiler_params=pltpu.CompilerParams(vmem_limit_bytes=VMEM_LIMIT),
        cost_estimate=pl.CostEstimate(flops=10**6, bytes_accessed=10**5, transcendentals=0),
        name="edge_columns",
    )(tall, after)


def extended(own, strip):
    height = own.shape[0]

    def column_strip(right):
        middle, above, below = strip(0, right), strip(-1, right), strip(1, right)
        return jnp.concatenate(
            [
                middle[:, :height],
                below[:, :ITERS],
                above[:, height - ITERS : height],
                jnp.zeros((ITERS, LANES - height - 2 * ITERS), jnp.float32),
            ],
            axis=1,
        )

    gap = jnp.zeros((LANES - 2 * ITERS, LANES), jnp.float32)
    sides = jnp.concatenate([column_strip(1), gap, column_strip(-1)], axis=0)
    sides = jnp.transpose(sides)[: height + 2 * ITERS]
    tall = jnp.concatenate([own, strip(1, 0), strip(-1, 0)], axis=0)
    return jnp.concatenate([tall, sides], axis=1)


def neighbour(down, right):
    row, column = lax.axis_index(region) + down, lax.axis_index("col") + right
    there = (row >= 0) & (row < lax.axis_size(region))
    there &= (column >= 0) & (column < lax.axis_size("col"))
    return jnp.where(there, row * lax.axis_size("col") + column, 0), jnp.where(there, 1.0, 0.0)


def static_halo_kernel(tall, before, after, out):
    height, width = tall.shape[1:]
    gap = jnp.zeros((LANES - 2 * ITERS, LANES), jnp.float32)
    for number in range(2):
        part = pl.ds(number * ITERS, ITERS)
        sides = jnp.transpose(jnp.concatenate([after[part, :], gap, before[part, :]], axis=0))
        out[number, :, :width] = tall[number]
        out[number, :, width:] = sides[:height]


def static_halo(tall, before, after):
    arrays, height, width = tall.shape
    return pl.pallas_call(
        static_halo_kernel,
        out_shape=jax.ShapeDtypeStruct((arrays, height, width + LANES), jnp.float32),
        compiler_params=pltpu.CompilerParams(vmem_limit_bytes=VMEM_LIMIT),
        cost_estimate=pl.CostEstimate(flops=10**6, bytes_accessed=10**6, transcendentals=0),
        name="static_halo",
    )(tall, before, after)


def river_kernel(state, strips, fixed, _, out):
    height, width = state.shape

    def strip(down, right):
        device, there = neighbour(down, right)
        return strips[pl.ds(device * ITERS, ITERS), :] * there

    storage = extended(state[...], strip)
    rate = fixed[0]
    code = fixed[1]
    rows, cols = storage.shape
    for _ in range(ITERS):
        outflow = rate * storage
        inflow = jnp.zeros_like(storage)
        for col_step in (-1, 0, 1):
            column = jnp.zeros_like(storage)
            for bit, (row_step, step) in enumerate(directions):
                if step != col_step:
                    continue
                leaving = jnp.where(code == float(1 << bit), outflow, 0.0)
                if row_step:
                    leaving = pltpu.roll(leaving, row_step % rows, 0)
                column = column + leaving
            if col_step:
                column = pltpu.roll(column, col_step % cols, 1)
            inflow = inflow + column
        storage = storage - outflow + inflow
    out[...] = storage[:height, :width]


def river(state, strips, fixed, after):
    return pl.pallas_call(
        river_kernel,
        in_specs=[pl.BlockSpec(memory_space=pltpu.VMEM)] * 3 + [pl.BlockSpec(memory_space=pl.ANY)],
        out_shape=jax.ShapeDtypeStruct(state.shape, jnp.float32),
        compiler_params=pltpu.CompilerParams(vmem_limit_bytes=VMEM_LIMIT),
        cost_estimate=pl.CostEstimate(flops=10**7, bytes_accessed=1 * MIB, transcendentals=0),
        name="river_steps",
    )(state, strips, fixed, in_hbm(after))


def exchange(value, over=axes):
    return lax.all_to_all(value, over, split_axis=0, concat_axis=0, tiled=True)


def shards(
    forcing,
    river_storage,
    river_rate,
    flow_code,
    home_slot,
    home_offset,
    worker_list,
    patch_cell,
    patch_area,
    canopy_water,
    canopy_cap,
    soil_water,
    porosity,
    drainage,
):
    homes = lax.axis_size(region) * lax.axis_size("col")
    capacity = home_slot.shape[1] // homes
    grid_rows, grid_cols = river_storage.shape
    lane_rows = grid_rows * grid_cols // LANES
    forcing = forcing.reshape(3, lane_rows, LANES)
    swap = [(0, 1), (1, 0)]
    far_slots = lax.ppermute(jnp.concatenate([home_slot, home_offset], axis=0), "half", swap)
    far_forcing = lax.ppermute(forcing, "half", swap)
    own = pack_own(homes // 2, capacity, home_slot, home_offset, forcing)
    outgoing = pack_both(homes // 2, capacity, own, far_slots, far_forcing)
    arrived = exchange(outgoing, ("near", "col"))
    home = worker_list // capacity
    position = worker_list - home * capacity
    pairs = capacity // 2
    own_half = home // (homes // 2) == lax.axis_index("half")
    first_rows = home % (homes // 2) * (6 * pairs) + jnp.where(own_half, 0, 3 * pairs)
    first_rows = first_rows + position // 2 + position % 2 * pairs
    meta = segment_plan(patch_cell, worker_list[:, None])
    fixed = rate_and_code(river_rate, flow_code, outgoing)
    above, below = halo_parts(fixed, region, 1, ITERS)
    through, lost, canopy, sums = land_sums(
        (homes * capacity, LANES), pairs, worker_list, first_rows, arrived, patch_cell, meta,
        patch_area, canopy_water, canopy_cap, soil_water, porosity, drainage, (above, below),
    )
    returned = exchange(sums)
    layers_of = (through, lost, canopy, soil_water, porosity, drainage)
    blocks = worker_list.shape[0] // 96
    early = blocks * 3 // 5
    made = new_soil(0, early, *layers_of)
    code, place = unpack_plan(homes, capacity, lane_rows, home_slot, home_offset)
    fixed = jnp.concatenate([fixed, below, above], axis=1)
    initial, last = edge_columns(fixed, sums)
    count = lax.axis_size("col")
    before = lax.ppermute(last, "col", [(i, i + 1) for i in range(count - 1)])
    after = lax.ppermute(initial, "col", [(i + 1, i) for i in range(count - 1)])
    fixed = static_halo(fixed, before, after)
    cell_runoff, storage, strips = unpack_runoff(
        homes, returned, code, place, river_storage.reshape(lane_rows, LANES), fixed,
        in_hbm(made[1]),
    )
    soil_new, canopy_new = new_soil(early, blocks, *layers_of, made, strips)
    cell_evap = unpack_evap(returned, code, place)
    river_new = river(
        storage.reshape(river_storage.shape), exchange(strips), fixed, canopy_new
    )
    return (
        soil_new,
        canopy_new,
        cell_runoff.reshape(river_storage.shape),
        cell_evap.reshape(river_storage.shape),
        river_new,
    )


def solution(mesh):
    rows, cols = mesh.devices.shape
    mesh = jax.sharding.Mesh(mesh.devices.reshape(2, rows // 2, cols), axes)
    placed = (
        P(None, region, "col"),
        P(region, "col"),
        P(region, "col"),
        P(region, "col"),
        P(axes, None),
        P(axes, None),
        P(axes),
        P(axes, None),
        P(axes, None),
        P(axes, None),
        P(axes, None),
        P(None, axes, None),
        P(None, axes, None),
        P(None, axes, None),
    )
    return jax.shard_map(
        shards,
        mesh=mesh,
        in_specs=placed,
        out_specs=(
            P(None, axes, None),
            P(axes, None),
            P(region, "col"),
            P(region, "col"),
            P(region, "col"),
        ),
        check_vma=False,
    )
```

```python
import functools

import jax
import jax.numpy as jnp
from jax import lax
from jax.experimental import pallas as pl
from jax.experimental.pallas import tpu as pltpu
from jax.sharding import PartitionSpec as P

ITERS = 4
WINDOW = 64
LANES = 128
MIB = 1024 * 1024
VMEM_LIMIT = 24 * MIB

directions = ((0, 1), (1, 1), (1, 0), (1, -1), (0, -1), (-1, -1), (-1, 0), (-1, 1))
region = ("half", "near")
axes = ("half", "near", "col")


def iota(shape, dim):
    return lax.broadcasted_iota(jnp.int32, shape, dim)


def onehot(mask):
    return jnp.where(mask, jnp.float32(1.0), jnp.float32(0.0)).astype(jnp.bfloat16)


def lane_pick(values, index):
    return jnp.take_along_axis(values, index, axis=1, mode="promise_in_bounds")


def in_hbm(value):
    return pltpu.with_memory_space_constraint(value, pltpu.HBM)


def thirds(value):
    high = value.astype(jnp.bfloat16)
    rest = value - high.astype(jnp.float32)
    middle = rest.astype(jnp.bfloat16)
    low = (rest - middle.astype(jnp.float32)).astype(jnp.bfloat16)
    return high, middle, low


def halves(value):
    high = value.astype(jnp.bfloat16)
    return high, (value - high.astype(jnp.float32)).astype(jnp.bfloat16)


def matmul(a, b, a_dim=1, b_dim=0):
    return lax.dot_general(
        a, b, (((a_dim,), (b_dim,)), ((), ())), preferred_element_type=jnp.float32
    )


def slot_factors(slot, offset, homes, capacity, first=0):
    slots = slot.shape[1]
    worker = slot // capacity if capacity & (capacity - 1) else slot >> (capacity.bit_length() - 1)
    position = slot - worker * capacity
    by_worker = onehot(iota((homes, slots), 0) + first == worker)
    at_position = iota((capacity, slots), 0) == position
    row = jnp.where(at_position, ((offset >> 7) + 1).astype(jnp.float32), 0.0)
    lane = jnp.where(at_position, (offset & 127).astype(jnp.float32), 0.0)
    return by_worker, row.astype(jnp.bfloat16), lane.astype(jnp.bfloat16)


def slot_table(slot, offset, homes, capacity, first=0, split=False):
    slots = homes * capacity
    by_worker, row, lane = slot_factors(slot, offset, homes, capacity, first)
    table = matmul(by_worker, jnp.concatenate([row, lane], axis=0), 1, 1)
    groups = 2 if split else 1
    spread = jnp.broadcast_to(
        table[:, None, :], (homes, capacity // groups, 2 * capacity)
    ).reshape(slots // groups, 2 * capacity)
    spread = jnp.concatenate([spread] * groups, axis=0)
    number = iota(spread.shape, 0)
    position = number % (capacity // groups) * groups + number // (slots // groups)
    place = position == iota(spread.shape, 1) % capacity
    return jnp.where(place, spread, 0.0).astype(jnp.bfloat16)


def slot_columns(table):
    width = table.shape[1]
    shape = (width, 2 * LANES)
    gather = onehot((iota(shape, 0) >= width // 2) == (iota(shape, 1) >= LANES))
    columns = matmul(table, gather).astype(jnp.int32)
    return columns[:, :LANES] - 1, columns[:, LANES:]


def slot_rows(slot, offset, homes, capacity):
    slots = slot.shape[1]
    by_worker, row, lane = slot_factors(slot, offset, homes, capacity)
    table = matmul(jnp.concatenate([row, lane], axis=0), by_worker, 1, 1).astype(jnp.bfloat16)
    number = iota((1, slots), 1)
    worker = number // capacity
    position = number - worker * capacity
    spread = matmul(table, onehot(iota((homes, slots), 0) == worker))
    at_position = iota((capacity, slots), 0) == position
    rows = jnp.sum(jnp.where(at_position, spread[:capacity], 0.0), axis=0, keepdims=True)
    lanes = jnp.sum(jnp.where(at_position, spread[capacity:], 0.0), axis=0, keepdims=True)
    return rows.astype(jnp.int32) - 1, lanes.astype(jnp.int32)


def put_windows(homes, capacity, stride, shift, out, rain, slots, offsets, values):
    first_home = lax.axis_index("half") * homes
    pairs = capacity // 2
    half = homes * pairs
    lane_rows = values.shape[1]
    chunk = 128
    here = iota((chunk, LANES), 1)
    places = slot_table(slots, offsets, homes, capacity, first_home, True)
    limit = pltpu.roll(values[2], WINDOW, 1)
    above = jnp.concatenate([limit[lane_rows - 1 :], limit[: lane_rows - 1]], axis=0)
    limit = jnp.where(iota(limit.shape, 1) < WINDOW, above, limit)
    parts = []
    for own in (values[0], values[1], limit):
        parts += [own, jnp.concatenate([own[1:], own[:1]], axis=0)]
    table = jnp.concatenate(thirds(jnp.concatenate(parts, axis=1)), axis=0)
    for start in range(0, 2 * half, chunk):
        odd = start >= half
        row, lane = slot_columns(places[start : start + chunk])
        shape = (chunk, 3 * lane_rows)
        wide = jnp.concatenate([row, row], axis=1)[:, : 3 * lane_rows]
        pick = onehot(wide == iota(shape, 1) % lane_rows)
        rows = matmul(pick, table)
        after = here >= lane
        joined = [
            jnp.where(
                after,
                rows[:, 2 * var * LANES : (2 * var + 1) * LANES],
                rows[:, (2 * var + 1) * LANES : (2 * var + 2) * LANES],
            )
            for var in range(3)
        ]
        first = (here + lane) & 127
        second = (first + WINDOW) & 127
        demanded = ((here - lane) & 127) < WINDOW
        losses = lane_pick(jnp.where(demanded, joined[1], joined[2]), first)
        base = start - half if odd else start
        if odd:
            rains = jnp.where(
                here < WINDOW, rain[pl.ds(base, chunk), :], lane_pick(joined[0], second)
            )
        else:
            rain[pl.ds(base, chunk), :] = lane_pick(joined[0], first)
        for part in range(0, chunk, pairs):
            place = (base + part) * stride + shift
            if odd:
                out[pl.ds(place + pairs, pairs), :] = rains[part : part + pairs]
                out[pl.ds(place + 2 * pairs, pairs), :] = losses[part : part + pairs]
            else:
                out[pl.ds(place, pairs), :] = losses[part : part + pairs]


def pack_own_kernel(
    homes, capacity, slot_in, offset_in, forcing_in, out, slot, offset, forcing, rain, ready
):
    copies = [
        pltpu.make_async_copy(source, target, ready.at[i])
        for i, (source, target) in enumerate(
            ((slot_in, slot), (offset_in, offset), (forcing_in, forcing))
        )
    ]
    for copy in copies:
        copy.start()
    for copy in copies:
        copy.wait()
    put_windows(homes, capacity, 3, 0, out, rain, slot[...], offset[...], forcing)


def pack_own(homes, capacity, slot, offset, forcing):
    rows = homes * capacity // 2
    return pl.pallas_call(
        functools.partial(pack_own_kernel, homes, capacity),
        in_specs=[pl.BlockSpec(memory_space=pltpu.HBM)] * 3,
        out_shape=jax.ShapeDtypeStruct((3 * rows, LANES), jnp.float32),
        scratch_shapes=[
            pltpu.VMEM(slot.shape, jnp.int32),
            pltpu.VMEM(offset.shape, jnp.int32),
            pltpu.VMEM(forcing.shape, jnp.float32),
            pltpu.VMEM((rows, LANES), jnp.float32),
            pltpu.SemaphoreType.DMA((3,)),
        ],
        compiler_params=pltpu.CompilerParams(vmem_limit_bytes=VMEM_LIMIT),
        cost_estimate=pl.CostEstimate(flops=10**9, bytes_accessed=2 * MIB, transcendentals=0),
        name="pack_own",
    )(in_hbm(slot), in_hbm(offset), in_hbm(forcing))


def pack_both_kernel(homes, capacity, own, far_slot, far_offset, far_forcing, out, rain):
    size = own.shape[0] // homes
    for home in range(homes):
        out[pl.ds(2 * size * home, size), :] = own[pl.ds(size * home, size), :]
    put_windows(
        homes, capacity, 6, size, out, rain, far_slot[...], far_offset[...], far_forcing
    )


def pack_both(homes, capacity, own, far_slot, far_offset, far_forcing):
    return pl.pallas_call(
        functools.partial(pack_both_kernel, homes, capacity),
        out_shape=jax.ShapeDtypeStruct((2 * own.shape[0], LANES), jnp.float32),
        scratch_shapes=[pltpu.VMEM((homes * capacity // 2, LANES), jnp.float32)],
        compiler_params=pltpu.CompilerParams(vmem_limit_bytes=VMEM_LIMIT),
        cost_estimate=pl.CostEstimate(flops=10**9, bytes_accessed=2 * MIB, transcendentals=0),
        name="pack_both",
    )(own, far_slot, far_offset, far_forcing)


def unpack_plan_kernel(homes, capacity, lane_rows, slot, offset, code, place):
    slots = slot.shape[1]
    row, lane = slot_columns(slot_table(slot[...], offset[...], homes, capacity))
    here = iota((slots, LANES), 1)
    index = (here - lane) & 127
    inside = (index < WINDOW) & (row >= 0)
    code[...] = jnp.where(inside, index + jnp.where(here >= lane, 0, LANES), -1)
    row_lane, _ = slot_rows(slot[...], offset[...], homes, capacity)
    place[...] = onehot(iota((lane_rows, slots), 0) == row_lane)


def unpack_plan(homes, capacity, lane_rows, slot, offset):
    slots = slot.shape[1]
    return pl.pallas_call(
        functools.partial(unpack_plan_kernel, homes, capacity, lane_rows),
        out_shape=(
            jax.ShapeDtypeStruct((slots, LANES), jnp.int32),
            jax.ShapeDtypeStruct((lane_rows, slots), jnp.bfloat16),
        ),
        compiler_params=pltpu.CompilerParams(vmem_limit_bytes=VMEM_LIMIT),
        cost_estimate=pl.CostEstimate(flops=10**9, bytes_accessed=2 * MIB, transcendentals=0),
        name="unpack_plan",
    )(slot, offset)


def strips_for_neighbours(state, rows):
    device = iota((rows, LANES), 0) // ITERS
    down = device // lax.axis_size("col") - lax.axis_index(region)
    right = device % lax.axis_size("col") - lax.axis_index("col")
    height, width = state.shape
    columns = jnp.transpose(state)
    empty = jnp.zeros((ITERS, LANES - height), jnp.float32)

    def repeated(strip):
        if strip.shape[1] < LANES:
            strip = jnp.concatenate([strip, empty], axis=1)
        return jnp.concatenate([strip] * (rows // ITERS), axis=0)

    near = (jnp.abs(down) <= 1).astype(jnp.int32)
    strips = jnp.zeros((rows, LANES), jnp.float32)
    strips = jnp.where((right == 0) & (down == 1), repeated(state[height - ITERS :]), strips)
    strips = jnp.where((right == 0) & (down == -1), repeated(state[:ITERS]), strips)
    strips = jnp.where((right == 1) & (near == 1), repeated(columns[width - ITERS :]), strips)
    return jnp.where((right == -1) & (near == 1), repeated(columns[:ITERS]), strips)


def cell_totals(arrived, code, place, first):
    lane_rows = place.shape[0]
    marks = code[...]
    window = lane_pick(arrived[...], (marks + first) & 127)
    placed = jnp.concatenate(
        [
            jnp.where((marks >= 0) & (marks < LANES), window, 0.0),
            jnp.where(marks >= LANES, window, 0.0),
        ],
        axis=1,
    )
    totals = matmul(place[...], jnp.concatenate(halves(placed), axis=1))
    totals = totals[:, :256] + totals[:, 256:]
    over = totals[:, LANES:]
    over = jnp.concatenate([over[lane_rows - 1 :], over[: lane_rows - 1]], axis=0)
    over = jnp.where(iota(over.shape, 0) == 0, 0.0, over)
    return totals[:, :LANES] + over


def unpack_runoff_kernel(arrived, code, place, river, _, __, runoff, storage, strips):
    total = cell_totals(arrived, code, place, 0)
    state = river[...] + total
    runoff[...] = total
    storage[...] = state
    strips[...] = strips_for_neighbours(state, strips.shape[0])


def unpack_runoff(homes, arrived, code, place, river, *after):
    shape = jax.ShapeDtypeStruct((place.shape[0], LANES), jnp.float32)
    strips = jax.ShapeDtypeStruct((homes * ITERS, LANES), jnp.float32)
    return pl.pallas_call(
        unpack_runoff_kernel,
        in_specs=[pl.BlockSpec(memory_space=pltpu.VMEM)] * 4
        + [pl.BlockSpec(memory_space=pl.ANY)] * 2,
        out_shape=(shape, shape, strips),
        compiler_params=pltpu.CompilerParams(vmem_limit_bytes=VMEM_LIMIT),
        cost_estimate=pl.CostEstimate(flops=10**9, bytes_accessed=1 * MIB, transcendentals=0),
        name="unpack_runoff",
    )(arrived, code, place, river, *after)


def unpack_evap_kernel(arrived, code, place, evap):
    evap[...] = cell_totals(arrived, code, place, WINDOW)


def unpack_evap(arrived, code, place):
    return pl.pallas_call(
        unpack_evap_kernel,
        out_shape=jax.ShapeDtypeStruct((place.shape[0], LANES), jnp.float32),
        compiler_params=pltpu.CompilerParams(vmem_limit_bytes=VMEM_LIMIT),
        cost_estimate=pl.CostEstimate(flops=10**9, bytes_accessed=1 * MIB, transcendentals=0),
        name="unpack_evap",
    )(arrived, code, place)


def segment_plan_kernel(cell, worker, meta):
    chunk = 96
    for start in range(0, cell.shape[0], chunk):
        values = cell[pl.ds(start, chunk), :]
        target = iota(values.shape, 1) & (WINDOW - 1)
        count = jnp.zeros_like(values)
        for step in (64, 32, 16, 8, 4, 2, 1):
            probe = lane_pick(values, count + (step - 1))
            count = jnp.where(probe <= target, count + step, count)
        count = jnp.where(lane_pick(values, count) <= target, count + 1, count)
        odd = worker[pl.ds(start, chunk), :] & 1
        meta[pl.ds(start, chunk), :] = count + (odd << 8)


def segment_plan(cell, worker):
    return pl.pallas_call(
        segment_plan_kernel,
        out_shape=jax.ShapeDtypeStruct(cell.shape, jnp.int32),
        compiler_params=pltpu.CompilerParams(vmem_limit_bytes=VMEM_LIMIT),
        cost_estimate=pl.CostEstimate(flops=10**8, bytes_accessed=1 * MIB, transcendentals=0),
        name="segment_plan",
    )(cell, worker)


def land_sums_kernel(
    pairs, slots, first_rows, arrived, cell, meta, area, water, cap, soil_in, porosity_in,
    drainage_in, _, __, through, lost, canopy_new, sums_out, soil, porosity, drainage, fetched,
    runoffs, evaps, ready,
):
    layers, rows = soil.shape[:2]
    steps = ready.shape[0]
    block = rows // steps
    chunk = block // 2
    arrays = ((soil_in, soil), (porosity_in, porosity), (drainage_in, drainage))

    def part_of(step):
        return pl.ds(step * block, block)

    def reads(step):
        return [
            pltpu.make_async_copy(
                source.at[:, part_of(step), :], target.at[:, part_of(step), :], ready.at[step, i]
            )
            for i, (source, target) in enumerate(arrays)
        ]

    def fetch(step):
        for i in range(step * block, (step + 1) * block):
            fetched[pl.ds(2 * i, 2), :] = arrived[pl.ds(first_rows[i], 2, stride=pairs), :]

    def cascade(start):
        part = pl.ds(start, chunk)
        index = cell[part, :]
        one = fetched[pl.ds(2 * start, chunk, stride=2), :]
        two = fetched[pl.ds(2 * start + 1, chunk, stride=2), :]
        odd = meta[part, :] >> 8
        loss = jnp.where(odd == 1, two, one)
        rain = lane_pick(jnp.where(odd == 1, one, two), index + odd * WINDOW)
        demand = lane_pick(loss, index)
        limit = lane_pick(loss, index + WINDOW)
        wetted = water[part, :] + rain
        flowing = jnp.maximum(wetted - cap[part, :], 0.0)
        retained = jnp.minimum(wetted, cap[part, :])
        canopy_loss = jnp.minimum(demand, retained)
        canopy_new[part, :] = retained - canopy_loss
        through[part, :] = flowing
        surface = jnp.zeros_like(flowing)
        for layer in range(layers):
            filled = soil[layer, part, :] + flowing
            excess = jnp.maximum(filled - porosity[layer, part, :], 0.0)
            surface = surface + excess
            filled = filled - excess
            flowing = drainage[layer, part, :] * filled
            if layer == 0:
                half = 0.5 * (filled - flowing)
                soil_loss = jnp.minimum(jnp.minimum(limit, demand - canopy_loss), half)
                lost[part, :] = soil_loss
                evaps[part, :] = area[part, :] * (canopy_loss + soil_loss)
        runoffs[part, :] = area[part, :] * (surface + flowing)

    def scan(step):
        part = part_of(step)
        shape = (2 * LANES, LANES)
        upto = onehot((iota(shape, 0) & 127) <= iota(shape, 1))
        patches = meta[part, :] & 255
        last = jnp.maximum(patches - 1, 0)
        here = iota((block, LANES), 1)
        picked = [
            lane_pick(matmul(jnp.concatenate(halves(value[part, :]), axis=1), upto), last)
            for value in (runoffs, evaps)
        ]
        reached = jnp.where(patches > 0, jnp.where(here < WINDOW, *picked), 0.0)
        before = jnp.where((here & (WINDOW - 1)) == 0, 0.0, pltpu.roll(reached, 1, 1))
        runoffs[part, :] = reached - before

    def hand_back(step):
        for i in range(step * block, (step + 1) * block):
            sums_out[pl.ds(slots[i], 1), :] = runoffs[pl.ds(i, 1), :]

    for step in range(steps):
        for copy in reads(step):
            copy.start()
    sums_out[...] = jnp.zeros_like(sums_out)
    for step in range(steps):
        fetch(step)
    for step in range(steps + 2):
        if step < steps:
            for copy in reads(step):
                copy.wait()
            for start in range(step * block, (step + 1) * block, chunk):
                cascade(start)
        if 1 <= step <= steps:
            scan(step - 1)
        if step >= 2:
            hand_back(step - 2)


def land_sums(
    sums_shape, pairs, slots, first_rows, arrived, cell, meta, area, water, cap, soil, porosity,
    drainage, after,
):
    layers, rows = soil.shape[:2]
    steps = 5
    near = pl.BlockSpec(memory_space=pltpu.VMEM)
    far = pl.BlockSpec(memory_space=pltpu.HBM)
    return pl.pallas_call(
        functools.partial(land_sums_kernel, pairs),
        in_specs=[pl.BlockSpec(memory_space=pltpu.SMEM)] * 2 + [near] * 6 + [far] * 3
        + [pl.BlockSpec(memory_space=pl.ANY)] * 2,
        out_specs=[near] * 4,
        scratch_shapes=[pltpu.VMEM(soil.shape, jnp.float32)] * 3
        + [pltpu.VMEM((2 * rows, LANES), jnp.float32)]
        + [pltpu.VMEM((rows, LANES), jnp.float32)] * 2
        + [pltpu.SemaphoreType.DMA((steps, 3))],
        out_shape=[jax.ShapeDtypeStruct((rows, LANES), jnp.float32)] * 3
        + [jax.ShapeDtypeStruct(sums_shape, jnp.float32)],
        compiler_params=pltpu.CompilerParams(vmem_limit_bytes=VMEM_LIMIT),
        cost_estimate=pl.CostEstimate(flops=10**8, bytes_accessed=20 * MIB, transcendentals=0),
        name="land_sums",
    )(
        slots, first_rows, arrived, cell, meta, area, water, cap,
        in_hbm(soil), in_hbm(porosity), in_hbm(drainage), *after,
    )


def new_soil_kernel(through, lost, canopy, soil, porosity, drainage, *rest):
    soil_new, canopy_new = rest[-2:]
    layers, block = soil.shape[:2]
    chunk = 48
    canopy_new[...] = canopy[...]
    for start in range(0, block, chunk):
        part = pl.ds(start, chunk)
        flowing = through[part, :]
        for layer in range(layers):
            filled = soil[layer, part, :] + flowing
            filled = filled - jnp.maximum(filled - porosity[layer, part, :], 0.0)
            flowing = drainage[layer, part, :] * filled
            middle = filled - flowing
            soil_new[layer, part, :] = middle - lost[part, :] if layer == 0 else middle


def new_soil(first, last, through, lost, canopy, soil, porosity, drainage, made=(), after=None):
    layers, rows = soil.shape[:2]
    block = 96
    flat = pl.BlockSpec((block, LANES), lambda i: (first + i, 0))
    deep = pl.BlockSpec((layers, block, LANES), lambda i: (0, first + i, 0))
    anywhere = pl.BlockSpec(memory_space=pl.ANY)
    more = [in_hbm(value) for value in made] + ([] if after is None else [after])
    return pl.pallas_call(
        new_soil_kernel,
        grid=(last - first,),
        in_specs=[flat, flat, flat, deep, deep, deep] + [anywhere] * len(more),
        out_specs=[deep, flat],
        out_shape=(
            jax.ShapeDtypeStruct(soil.shape, jnp.float32),
            jax.ShapeDtypeStruct((rows, LANES), jnp.float32),
        ),
        input_output_aliases={6: 0, 7: 1} if made else {},
        compiler_params=pltpu.CompilerParams(vmem_limit_bytes=VMEM_LIMIT),
        cost_estimate=pl.CostEstimate(
            flops=10**8, bytes_accessed=3 * MIB * (last - first), transcendentals=0
        ),
        name="new_soil",
    )(through, lost, canopy, in_hbm(soil), in_hbm(porosity), in_hbm(drainage), *more)


def halo_parts(value, axis, dim, width):
    count, length = (lax.axis_size(axis), value.shape[dim])
    up = [(i, i + 1) for i in range(count - 1)]
    down = [(j, i) for i, j in up]
    last = lax.slice_in_dim(value, length - width, length, axis=dim)
    initial = lax.slice_in_dim(value, 0, width, axis=dim)
    return lax.ppermute(last, axis, up), lax.ppermute(initial, axis, down)


def rate_and_code_kernel(rate, code, _, out):
    out[0] = rate[...]
    out[1] = code[...].astype(jnp.float32)


def rate_and_code(rate, code, after):
    return pl.pallas_call(
        rate_and_code_kernel,
        in_specs=[pl.BlockSpec(memory_space=pltpu.VMEM)] * 2 + [pl.BlockSpec(memory_space=pl.ANY)],
        out_shape=jax.ShapeDtypeStruct((2,) + rate.shape, jnp.float32),
        compiler_params=pltpu.CompilerParams(vmem_limit_bytes=VMEM_LIMIT),
        cost_estimate=pl.CostEstimate(flops=10**5, bytes_accessed=10**5, transcendentals=0),
        name="rate_and_code",
    )(rate, code, after)


def edge_columns_kernel(tall, _, first, last):
    arrays, height, width = tall.shape
    for number in range(arrays):
        values = tall[number]
        values = jnp.concatenate([values, jnp.zeros((LANES - height, width), jnp.float32)], axis=0)
        columns = jnp.transpose(values)
        part = pl.ds(number * ITERS, ITERS)
        first[part, :] = columns[:ITERS]
        last[part, :] = columns[width - ITERS :]


def edge_columns(tall, after):
    shape = jax.ShapeDtypeStruct((2 * ITERS, LANES), jnp.float32)
    return pl.pallas_call(
        edge_columns_kernel,
        in_specs=[pl.BlockSpec(memory_space=pltpu.VMEM), pl.BlockSpec(memory_space=pl.ANY)],
        out_shape=(shape, shape),
        compiler_params=pltpu.CompilerParams(vmem_limit_bytes=VMEM_LIMIT),
        cost_estimate=pl.CostEstimate(flops=10**6, bytes_accessed=10**5, transcendentals=0),
        name="edge_columns",
    )(tall, after)


def extended(own, strip):
    height = own.shape[0]

    def column_strip(right):
        middle, above, below = strip(0, right), strip(-1, right), strip(1, right)
        return jnp.concatenate(
            [
                middle[:, :height],
                below[:, :ITERS],
                above[:, height - ITERS : height],
                jnp.zeros((ITERS, LANES - height - 2 * ITERS), jnp.float32),
            ],
            axis=1,
        )

    gap = jnp.zeros((LANES - 2 * ITERS, LANES), jnp.float32)
    sides = jnp.concatenate([column_strip(1), gap, column_strip(-1)], axis=0)
    sides = jnp.transpose(sides)[: height + 2 * ITERS]
    tall = jnp.concatenate([own, strip(1, 0), strip(-1, 0)], axis=0)
    return jnp.concatenate([tall, sides], axis=1)


def neighbour(down, right):
    row, column = lax.axis_index(region) + down, lax.axis_index("col") + right
    there = (row >= 0) & (row < lax.axis_size(region))
    there &= (column >= 0) & (column < lax.axis_size("col"))
    return jnp.where(there, row * lax.axis_size("col") + column, 0), jnp.where(there, 1.0, 0.0)


def static_halo_kernel(tall, before, after, out):
    height, width = tall.shape[1:]
    gap = jnp.zeros((LANES - 2 * ITERS, LANES), jnp.float32)
    for number in range(2):
        part = pl.ds(number * ITERS, ITERS)
        sides = jnp.transpose(jnp.concatenate([after[part, :], gap, before[part, :]], axis=0))
        out[number, :, :width] = tall[number]
        out[number, :, width:] = sides[:height]


def static_halo(tall, before, after):
    arrays, height, width = tall.shape
    return pl.pallas_call(
        static_halo_kernel,
        out_shape=jax.ShapeDtypeStruct((arrays, height, width + LANES), jnp.float32),
        compiler_params=pltpu.CompilerParams(vmem_limit_bytes=VMEM_LIMIT),
        cost_estimate=pl.CostEstimate(flops=10**6, bytes_accessed=10**6, transcendentals=0),
        name="static_halo",
    )(tall, before, after)


def river_kernel(state, strips, fixed, _, out):
    height, width = state.shape

    def strip(down, right):
        device, there = neighbour(down, right)
        return strips[pl.ds(device * ITERS, ITERS), :] * there

    storage = extended(state[...], strip)
    rate = fixed[0]
    code = fixed[1]
    rows, cols = storage.shape
    for _ in range(ITERS):
        outflow = rate * storage
        inflow = jnp.zeros_like(storage)
        for col_step in (-1, 0, 1):
            column = jnp.zeros_like(storage)
            for bit, (row_step, step) in enumerate(directions):
                if step != col_step:
                    continue
                leaving = jnp.where(code == float(1 << bit), outflow, 0.0)
                if row_step:
                    leaving = pltpu.roll(leaving, row_step % rows, 0)
                column = column + leaving
            if col_step:
                column = pltpu.roll(column, col_step % cols, 1)
            inflow = inflow + column
        storage = storage - outflow + inflow
    out[...] = storage[:height, :width]


def river(state, strips, fixed, after):
    return pl.pallas_call(
        river_kernel,
        in_specs=[pl.BlockSpec(memory_space=pltpu.VMEM)] * 3 + [pl.BlockSpec(memory_space=pl.ANY)],
        out_shape=jax.ShapeDtypeStruct(state.shape, jnp.float32),
        compiler_params=pltpu.CompilerParams(vmem_limit_bytes=VMEM_LIMIT),
        cost_estimate=pl.CostEstimate(flops=10**7, bytes_accessed=1 * MIB, transcendentals=0),
        name="river_steps",
    )(state, strips, fixed, in_hbm(after))


def exchange(value, over=axes):
    return lax.all_to_all(value, over, split_axis=0, concat_axis=0, tiled=True)


def shards(
    forcing,
    river_storage,
    river_rate,
    flow_code,
    home_slot,
    home_offset,
    worker_list,
    patch_cell,
    patch_area,
    canopy_water,
    canopy_cap,
    soil_water,
    porosity,
    drainage,
):
    homes = lax.axis_size(region) * lax.axis_size("col")
    capacity = home_slot.shape[1] // homes
    grid_rows, grid_cols = river_storage.shape
    lane_rows = grid_rows * grid_cols // LANES
    forcing = forcing.reshape(3, lane_rows, LANES)
    swap = [(0, 1), (1, 0)]
    far_slot = lax.ppermute(home_slot, "half", swap)
    far_offset = lax.ppermute(home_offset, "half", swap)
    far_forcing = lax.ppermute(forcing, "half", swap)
    own = pack_own(homes // 2, capacity, home_slot, home_offset, forcing)
    outgoing = pack_both(homes // 2, capacity, own, far_slot, far_offset, far_forcing)
    arrived = exchange(outgoing, ("near", "col"))
    home = worker_list // capacity
    position = worker_list - home * capacity
    pairs = capacity // 2
    own_half = home // (homes // 2) == lax.axis_index("half")
    first_rows = home % (homes // 2) * (6 * pairs) + jnp.where(own_half, 0, 3 * pairs)
    first_rows = first_rows + position // 2 + position % 2 * pairs
    meta = segment_plan(patch_cell, worker_list[:, None])
    fixed = rate_and_code(river_rate, flow_code, outgoing)
    above, below = halo_parts(fixed, region, 1, ITERS)
    through, lost, canopy, sums = land_sums(
        (homes * capacity, LANES), pairs, worker_list, first_rows, arrived, patch_cell, meta,
        patch_area, canopy_water, canopy_cap, soil_water, porosity, drainage, (above, below),
    )
    returned = exchange(sums)
    layers_of = (through, lost, canopy, soil_water, porosity, drainage)
    blocks = worker_list.shape[0] // 96
    early = blocks * 3 // 5
    made = new_soil(0, early, *layers_of)
    code, place = unpack_plan(homes, capacity, lane_rows, home_slot, home_offset)
    fixed = jnp.concatenate([fixed, below, above], axis=1)
    initial, last = edge_columns(fixed, sums)
    count = lax.axis_size("col")
    before = lax.ppermute(last, "col", [(i, i + 1) for i in range(count - 1)])
    after = lax.ppermute(initial, "col", [(i + 1, i) for i in range(count - 1)])
    fixed = static_halo(fixed, before, after)
    cell_runoff, storage, strips = unpack_runoff(
        homes, returned, code, place, river_storage.reshape(lane_rows, LANES), fixed,
        in_hbm(made[1]),
    )
    soil_new, canopy_new = new_soil(early, blocks, *layers_of, made, strips)
    cell_evap = unpack_evap(returned, code, place)
    river_new = river(
        storage.reshape(river_storage.shape), exchange(strips), fixed, canopy_new
    )
    return (
        soil_new,
        canopy_new,
        cell_runoff.reshape(river_storage.shape),
        cell_evap.reshape(river_storage.shape),
        river_new,
    )


def solution(mesh):
    rows, cols = mesh.devices.shape
    mesh = jax.sharding.Mesh(mesh.devices.reshape(2, rows // 2, cols), axes)
    placed = (
        P(None, region, "col"),
        P(region, "col"),
        P(region, "col"),
        P(region, "col"),
        P(axes, None),
        P(axes, None),
        P(axes),
        P(axes, None),
        P(axes, None),
        P(axes, None),
        P(axes, None),
        P(None, axes, None),
        P(None, axes, None),
        P(None, axes, None),
    )
    return jax.shard_map(
        shards,
        mesh=mesh,
        in_specs=placed,
        out_specs=(
            P(None, axes, None),
            P(axes, None),
            P(region, "col"),
            P(region, "col"),
            P(region, "col"),
        ),
        check_vma=False,
    )
```
